32 devices in a mesh: sta: 8 (over z, y), seg: 4 (over x, core).
Axes of the slice: x: 2, y: 2, z: 4, core: 2. Of those that a mesh axis runs over, the one named last changes fastest.
Arguments:
- records: float32 [128, 16, 2048], P('sta', 'seg'), as said below
- plan: int32 [4, 8], replicated, may hold values from 0 to 7, as said below
Outputs:
- correlations: float32 [2048, 4, 2048], P('seg', None, 'sta')
The draws below stay inside these ranges and needn't reach their ends.
Inputs may be any that keep to these rules, and one draw needn't show every extreme that they name: Row r pairs the 8 blocks: plan[r, plan[r, b]] = b and plan[r, b] != b; no two rows pair the same two blocks. `records`: raw ground-motion samples.
All inputs are finite; a program needn't handle non-finite values.
Results may differ from the reference program's by a relative error of at most 0.0075.
Values may be sent and summed in bfloat16 or wider, within the bound.
No kernel may reach another device: no remote copies, remote signals or barrier semaphores. Data moves between devices by JAX's collectives and lax.ppermute only.
A program may use at most 128 MiB of HBM per device.

```python
import math
import jax
import jax.numpy as jnp
from jax import lax

S = 16
NWIN = 4
WLEN = 2048
NBIN = 1024
HALF = 64
ROUNDS = 4
NB = 8
STATIONS = 128
WINS = 16
LAGS = 2048
N_SEG = 4


def draw_records(key, part):
    subkeys = jax.random.split(key, 7)
    noise_part = jax.random.normal(subkeys[0], (STATIONS, WINS, WLEN), jnp.float32)
    top_env = 10.0
    common_weight = 0.1
    envelope = jnp.exp(jax.random.uniform(subkeys[1], (STATIONS, WINS, WLEN // 128), jnp.float32, 0.0, math.log(top_env)))
    envelope = jnp.repeat(envelope, 128, axis=2)
    delay_reach = WLEN // 2
    source = jax.random.normal(subkeys[2], (WINS, WLEN + delay_reach), jnp.float32)
    delays = jax.random.randint(subkeys[3], (STATIONS,), 0, delay_reach).astype(jnp.int32)
    position = jnp.arange(WLEN, dtype=jnp.int32)
    shared = source[:, position[None, :] + delays[:, None]]
    shared = jnp.transpose(shared, (1, 0, 2))
    loudness = jnp.exp(jax.random.uniform(subkeys[4], (STATIONS, 1, 1), jnp.float32, 0.0, math.log(5.0)))
    frequency = jax.random.uniform(subkeys[5], (STATIONS, 1, 1), jnp.float32, 0.5, 3.0)
    offset = jax.random.uniform(subkeys[6], (STATIONS, WINS, 1), jnp.float32, -math.pi, math.pi)
    tone_part = loudness * jnp.sin(2.0 * math.pi * frequency * position.astype(jnp.float32)[None, None, :] / 40.0 + offset)
    return envelope * (noise_part + common_weight * shared) + tone_part


def draw_plan(key, part):
    first_key, second_key = jax.random.split(key)
    labels = jax.random.permutation(first_key, NB).astype(jnp.int32)
    picked = jax.random.permutation(second_key, NB - 1)[:ROUNDS].astype(jnp.int32)
    slot_index = jnp.arange(NB, dtype=jnp.int32)

    def one_round(round_pivot):
        mirror = jnp.mod(2 * round_pivot - slot_index, NB - 1)
        partner = jnp.where(slot_index == NB - 1, round_pivot, jnp.where(slot_index == round_pivot, NB - 1, mirror))
        return jnp.zeros((NB,), jnp.int32).at[labels].set(labels[partner])
    return jax.vmap(one_round)(picked).astype(jnp.int32)


def setup_inputs(seed: int = 0) -> dict:
    arg_keys = jax.random.split(jax.random.key(seed), 3)
    return {
        "records": draw_records(jax.random.fold_in(arg_keys[2], 71), 0),
        "plan": draw_plan(jax.random.fold_in(arg_keys[2], 71), 0),
    }


def band_mean(values, half_width):
    row_count, length = values.shape
    block_width = 2 * half_width
    blocks_count = length // block_width
    inside = jnp.arange(block_width, dtype=jnp.int32)
    source = inside[:, None]
    target = inside[None, :]
    inner_band = (jnp.abs(source - target) <= half_width).astype(jnp.bfloat16)
    before = (target + block_width - source <= half_width).astype(jnp.bfloat16)
    after_band = (source + block_width - target <= half_width).astype(jnp.bfloat16)
    blocks = values.reshape(row_count, blocks_count, block_width)
    earlier = jnp.pad(blocks[:, :-1], ((0, 0), (1, 0), (0, 0)))
    following = jnp.pad(blocks[:, 1:], ((0, 0), (0, 1), (0, 0)))
    flat_shape = (row_count * blocks_count, block_width)
    running = jnp.dot(blocks.reshape(flat_shape), inner_band, preferred_element_type=jnp.float32)
    running = running + jnp.dot(earlier.reshape(flat_shape), before, preferred_element_type=jnp.float32)
    running = running + jnp.dot(following.reshape(flat_shape), after_band, preferred_element_type=jnp.float32)
    position = jnp.arange(length, dtype=jnp.int32)
    counted = (jnp.minimum(position, half_width) + jnp.minimum(length - 1 - position, half_width) + 1).astype(jnp.float32)
    return running.reshape(row_count, length) / counted

def forward_table(first_bin, bin_count, length, transform):
    samples = jnp.arange(length, dtype=jnp.int32)
    bin_index = first_bin + jnp.arange(bin_count, dtype=jnp.int32)
    phase_int = samples[:, None] * bin_index[None, :] % transform
    angles = phase_int.astype(jnp.float32) * (2.0 * math.pi / transform)
    return jnp.concatenate([jnp.cos(angles), -jnp.sin(angles)], axis=1).astype(jnp.bfloat16)

def lag_table(first_lag, lag_count, bin_total, transform):
    lag_index = first_lag + jnp.arange(lag_count, dtype=jnp.int32)
    bin_index = jnp.arange(bin_total, dtype=jnp.int32)
    phase_int = lag_index[:, None] * bin_index[None, :] % transform
    angles = phase_int.astype(jnp.float32) * (2.0 * math.pi / transform)
    weight = jnp.where(bin_index == 0, 1.0, 2.0).astype(jnp.float32)[None, :]
    paired = jnp.stack([weight * jnp.cos(angles), -weight * jnp.sin(angles)], axis=2)
    return paired.reshape(lag_count, 2 * bin_total).astype(jnp.bfloat16)

def reference(records, plan):
    fourier = forward_table(0, NBIN, WLEN, 2 * WLEN)

    def prepare(block):
        signal = block.reshape(S * WINS, WLEN)
        mean_level = band_mean(jnp.abs(signal).astype(jnp.bfloat16), HALF)
        flattened = (signal / (mean_level + 1e-05)).astype(jnp.bfloat16)
        product = jnp.dot(flattened, fourier, preferred_element_type=jnp.float32)
        spec_real = product[:, :NBIN]
        spec_imag = product[:, NBIN:]
        magnitude = jnp.sqrt(spec_real * spec_real + spec_imag * spec_imag).astype(jnp.bfloat16)
        smooth = band_mean(magnitude, HALF)
        whitened = jnp.stack([spec_real / (smooth + 1e-06), spec_imag / (smooth + 1e-06)], axis=1).astype(jnp.bfloat16)
        return whitened.reshape(S, WINS, 2, NBIN)
    whitened = lax.map(prepare, records.reshape(NB, S, WINS, WLEN))
    inverse = lax.optimization_barrier(lag_table(0, LAGS, NBIN, 2 * WLEN)).astype(jnp.float32)
    scaling = 1.0 / math.sqrt(4.0 * NBIN * WINS)

    def round_corr(partners):

        def pair_block(block_index):
            own_block = whitened[block_index].astype(jnp.float32).reshape(S, N_SEG, NWIN, 2, NBIN)
            partner = whitened[partners[block_index]].astype(jnp.float32).reshape(S, N_SEG, NWIN, 2, NBIN)
            turned = jnp.stack([-partner[:, :, :, 1], partner[:, :, :, 0]], axis=3)
            real_cross = jnp.einsum('sgwck,tgwck->gkst', own_block, partner, precision=lax.Precision.HIGHEST)
            imag_cross = jnp.einsum('sgwck,tgwck->gkst', own_block, turned, precision=lax.Precision.HIGHEST)
            crossed = jnp.stack([real_cross, imag_cross], axis=2).astype(jnp.bfloat16)
            crossed = lax.optimization_barrier(crossed).astype(jnp.float32)
            return lax.optimization_barrier(jnp.sum(crossed, axis=0)).reshape(2 * NBIN, S * S)
        blocks = lax.map(pair_block, jnp.arange(NB, dtype=jnp.int32))
        operand = jnp.transpose(blocks, (1, 0, 2)).reshape(2 * NBIN, NB * S * S)
        return jnp.dot(inverse, operand, precision=lax.Precision.HIGHEST, preferred_element_type=jnp.float32) * scaling
    lagged = lax.map(round_corr, plan)
    return jnp.transpose(lagged, (1, 0, 2))
```

```python
import functools
import math

import jax
import jax.numpy as jnp
import ml_dtypes
import numpy as np
from jax import lax
from jax.experimental import pallas as pl
from jax.experimental.pallas import tpu as pltpu
from jax.sharding import PartitionSpec as P

NBIN = 1024
HALF = 64
ROUNDS = 4
LAGS = 2048
LANES = 128
TILES = NBIN // LANES
BF = jnp.bfloat16
F32 = jnp.float32


def make_table(rows, transform):
    phase = (np.arange(rows)[:, None] * np.arange(NBIN)[None, :]) % transform
    angle = phase * (2.0 * math.pi / transform)
    return np.concatenate([np.cos(angle), -np.sin(angle)], axis=1).astype(ml_dtypes.bfloat16)


def make_band():
    source = np.arange(3 * LANES)[:, None] - LANES
    target = np.arange(LANES)[None, :]
    return (np.abs(source - target) <= HALF).astype(ml_dtypes.bfloat16)


def make_counts(length):
    position = np.arange(length)
    counted = np.minimum(position, HALF) + np.minimum(length - 1 - position, HALF) + 1
    return (1.0 / counted).astype(np.float32)[None, :]


def make_placing(stations, quarter, parts):
    width = stations * quarter
    place = np.zeros((parts, 2 * width, 2 * stations * stations), np.float32)
    for part in range(parts):
        for second in range(2):
            for s in range(stations):
                for t in range(quarter):
                    row = second * width + s * quarter + t
                    column = (second * stations + s) * stations + part * quarter + t
                    place[part, row, column] = 1.0
    return place.astype(ml_dtypes.bfloat16)


def lane_cycle(values):
    phase = lax.broadcasted_iota(jnp.int32, (1, LANES), 1) % 4
    out = jnp.full((1, LANES), values[3], F32)
    for index in range(3):
        out = jnp.where(phase == index, values[index], out)
    return out


def even_lanes(shape):
    return lax.broadcasted_iota(jnp.int32, shape, 1) % 2 == 0


def banded_sum(stack, values, band):
    rows, length = values.shape
    blocks = length // LANES
    zero = jnp.zeros((rows, LANES), BF)
    for j in range(blocks):
        at = pl.ds(j * rows, rows)
        for k in range(3):
            b = j + k - 1
            block = values[:, b * LANES : (b + 1) * LANES] if 0 <= b < blocks else zero
            stack[at, k * LANES : (k + 1) * LANES] = block
    total = jnp.dot(stack[: blocks * rows, :], band, preferred_element_type=F32)
    return [total[j * rows : (j + 1) * rows, :] for j in range(blocks)]


def prep_kernel(
    quarter, records, table_hbm, band, count_t, count_f, white, *rest
):
    parts = len(rest) - 6
    quarters = rest[:parts]
    table, stack, flat, spread, sem, _ = rest[parts:]
    copy = pltpu.make_async_copy(table_hbm, table, sem)
    copy.start()
    stations, windows, length = records.shape
    rows = stations * windows
    half = length // 2
    signal = jnp.concatenate([records[:, w, :] for w in range(windows)], axis=0)
    band_values = band[...]
    sums = banded_sum(stack, jnp.abs(signal).astype(BF), band_values)
    for j, total in enumerate(sums):
        at = slice(j * LANES, (j + 1) * LANES)
        level = total * count_t[:, at]
        value = (signal[:, at] / (level + 1e-05)).astype(BF)
        if j * LANES < half:
            flat[:rows, at] = value
        else:
            flat[rows:, j * LANES - half : (j + 1) * LANES - half] = value
    copy.wait()
    product = jnp.dot(flat[...], table[...], preferred_element_type=F32)
    even = even_lanes((rows, LANES))
    sign_real = lane_cycle([1.0, 1.0, -1.0, -1.0])
    sign_imag = lane_cycle([1.0, -1.0, -1.0, 1.0])
    reals, imags, mags = [], [], []
    for j in range(TILES):
        at = slice(j * LANES, (j + 1) * LANES)
        at_imag = slice(NBIN + j * LANES, NBIN + (j + 1) * LANES)
        later_real, later_imag = product[rows:, at], product[rows:, at_imag]
        real = product[:rows, at] + sign_real * jnp.where(even, later_real, later_imag)
        imag = product[:rows, at_imag] + sign_imag * jnp.where(even, later_imag, later_real)
        reals.append(real)
        imags.append(imag)
        mags.append(jnp.sqrt(real * real + imag * imag).astype(BF))
    sums = banded_sum(stack, jnp.concatenate(mags, axis=1), band_values)
    for j, total in enumerate(sums):
        at = slice(j * LANES, (j + 1) * LANES)
        smooth = total * count_f[:, at] + 1e-06
        spread[pl.ds(j, rows, stride=2 * TILES), :] = reals[j] / smooth
        spread[pl.ds(TILES + j, rows, stride=2 * TILES), :] = imags[j] / smooth
    me = lax.axis_index("seg")
    out = spread[...].reshape(windows, stations, 2 * TILES, LANES).astype(BF)
    white[...] = out
    for j in range(parts):
        first = (me ^ j) * quarter
        for w in range(windows):
            quarters[j][w] = white[w, pl.ds(first, quarter)]


def prepare(records, table, parts):
    stations, windows, length = records.shape
    rows = stations * windows
    quarter = stations // parts
    band = make_band()
    small = jax.ShapeDtypeStruct((windows, quarter, 2 * TILES, LANES), BF)
    vmem = pl.BlockSpec(memory_space=pltpu.VMEM)
    return pl.pallas_call(
        functools.partial(prep_kernel, quarter),
        out_shape=[jax.ShapeDtypeStruct((windows, stations, 2 * TILES, LANES), BF)]
        + [small] * parts,
        in_specs=[vmem, pl.BlockSpec(memory_space=pl.ANY), vmem, vmem, vmem],
        out_specs=[vmem] * (parts + 1),
        scratch_shapes=[
            pltpu.VMEM(table.shape, BF),
            pltpu.VMEM((rows * (length // LANES), 3 * LANES), BF),
            pltpu.VMEM((2 * rows, length // 2), BF),
            pltpu.VMEM((rows * 2 * TILES, LANES), F32),
            pltpu.SemaphoreType.DMA,
            pltpu.SMEM((1,), jnp.int32),
        ],
        compiler_params=pltpu.CompilerParams(vmem_limit_bytes=40 * 2**20),
        cost_estimate=pl.CostEstimate(
            flops=2 * 2 * rows * (length // 2) * 2 * NBIN, bytes_accessed=6 * 2**20, transcendentals=0
        ),
        name="prep",
    )(records, table, band, make_counts(length), make_counts(NBIN))


def ring_place(block, count):
    return jnp.where(block % 2 == 0, block // 2, count - 1 - block // 2)


def partner_steps(plan, count):
    me = lax.axis_index("sta")
    mine = ring_place(me, count)
    steps, keys = [], []
    for number in range(ROUNDS):
        step = (ring_place(plan[number, me], count) - mine + count) % count
        steps.append(step)
        keys.append(jnp.minimum(step, count - step) * ROUNDS + number)
    ranks = []
    for number in range(ROUNDS):
        rank = jnp.int32(0)
        for other in range(ROUNDS):
            if other != number:
                rank = rank + jnp.where(keys[other] < keys[number], 1, 0)
        ranks.append(rank)
    return steps, ranks


def cross_kernel(first_slot, slots, count, scaling, offsets, parts, plan, table_hbm, *rest):
    owns = rest[:parts]
    candidates = rest[parts : parts + len(offsets)]
    rest = rest[parts + len(offsets) :]
    outs = rest[:parts]
    table, own_raw, other_raw, own, other, crossed, operand, result, sems = rest[parts:]
    windows, stations = owns[0].shape[:2]
    all_windows = windows * parts
    quarter = other_raw.shape[2]
    width = stations * quarter
    columns = slots * width

    table_copy = pltpu.make_async_copy(table_hbm, table, sems.at[0])
    steps, ranks = partner_steps(plan, count)
    own_copies = [
        pltpu.make_async_copy(owns[j], own_raw.at[pl.ds(j * windows, windows)], sems.at[1 + j])
        for j in range(parts)
    ]
    for copy in own_copies:
        copy.start()
    for slot in range(slots):
        step = jnp.int32(0)
        for number in range(ROUNDS):
            step = jnp.where(ranks[number] == first_slot + slot, steps[number], step)
        for (offset, start), candidate in zip(offsets, candidates):
            size = candidate.shape[0]

            @pl.when(step == offset)
            def _(candidate=candidate, slot=slot, start=start, size=size):
                pltpu.make_async_copy(
                    candidate, other_raw.at[slot, pl.ds(start, size)], sems.at[1 + parts + slot]
                ).start()

    table_copy.start()
    for copy in own_copies:
        copy.wait()

    def widen_own(w, carry):
        raw = own_raw[w].astype(F32)
        real, imag = raw[:, :TILES], raw[:, TILES:]
        own[0, w] = real + imag
        own[1, w] = real
        own[2, w] = imag
        return carry

    lax.fori_loop(0, all_windows, widen_own, 0)
    for slot in range(slots):
        pltpu.make_async_copy(
            other_raw.at[slot], other_raw.at[slot], sems.at[1 + parts + slot]
        ).wait()

        def widen_other(w, carry, slot=slot):
            raw = other_raw[slot, w].astype(F32)
            real, imag = raw[:, :TILES], raw[:, TILES:]
            other[0, slot, w] = real
            other[1, slot, w] = real + imag
            other[2, slot, w] = imag - real
            return carry

        lax.fori_loop(0, all_windows, widen_other, 0)

    group = 4
    groups = stations // group
    first_bin = (lax.broadcasted_iota(jnp.int32, (TILES, LANES), 0) == 0) & (
        lax.broadcasted_iota(jnp.int32, (TILES, LANES), 1) == 0
    )
    weight = jnp.where(first_bin, 1.0, 2.0).astype(F32)

    def one_group(index, carry):
        slot = index // groups
        first = (index % groups) * group

        def sums(kind):
            totals = [None] * (group * quarter)
            for w in range(all_windows):
                left = [own[kind, w, first + s] for s in range(group)]
                right = [other[kind, slot, w, t] for t in range(quarter)]
                for s in range(group):
                    for t in range(quarter):
                        term = left[s] * right[t]
                        place = s * quarter + t
                        totals[place] = term if w == 0 else totals[place] + term
            return totals

        base = slot * width + first * quarter
        shared = sums(0)
        third = sums(2)
        for place in range(group * quarter):
            at = pl.multiple_of((base + place) * 2 * TILES, 2 * TILES)
            crossed[pl.ds(at, TILES), :] = (shared[place] + third[place]) * weight
        second = sums(1)
        for place in range(group * quarter):
            at = pl.multiple_of((base + place) * 2 * TILES + TILES, TILES)
            crossed[pl.ds(at, TILES), :] = (shared[place] - second[place]) * weight
        return carry

    lax.fori_loop(0, slots * groups, one_group, 0)

    even = even_lanes((columns, LANES))
    sign_real = lane_cycle([1.0, -1.0, -1.0, 1.0])
    sign_imag = lane_cycle([1.0, 1.0, -1.0, -1.0])
    for j in range(TILES):
        at = slice(j * LANES, (j + 1) * LANES)
        at_imag = slice(NBIN + j * LANES, NBIN + (j + 1) * LANES)
        real = crossed[pl.ds(j, columns, stride=2 * TILES), :]
        imag = crossed[pl.ds(TILES + j, columns, stride=2 * TILES), :]
        operand[:columns, at] = real.astype(BF)
        operand[:columns, at_imag] = imag.astype(BF)
        operand[columns:, at] = (sign_real * jnp.where(even, real, imag)).astype(BF)
        operand[columns:, at_imag] = (sign_imag * jnp.where(even, imag, real)).astype(BF)
    table_copy.wait()
    share = outs[0].shape[0]
    per_half = table.shape[0] // share
    for q in range(per_half):
        block = lax.dot_general(
            table[q * share : (q + 1) * share, :],
            operand[...],
            (((1,), (1,)), ((), ())),
            preferred_element_type=F32,
        )
        block = (block * scaling).astype(BF)
        for h in range(2):
            result[h * per_half + q] = block[:, h * columns : (h + 1) * columns]
    me = lax.axis_index("seg")
    for j in range(parts):
        outs[j][...] = result[me ^ j]


def cross_lags(plan, table, owns, offsets, candidates, first_slot, slots, count, scaling):
    parts = len(owns)
    windows, stations = owns[0].shape[:2]
    all_windows = windows * parts
    quarter = candidates[0].shape[1]
    columns = slots * stations * quarter
    share = LAGS // parts
    smem = pl.BlockSpec(memory_space=pltpu.SMEM)
    any_space = pl.BlockSpec(memory_space=pl.ANY)
    vmem = pl.BlockSpec(memory_space=pltpu.VMEM)
    return pl.pallas_call(
        functools.partial(
            cross_kernel, first_slot, slots, count, scaling, tuple(offsets), parts
        ),
        out_shape=[jax.ShapeDtypeStruct((share, columns), BF)] * parts,
        in_specs=[smem] + [any_space] * (1 + parts + len(candidates)),
        out_specs=[vmem] * parts,
        scratch_shapes=[
            pltpu.VMEM(table.shape, BF),
            pltpu.VMEM((all_windows, stations, 2 * TILES, LANES), BF),
            pltpu.VMEM((slots, all_windows, quarter, 2 * TILES, LANES), BF),
            pltpu.VMEM((3, all_windows, stations, TILES, LANES), F32),
            pltpu.VMEM((3, slots, all_windows, quarter, TILES, LANES), F32),
            pltpu.VMEM((columns * 2 * TILES, LANES), F32),
            pltpu.VMEM((2 * columns, 2 * NBIN), BF),
            pltpu.VMEM((parts, share, columns), BF),
            pltpu.SemaphoreType.DMA((1 + parts + slots,)),
        ],
        compiler_params=pltpu.CompilerParams(vmem_limit_bytes=40 * 2**20),
        cost_estimate=pl.CostEstimate(
            flops=2 * LAGS * 2 * NBIN * columns * 2, bytes_accessed=8 * 2**20, transcendentals=0
        ),
        name="cross",
    )(plan, table, *owns, *candidates)


def place_kernel(count, groups, parts, plan, place, *rest):
    pieces = rest[: groups * parts]
    out, result = rest[groups * parts :]
    share, rounds, pairs = out.shape
    me = lax.axis_index("seg")
    _, ranks = partner_steps(plan, count)
    matrix = jnp.concatenate([place[me ^ j] for j in range(parts)], axis=0)
    for p in range(groups):
        joined = jnp.concatenate([pieces[p * parts + j][...] for j in range(parts)], axis=1)
        block = jnp.dot(joined, matrix, preferred_element_type=F32)
        result[2 * p] = block[:, :pairs]
        result[2 * p + 1] = block[:, pairs:]
    for number in range(rounds):
        out[:, number, :] = result[ranks[number]]


def place_lags(plan, pieces, parts, count, stations):
    groups = len(pieces) // parts
    share = pieces[0].shape[0]
    pairs = stations * stations
    vmem = pl.BlockSpec(memory_space=pltpu.VMEM)
    return pl.pallas_call(
        functools.partial(place_kernel, count, groups, parts),
        out_shape=jax.ShapeDtypeStruct((share, ROUNDS, pairs), F32),
        in_specs=[pl.BlockSpec(memory_space=pltpu.SMEM)] + [vmem] * (1 + len(pieces)),
        out_specs=vmem,
        scratch_shapes=[pltpu.VMEM((ROUNDS, share, pairs), F32)],
        compiler_params=pltpu.CompilerParams(vmem_limit_bytes=40 * 2**20),
        cost_estimate=pl.CostEstimate(
            flops=2 * share * 4 * pairs * ROUNDS * pairs, bytes_accessed=4 * 2**20, transcendentals=0
        ),
        name="place",
    )(plan, make_placing(stations, stations // parts, parts), *pieces)


def exchange(pieces):
    parts = len(pieces)
    out = [pieces[0]]
    for j in range(1, parts):
        out.append(lax.ppermute(pieces[j], "seg", [(i, i ^ j) for i in range(parts)]))
    return out


def per_device(records, plan):
    stations, windows, length = records.shape
    count = lax.axis_size("sta")
    parts = lax.axis_size("seg")
    table = jnp.asarray(make_table(length // 2, 2 * length))
    scaling = 1.0 / math.sqrt(4.0 * NBIN * windows * parts)

    white, *quarters = prepare(records, table, parts)
    shared = jnp.concatenate(exchange(quarters), axis=0)
    owns = exchange([white] * parts)

    ring = sorted(range(count), key=lambda b: b // 2 if b % 2 == 0 else count - 1 - b // 2)
    forward = [(ring[i], ring[(i + 1) % count]) for i in range(count)]
    backward = [(ring[i], ring[i - 1]) for i in range(count)]
    offsets, candidates = [], []
    from_left = from_right = shared
    for step in range(1, (count - 1) // 2 + 1):
        from_left = lax.ppermute(from_left, "sta", forward)
        from_right = lax.ppermute(from_right, "sta", backward)
        offsets += [(count - step, 0), (step, 0)]
        candidates += [from_left, from_right]
    early = (list(offsets), list(candidates))
    if count % 2 == 0:
        middle = shared.shape[0] // 2
        offsets += [(count // 2, 0), (count // 2, middle)]
        candidates += [
            lax.ppermute(from_left[:middle], "sta", forward),
            lax.ppermute(from_right[middle:], "sta", backward),
        ]
    pieces = []
    for first_slot, (spots, blocks) in ((0, early), (2, (offsets, candidates))):
        lags = cross_lags(plan, table, owns, spots, blocks, first_slot, 2, count, scaling)
        pieces += exchange(lags)
    return place_lags(plan, pieces, parts, count, stations)


def solution(mesh):
    in_specs = (P("sta", "seg", None), P())
    out_specs = P("seg", None, "sta")
    return jax.shard_map(
        per_device, mesh=mesh, in_specs=in_specs, out_specs=out_specs, check_vma=False
    )
```

```python
import functools
import math

import jax
import jax.numpy as jnp
import ml_dtypes
import numpy as np
from jax import lax
from jax.experimental import pallas as pl
from jax.experimental.pallas import tpu as pltpu
from jax.sharding import PartitionSpec as P

NBIN = 1024
HALF = 64
ROUNDS = 4
LAGS = 2048
LANES = 128
TILES = NBIN // LANES
BF = jnp.bfloat16
F32 = jnp.float32


def make_table(rows, transform):
    phase = (np.arange(rows)[:, None] * np.arange(NBIN)[None, :]) % transform
    angle = phase * (2.0 * math.pi / transform)
    return np.concatenate([np.cos(angle), -np.sin(angle)], axis=1).astype(ml_dtypes.bfloat16)


def band_matrix():
    source = lax.broadcasted_iota(jnp.int32, (3 * LANES, LANES), 0) - LANES
    target = lax.broadcasted_iota(jnp.int32, (3 * LANES, LANES), 1)
    return jnp.where(jnp.abs(source - target) <= HALF, 1.0, 0.0).astype(BF)


def inverse_count(block, length):
    position = lax.broadcasted_iota(jnp.int32, (1, LANES), 1) + block * LANES
    counted = jnp.minimum(position, HALF) + jnp.minimum(length - 1 - position, HALF) + 1
    return 1.0 / counted.astype(F32)


def make_placing(stations, quarter, parts):
    width = stations * quarter
    place = np.zeros((parts, 2 * width, 2 * stations * stations), np.float32)
    for part in range(parts):
        for second in range(2):
            for s in range(stations):
                for t in range(quarter):
                    row = second * width + s * quarter + t
                    column = (second * stations + s) * stations + part * quarter + t
                    place[part, row, column] = 1.0
    return place.astype(ml_dtypes.bfloat16)


def lane_cycle(values):
    phase = lax.broadcasted_iota(jnp.int32, (1, LANES), 1) % 4
    out = jnp.full((1, LANES), values[3], F32)
    for index in range(3):
        out = jnp.where(phase == index, values[index], out)
    return out


def even_lanes(shape):
    return lax.broadcasted_iota(jnp.int32, shape, 1) % 2 == 0


def banded_sum(stack, values, band):
    rows, length = values.shape
    blocks = length // LANES
    zero = jnp.zeros((rows, LANES), BF)
    for j in range(blocks):
        at = pl.ds(j * rows, rows)
        for k in range(3):
            b = j + k - 1
            block = values[:, b * LANES : (b + 1) * LANES] if 0 <= b < blocks else zero
            stack[at, k * LANES : (k + 1) * LANES] = block
    total = jnp.dot(stack[: blocks * rows, :], band, preferred_element_type=F32)
    return [total[j * rows : (j + 1) * rows, :] for j in range(blocks)]


def prep_kernel(quarter, records_hbm, table_hbm, white, *rest):
    parts = len(rest) - 6
    quarters = rest[:parts]
    records, table, stack, flat, spread, sems = rest[parts:]
    records_copy = pltpu.make_async_copy(records_hbm, records, sems.at[0])
    records_copy.start()
    copy = pltpu.make_async_copy(table_hbm, table, sems.at[1])
    copy.start()
    band_values = band_matrix()
    records_copy.wait()
    stations, windows, length = records.shape
    rows = stations * windows
    half = length // 2
    signal = jnp.concatenate([records[:, w, :] for w in range(windows)], axis=0)
    sums = banded_sum(stack, jnp.abs(signal).astype(BF), band_values)
    for j, total in enumerate(sums):
        at = slice(j * LANES, (j + 1) * LANES)
        level = total * inverse_count(j, length)
        value = (signal[:, at] / (level + 1e-05)).astype(BF)
        if j * LANES < half:
            flat[:rows, at] = value
        else:
            flat[rows:, j * LANES - half : (j + 1) * LANES - half] = value
    copy.wait()
    product = jnp.dot(flat[...], table[...], preferred_element_type=F32)
    even = even_lanes((rows, LANES))
    sign_real = lane_cycle([1.0, 1.0, -1.0, -1.0])
    sign_imag = lane_cycle([1.0, -1.0, -1.0, 1.0])
    reals, imags, mags = [], [], []
    for j in range(TILES):
        at = slice(j * LANES, (j + 1) * LANES)
        at_imag = slice(NBIN + j * LANES, NBIN + (j + 1) * LANES)
        later_real, later_imag = product[rows:, at], product[rows:, at_imag]
        real = product[:rows, at] + sign_real * jnp.where(even, later_real, later_imag)
        imag = product[:rows, at_imag] + sign_imag * jnp.where(even, later_imag, later_real)
        reals.append(real)
        imags.append(imag)
        mags.append(jnp.sqrt(real * real + imag * imag).astype(BF))
    sums = banded_sum(stack, jnp.concatenate(mags, axis=1), band_values)
    for j, total in enumerate(sums):
        at = slice(j * LANES, (j + 1) * LANES)
        smooth = total * inverse_count(j, NBIN) + 1e-06
        spread[pl.ds(j, rows, stride=2 * TILES), :] = reals[j] / smooth
        spread[pl.ds(TILES + j, rows, stride=2 * TILES), :] = imags[j] / smooth
    me = lax.axis_index("seg")
    out = spread[...].reshape(windows, stations, 2 * TILES, LANES).astype(BF)
    white[...] = out
    for j in range(parts):
        first = (me ^ j) * quarter
        for w in range(windows):
            quarters[j][w] = white[w, pl.ds(first, quarter)]


def prepare(records, table, parts):
    stations, windows, length = records.shape
    rows = stations * windows
    quarter = stations // parts
    small = jax.ShapeDtypeStruct((windows, quarter, 2 * TILES, LANES), BF)
    vmem = pl.BlockSpec(memory_space=pltpu.VMEM)
    return pl.pallas_call(
        functools.partial(prep_kernel, quarter),
        out_shape=[jax.ShapeDtypeStruct((windows, stations, 2 * TILES, LANES), BF)]
        + [small] * parts,
        in_specs=[pl.BlockSpec(memory_space=pl.ANY)] * 2,
        out_specs=[vmem] * (parts + 1),
        scratch_shapes=[
            pltpu.VMEM(records.shape, F32),
            pltpu.VMEM(table.shape, BF),
            pltpu.VMEM((rows * (length // LANES), 3 * LANES), BF),
            pltpu.VMEM((2 * rows, length // 2), BF),
            pltpu.VMEM((rows * 2 * TILES, LANES), F32),
            pltpu.SemaphoreType.DMA((2,)),
        ],
        compiler_params=pltpu.CompilerParams(vmem_limit_bytes=58 * 2**20),
        cost_estimate=pl.CostEstimate(
            flops=2 * 2 * rows * (length // 2) * 2 * NBIN, bytes_accessed=6 * 2**20, transcendentals=0
        ),
        name="prep",
    )(records, table)


def cross_kernel(scaling, parts, plan, table, gathered, *rest):
    owns = rest[:parts]
    outs = rest[parts : 2 * parts]
    own, other, crossed, operand, result = rest[2 * parts :]
    windows, stations = owns[0].shape[:2]
    all_windows = windows * parts
    quarter = gathered.shape[2]
    slots = ROUNDS
    width = stations * quarter
    columns = slots * width
    block = lax.axis_index("sta")

    for j in range(parts):

        def widen_own(w, carry, j=j):
            raw = owns[j][w].astype(F32)
            real, imag = raw[:, :TILES], raw[:, TILES:]
            own[0, j * windows + w] = real + imag
            own[1, j * windows + w] = real
            own[2, j * windows + w] = imag
            return carry

        lax.fori_loop(0, windows, widen_own, 0)
    for slot in range(slots):
        partner = plan[slot, block]

        def widen_other(w, carry, slot=slot, partner=partner):
            raw = gathered[partner, w].astype(F32)
            real, imag = raw[:, :TILES], raw[:, TILES:]
            other[0, slot, w] = real
            other[1, slot, w] = real + imag
            other[2, slot, w] = imag - real
            return carry

        lax.fori_loop(0, all_windows, widen_other, 0)

    group = 4
    groups = stations // group
    first_bin = (lax.broadcasted_iota(jnp.int32, (TILES, LANES), 0) == 0) & (
        lax.broadcasted_iota(jnp.int32, (TILES, LANES), 1) == 0
    )
    weight = jnp.where(first_bin, 1.0, 2.0).astype(F32)

    def one_group(index, carry):
        slot = index // groups
        first = (index % groups) * group

        def sums(kind):
            totals = [None] * (group * quarter)
            for w in range(all_windows):
                left = [own[kind, w, first + s] for s in range(group)]
                right = [other[kind, slot, w, t] for t in range(quarter)]
                for s in range(group):
                    for t in range(quarter):
                        term = left[s] * right[t]
                        place = s * quarter + t
                        totals[place] = term if w == 0 else totals[place] + term
            return totals

        base = slot * width + first * quarter
        shared = sums(0)
        third = sums(2)
        for place in range(group * quarter):
            at = pl.multiple_of((base + place) * 2 * TILES, 2 * TILES)
            crossed[pl.ds(at, TILES), :] = (shared[place] + third[place]) * weight
        second = sums(1)
        for place in range(group * quarter):
            at = pl.multiple_of((base + place) * 2 * TILES + TILES, TILES)
            crossed[pl.ds(at, TILES), :] = (shared[place] - second[place]) * weight
        return carry

    lax.fori_loop(0, slots * groups, one_group, 0)

    even = even_lanes((columns, LANES))
    sign_real = lane_cycle([1.0, -1.0, -1.0, 1.0])
    sign_imag = lane_cycle([1.0, 1.0, -1.0, -1.0])
    for j in range(TILES):
        at = slice(j * LANES, (j + 1) * LANES)
        at_imag = slice(NBIN + j * LANES, NBIN + (j + 1) * LANES)
        real = crossed[pl.ds(j, columns, stride=2 * TILES), :]
        imag = crossed[pl.ds(TILES + j, columns, stride=2 * TILES), :]
        operand[:columns, at] = real.astype(BF)
        operand[:columns, at_imag] = imag.astype(BF)
        operand[columns:, at] = (sign_real * jnp.where(even, real, imag)).astype(BF)
        operand[columns:, at_imag] = (sign_imag * jnp.where(even, imag, real)).astype(BF)
    share = outs[0].shape[0]
    per_half = table.shape[0] // share
    for q in range(per_half):
        block = lax.dot_general(
            table[q * share : (q + 1) * share, :],
            operand[...],
            (((1,), (1,)), ((), ())),
            preferred_element_type=F32,
        )
        block = (block * scaling).astype(BF)
        for h in range(2):
            result[h * per_half + q] = block[:, h * columns : (h + 1) * columns]
    me = lax.axis_index("seg")
    for j in range(parts):
        outs[j][...] = result[me ^ j]


def cross_lags(plan, table, owns, gathered, scaling):
    parts = len(owns)
    windows, stations = owns[0].shape[:2]
    all_windows = windows * parts
    quarter = gathered.shape[2]
    slots = ROUNDS
    columns = slots * stations * quarter
    share = LAGS // parts
    smem = pl.BlockSpec(memory_space=pltpu.SMEM)
    vmem = pl.BlockSpec(memory_space=pltpu.VMEM)
    return pl.pallas_call(
        functools.partial(cross_kernel, scaling, parts),
        out_shape=[jax.ShapeDtypeStruct((share, columns), BF)] * parts,
        in_specs=[smem] + [vmem] * (2 + parts),
        out_specs=[vmem] * parts,
        scratch_shapes=[
            pltpu.VMEM((3, all_windows, stations, TILES, LANES), F32),
            pltpu.VMEM((3, slots, all_windows, quarter, TILES, LANES), F32),
            pltpu.VMEM((columns * 2 * TILES, LANES), F32),
            pltpu.VMEM((2 * columns, 2 * NBIN), BF),
            pltpu.VMEM((parts, share, columns), BF),
        ],
        compiler_params=pltpu.CompilerParams(vmem_limit_bytes=32 * 2**20),
        cost_estimate=pl.CostEstimate(
            flops=2 * LAGS * 2 * NBIN * columns * 2, bytes_accessed=8 * 2**20, transcendentals=0
        ),
        name="cross",
    )(plan, table, gathered, *owns)


def place_kernel(parts, place, *rest):
    pieces = rest[:parts]
    out = rest[parts]
    pairs = out.shape[2]
    me = lax.axis_index("seg")
    matrix = jnp.concatenate([place[me ^ j] for j in range(parts)], axis=0)
    for p in range(ROUNDS // 2):
        at = slice(p * pairs // 2, (p + 1) * pairs // 2)
        joined = jnp.concatenate([piece[:, at] for piece in pieces], axis=1)
        block = jnp.dot(joined, matrix, preferred_element_type=F32)
        out[:, 2 * p, :] = block[:, :pairs]
        out[:, 2 * p + 1, :] = block[:, pairs:]


def place_lags(pieces, stations):
    parts = len(pieces)
    share, columns = pieces[0].shape
    pairs = stations * stations
    steps = 4
    rows = share // steps
    place = make_placing(stations, stations // parts, parts)
    return pl.pallas_call(
        functools.partial(place_kernel, parts),
        out_shape=jax.ShapeDtypeStruct((share, ROUNDS, pairs), F32),
        grid=(steps,),
        in_specs=[pl.BlockSpec(place.shape, lambda i: (0, 0, 0))]
        + [pl.BlockSpec((rows, columns), lambda i: (i, 0))] * parts,
        out_specs=pl.BlockSpec((rows, ROUNDS, pairs), lambda i: (i, 0, 0)),
        compiler_params=pltpu.CompilerParams(vmem_limit_bytes=32 * 2**20),
        cost_estimate=pl.CostEstimate(
            flops=2 * share * 4 * pairs * ROUNDS * pairs, bytes_accessed=4 * 2**20, transcendentals=0
        ),
        name="place",
    )(place, *pieces)


def exchange(pieces):
    parts = len(pieces)
    out = [pieces[0]]
    for j in range(1, parts):
        out.append(lax.ppermute(pieces[j], "seg", [(i, i ^ j) for i in range(parts)]))
    return out


def per_device(records, plan):
    stations, windows, length = records.shape
    parts = lax.axis_size("seg")
    table = jnp.asarray(make_table(length // 2, 2 * length))
    scaling = 1.0 / math.sqrt(4.0 * NBIN * windows * parts)

    white, *quarters = prepare(records, table, parts)
    shared = jnp.concatenate(exchange(quarters), axis=0)
    gathered = lax.all_gather(shared, "sta")
    owns = exchange([white] * parts)
    lags = cross_lags(plan, table, owns, gathered, scaling)
    return place_lags(exchange(lags), stations)


def solution(mesh):
    in_specs = (P("sta", "seg", None), P())
    out_specs = P("seg", None, "sta")
    return jax.shard_map(
        per_device, mesh=mesh, in_specs=in_specs, out_specs=out_specs, check_vma=False
    )
```

```python
import functools
import math

import jax
import jax.numpy as jnp
import ml_dtypes
import numpy as np
from jax import lax
from jax.experimental import pallas as pl
from jax.experimental.pallas import tpu as pltpu
from jax.sharding import PartitionSpec as P

NBIN = 1024
HALF = 64
ROUNDS = 4
LAGS = 2048
LANES = 128
TILES = NBIN // LANES
CHUNKS = 4
BF = jnp.bfloat16
F32 = jnp.float32


def make_table(rows, transform):
    phase = (np.arange(rows)[:, None] * np.arange(NBIN)[None, :]) % transform
    angle = phase * (2.0 * math.pi / transform)
    return np.concatenate([np.cos(angle), -np.sin(angle)], axis=1).astype(ml_dtypes.bfloat16)


def band_matrix():
    source = lax.broadcasted_iota(jnp.int32, (3 * LANES, LANES), 0) - LANES
    target = lax.broadcasted_iota(jnp.int32, (3 * LANES, LANES), 1)
    return jnp.where(jnp.abs(source - target) <= HALF, 1.0, 0.0).astype(BF)


def inverse_count(block, length):
    position = lax.broadcasted_iota(jnp.int32, (1, LANES), 1) + block * LANES
    counted = jnp.minimum(position, HALF) + jnp.minimum(length - 1 - position, HALF) + 1
    return 1.0 / counted.astype(F32)


def make_placing(stations, quarter, parts):
    width = stations * quarter
    place = np.zeros((parts, 2 * width, 2 * stations * stations), np.float32)
    for part in range(parts):
        for second in range(2):
            for s in range(stations):
                for t in range(quarter):
                    row = second * width + s * quarter + t
                    column = (second * stations + s) * stations + part * quarter + t
                    place[part, row, column] = 1.0
    return place.astype(ml_dtypes.bfloat16)


def lane_cycle(values):
    period = len(values)
    phase = lax.broadcasted_iota(jnp.int32, (1, LANES), 1) % period
    out = jnp.full((1, LANES), values[-1], F32)
    for index in range(period - 1):
        out = jnp.where(phase == index, values[index], out)
    return out


def even_lanes(shape):
    return lax.broadcasted_iota(jnp.int32, shape, 1) % 2 == 0


def eighth_turn():
    turns = [math.pi * k / 4.0 for k in range(8)]
    return lane_cycle([math.cos(t) for t in turns]), lane_cycle([math.sin(t) for t in turns])


def quarter_turns(real, imag, even, sign_real, sign_imag):
    return sign_real * jnp.where(even, real, imag), sign_imag * jnp.where(even, imag, real)


def banded_sum(stack, values, band):
    rows, length = values.shape
    blocks = length // LANES
    zero = jnp.zeros((rows, LANES), BF)
    for j in range(blocks):
        at = pl.ds(j * rows, rows)
        for k in range(3):
            b = j + k - 1
            block = values[:, b * LANES : (b + 1) * LANES] if 0 <= b < blocks else zero
            stack[at, k * LANES : (k + 1) * LANES] = block
    total = jnp.dot(stack[: blocks * rows, :], band, preferred_element_type=F32)
    return [total[j * rows : (j + 1) * rows, :] for j in range(blocks)]


def prep_kernel(parts, records_hbm, table_hbm, white, mine, *rest):
    others = rest[: parts - 2]
    records, table, stack, flat, spread, sems = rest[parts - 2 :]
    records_copy = pltpu.make_async_copy(records_hbm, records, sems.at[0])
    records_copy.start()
    copy = pltpu.make_async_copy(table_hbm, table, sems.at[1])
    copy.start()
    band_values = band_matrix()
    records_copy.wait()
    stations, windows, length = records.shape
    rows = stations * windows
    chunk = length // CHUNKS
    signal = jnp.concatenate([records[:, w, :] for w in range(windows)], axis=0)
    sums = banded_sum(stack, jnp.abs(signal).astype(BF), band_values)
    for j, total in enumerate(sums):
        at = slice(j * LANES, (j + 1) * LANES)
        level = total * inverse_count(j, length)
        value = (signal[:, at] / (level + 1e-05)).astype(BF)
        q, inside = divmod(j * LANES, chunk)
        flat[q * rows : (q + 1) * rows, inside : inside + LANES] = value
    copy.wait()
    product = jnp.dot(flat[...], table[...], preferred_element_type=F32)
    even = even_lanes((rows, LANES))
    sign_real = lane_cycle([1.0, 1.0, -1.0, -1.0])
    sign_imag = lane_cycle([1.0, -1.0, -1.0, 1.0])
    cosine, sine = eighth_turn()
    reals, imags, mags = [], [], []
    for j in range(TILES):
        at = slice(j * LANES, (j + 1) * LANES)
        at_imag = slice(NBIN + j * LANES, NBIN + (j + 1) * LANES)
        pr = [product[q * rows : (q + 1) * rows, at] for q in range(CHUNKS)]
        pi = [product[q * rows : (q + 1) * rows, at_imag] for q in range(CHUNKS)]
        turned = [
            quarter_turns(pr[q], pi[q], even, sign_real, sign_imag) for q in range(2, CHUNKS)
        ]
        first_real, first_imag = pr[0] + turned[0][0], pi[0] + turned[0][1]
        odd_real, odd_imag = pr[1] + turned[1][0], pi[1] + turned[1][1]
        real = first_real + (odd_real * cosine + odd_imag * sine)
        imag = first_imag + (odd_imag * cosine - odd_real * sine)
        reals.append(real)
        imags.append(imag)
        mags.append(jnp.sqrt(real * real + imag * imag).astype(BF))
    sums = banded_sum(stack, jnp.concatenate(mags, axis=1), band_values)
    for j, total in enumerate(sums):
        at = slice(j * LANES, (j + 1) * LANES)
        smooth = total * inverse_count(j, NBIN) + 1e-06
        spread[pl.ds(j, rows, stride=2 * TILES), :] = reals[j] / smooth
        spread[pl.ds(TILES + j, rows, stride=2 * TILES), :] = imags[j] / smooth
    me = lax.axis_index("seg")
    quarter = stations // parts
    white[...] = spread[...].reshape(windows, stations, 2 * TILES, LANES).astype(BF)
    for j, out in [(0, mine)] + list(zip(range(2, parts), others)):
        for w in range(windows):
            out[w] = white[w, pl.ds((me ^ j) * quarter, quarter)]


def prepare(records, table, parts):
    stations, windows, length = records.shape
    rows = stations * windows
    quarter = stations // parts
    small = jax.ShapeDtypeStruct((windows, quarter, 2 * TILES, LANES), BF)
    vmem = pl.BlockSpec(memory_space=pltpu.VMEM)
    return pl.pallas_call(
        functools.partial(prep_kernel, parts),
        out_shape=[jax.ShapeDtypeStruct((windows, stations, 2 * TILES, LANES), BF)]
        + [small] * (parts - 1),
        in_specs=[pl.BlockSpec(memory_space=pltpu.HBM)] * 2,
        out_specs=[vmem] * parts,
        scratch_shapes=[
            pltpu.VMEM(records.shape, F32),
            pltpu.VMEM(table.shape, BF),
            pltpu.VMEM((rows * (length // LANES), 3 * LANES), BF),
            pltpu.VMEM((CHUNKS * rows, length // CHUNKS), BF),
            pltpu.VMEM((rows * 2 * TILES, LANES), F32),
            pltpu.SemaphoreType.DMA((2,)),
        ],
        compiler_params=pltpu.CompilerParams(vmem_limit_bytes=24 * 2**20),
        cost_estimate=pl.CostEstimate(
            flops=2 * rows * length * 2 * NBIN, bytes_accessed=3 * 2**20, transcendentals=0
        ),
        name="prep",
    )(records, table)


def ring_place(block, count):
    return jnp.where(block % 2 == 0, block // 2, count - 1 - block // 2)


def partner_steps(plan, count):
    me = lax.axis_index("sta")
    mine = ring_place(me, count)
    steps, keys = [], []
    for number in range(ROUNDS):
        step = (ring_place(plan[number, me], count) - mine + count) % count
        steps.append(step)
        keys.append(jnp.minimum(step, count - step) * ROUNDS + number)
    ranks = []
    for number in range(ROUNDS):
        rank = jnp.int32(0)
        for other in range(ROUNDS):
            if other != number:
                rank = rank + jnp.where(keys[other] < keys[number], 1, 0)
        ranks.append(rank)
    return steps, ranks


def cross_kernel(first_slot, slots, count, scaling, offsets, parts, plan, table, *rest):
    owns = rest[:parts]
    candidates = rest[parts : parts + len(offsets)]
    rest = rest[parts + len(offsets) :]
    outs = rest[:parts]
    own, other, crossed, operand, result = rest[parts:]
    windows, stations = owns[0].shape[:2]
    all_windows = windows * parts
    quarter = candidates[0].shape[1]
    width = stations * quarter
    columns = slots * width
    steps, ranks = partner_steps(plan, count)

    for j in range(parts):

        def widen_own(w, carry, j=j):
            raw = owns[j][w].astype(F32)
            real, imag = raw[:, :TILES], raw[:, TILES:]
            own[0, j * windows + w] = real + imag
            own[1, j * windows + w] = real
            own[2, j * windows + w] = imag
            return carry

        lax.fori_loop(0, windows, widen_own, 0)
    for slot in range(slots):
        step = jnp.int32(0)
        for number in range(ROUNDS):
            step = jnp.where(ranks[number] == first_slot + slot, steps[number], step)
        for (offset, start), candidate in zip(offsets, candidates):

            @pl.when(step == offset)
            def _(candidate=candidate, slot=slot, start=start):
                def widen_other(w, carry):
                    raw = candidate[w].astype(F32)
                    real, imag = raw[:, :TILES], raw[:, TILES:]
                    other[0, slot, start + w] = real
                    other[1, slot, start + w] = real + imag
                    other[2, slot, start + w] = imag - real
                    return carry

                lax.fori_loop(0, candidate.shape[0], widen_other, 0)

    group = 4
    groups = stations // group
    first_bin = (lax.broadcasted_iota(jnp.int32, (TILES, LANES), 0) == 0) & (
        lax.broadcasted_iota(jnp.int32, (TILES, LANES), 1) == 0
    )
    weight = jnp.where(first_bin, 1.0, 2.0).astype(F32)

    def one_group(index, carry):
        slot = index // groups
        first = (index % groups) * group

        def sums(kind):
            totals = [None] * (group * quarter)
            for w in range(all_windows):
                left = [own[kind, w, first + s] for s in range(group)]
                right = [other[kind, slot, w, t] for t in range(quarter)]
                for s in range(group):
                    for t in range(quarter):
                        term = left[s] * right[t]
                        place = s * quarter + t
                        totals[place] = term if w == 0 else totals[place] + term
            return totals

        base = slot * width + first * quarter
        shared = sums(0)
        third = sums(2)
        for place in range(group * quarter):
            at = pl.multiple_of((base + place) * 2 * TILES, 2 * TILES)
            crossed[pl.ds(at, TILES), :] = (shared[place] + third[place]) * weight
        second = sums(1)
        for place in range(group * quarter):
            at = pl.multiple_of((base + place) * 2 * TILES + TILES, TILES)
            crossed[pl.ds(at, TILES), :] = (shared[place] - second[place]) * weight
        return carry

    lax.fori_loop(0, slots * groups, one_group, 0)

    even = even_lanes((columns, LANES))
    sign_real = lane_cycle([1.0, -1.0, -1.0, 1.0])
    sign_imag = lane_cycle([1.0, 1.0, -1.0, -1.0])
    cosine, sine = eighth_turn()
    for j in range(TILES):
        at = slice(j * LANES, (j + 1) * LANES)
        at_imag = slice(NBIN + j * LANES, NBIN + (j + 1) * LANES)
        real = crossed[pl.ds(j, columns, stride=2 * TILES), :]
        imag = crossed[pl.ds(TILES + j, columns, stride=2 * TILES), :]
        turned = [(real, imag), (real * cosine - imag * sine, imag * cosine + real * sine)]
        turned += [quarter_turns(r, i, even, sign_real, sign_imag) for r, i in turned]
        for q in range(CHUNKS):
            rows = slice(q * columns, (q + 1) * columns)
            operand[rows, at] = turned[q][0].astype(BF)
            operand[rows, at_imag] = turned[q][1].astype(BF)
    block = lax.dot_general(
        table[...], operand[...], (((1,), (1,)), ((), ())), preferred_element_type=F32
    )
    block = block * scaling
    if slots == 1:
        half = table.shape[0] // 2
        low_lanes = lax.broadcasted_iota(jnp.int32, (half, LANES), 1) < width
        for p in range(CHUNKS // 2):
            at = slice(p * LANES, (p + 1) * LANES)
            low, high = block[:half, at], block[half:, at]
            pair = (
                jnp.where(low_lanes, low, pltpu.roll(high, width, 1)),
                jnp.where(low_lanes, pltpu.roll(low, width, 1), high),
            )
            for second in range(2):
                result[2 * p + second] = pair[second].astype(BF)
    else:
        for q in range(CHUNKS):
            result[q] = block[:, q * columns : (q + 1) * columns].astype(BF)
    me = lax.axis_index("seg")
    for j in range(parts):
        outs[j][...] = result[me ^ j]


def cross_lags(plan, table, owns, offsets, candidates, first_slot, slots, count, scaling):
    parts = len(owns)
    windows, stations = owns[0].shape[:2]
    all_windows = windows * parts
    quarter = candidates[0].shape[1]
    columns = slots * stations * quarter
    share = LAGS // parts
    out = (share, columns) if slots > 1 else (share // 2, 2 * columns)
    smem = pl.BlockSpec(memory_space=pltpu.SMEM)
    vmem = pl.BlockSpec(memory_space=pltpu.VMEM)
    return pl.pallas_call(
        functools.partial(
            cross_kernel, first_slot, slots, count, scaling, tuple(offsets), parts
        ),
        out_shape=[jax.ShapeDtypeStruct(out, BF)] * parts,
        in_specs=[smem] + [vmem] * (1 + parts + len(candidates)),
        out_specs=[vmem] * parts,
        scratch_shapes=[
            pltpu.VMEM((3, all_windows, stations, TILES, LANES), F32),
            pltpu.VMEM((3, slots, all_windows, quarter, TILES, LANES), F32),
            pltpu.VMEM((columns * 2 * TILES, LANES), F32),
            pltpu.VMEM((CHUNKS * columns, 2 * NBIN), BF),
            pltpu.VMEM((parts,) + out, BF),
        ],
        compiler_params=pltpu.CompilerParams(vmem_limit_bytes=24 * 2**20),
        cost_estimate=pl.CostEstimate(
            flops=2 * LAGS * 2 * NBIN * columns * 4, bytes_accessed=2 * 2**20, transcendentals=0
        ),
        name="cross",
    )(plan, table, *owns, *candidates)


def place_kernel(count, parts, groups, plan, place, *rest):
    pieces = rest[: parts * len(groups)]
    out, result = rest[parts * len(groups) :]
    pairs = out.shape[3]
    me = lax.axis_index("seg")
    _, ranks = partner_steps(plan, count)
    matrix = jnp.concatenate([place[me ^ j] for j in range(parts)], axis=0)
    for index, (first_slot, slots) in enumerate(groups):
        joined = jnp.concatenate(
            [piece[...].reshape(-1, LANES) for piece in pieces[index * parts : (index + 1) * parts]],
            axis=1,
        )
        block = jnp.dot(joined, matrix, preferred_element_type=F32)
        half = out.shape[1]
        if slots == 1:
            result[first_slot, 0] = block[:, :pairs]
            result[first_slot, 1] = block[:, pairs:]
        else:
            for slot in range(2):
                for h in range(2):
                    result[first_slot + slot, h] = block[
                        h * half : (h + 1) * half, slot * pairs : (slot + 1) * pairs
                    ]
    for number in range(ROUNDS):
        for h in range(2):
            out[h, :, number, :] = result[ranks[number], h]


def place_lags(plan, groups, pieces, count, stations, parts):
    pairs = stations * stations
    share = LAGS // parts
    half = share // 2
    steps = 4
    rows = half // steps
    place = make_placing(stations, stations // parts, parts)
    blocks, specs = [], []
    for index, (_, slots) in enumerate(groups):
        for piece in pieces[index * parts : (index + 1) * parts]:
            if slots == 1:
                blocks.append(piece)
                specs.append(pl.BlockSpec((rows, LANES), lambda i: (i, 0)))
            else:
                blocks.append(piece.reshape(2, half, LANES))
                specs.append(pl.BlockSpec((2, rows, LANES), lambda i: (0, i, 0)))
    out = pl.pallas_call(
        functools.partial(place_kernel, count, parts, tuple(groups)),
        out_shape=jax.ShapeDtypeStruct((2, half, ROUNDS, pairs), F32),
        grid=(steps,),
        in_specs=[
            pl.BlockSpec(memory_space=pltpu.SMEM),
            pl.BlockSpec(place.shape, lambda i: (0, 0, 0)),
        ]
        + specs,
        out_specs=pl.BlockSpec((2, rows, ROUNDS, pairs), lambda i: (0, i, 0, 0)),
        scratch_shapes=[pltpu.VMEM((ROUNDS, 2, rows, pairs), F32)],
        compiler_params=pltpu.CompilerParams(vmem_limit_bytes=24 * 2**20),
        cost_estimate=pl.CostEstimate(
            flops=2 * share * 4 * pairs * ROUNDS * pairs, bytes_accessed=4 * 2**20, transcendentals=0
        ),
        name="place",
    )(plan, place, *blocks)
    return out.reshape(share, ROUNDS, pairs)


def swap(value, j):
    parts = lax.axis_size("seg")
    return lax.ppermute(value, "seg", [(i, i ^ j) for i in range(parts)])


def exchange(pieces):
    return [pieces[0]] + [swap(pieces[j], j) for j in range(1, len(pieces))]


def per_device(records, plan):
    stations, windows, length = records.shape
    count = lax.axis_size("sta")
    parts = lax.axis_size("seg")
    quarter = stations // parts
    table = jnp.asarray(make_table(length // CHUNKS, 2 * length))
    scaling = 1.0 / math.sqrt(4.0 * NBIN * windows * parts)

    white, mine, *far = prepare(records, table, parts)
    sibling = swap(white, 1)
    first = lax.axis_index("seg") * quarter
    near = jnp.concatenate([mine, lax.dynamic_slice_in_dim(sibling, first, quarter, 1)])
    far = jnp.concatenate([swap(piece, 2 + j) for j, piece in enumerate(far)])
    far, white_far = lax.optimization_barrier((far, white))
    across = swap(white_far, 2)

    ring = sorted(range(count), key=lambda b: b // 2 if b % 2 == 0 else count - 1 - b // 2)
    upward = [(ring[i], ring[(i + 1) % count]) for i in range(count)]
    downward = [(ring[i], ring[i - 1]) for i in range(count)]

    def up(value):
        return lax.ppermute(value, "sta", upward)

    def down(value):
        return lax.ppermute(value, "sta", downward)

    spots, blocks = [], []
    near_up = near_down = near
    far_up = far_down = far
    steps = (count - 1) // 2
    for step in range(1, steps + 1):
        near_up, near_down = up(near_up), down(near_down)
        if step == min(3, steps):
            far_up, far_down, across = lax.optimization_barrier((far_up, far_down, across))
        far_up, far_down = up(far_up), down(far_down)
        spots += [(count - step, 0), (step, 0), (count - step, 2 * windows), (step, 2 * windows)]
        blocks += [near_up, near_down, far_up, far_down]
    owns = [white, sibling, across, swap(across, 1)]
    late_spots, late_blocks = list(spots), list(blocks)
    if count % 2 == 0:
        late_spots += [(count // 2, 0), (count // 2, 2 * windows)]
        late_blocks += [up(near_up), down(far_down)]
    groups = [(0, 2), (2, 2)]
    pieces = []
    for (first_slot, slots), at, values in zip(
        groups, (spots, late_spots), (blocks, late_blocks)
    ):
        lags = cross_lags(plan, table, owns, at, values, first_slot, slots, count, scaling)
        pieces += exchange(lags)
    return place_lags(plan, groups, pieces, count, stations, parts)


def solution(mesh):
    in_specs = (P("sta", "seg", None), P())
    out_specs = P("seg", None, "sta")
    return jax.shard_map(
        per_device, mesh=mesh, in_specs=in_specs, out_specs=out_specs, check_vma=False
    )
```

```python
import functools
import math

import jax
import jax.numpy as jnp
import ml_dtypes
import numpy as np
from jax import lax
from jax.experimental import pallas as pl
from jax.experimental.pallas import tpu as pltpu
from jax.sharding import PartitionSpec as P

NBIN = 1024
HALF = 64
ROUNDS = 4
LAGS = 2048
LANES = 128
TILES = NBIN // LANES
CHUNKS = 4
BF = jnp.bfloat16
F32 = jnp.float32


def make_table(rows, transform):
    phase = (np.arange(rows)[:, None] * np.arange(NBIN)[None, :]) % transform
    angle = phase * (2.0 * math.pi / transform)
    return np.concatenate([np.cos(angle), -np.sin(angle)], axis=1).astype(ml_dtypes.bfloat16)


def band_matrix():
    source = lax.broadcasted_iota(jnp.int32, (3 * LANES, LANES), 0) - LANES
    target = lax.broadcasted_iota(jnp.int32, (3 * LANES, LANES), 1)
    return jnp.where(jnp.abs(source - target) <= HALF, 1.0, 0.0).astype(BF)


def inverse_count(block, length):
    position = lax.broadcasted_iota(jnp.int32, (1, LANES), 1) + block * LANES
    counted = jnp.minimum(position, HALF) + jnp.minimum(length - 1 - position, HALF) + 1
    return 1.0 / counted.astype(F32)


def make_placing(stations, quarter, parts):
    width = stations * quarter
    place = np.zeros((parts, 2 * width, 2 * stations * stations), np.float32)
    for part in range(parts):
        for second in range(2):
            for s in range(stations):
                for t in range(quarter):
                    row = second * width + s * quarter + t
                    column = (second * stations + s) * stations + part * quarter + t
                    place[part, row, column] = 1.0
    return place.astype(ml_dtypes.bfloat16)


def lane_cycle(values):
    period = len(values)
    phase = lax.broadcasted_iota(jnp.int32, (1, LANES), 1) % period
    out = jnp.full((1, LANES), values[-1], F32)
    for index in range(period - 1):
        out = jnp.where(phase == index, values[index], out)
    return out


def even_lanes(shape):
    return lax.broadcasted_iota(jnp.int32, shape, 1) % 2 == 0


def eighth_turn():
    turns = [math.pi * k / 4.0 for k in range(8)]
    return lane_cycle([math.cos(t) for t in turns]), lane_cycle([math.sin(t) for t in turns])


def quarter_turns(real, imag, even, sign_real, sign_imag):
    return sign_real * jnp.where(even, real, imag), sign_imag * jnp.where(even, imag, real)


def banded_sum(stack, values, band):
    rows, length = values.shape
    blocks = length // LANES
    zero = jnp.zeros((rows, LANES), BF)
    for j in range(blocks):
        at = pl.ds(j * rows, rows)
        for k in range(3):
            b = j + k - 1
            block = values[:, b * LANES : (b + 1) * LANES] if 0 <= b < blocks else zero
            stack[at, k * LANES : (k + 1) * LANES] = block
    total = jnp.dot(stack[: blocks * rows, :], band, preferred_element_type=F32)
    return [total[j * rows : (j + 1) * rows, :] for j in range(blocks)]


def prep_kernel(parts, records_hbm, table_hbm, white, mine, *rest):
    others = rest[: parts - 2]
    records, table, stack, flat, spread, sems = rest[parts - 2 :]
    records_copy = pltpu.make_async_copy(records_hbm, records, sems.at[0])
    records_copy.start()
    copy = pltpu.make_async_copy(table_hbm, table, sems.at[1])
    copy.start()
    band_values = band_matrix()
    records_copy.wait()
    stations, windows, length = records.shape
    rows = stations * windows
    chunk = length // CHUNKS
    signal = jnp.concatenate([records[:, w, :] for w in range(windows)], axis=0)
    sums = banded_sum(stack, jnp.abs(signal).astype(BF), band_values)
    for j, total in enumerate(sums):
        at = slice(j * LANES, (j + 1) * LANES)
        level = total * inverse_count(j, length)
        value = (signal[:, at] / (level + 1e-05)).astype(BF)
        q, inside = divmod(j * LANES, chunk)
        flat[q * rows : (q + 1) * rows, inside : inside + LANES] = value
    copy.wait()
    product = jnp.dot(flat[...], table[...], preferred_element_type=F32)
    even = even_lanes((rows, LANES))
    sign_real = lane_cycle([1.0, 1.0, -1.0, -1.0])
    sign_imag = lane_cycle([1.0, -1.0, -1.0, 1.0])
    cosine, sine = eighth_turn()
    reals, imags, mags = [], [], []
    for j in range(TILES):
        at = slice(j * LANES, (j + 1) * LANES)
        at_imag = slice(NBIN + j * LANES, NBIN + (j + 1) * LANES)
        pr = [product[q * rows : (q + 1) * rows, at] for q in range(CHUNKS)]
        pi = [product[q * rows : (q + 1) * rows, at_imag] for q in range(CHUNKS)]
        turned = [
            quarter_turns(pr[q], pi[q], even, sign_real, sign_imag) for q in range(2, CHUNKS)
        ]
        first_real, first_imag = pr[0] + turned[0][0], pi[0] + turned[0][1]
        odd_real, odd_imag = pr[1] + turned[1][0], pi[1] + turned[1][1]
        real = first_real + (odd_real * cosine + odd_imag * sine)
        imag = first_imag + (odd_imag * cosine - odd_real * sine)
        reals.append(real)
        imags.append(imag)
        mags.append(jnp.sqrt(real * real + imag * imag).astype(BF))
    sums = banded_sum(stack, jnp.concatenate(mags, axis=1), band_values)
    for j, total in enumerate(sums):
        at = slice(j * LANES, (j + 1) * LANES)
        smooth = total * inverse_count(j, NBIN) + 1e-06
        spread[pl.ds(j, rows, stride=2 * TILES), :] = reals[j] / smooth
        spread[pl.ds(TILES + j, rows, stride=2 * TILES), :] = imags[j] / smooth
    me = lax.axis_index("seg")
    quarter = stations // parts
    white[...] = spread[...].reshape(windows, stations, 2 * TILES, LANES).astype(BF)
    for j, out in [(0, mine)] + list(zip(range(2, parts), others)):
        for w in range(windows):
            out[w] = white[w, pl.ds((me ^ j) * quarter, quarter)]


def prepare(records, table, parts):
    stations, windows, length = records.shape
    rows = stations * windows
    quarter = stations // parts
    small = jax.ShapeDtypeStruct((windows, quarter, 2 * TILES, LANES), BF)
    vmem = pl.BlockSpec(memory_space=pltpu.VMEM)
    return pl.pallas_call(
        functools.partial(prep_kernel, parts),
        out_shape=[jax.ShapeDtypeStruct((windows, stations, 2 * TILES, LANES), BF)]
        + [small] * (parts - 1),
        in_specs=[pl.BlockSpec(memory_space=pltpu.HBM)] * 2,
        out_specs=[vmem] * parts,
        scratch_shapes=[
            pltpu.VMEM(records.shape, F32),
            pltpu.VMEM(table.shape, BF),
            pltpu.VMEM((rows * (length // LANES), 3 * LANES), BF),
            pltpu.VMEM((CHUNKS * rows, length // CHUNKS), BF),
            pltpu.VMEM((rows * 2 * TILES, LANES), F32),
            pltpu.SemaphoreType.DMA((2,)),
        ],
        compiler_params=pltpu.CompilerParams(vmem_limit_bytes=58 * 2**20),
        cost_estimate=pl.CostEstimate(
            flops=2 * rows * length * 2 * NBIN, bytes_accessed=3 * 2**20, transcendentals=0
        ),
        name="prep",
    )(records, table)


def ring_place(block, count):
    return jnp.where(block % 2 == 0, block // 2, count - 1 - block // 2)


def partner_steps(plan, count):
    me = lax.axis_index("sta")
    mine = ring_place(me, count)
    steps, keys = [], []
    for number in range(ROUNDS):
        step = (ring_place(plan[number, me], count) - mine + count) % count
        steps.append(step)
        keys.append(jnp.minimum(step, count - step) * ROUNDS + number)
    ranks = []
    for number in range(ROUNDS):
        rank = jnp.int32(0)
        for other in range(ROUNDS):
            if other != number:
                rank = rank + jnp.where(keys[other] < keys[number], 1, 0)
        ranks.append(rank)
    return steps, ranks


def cross_kernel(first_slot, slots, count, scaling, offsets, parts, plan, table, *rest):
    owns = rest[:parts]
    candidates = rest[parts : parts + len(offsets)]
    rest = rest[parts + len(offsets) :]
    outs = rest[:parts]
    own, other, crossed, operand, result = rest[parts:]
    windows, stations = owns[0].shape[:2]
    all_windows = windows * parts
    quarter = candidates[0].shape[1]
    width = stations * quarter
    columns = slots * width
    steps, ranks = partner_steps(plan, count)

    for j in range(parts):

        def widen_own(w, carry, j=j):
            raw = owns[j][w].astype(F32)
            real, imag = raw[:, :TILES], raw[:, TILES:]
            own[0, j * windows + w] = real + imag
            own[1, j * windows + w] = real
            own[2, j * windows + w] = imag
            return carry

        lax.fori_loop(0, windows, widen_own, 0)
    for slot in range(slots):
        step = jnp.int32(0)
        for number in range(ROUNDS):
            step = jnp.where(ranks[number] == first_slot + slot, steps[number], step)
        for (offset, start), candidate in zip(offsets, candidates):

            @pl.when(step == offset)
            def _(candidate=candidate, slot=slot, start=start):
                def widen_other(w, carry):
                    raw = candidate[w].astype(F32)
                    real, imag = raw[:, :TILES], raw[:, TILES:]
                    other[0, slot, start + w] = real
                    other[1, slot, start + w] = real + imag
                    other[2, slot, start + w] = imag - real
                    return carry

                lax.fori_loop(0, candidate.shape[0], widen_other, 0)

    group = 4
    groups = stations // group
    first_bin = (lax.broadcasted_iota(jnp.int32, (TILES, LANES), 0) == 0) & (
        lax.broadcasted_iota(jnp.int32, (TILES, LANES), 1) == 0
    )
    weight = jnp.where(first_bin, 1.0, 2.0).astype(F32)

    def one_group(index, carry):
        slot = index // groups
        first = (index % groups) * group

        def sums(kind):
            totals = [None] * (group * quarter)
            for w in range(all_windows):
                left = [own[kind, w, first + s] for s in range(group)]
                right = [other[kind, slot, w, t] for t in range(quarter)]
                for s in range(group):
                    for t in range(quarter):
                        term = left[s] * right[t]
                        place = s * quarter + t
                        totals[place] = term if w == 0 else totals[place] + term
            return totals

        base = slot * width + first * quarter
        shared = sums(0)
        third = sums(2)
        for place in range(group * quarter):
            at = pl.multiple_of((base + place) * 2 * TILES, 2 * TILES)
            crossed[pl.ds(at, TILES), :] = (shared[place] + third[place]) * weight
        second = sums(1)
        for place in range(group * quarter):
            at = pl.multiple_of((base + place) * 2 * TILES + TILES, TILES)
            crossed[pl.ds(at, TILES), :] = (shared[place] - second[place]) * weight
        return carry

    lax.fori_loop(0, slots * groups, one_group, 0)

    even = even_lanes((columns, LANES))
    sign_real = lane_cycle([1.0, -1.0, -1.0, 1.0])
    sign_imag = lane_cycle([1.0, 1.0, -1.0, -1.0])
    cosine, sine = eighth_turn()
    for j in range(TILES):
        at = slice(j * LANES, (j + 1) * LANES)
        at_imag = slice(NBIN + j * LANES, NBIN + (j + 1) * LANES)
        real = crossed[pl.ds(j, columns, stride=2 * TILES), :]
        imag = crossed[pl.ds(TILES + j, columns, stride=2 * TILES), :]
        turned = [(real, imag), (real * cosine - imag * sine, imag * cosine + real * sine)]
        turned += [quarter_turns(r, i, even, sign_real, sign_imag) for r, i in turned]
        for q in range(CHUNKS):
            rows = slice(q * columns, (q + 1) * columns)
            operand[rows, at] = turned[q][0].astype(BF)
            operand[rows, at_imag] = turned[q][1].astype(BF)
    block = lax.dot_general(
        table[...], operand[...], (((1,), (1,)), ((), ())), preferred_element_type=F32
    )
    block = block * scaling
    if slots == 1:
        half = table.shape[0] // 2
        low_lanes = lax.broadcasted_iota(jnp.int32, (half, LANES), 1) < width
        for p in range(CHUNKS // 2):
            at = slice(p * LANES, (p + 1) * LANES)
            low, high = block[:half, at], block[half:, at]
            pair = (
                jnp.where(low_lanes, low, pltpu.roll(high, width, 1)),
                jnp.where(low_lanes, pltpu.roll(low, width, 1), high),
            )
            for second in range(2):
                result[2 * p + second] = pair[second].astype(BF)
    else:
        for q in range(CHUNKS):
            result[q] = block[:, q * columns : (q + 1) * columns].astype(BF)
    me = lax.axis_index("seg")
    for j in range(parts):
        outs[j][...] = result[me ^ j]


def cross_lags(plan, table, owns, offsets, candidates, first_slot, slots, count, scaling):
    parts = len(owns)
    windows, stations = owns[0].shape[:2]
    all_windows = windows * parts
    quarter = candidates[0].shape[1]
    columns = slots * stations * quarter
    share = LAGS // parts
    out = (share, columns) if slots > 1 else (share // 2, 2 * columns)
    smem = pl.BlockSpec(memory_space=pltpu.SMEM)
    vmem = pl.BlockSpec(memory_space=pltpu.VMEM)
    return pl.pallas_call(
        functools.partial(
            cross_kernel, first_slot, slots, count, scaling, tuple(offsets), parts
        ),
        out_shape=[jax.ShapeDtypeStruct(out, BF)] * parts,
        in_specs=[smem] + [vmem] * (1 + parts + len(candidates)),
        out_specs=[vmem] * parts,
        scratch_shapes=[
            pltpu.VMEM((3, all_windows, stations, TILES, LANES), F32),
            pltpu.VMEM((3, slots, all_windows, quarter, TILES, LANES), F32),
            pltpu.VMEM((columns * 2 * TILES, LANES), F32),
            pltpu.VMEM((CHUNKS * columns, 2 * NBIN), BF),
            pltpu.VMEM((parts,) + out, BF),
        ],
        compiler_params=pltpu.CompilerParams(vmem_limit_bytes=24 * 2**20),
        cost_estimate=pl.CostEstimate(
            flops=2 * LAGS * 2 * NBIN * columns * 4, bytes_accessed=2 * 2**20, transcendentals=0
        ),
        name="cross",
    )(plan, table, *owns, *candidates)


def place_kernel(count, parts, groups, steps, plan, place, *rest):
    pieces = rest[: parts * len(groups)]
    out_hbm, out, sems = rest[parts * len(groups) :]
    pairs = out.shape[3]
    half = out.shape[1]
    rows = half // steps
    me = lax.axis_index("seg")
    _, ranks = partner_steps(plan, count)
    round_of = []
    for slot in range(ROUNDS):
        number = jnp.int32(0)
        for other in range(1, ROUNDS):
            number = jnp.where(ranks[other] == slot, other, number)
        round_of.append(number)
    matrix = jnp.concatenate([place[me ^ j] for j in range(parts)], axis=0)
    copies = []
    for step in range(steps):
        at = slice(step * rows, (step + 1) * rows)
        for index, (first_slot, slots) in enumerate(groups):
            own = pieces[index * parts : (index + 1) * parts]
            lows = [piece[at, :] for piece in own]
            if slots == 1:
                joined = jnp.concatenate(lows, axis=1)
            else:
                later = slice(half + step * rows, half + (step + 1) * rows)
                highs = [piece[later, :] for piece in own]
                joined = jnp.concatenate(
                    [jnp.concatenate(lows, axis=1), jnp.concatenate(highs, axis=1)], axis=0
                )
            block = jnp.dot(joined, matrix, preferred_element_type=F32)
            if slots == 1:
                out[0, at, round_of[first_slot], :] = block[:, :pairs]
                out[1, at, round_of[first_slot], :] = block[:, pairs:]
            else:
                for slot in range(2):
                    columns = slice(slot * pairs, (slot + 1) * pairs)
                    out[0, at, round_of[first_slot + slot], :] = block[:rows, columns]
                    out[1, at, round_of[first_slot + slot], :] = block[rows:, columns]
        for h in range(2):
            copy = pltpu.make_async_copy(
                out.at[h, at], out_hbm.at[h, at], sems.at[2 * step + h]
            )
            copy.start()
            copies.append(copy)
    for copy in copies:
        copy.wait()


def place_lags(plan, groups, pieces, count, stations, parts):
    pairs = stations * stations
    share = LAGS // parts
    half = share // 2
    steps = 2
    place = make_placing(stations, stations // parts, parts)
    vmem = pl.BlockSpec(memory_space=pltpu.VMEM)
    shape = (2, half, ROUNDS, pairs)
    out = pl.pallas_call(
        functools.partial(place_kernel, count, parts, tuple(groups), steps),
        out_shape=jax.ShapeDtypeStruct(shape, F32),
        in_specs=[pl.BlockSpec(memory_space=pltpu.SMEM)] + [vmem] * (1 + len(pieces)),
        out_specs=pl.BlockSpec(memory_space=pl.ANY),
        scratch_shapes=[pltpu.VMEM(shape, F32), pltpu.SemaphoreType.DMA((2 * steps,))],
        compiler_params=pltpu.CompilerParams(vmem_limit_bytes=24 * 2**20),
        cost_estimate=pl.CostEstimate(
            flops=2 * share * 4 * pairs * ROUNDS * pairs, bytes_accessed=4 * 2**20, transcendentals=0
        ),
        name="place",
    )(plan, place, *pieces)
    return out.reshape(share, ROUNDS, pairs)


def swap(value, j):
    parts = lax.axis_size("seg")
    return lax.ppermute(value, "seg", [(i, i ^ j) for i in range(parts)])


def exchange(pieces):
    return [pieces[0]] + [swap(pieces[j], j) for j in range(1, len(pieces))]


def per_device(records, plan):
    stations, windows, length = records.shape
    count = lax.axis_size("sta")
    parts = lax.axis_size("seg")
    quarter = stations // parts
    table = jnp.asarray(make_table(length // CHUNKS, 2 * length))
    scaling = 1.0 / math.sqrt(4.0 * NBIN * windows * parts)

    white, mine, *far = prepare(records, table, parts)
    sibling = swap(white, 1)
    first = lax.axis_index("seg") * quarter
    near = jnp.concatenate([mine, lax.dynamic_slice_in_dim(sibling, first, quarter, 1)])
    far = jnp.concatenate([swap(piece, 2 + j) for j, piece in enumerate(far)])
    far, white_far = lax.optimization_barrier((far, white))
    across = swap(white_far, 2)

    ring = sorted(range(count), key=lambda b: b // 2 if b % 2 == 0 else count - 1 - b // 2)
    upward = [(ring[i], ring[(i + 1) % count]) for i in range(count)]
    downward = [(ring[i], ring[i - 1]) for i in range(count)]

    def up(value):
        return lax.ppermute(value, "sta", upward)

    def down(value):
        return lax.ppermute(value, "sta", downward)

    spots, blocks = [], []
    near_up = near_down = near
    far_up = far_down = far
    steps = (count - 1) // 2
    for step in range(1, steps + 1):
        if step == 2:
            near_up, near_down = lax.optimization_barrier((near_up, near_down))
        elif step > 2:
            near_up, near_down, last_up, last_down = lax.optimization_barrier(
                (near_up, near_down, last_up, last_down)
            )
        last_up, last_down = far_up, far_down
        next_near = up(near_up), down(near_down)
        if step == 3:
            far_up, far_down, near_up, near_down, across = lax.optimization_barrier(
                (far_up, far_down, near_up, near_down, across)
            )
        elif step > 1:
            far_up, far_down, near_up, near_down = lax.optimization_barrier(
                (far_up, far_down, near_up, near_down)
            )
        far_up, far_down = up(far_up), down(far_down)
        near_up, near_down = next_near
        spots += [(count - step, 0), (step, 0), (count - step, 2 * windows), (step, 2 * windows)]
        blocks += [near_up, near_down, far_up, far_down]
    owns = [white, sibling, across, swap(across, 1)]
    late_spots, late_blocks = list(spots), list(blocks)
    if count % 2 == 0:
        late_spots += [(count // 2, 0), (count // 2, 2 * windows)]
        middle_up = up(near_up)
        far_down, near_up, near_down = lax.optimization_barrier((far_down, near_up, near_down))
        late_blocks += [middle_up, down(far_down)]
    groups = [(0, 2), (2, 2)]
    pieces = []
    for (first_slot, slots), at, values in zip(
        groups, (spots, late_spots), (blocks, late_blocks)
    ):
        lags = cross_lags(plan, table, owns, at, values, first_slot, slots, count, scaling)
        pieces += exchange(lags)
    return place_lags(plan, groups, pieces, count, stations, parts)


def solution(mesh):
    in_specs = (P("sta", "seg", None), P())
    out_specs = P("seg", None, "sta")
    return jax.shard_map(
        per_device, mesh=mesh, in_specs=in_specs, out_specs=out_specs, check_vma=False
    )
```

```python
import functools
import math

import jax
import jax.numpy as jnp
import ml_dtypes
import numpy as np
from jax import lax
from jax.experimental import pallas as pl
from jax.experimental.pallas import tpu as pltpu
from jax.sharding import PartitionSpec as P

NBIN = 1024
HALF = 64
ROUNDS = 4
LAGS = 2048
LANES = 128
TILES = NBIN // LANES
CHUNKS = 4
BF = jnp.bfloat16
F32 = jnp.float32


def make_table(rows, transform):
    phase = (np.arange(rows)[:, None] * np.arange(NBIN)[None, :]) % transform
    angle = phase * (2.0 * math.pi / transform)
    return np.concatenate([np.cos(angle), -np.sin(angle)], axis=1).astype(ml_dtypes.bfloat16)


def band_matrix():
    source = lax.broadcasted_iota(jnp.int32, (3 * LANES, LANES), 0) - LANES
    target = lax.broadcasted_iota(jnp.int32, (3 * LANES, LANES), 1)
    return jnp.where(jnp.abs(source - target) <= HALF, 1.0, 0.0).astype(BF)


def inverse_count(block, length):
    position = lax.broadcasted_iota(jnp.int32, (1, LANES), 1) + block * LANES
    counted = jnp.minimum(position, HALF) + jnp.minimum(length - 1 - position, HALF) + 1
    return 1.0 / counted.astype(F32)


def make_placing(stations, quarter, parts):
    width = stations * quarter
    place = np.zeros((parts, 2 * width, 2 * stations * stations), np.float32)
    for part in range(parts):
        for second in range(2):
            for s in range(stations):
                for t in range(quarter):
                    row = second * width + s * quarter + t
                    column = (second * stations + s) * stations + part * quarter + t
                    place[part, row, column] = 1.0
    return place.astype(ml_dtypes.bfloat16)


def lane_cycle(values):
    period = len(values)
    phase = lax.broadcasted_iota(jnp.int32, (1, LANES), 1) % period
    out = jnp.full((1, LANES), values[-1], F32)
    for index in range(period - 1):
        out = jnp.where(phase == index, values[index], out)
    return out


def even_lanes(shape):
    return lax.broadcasted_iota(jnp.int32, shape, 1) % 2 == 0


def eighth_turn():
    turns = [math.pi * k / 4.0 for k in range(8)]
    return lane_cycle([math.cos(t) for t in turns]), lane_cycle([math.sin(t) for t in turns])


def quarter_turns(real, imag, even, sign_real, sign_imag):
    return sign_real * jnp.where(even, real, imag), sign_imag * jnp.where(even, imag, real)


def banded_sum(stack, values, band):
    rows, length = values.shape
    blocks = length // LANES
    zero = jnp.zeros((rows, LANES), BF)
    for j in range(blocks):
        at = pl.ds(j * rows, rows)
        for k in range(3):
            b = j + k - 1
            block = values[:, b * LANES : (b + 1) * LANES] if 0 <= b < blocks else zero
            stack[at, k * LANES : (k + 1) * LANES] = block
    total = jnp.dot(stack[: blocks * rows, :], band, preferred_element_type=F32)
    return [total[j * rows : (j + 1) * rows, :] for j in range(blocks)]


def prep_kernel(parts, records_hbm, table_hbm, white, mine, *rest):
    others = rest[: parts - 2]
    records, table, stack, flat, spread, sems = rest[parts - 2 :]
    records_copy = pltpu.make_async_copy(records_hbm, records, sems.at[0])
    records_copy.start()
    copy = pltpu.make_async_copy(table_hbm, table, sems.at[1])
    copy.start()
    band_values = band_matrix()
    records_copy.wait()
    stations, windows, length = records.shape
    rows = stations * windows
    chunk = length // CHUNKS
    signal = jnp.concatenate([records[:, w, :] for w in range(windows)], axis=0)
    sums = banded_sum(stack, jnp.abs(signal).astype(BF), band_values)
    for j, total in enumerate(sums):
        at = slice(j * LANES, (j + 1) * LANES)
        level = total * inverse_count(j, length)
        value = (signal[:, at] / (level + 1e-05)).astype(BF)
        q, inside = divmod(j * LANES, chunk)
        flat[q * rows : (q + 1) * rows, inside : inside + LANES] = value
    copy.wait()
    product = jnp.dot(flat[...], table[...], preferred_element_type=F32)
    even = even_lanes((rows, LANES))
    sign_real = lane_cycle([1.0, 1.0, -1.0, -1.0])
    sign_imag = lane_cycle([1.0, -1.0, -1.0, 1.0])
    cosine, sine = eighth_turn()
    reals, imags, mags = [], [], []
    for j in range(TILES):
        at = slice(j * LANES, (j + 1) * LANES)
        at_imag = slice(NBIN + j * LANES, NBIN + (j + 1) * LANES)
        pr = [product[q * rows : (q + 1) * rows, at] for q in range(CHUNKS)]
        pi = [product[q * rows : (q + 1) * rows, at_imag] for q in range(CHUNKS)]
        turned = [
            quarter_turns(pr[q], pi[q], even, sign_real, sign_imag) for q in range(2, CHUNKS)
        ]
        first_real, first_imag = pr[0] + turned[0][0], pi[0] + turned[0][1]
        odd_real, odd_imag = pr[1] + turned[1][0], pi[1] + turned[1][1]
        real = first_real + (odd_real * cosine + odd_imag * sine)
        imag = first_imag + (odd_imag * cosine - odd_real * sine)
        reals.append(real)
        imags.append(imag)
        mags.append(jnp.sqrt(real * real + imag * imag).astype(BF))
    sums = banded_sum(stack, jnp.concatenate(mags, axis=1), band_values)
    for j, total in enumerate(sums):
        at = slice(j * LANES, (j + 1) * LANES)
        smooth = total * inverse_count(j, NBIN) + 1e-06
        spread[pl.ds(j, rows, stride=2 * TILES), :] = reals[j] / smooth
        spread[pl.ds(TILES + j, rows, stride=2 * TILES), :] = imags[j] / smooth
    me = lax.axis_index("seg")
    quarter = stations // parts
    white[...] = spread[...].reshape(windows, stations, 2 * TILES, LANES).astype(BF)
    for j, out in [(0, mine)] + list(zip(range(2, parts), others)):
        for w in range(windows):
            out[w] = white[w, pl.ds((me ^ j) * quarter, quarter)]


def prepare(records, table, parts):
    stations, windows, length = records.shape
    rows = stations * windows
    quarter = stations // parts
    small = jax.ShapeDtypeStruct((windows, quarter, 2 * TILES, LANES), BF)
    vmem = pl.BlockSpec(memory_space=pltpu.VMEM)
    return pl.pallas_call(
        functools.partial(prep_kernel, parts),
        out_shape=[jax.ShapeDtypeStruct((windows, stations, 2 * TILES, LANES), BF)]
        + [small] * (parts - 1),
        in_specs=[pl.BlockSpec(memory_space=pltpu.HBM)] * 2,
        out_specs=[vmem] * parts,
        scratch_shapes=[
            pltpu.VMEM(records.shape, F32),
            pltpu.VMEM(table.shape, BF),
            pltpu.VMEM((rows * (length // LANES), 3 * LANES), BF),
            pltpu.VMEM((CHUNKS * rows, length // CHUNKS), BF),
            pltpu.VMEM((rows * 2 * TILES, LANES), F32),
            pltpu.SemaphoreType.DMA((2,)),
        ],
        compiler_params=pltpu.CompilerParams(vmem_limit_bytes=58 * 2**20),
        cost_estimate=pl.CostEstimate(
            flops=2 * rows * length * 2 * NBIN, bytes_accessed=3 * 2**20, transcendentals=0
        ),
        name="prep",
    )(records, table)


def ring_place(block, count):
    return jnp.where(block % 2 == 0, block // 2, count - 1 - block // 2)


def partner_steps(plan, count):
    me = lax.axis_index("sta")
    mine = ring_place(me, count)
    steps, keys = [], []
    for number in range(ROUNDS):
        step = (ring_place(plan[number, me], count) - mine + count) % count
        steps.append(step)
        keys.append(jnp.minimum(step, count - step) * ROUNDS + number)
    ranks = []
    for number in range(ROUNDS):
        rank = jnp.int32(0)
        for other in range(ROUNDS):
            if other != number:
                rank = rank + jnp.where(keys[other] < keys[number], 1, 0)
        ranks.append(rank)
    return steps, ranks


def expected(microseconds):
    return pl.CostEstimate(
        flops=int(microseconds * 1.15e9), bytes_accessed=1024, transcendentals=0
    )


def widen_kernel(*refs):
    blocks, own = refs[:-1], refs[-1]
    windows = blocks[0].shape[0]
    for j, block in enumerate(blocks):

        def widen(w, carry, j=j, block=block):
            raw = block[w].astype(F32)
            real, imag = raw[:, :TILES], raw[:, TILES:]
            own[0, j * windows + w] = real + imag
            own[1, j * windows + w] = real
            own[2, j * windows + w] = imag
            return carry

        lax.fori_loop(0, windows, widen, 0)


def widen_own(blocks):
    windows, stations = blocks[0].shape[:2]
    vmem = pl.BlockSpec(memory_space=pltpu.VMEM)
    return pl.pallas_call(
        widen_kernel,
        out_shape=jax.ShapeDtypeStruct((3, len(blocks) * windows, stations, TILES, LANES), F32),
        in_specs=[vmem] * len(blocks),
        out_specs=vmem,
        compiler_params=pltpu.CompilerParams(vmem_limit_bytes=16 * 2**20),
        cost_estimate=expected(0.6),
        name="widen",
    )(*blocks)


def sum_windows(first_slot, slots, count, offsets, plan, own, candidates, other, before, crossed):
    windows, stations = own.shape[1:3]
    quarter = other.shape[3]
    width = stations * quarter
    steps, ranks = partner_steps(plan, count)
    for slot in range(slots):
        step = jnp.int32(0)
        for number in range(ROUNDS):
            step = jnp.where(ranks[number] == first_slot + slot, steps[number], step)
        for offset, candidate in zip(offsets, candidates):

            @pl.when(step == offset)
            def _(candidate=candidate, slot=slot):
                def widen_other(w, carry):
                    raw = candidate[w].astype(F32)
                    real, imag = raw[:, :TILES], raw[:, TILES:]
                    other[0, slot, w] = real
                    other[1, slot, w] = real + imag
                    other[2, slot, w] = imag - real
                    return carry

                lax.fori_loop(0, windows, widen_other, 0)

    group = 4
    groups = stations // group

    def one_group(index, carry):
        slot = index // groups
        first = (index % groups) * group

        def sums(kind):
            totals = [None] * (group * quarter)
            for w in range(windows):
                left = [own[kind, w, first + s] for s in range(group)]
                right = [other[kind, slot, w, t] for t in range(quarter)]
                for s in range(group):
                    for t in range(quarter):
                        term = left[s] * right[t]
                        place = s * quarter + t
                        totals[place] = term if w == 0 else totals[place] + term
            return totals

        def store(place, part, value):
            at = pl.multiple_of((base + place) * 2 * TILES + part * TILES, TILES)
            if before is not None:
                value = value + before[pl.ds(at, TILES), :]
            crossed[pl.ds(at, TILES), :] = value

        base = slot * width + first * quarter
        shared = sums(0)
        third = sums(2)
        for place in range(group * quarter):
            store(place, 0, shared[place] + third[place])
        second = sums(1)
        for place in range(group * quarter):
            store(place, 1, shared[place] - second[place])
        return carry

    lax.fori_loop(0, slots * groups, one_group, 0)


def near_kernel(first_slot, slots, count, offsets, plan, own, *rest):
    candidates = rest[: len(offsets)]
    crossed, other = rest[len(offsets) :]
    sum_windows(
        first_slot, slots, count, offsets, plan, own, candidates, other, None, crossed
    )


def near_sums(plan, own, offsets, candidates, first_slot, slots, count):
    windows, stations = own.shape[1:3]
    quarter = candidates[0].shape[1]
    columns = slots * stations * quarter
    vmem = pl.BlockSpec(memory_space=pltpu.VMEM)
    return pl.pallas_call(
        functools.partial(near_kernel, first_slot, slots, count, tuple(offsets)),
        out_shape=jax.ShapeDtypeStruct((columns * 2 * TILES, LANES), F32),
        in_specs=[pl.BlockSpec(memory_space=pltpu.SMEM)] + [vmem] * (1 + len(candidates)),
        out_specs=vmem,
        scratch_shapes=[pltpu.VMEM((3, slots, windows, quarter, TILES, LANES), F32)],
        compiler_params=pltpu.CompilerParams(vmem_limit_bytes=16 * 2**20),
        cost_estimate=expected(0.4 + 0.7 * slots),
        name="near",
    )(plan, own, *candidates)


def far_kernel(first_slot, slots, count, scaling, offsets, parts, plan, table, own, before, *rest):
    candidates = rest[: len(offsets)]
    outs = rest[len(offsets) : len(offsets) + parts]
    other, crossed, operand, result = rest[len(offsets) + parts :]
    sum_windows(
        first_slot, slots, count, offsets, plan, own, candidates, other, before, crossed
    )
    width = own.shape[2] * other.shape[3]
    columns = slots * width
    even = even_lanes((columns, LANES))
    sign_real = lane_cycle([1.0, -1.0, -1.0, 1.0])
    sign_imag = lane_cycle([1.0, 1.0, -1.0, -1.0])
    cosine, sine = eighth_turn()
    lane = lax.broadcasted_iota(jnp.int32, (1, LANES), 1)
    first_weight = jnp.where(lane == 0, 1.0, 2.0).astype(F32)
    for j in range(TILES):
        at = slice(j * LANES, (j + 1) * LANES)
        at_imag = slice(NBIN + j * LANES, NBIN + (j + 1) * LANES)
        weight = first_weight if j == 0 else 2.0
        real = crossed[pl.ds(j, columns, stride=2 * TILES), :] * weight
        imag = crossed[pl.ds(TILES + j, columns, stride=2 * TILES), :] * weight
        turned = [(real, imag), (real * cosine - imag * sine, imag * cosine + real * sine)]
        turned += [quarter_turns(r, i, even, sign_real, sign_imag) for r, i in turned]
        for q in range(CHUNKS):
            rows = slice(q * columns, (q + 1) * columns)
            operand[rows, at] = turned[q][0].astype(BF)
            operand[rows, at_imag] = turned[q][1].astype(BF)
    block = lax.dot_general(
        table[...], operand[...], (((1,), (1,)), ((), ())), preferred_element_type=F32
    )
    block = block * scaling
    if slots == 1:
        half = table.shape[0] // 2
        low_lanes = lax.broadcasted_iota(jnp.int32, (half, LANES), 1) < width
        for p in range(CHUNKS // 2):
            at = slice(p * LANES, (p + 1) * LANES)
            low, high = block[:half, at], block[half:, at]
            pair = (
                jnp.where(low_lanes, low, pltpu.roll(high, width, 1)),
                jnp.where(low_lanes, pltpu.roll(low, width, 1), high),
            )
            for second in range(2):
                result[2 * p + second] = pair[second].astype(BF)
    else:
        for q in range(CHUNKS):
            result[q] = block[:, q * columns : (q + 1) * columns].astype(BF)
    me = lax.axis_index("seg")
    for j in range(parts):
        outs[j][...] = result[me ^ j]


def cross_lags(plan, table, own, before, offsets, candidates, first_slot, slots, count, parts, scaling):
    windows, stations = own.shape[1:3]
    quarter = candidates[0].shape[1]
    columns = slots * stations * quarter
    share = LAGS // parts
    out = (share, columns) if slots > 1 else (share // 2, 2 * columns)
    smem = pl.BlockSpec(memory_space=pltpu.SMEM)
    vmem = pl.BlockSpec(memory_space=pltpu.VMEM)
    return pl.pallas_call(
        functools.partial(
            far_kernel, first_slot, slots, count, scaling, tuple(offsets), parts
        ),
        out_shape=[jax.ShapeDtypeStruct(out, BF)] * parts,
        in_specs=[smem] + [vmem] * (3 + len(candidates)),
        out_specs=[vmem] * parts,
        scratch_shapes=[
            pltpu.VMEM((3, slots, windows, quarter, TILES, LANES), F32),
            pltpu.VMEM((columns * 2 * TILES, LANES), F32),
            pltpu.VMEM((CHUNKS * columns, 2 * NBIN), BF),
            pltpu.VMEM((parts,) + out, BF),
        ],
        compiler_params=pltpu.CompilerParams(vmem_limit_bytes=24 * 2**20),
        cost_estimate=expected(0.5 + 1.2 * slots),
        name="far",
    )(plan, table, own, before, *candidates)


def slot_rounds(plan, count):
    _, ranks = partner_steps(plan, count)
    rounds = []
    for slot in range(ROUNDS):
        number = jnp.int32(0)
        for other in range(1, ROUNDS):
            number = jnp.where(ranks[other] == slot, other, number)
        rounds.append(number)
    return rounds


def placed_block(pieces, matrix, at, half):
    joined = jnp.concatenate([piece[at, :] for piece in pieces], axis=1)
    if pieces[0].shape[0] > half:
        later = slice(half + at.start, half + at.stop)
        high = jnp.concatenate([piece[later, :] for piece in pieces], axis=1)
        joined = jnp.concatenate([joined, high], axis=0)
    return jnp.dot(joined, matrix, preferred_element_type=F32)


def joined_matrix(place, parts):
    me = lax.axis_index("seg")
    return jnp.concatenate([place[me ^ j] for j in range(parts)], axis=0)


def early_kernel(parts, groups, place, *rest):
    pieces, out = rest[:-1], rest[-1]
    half, pairs = out.shape[2:]
    matrix = joined_matrix(place, parts)
    at = slice(0, half)
    for index, (first_slot, slots) in enumerate(groups):
        block = placed_block(pieces[index * parts : (index + 1) * parts], matrix, at, half)
        if slots == 1:
            out[first_slot, 0] = block[:, :pairs]
            out[first_slot, 1] = block[:, pairs:]
        else:
            for slot in range(2):
                columns = slice(slot * pairs, (slot + 1) * pairs)
                out[first_slot + slot, 0] = block[:half, columns]
                out[first_slot + slot, 1] = block[half:, columns]


def late_kernel(count, parts, steps, plan, place, early, *rest):
    pieces = rest[:parts]
    out_hbm, out, sems = rest[parts:]
    half, _, pairs = out.shape[1:]
    rows = half // steps
    rounds = slot_rounds(plan, count)
    matrix = joined_matrix(place, parts)
    copies = []
    for step in range(steps):
        at = slice(step * rows, (step + 1) * rows)
        block = placed_block(pieces, matrix, at, half)
        for h in range(2):
            for slot in range(ROUNDS - 1):
                out[h, at, rounds[slot], :] = early[slot, h, at, :]
            out[h, at, rounds[ROUNDS - 1], :] = block[:, h * pairs : (h + 1) * pairs]
            copy = pltpu.make_async_copy(
                out.at[h, at], out_hbm.at[h, at], sems.at[2 * step + h]
            )
            copy.start()
            copies.append(copy)
    for copy in copies:
        copy.wait()


def place_lags(plan, groups, pieces, count, stations, parts):
    pairs = stations * stations
    share = LAGS // parts
    half = share // 2
    steps = 2
    place = jnp.asarray(make_placing(stations, stations // parts, parts))
    vmem = pl.BlockSpec(memory_space=pltpu.VMEM)
    early = pl.pallas_call(
        functools.partial(early_kernel, parts, tuple(groups[:-1])),
        out_shape=jax.ShapeDtypeStruct((ROUNDS - 1, 2, half, pairs), F32),
        in_specs=[vmem] * (1 + len(pieces) - parts),
        out_specs=vmem,
        compiler_params=pltpu.CompilerParams(vmem_limit_bytes=16 * 2**20),
        cost_estimate=expected(1.0),
        name="early",
    )(place, *pieces[:-parts])
    shape = (2, half, ROUNDS, pairs)
    out = pl.pallas_call(
        functools.partial(late_kernel, count, parts, steps),
        out_shape=jax.ShapeDtypeStruct(shape, F32),
        in_specs=[pl.BlockSpec(memory_space=pltpu.SMEM)] + [vmem] * (2 + parts),
        out_specs=pl.BlockSpec(memory_space=pl.ANY),
        scratch_shapes=[pltpu.VMEM(shape, F32), pltpu.SemaphoreType.DMA((2 * steps,))],
        compiler_params=pltpu.CompilerParams(vmem_limit_bytes=24 * 2**20),
        cost_estimate=expected(1.5),
        name="late",
    )(plan, place, early, *pieces[-parts:])
    return out.reshape(share, ROUNDS, pairs)


def swap(value, j):
    parts = lax.axis_size("seg")
    return lax.ppermute(value, "seg", [(i, i ^ j) for i in range(parts)])


def exchange(pieces):
    return [pieces[0]] + [swap(pieces[j], j) for j in range(1, len(pieces))]


def after(value, others):
    return lax.optimization_barrier((value, others))[0]


def per_device(records, plan):
    stations, windows, length = records.shape
    count = lax.axis_size("sta")
    parts = lax.axis_size("seg")
    quarter = stations // parts
    table = jnp.asarray(make_table(length // CHUNKS, 2 * length))
    scaling = 1.0 / math.sqrt(4.0 * NBIN * windows * parts)

    white, mine, *far = prepare(records, table, parts)
    sibling = swap(white, 1)
    first = lax.axis_index("seg") * quarter
    near = jnp.concatenate([mine, lax.dynamic_slice_in_dim(sibling, first, quarter, 1)])
    far = jnp.concatenate([swap(piece, 2 + j) for j, piece in enumerate(far)])
    far, white_far = lax.optimization_barrier((far, white))
    across = swap(white_far, 2)

    ring = sorted(range(count), key=lambda b: b // 2 if b % 2 == 0 else count - 1 - b // 2)
    upward = [(ring[i], ring[(i + 1) % count]) for i in range(count)]
    downward = [(ring[i], ring[i - 1]) for i in range(count)]

    def up(value):
        return lax.ppermute(value, "sta", upward)

    def down(value):
        return lax.ppermute(value, "sta", downward)

    near_up = near_down = near
    far_up = far_down = far
    near_own = widen_own([white, sibling])
    steps = (count - 1) // 2
    groups = [(0, 1), (1, 2), (3, 1)]
    arrived = []
    spots, near_blocks, far_blocks = [], [], []
    lags, pieces = [], []

    def group_lags(index, near_own, far_own):
        first_slot, slots = groups[index]
        at, nears, fars = arrived[index - len(groups)]
        before = near_sums(plan, near_own, at, nears, first_slot, slots, count)
        if index == 1:
            before = after(before, pieces)
        return cross_lags(
            plan, table, far_own, before, at, fars, first_slot, slots, count, parts, scaling
        )

    for step in range(1, steps + 1):
        if step == 2:
            near_up, near_down = lax.optimization_barrier((near_up, near_down))
        elif step > 2:
            near_up, near_down, last_up, last_down = lax.optimization_barrier(
                (near_up, near_down, last_up, last_down)
            )
        last_up, last_down = far_up, far_down
        next_near = up(near_up), down(near_down)
        if step == 2:
            far_up, far_down, near_up, near_down, near_own = lax.optimization_barrier(
                (far_up, far_down, near_up, near_down, near_own)
            )
        elif step == 3:
            far_up, far_down, near_up, near_down, across = lax.optimization_barrier(
                (far_up, far_down, near_up, near_down, across)
            )
        elif step > 1:
            far_up, far_down, near_up, near_down = lax.optimization_barrier(
                (far_up, far_down, near_up, near_down)
            )
        far_up, far_down = up(far_up), down(far_down)
        near_up, near_down = next_near
        spots += [count - step, step]
        near_blocks += [near_up, near_down]
        far_blocks += [far_up, far_down]
        arrived.append((list(spots), list(near_blocks), list(far_blocks)))
    far_own = widen_own([across, swap(across, 1)])
    arrived.append(arrived[-1])
    lags = group_lags(0, near_own, far_own)
    pieces = exchange(lags)
    if count % 2 == 0:
        near_up = after(near_up, lags)
        middle_up = up(near_up)
        far_down = after(far_down, (near_up, near_down))
        arrived[-1] = (
            spots + [count // 2], near_blocks + [middle_up], far_blocks + [down(far_down)]
        )
    for index in range(1, len(groups)):
        near_own = after(near_own, lags)
        lags = group_lags(index, near_own, far_own)
        pieces = pieces + exchange(lags)
    return place_lags(plan, groups, pieces, count, stations, parts)


def solution(mesh):
    in_specs = (P("sta", "seg", None), P())
    out_specs = P("seg", None, "sta")
    return jax.shard_map(
        per_device, mesh=mesh, in_specs=in_specs, out_specs=out_specs, check_vma=False
    )
```

```python
import functools
import math

import jax
import jax.numpy as jnp
import ml_dtypes
import numpy as np
from jax import lax
from jax.experimental import pallas as pl
from jax.experimental.pallas import tpu as pltpu
from jax.sharding import PartitionSpec as P

NBIN = 1024
HALF = 64
ROUNDS = 4
LAGS = 2048
LANES = 128
TILES = NBIN // LANES
CHUNKS = 4
BF = jnp.bfloat16
F32 = jnp.float32


def make_table(rows, transform):
    phase = (np.arange(rows)[:, None] * np.arange(NBIN)[None, :]) % transform
    angle = phase * (2.0 * math.pi / transform)
    return np.concatenate([np.cos(angle), -np.sin(angle)], axis=1).astype(ml_dtypes.bfloat16)


def band_matrix():
    source = lax.broadcasted_iota(jnp.int32, (3 * LANES, LANES), 0) - LANES
    target = lax.broadcasted_iota(jnp.int32, (3 * LANES, LANES), 1)
    return jnp.where(jnp.abs(source - target) <= HALF, 1.0, 0.0).astype(BF)


def inverse_count(block, length):
    position = lax.broadcasted_iota(jnp.int32, (1, LANES), 1) + block * LANES
    counted = jnp.minimum(position, HALF) + jnp.minimum(length - 1 - position, HALF) + 1
    return 1.0 / counted.astype(F32)


def make_placing(stations, quarter, parts):
    width = stations * quarter
    place = np.zeros((parts, 2 * width, 2 * stations * stations), np.float32)
    for part in range(parts):
        for second in range(2):
            for s in range(stations):
                for t in range(quarter):
                    row = second * width + s * quarter + t
                    column = (second * stations + s) * stations + part * quarter + t
                    place[part, row, column] = 1.0
    return place.astype(ml_dtypes.bfloat16)


def lane_cycle(values):
    period = len(values)
    phase = lax.broadcasted_iota(jnp.int32, (1, LANES), 1) % period
    out = jnp.full((1, LANES), values[-1], F32)
    for index in range(period - 1):
        out = jnp.where(phase == index, values[index], out)
    return out


def even_lanes(shape):
    return lax.broadcasted_iota(jnp.int32, shape, 1) % 2 == 0


def eighth_turn():
    turns = [math.pi * k / 4.0 for k in range(8)]
    return lane_cycle([math.cos(t) for t in turns]), lane_cycle([math.sin(t) for t in turns])


def quarter_turns(real, imag, even, sign_real, sign_imag):
    return sign_real * jnp.where(even, real, imag), sign_imag * jnp.where(even, imag, real)


def banded_sum(stack, values, band):
    rows, length = values.shape
    blocks = length // LANES
    zero = jnp.zeros((rows, LANES), BF)
    for j in range(blocks):
        at = pl.ds(j * rows, rows)
        for k in range(3):
            b = j + k - 1
            block = values[:, b * LANES : (b + 1) * LANES] if 0 <= b < blocks else zero
            stack[at, k * LANES : (k + 1) * LANES] = block
    total = jnp.dot(stack[: blocks * rows, :], band, preferred_element_type=F32)
    return [total[j * rows : (j + 1) * rows, :] for j in range(blocks)]


def prep_kernel(parts, records_hbm, table_hbm, white, mine, *rest):
    others = rest[: parts - 2]
    records, table, stack, flat, spread, sems = rest[parts - 2 :]
    records_copy = pltpu.make_async_copy(records_hbm, records, sems.at[0])
    records_copy.start()
    copy = pltpu.make_async_copy(table_hbm, table, sems.at[1])
    copy.start()
    band_values = band_matrix()
    records_copy.wait()
    stations, windows, length = records.shape
    rows = stations * windows
    chunk = length // CHUNKS
    signal = jnp.concatenate([records[:, w, :] for w in range(windows)], axis=0)
    sums = banded_sum(stack, jnp.abs(signal).astype(BF), band_values)
    for j, total in enumerate(sums):
        at = slice(j * LANES, (j + 1) * LANES)
        level = total * inverse_count(j, length)
        value = (signal[:, at] / (level + 1e-05)).astype(BF)
        q, inside = divmod(j * LANES, chunk)
        flat[q * rows : (q + 1) * rows, inside : inside + LANES] = value
    copy.wait()
    product = jnp.dot(flat[...], table[...], preferred_element_type=F32)
    even = even_lanes((rows, LANES))
    sign_real = lane_cycle([1.0, 1.0, -1.0, -1.0])
    sign_imag = lane_cycle([1.0, -1.0, -1.0, 1.0])
    cosine, sine = eighth_turn()
    reals, imags, mags = [], [], []
    for j in range(TILES):
        at = slice(j * LANES, (j + 1) * LANES)
        at_imag = slice(NBIN + j * LANES, NBIN + (j + 1) * LANES)
        pr = [product[q * rows : (q + 1) * rows, at] for q in range(CHUNKS)]
        pi = [product[q * rows : (q + 1) * rows, at_imag] for q in range(CHUNKS)]
        turned = [
            quarter_turns(pr[q], pi[q], even, sign_real, sign_imag) for q in range(2, CHUNKS)
        ]
        first_real, first_imag = pr[0] + turned[0][0], pi[0] + turned[0][1]
        odd_real, odd_imag = pr[1] + turned[1][0], pi[1] + turned[1][1]
        real = first_real + (odd_real * cosine + odd_imag * sine)
        imag = first_imag + (odd_imag * cosine - odd_real * sine)
        reals.append(real)
        imags.append(imag)
        mags.append(jnp.sqrt(real * real + imag * imag).astype(BF))
    sums = banded_sum(stack, jnp.concatenate(mags, axis=1), band_values)
    for j, total in enumerate(sums):
        at = slice(j * LANES, (j + 1) * LANES)
        smooth = total * inverse_count(j, NBIN) + 1e-06
        spread[pl.ds(j, rows, stride=2 * TILES), :] = reals[j] / smooth
        spread[pl.ds(TILES + j, rows, stride=2 * TILES), :] = imags[j] / smooth
    me = lax.axis_index("seg")
    quarter = stations // parts
    white[...] = spread[...].reshape(windows, stations, 2 * TILES, LANES).astype(BF)
    for j, out in [(0, mine)] + list(zip(range(2, parts), others)):
        for w in range(windows):
            out[w] = white[w, pl.ds((me ^ j) * quarter, quarter)]


def prepare(records, table, parts):
    stations, windows, length = records.shape
    rows = stations * windows
    quarter = stations // parts
    small = jax.ShapeDtypeStruct((windows, quarter, 2 * TILES, LANES), BF)
    vmem = pl.BlockSpec(memory_space=pltpu.VMEM)
    return pl.pallas_call(
        functools.partial(prep_kernel, parts),
        out_shape=[jax.ShapeDtypeStruct((windows, stations, 2 * TILES, LANES), BF)]
        + [small] * (parts - 1),
        in_specs=[pl.BlockSpec(memory_space=pltpu.HBM)] * 2,
        out_specs=[vmem] * parts,
        scratch_shapes=[
            pltpu.VMEM(records.shape, F32),
            pltpu.VMEM(table.shape, BF),
            pltpu.VMEM((rows * (length // LANES), 3 * LANES), BF),
            pltpu.VMEM((CHUNKS * rows, length // CHUNKS), BF),
            pltpu.VMEM((rows * 2 * TILES, LANES), F32),
            pltpu.SemaphoreType.DMA((2,)),
        ],
        compiler_params=pltpu.CompilerParams(vmem_limit_bytes=52 * 2**20),
        cost_estimate=pl.CostEstimate(
            flops=2 * rows * length * 2 * NBIN, bytes_accessed=3 * 2**20, transcendentals=0
        ),
        name="prep",
    )(
        pltpu.with_memory_space_constraint(records, pltpu.HBM),
        pltpu.with_memory_space_constraint(table, pltpu.HBM),
    )


def ring_place(block, count):
    half = block >> 1
    return jnp.where((block & 1) == 0, half, count - 1 - half)


def partner_steps(plan, count):
    me = lax.axis_index("sta")
    mine = ring_place(me, count)
    steps, keys = [], []
    for number in range(ROUNDS):
        step = ring_place(plan[number, me], count) - mine
        step = jnp.where(step < 0, step + count, step)
        steps.append(step)
        keys.append(jnp.minimum(step, count - step) * ROUNDS + number)
    ranks = []
    for number in range(ROUNDS):
        rank = jnp.int32(0)
        for other in range(ROUNDS):
            if other != number:
                rank = rank + jnp.where(keys[other] < keys[number], 1, 0)
        ranks.append(rank)
    return steps, ranks


def expected(microseconds):
    return pl.CostEstimate(
        flops=int(microseconds * 1.15e9), bytes_accessed=1024, transcendentals=0
    )


def widen_kernel(*refs):
    blocks, own = refs[:-1], refs[-1]
    windows = blocks[0].shape[0]
    for j, block in enumerate(blocks):

        def widen(w, carry, j=j, block=block):
            raw = block[w].astype(F32)
            real, imag = raw[:, :TILES], raw[:, TILES:]
            own[0, j * windows + w] = real + imag
            own[1, j * windows + w] = real
            own[2, j * windows + w] = imag
            return carry

        lax.fori_loop(0, windows, widen, 0)


def widen_own(blocks):
    windows, stations = blocks[0].shape[:2]
    vmem = pl.BlockSpec(memory_space=pltpu.VMEM)
    return pl.pallas_call(
        widen_kernel,
        out_shape=jax.ShapeDtypeStruct((3, len(blocks) * windows, stations, TILES, LANES), F32),
        in_specs=[vmem] * len(blocks),
        out_specs=vmem,
        compiler_params=pltpu.CompilerParams(vmem_limit_bytes=16 * 2**20),
        cost_estimate=expected(0.05),
        name="widen",
    )(*blocks)


def widen_others(first_slot, slots, count, offsets, plan, candidates, first, other):
    steps, ranks = partner_steps(plan, count)
    windows = candidates[0].shape[0]
    for slot in range(slots):
        step = jnp.int32(0)
        for number in range(ROUNDS):
            step = jnp.where(ranks[number] == first_slot + slot, steps[number], step)
        for offset, candidate in zip(offsets, candidates):

            @pl.when(step == offset)
            def _(candidate=candidate, slot=slot):
                def widen_other(w, carry):
                    raw = candidate[w].astype(F32)
                    real, imag = raw[:, :TILES], raw[:, TILES:]
                    other[0, slot, first + w] = real
                    other[1, slot, first + w] = real + imag
                    other[2, slot, first + w] = imag - real
                    return carry

                lax.fori_loop(0, windows, widen_other, 0)


def sum_windows(owns, other, before, crossed):
    windows, stations = owns[0].shape[1:3]
    slots, _, quarter = other.shape[1:4]
    width = stations * quarter
    group = 4
    groups = stations // group

    def one_group(slot, index):
        first = index * group

        def sums(kind):
            totals = [None] * (group * quarter)
            for part, own in enumerate(owns):
                for w in range(windows):
                    left = [own[kind, w, first + s] for s in range(group)]
                    right = [other[kind, slot, part * windows + w, t] for t in range(quarter)]
                    for s in range(group):
                        for t in range(quarter):
                            term = left[s] * right[t]
                            place = s * quarter + t
                            old = totals[place]
                            totals[place] = term if old is None else old + term
            return totals

        def store(place, part, value):
            at = pl.multiple_of((base + place) * 2 * TILES + part * TILES, TILES)
            if before is not None:
                value = value + before[pl.ds(at, TILES), :]
            crossed[pl.ds(at, TILES), :] = value

        base = slot * width + first * quarter
        shared = sums(0)
        third = sums(2)
        for place in range(group * quarter):
            store(place, 0, shared[place] + third[place])
        second = sums(1)
        for place in range(group * quarter):
            store(place, 1, shared[place] - second[place])

    for slot in range(slots):

        def body(index, carry, slot=slot):
            one_group(slot, index)
            return carry

        lax.fori_loop(0, groups, body, 0)


def near_kernel(first_slot, slots, count, offsets, plan, own, *rest):
    candidates = rest[: len(offsets)]
    crossed, other = rest[len(offsets) :]
    widen_others(first_slot, slots, count, offsets, plan, candidates, 0, other)
    sum_windows([own], other, None, crossed)


def near_sums(plan, own, offsets, candidates, first_slot, slots, count):
    windows, stations = own.shape[1:3]
    quarter = candidates[0].shape[1]
    columns = slots * stations * quarter
    vmem = pl.BlockSpec(memory_space=pltpu.VMEM)
    return pl.pallas_call(
        functools.partial(near_kernel, first_slot, slots, count, tuple(offsets)),
        out_shape=jax.ShapeDtypeStruct((columns * 2 * TILES, LANES), F32),
        in_specs=[pl.BlockSpec(memory_space=pltpu.SMEM)] + [vmem] * (1 + len(candidates)),
        out_specs=vmem,
        scratch_shapes=[pltpu.VMEM((3, slots, windows, quarter, TILES, LANES), F32)],
        compiler_params=pltpu.CompilerParams(vmem_limit_bytes=16 * 2**20),
        cost_estimate=expected(0.05),
        name="near",
    )(plan, own, *candidates)


def cross_kernel(first_slot, slots, count, scaling, offsets, parts, joint, plan, table, *rest):
    size = len(offsets)
    owns, rest = rest[: 1 + joint], rest[1 + joint :]
    before = None
    if not joint:
        before, rest = rest[0], rest[1:]
    others, rest = rest[: size * (1 + joint)], rest[size * (1 + joint) :]
    outs = rest[:parts]
    other, crossed, operand, result = rest[parts:]
    windows, stations = owns[0].shape[1:3]
    for part in range(1 + joint):
        widen_others(
            first_slot, slots, count, offsets, plan, others[part * size : (part + 1) * size],
            part * windows, other,
        )
    sum_windows(owns, other, before, crossed)
    width = stations * other.shape[3]
    columns = slots * width
    even = even_lanes((columns, LANES))
    sign_real = lane_cycle([1.0, -1.0, -1.0, 1.0])
    sign_imag = lane_cycle([1.0, 1.0, -1.0, -1.0])
    cosine, sine = eighth_turn()
    lane = lax.broadcasted_iota(jnp.int32, (1, LANES), 1)
    first_weight = jnp.where(lane == 0, 1.0, 2.0).astype(F32)
    for j in range(TILES):
        at = slice(j * LANES, (j + 1) * LANES)
        at_imag = slice(NBIN + j * LANES, NBIN + (j + 1) * LANES)
        weight = first_weight if j == 0 else 2.0
        real = crossed[pl.ds(j, columns, stride=2 * TILES), :] * weight
        imag = crossed[pl.ds(TILES + j, columns, stride=2 * TILES), :] * weight
        turned = [(real, imag), (real * cosine - imag * sine, imag * cosine + real * sine)]
        turned += [quarter_turns(r, i, even, sign_real, sign_imag) for r, i in turned]
        for q in range(CHUNKS):
            rows = slice(q * columns, (q + 1) * columns)
            operand[rows, at] = turned[q][0].astype(BF)
            operand[rows, at_imag] = turned[q][1].astype(BF)
    block = lax.dot_general(
        table[...], operand[...], (((1,), (1,)), ((), ())), preferred_element_type=F32
    )
    block = block * scaling
    if slots == 1:
        half = table.shape[0] // 2
        low_lanes = lax.broadcasted_iota(jnp.int32, (half, LANES), 1) < width
        for p in range(CHUNKS // 2):
            at = slice(p * LANES, (p + 1) * LANES)
            low, high = block[:half, at], block[half:, at]
            pair = (
                jnp.where(low_lanes, low, pltpu.roll(high, width, 1)),
                jnp.where(low_lanes, pltpu.roll(low, width, 1), high),
            )
            for second in range(2):
                result[2 * p + second] = pair[second].astype(BF)
    else:
        for q in range(CHUNKS):
            result[q] = block[:, q * columns : (q + 1) * columns].astype(BF)
    me = lax.axis_index("seg")
    for j in range(parts):
        outs[j][...] = result[me ^ j]


def cross_lags(
    plan, table, owns, before, offsets, candidates, first_slot, slots, count, parts, scaling
):
    joint = len(owns) - 1
    windows, stations = owns[0].shape[1:3]
    quarter = candidates[0].shape[1]
    columns = slots * stations * quarter
    share = LAGS // parts
    out = (share, columns) if slots > 1 else (share // 2, 2 * columns)
    smem = pl.BlockSpec(memory_space=pltpu.SMEM)
    vmem = pl.BlockSpec(memory_space=pltpu.VMEM)
    operands = [table, *owns] + ([] if joint else [before]) + list(candidates)
    return pl.pallas_call(
        functools.partial(
            cross_kernel, first_slot, slots, count, scaling, tuple(offsets), parts, joint
        ),
        out_shape=[jax.ShapeDtypeStruct(out, BF)] * parts,
        in_specs=[smem] + [vmem] * len(operands),
        out_specs=[vmem] * parts,
        scratch_shapes=[
            pltpu.VMEM((3, slots, (1 + joint) * windows, quarter, TILES, LANES), F32),
            pltpu.VMEM((columns * 2 * TILES, LANES), F32),
            pltpu.VMEM((CHUNKS * columns, 2 * NBIN), BF),
            pltpu.VMEM((parts,) + out, BF),
        ],
        compiler_params=pltpu.CompilerParams(vmem_limit_bytes=24 * 2**20),
        cost_estimate=expected(1 * (0.6 + 2.0 * slots) if joint else 1.7),
        name="cross",
    )(plan, *operands)


def slot_rounds(plan, count):
    _, ranks = partner_steps(plan, count)
    rounds = []
    for slot in range(ROUNDS):
        number = jnp.int32(0)
        for other in range(1, ROUNDS):
            number = jnp.where(ranks[other] == slot, other, number)
        rounds.append(number)
    return rounds


def placed_block(pieces, matrix, at, half):
    joined = jnp.concatenate([piece[at, :] for piece in pieces], axis=1)
    if pieces[0].shape[0] > half:
        later = slice(half + at.start, half + at.stop)
        high = jnp.concatenate([piece[later, :] for piece in pieces], axis=1)
        joined = jnp.concatenate([joined, high], axis=0)
    return jnp.dot(joined, matrix, preferred_element_type=F32)


def joined_matrix(place, parts):
    me = lax.axis_index("seg")
    return jnp.concatenate([place[me ^ j] for j in range(parts)], axis=0)


def early_kernel(parts, groups, place, *rest):
    pieces, out = rest[:-1], rest[-1]
    half, pairs = out.shape[2:]
    matrix = joined_matrix(place, parts)
    at = slice(0, half)
    for index, (first_slot, slots) in enumerate(groups):
        block = placed_block(pieces[index * parts : (index + 1) * parts], matrix, at, half)
        if slots == 1:
            out[first_slot, 0] = block[:, :pairs]
            out[first_slot, 1] = block[:, pairs:]
        else:
            for slot in range(2):
                columns = slice(slot * pairs, (slot + 1) * pairs)
                out[first_slot + slot, 0] = block[:half, columns]
                out[first_slot + slot, 1] = block[half:, columns]


def late_kernel(count, parts, steps, plan, place, early, *rest):
    pieces = rest[:parts]
    out_hbm, out, sems = rest[parts:]
    half, _, pairs = out.shape[1:]
    rows = half // steps
    rounds = slot_rounds(plan, count)
    matrix = joined_matrix(place, parts)
    block = placed_block(pieces, matrix, slice(0, half), half)
    copies = []
    for step in range(steps):
        at = slice(step * rows, (step + 1) * rows)
        for h in range(2):
            for slot in range(ROUNDS - 1):
                out[h, at, rounds[slot], :] = early[slot, h, at, :]
            out[h, at, rounds[ROUNDS - 1], :] = block[at, h * pairs : (h + 1) * pairs]
            copy = pltpu.make_async_copy(
                out.at[h, at], out_hbm.at[h, at], sems.at[2 * step + h]
            )
            copy.start()
            copies.append(copy)
    for copy in copies:
        copy.wait()


def place_lags(plan, groups, pieces, count, stations, parts):
    pairs = stations * stations
    share = LAGS // parts
    half = share // 2
    steps = 4
    place = jnp.asarray(make_placing(stations, stations // parts, parts))
    vmem = pl.BlockSpec(memory_space=pltpu.VMEM)
    early = pl.pallas_call(
        functools.partial(early_kernel, parts, tuple(groups[:-1])),
        out_shape=jax.ShapeDtypeStruct((ROUNDS - 1, 2, half, pairs), F32),
        in_specs=[vmem] * (1 + len(pieces) - parts),
        out_specs=vmem,
        compiler_params=pltpu.CompilerParams(vmem_limit_bytes=16 * 2**20),
        cost_estimate=expected(0.05),
        name="early",
    )(place, *pieces[:-parts])
    shape = (2, half, ROUNDS, pairs)
    out = pl.pallas_call(
        functools.partial(late_kernel, count, parts, steps),
        out_shape=jax.ShapeDtypeStruct(shape, F32),
        in_specs=[pl.BlockSpec(memory_space=pltpu.SMEM)] + [vmem] * (2 + parts),
        out_specs=pl.BlockSpec(memory_space=pl.ANY),
        scratch_shapes=[pltpu.VMEM(shape, F32), pltpu.SemaphoreType.DMA((2 * steps,))],
        compiler_params=pltpu.CompilerParams(vmem_limit_bytes=24 * 2**20),
        cost_estimate=expected(0.05),
        name="late",
    )(plan, place, early, *pieces[-parts:])
    return out.reshape(share, ROUNDS, pairs)


def swap(value, j):
    parts = lax.axis_size("seg")
    return lax.ppermute(value, "seg", [(i, i ^ j) for i in range(parts)])


def exchange(pieces):
    return [pieces[0]] + [swap(pieces[j], j) for j in range(1, len(pieces))]


def after(value, others):
    return lax.optimization_barrier((value, others))[0]


def per_device(records, plan):
    stations, windows, length = records.shape
    count = lax.axis_size("sta")
    parts = lax.axis_size("seg")
    quarter = stations // parts
    table = jnp.asarray(make_table(length // CHUNKS, 2 * length))
    scaling = 1.0 / math.sqrt(4.0 * NBIN * windows * parts)

    white, mine, *far = prepare(records, table, parts)
    sibling = swap(white, 1)
    first = lax.axis_index("seg") * quarter
    near = jnp.concatenate([mine, lax.dynamic_slice_in_dim(sibling, first, quarter, 1)])
    far = jnp.concatenate([swap(piece, 2 + j) for j, piece in enumerate(far)])

    ring = sorted(range(count), key=lambda b: b // 2 if b % 2 == 0 else count - 1 - b // 2)
    upward = [(ring[i], ring[(i + 1) % count]) for i in range(count)]
    downward = [(ring[i], ring[i - 1]) for i in range(count)]

    def up(value):
        return lax.ppermute(value, "sta", upward)

    def down(value):
        return lax.ppermute(value, "sta", downward)

    far, white_far = lax.optimization_barrier((far, white))
    across = swap(white_far, 2)
    near_up = near_down = near
    far_up = far_down = far
    near_own = widen_own([white, sibling])
    steps = (count - 1) // 2
    groups = [(0, 1), (1, 2), (3, 1)]
    arrived = []
    spots, near_blocks, far_blocks = [], [], []
    lags, pieces = [], []

    def group_lags(index, near_own, far_own):
        first_slot, slots = groups[index]
        at, nears, fars = arrived[index - len(groups)]
        return cross_lags(
            plan, table, [near_own, far_own], None, at, nears + fars, first_slot, slots, count,
            parts, scaling,
        )

    for step in range(1, steps + 1):
        if step == 2:
            near_up, near_down = lax.optimization_barrier((near_up, near_down))
        elif step > 2:
            near_up, near_down, last_up, last_down = lax.optimization_barrier(
                (near_up, near_down, last_up, last_down)
            )
        last_up, last_down = far_up, far_down
        next_near = up(near_up), down(near_down)
        if step == 2:
            far_up, far_down, near_up, near_down, near_own = lax.optimization_barrier(
                (far_up, far_down, near_up, near_down, near_own)
            )
        elif step == 3:
            far_up, far_down, near_up, near_down, across = lax.optimization_barrier(
                (far_up, far_down, near_up, near_down, across)
            )
        elif step > 3:
            far_up, far_down, near_up, near_down = lax.optimization_barrier(
                (far_up, far_down, near_up, near_down)
            )
        if step == steps and step > 1:
            at, nears, _ = arrived[-1]
            first_sums = near_sums(plan, near_own, at, nears, 0, 1, count)
        far_up, far_down = up(far_up), down(far_down)
        near_up, near_down = next_near
        spots += [count - step, step]
        near_blocks += [near_up, near_down]
        far_blocks += [far_up, far_down]
        arrived.append((list(spots), list(near_blocks), list(far_blocks)))
    far_own = widen_own([across, swap(across, 1)])
    arrived.append(arrived[-1])
    at, _, fars = arrived[-3]
    first_sums = after(first_sums, (near_up, near_down))
    lags = cross_lags(
        plan, table, [far_own], first_sums, at, fars, 0, 1, count, parts, scaling
    )
    pieces = exchange(lags)
    if count % 2 == 0:
        near_up = after(near_up, lags)
        middle_up = up(near_up)
        far_down = after(far_down, (near_up, near_down))
        arrived[-1] = (
            spots + [count // 2], near_blocks + [middle_up], far_blocks + [down(far_down)]
        )
    for index in range(1, len(groups)):
        if index == 1:
            near_own = after(near_own, pieces[:parts])
        near_own = after(near_own, lags)
        lags = group_lags(index, near_own, far_own)
        pieces = pieces + exchange(lags)
    return place_lags(plan, groups, pieces, count, stations, parts)


def solution(mesh):
    in_specs = (P("sta", "seg", None), P())
    out_specs = P("seg", None, "sta")
    return jax.shard_map(
        per_device, mesh=mesh, in_specs=in_specs, out_specs=out_specs, check_vma=False
    )
```

```python
import functools
import math

import jax
import jax.numpy as jnp
import ml_dtypes
import numpy as np
from jax import lax
from jax.experimental import pallas as pl
from jax.experimental.pallas import tpu as pltpu
from jax.sharding import PartitionSpec as P

NBIN = 1024
HALF = 64
ROUNDS = 4
LAGS = 2048
LANES = 128
TILES = NBIN // LANES
CHUNKS = 4
BF = jnp.bfloat16
F32 = jnp.float32


def make_table(rows, transform):
    phase = (np.arange(rows)[:, None] * np.arange(NBIN)[None, :]) % transform
    angle = phase * (2.0 * math.pi / transform)
    return np.concatenate([np.cos(angle), -np.sin(angle)], axis=1).astype(ml_dtypes.bfloat16)


def band_matrix():
    source = lax.broadcasted_iota(jnp.int32, (3 * LANES, LANES), 0) - LANES
    target = lax.broadcasted_iota(jnp.int32, (3 * LANES, LANES), 1)
    return jnp.where(jnp.abs(source - target) <= HALF, 1.0, 0.0).astype(BF)


def inverse_count(block, length):
    position = lax.broadcasted_iota(jnp.int32, (1, LANES), 1) + block * LANES
    counted = jnp.minimum(position, HALF) + jnp.minimum(length - 1 - position, HALF) + 1
    return 1.0 / counted.astype(F32)


def make_placing(stations, quarter, parts):
    width = stations * quarter
    place = np.zeros((parts, 2 * width, 2 * stations * stations), np.float32)
    for part in range(parts):
        for second in range(2):
            for s in range(stations):
                for t in range(quarter):
                    row = second * width + s * quarter + t
                    column = (second * stations + s) * stations + part * quarter + t
                    place[part, row, column] = 1.0
    return place.astype(ml_dtypes.bfloat16)


def lane_cycle(values):
    period = len(values)
    phase = lax.broadcasted_iota(jnp.int32, (1, LANES), 1) % period
    out = jnp.full((1, LANES), values[-1], F32)
    for index in range(period - 1):
        out = jnp.where(phase == index, values[index], out)
    return out


def even_lanes(shape):
    return lax.broadcasted_iota(jnp.int32, shape, 1) % 2 == 0


def eighth_turn():
    turns = [math.pi * k / 4.0 for k in range(8)]
    return lane_cycle([math.cos(t) for t in turns]), lane_cycle([math.sin(t) for t in turns])


def quarter_turns(real, imag, even, sign_real, sign_imag):
    return sign_real * jnp.where(even, real, imag), sign_imag * jnp.where(even, imag, real)


def banded_sum(stack, values, band):
    rows, length = values.shape
    blocks = length // LANES
    zero = jnp.zeros((rows, LANES), BF)
    for j in range(blocks):
        at = pl.ds(j * rows, rows)
        for k in range(3):
            b = j + k - 1
            block = values[:, b * LANES : (b + 1) * LANES] if 0 <= b < blocks else zero
            stack[at, k * LANES : (k + 1) * LANES] = block
    total = jnp.dot(stack[: blocks * rows, :], band, preferred_element_type=F32)
    return [total[j * rows : (j + 1) * rows, :] for j in range(blocks)]


def prep_kernel(parts, records_hbm, table_hbm, white, mine, *rest):
    others = rest[: parts - 2]
    records, table, stack, flat, spread, sems = rest[parts - 2 :]
    records_copy = pltpu.make_async_copy(records_hbm, records, sems.at[0])
    records_copy.start()
    copy = pltpu.make_async_copy(table_hbm, table, sems.at[1])
    copy.start()
    band_values = band_matrix()
    records_copy.wait()
    stations, windows, length = records.shape
    rows = stations * windows
    chunk = length // CHUNKS
    signal = jnp.concatenate([records[:, w, :] for w in range(windows)], axis=0)
    sums = banded_sum(stack, jnp.abs(signal).astype(BF), band_values)
    for j, total in enumerate(sums):
        at = slice(j * LANES, (j + 1) * LANES)
        level = total * inverse_count(j, length)
        value = (signal[:, at] / (level + 1e-05)).astype(BF)
        q, inside = divmod(j * LANES, chunk)
        flat[q * rows : (q + 1) * rows, inside : inside + LANES] = value
    copy.wait()
    product = jnp.dot(flat[...], table[...], preferred_element_type=F32)
    even = even_lanes((rows, LANES))
    sign_real = lane_cycle([1.0, 1.0, -1.0, -1.0])
    sign_imag = lane_cycle([1.0, -1.0, -1.0, 1.0])
    cosine, sine = eighth_turn()
    reals, imags, mags = [], [], []
    for j in range(TILES):
        at = slice(j * LANES, (j + 1) * LANES)
        at_imag = slice(NBIN + j * LANES, NBIN + (j + 1) * LANES)
        pr = [product[q * rows : (q + 1) * rows, at] for q in range(CHUNKS)]
        pi = [product[q * rows : (q + 1) * rows, at_imag] for q in range(CHUNKS)]
        turned = [
            quarter_turns(pr[q], pi[q], even, sign_real, sign_imag) for q in range(2, CHUNKS)
        ]
        first_real, first_imag = pr[0] + turned[0][0], pi[0] + turned[0][1]
        odd_real, odd_imag = pr[1] + turned[1][0], pi[1] + turned[1][1]
        real = first_real + (odd_real * cosine + odd_imag * sine)
        imag = first_imag + (odd_imag * cosine - odd_real * sine)
        reals.append(real)
        imags.append(imag)
        mags.append(jnp.sqrt(real * real + imag * imag).astype(BF))
    sums = banded_sum(stack, jnp.concatenate(mags, axis=1), band_values)
    for j, total in enumerate(sums):
        at = slice(j * LANES, (j + 1) * LANES)
        smooth = total * inverse_count(j, NBIN) + 1e-06
        spread[pl.ds(j, rows, stride=2 * TILES), :] = reals[j] / smooth
        spread[pl.ds(TILES + j, rows, stride=2 * TILES), :] = imags[j] / smooth
    me = lax.axis_index("seg")
    quarter = stations // parts
    white[...] = spread[...].reshape(windows, stations, 2 * TILES, LANES).astype(BF)
    for j, out in [(0, mine)] + list(zip(range(2, parts), others)):
        for w in range(windows):
            out[w] = white[w, pl.ds((me ^ j) * quarter, quarter)]


def prepare(records, table, parts):
    stations, windows, length = records.shape
    rows = stations * windows
    quarter = stations // parts
    small = jax.ShapeDtypeStruct((windows, quarter, 2 * TILES, LANES), BF)
    vmem = pl.BlockSpec(memory_space=pltpu.VMEM)
    return pl.pallas_call(
        functools.partial(prep_kernel, parts),
        out_shape=[jax.ShapeDtypeStruct((windows, stations, 2 * TILES, LANES), BF)]
        + [small] * (parts - 1),
        in_specs=[pl.BlockSpec(memory_space=pltpu.HBM)] * 2,
        out_specs=[vmem] * parts,
        scratch_shapes=[
            pltpu.VMEM(records.shape, F32),
            pltpu.VMEM(table.shape, BF),
            pltpu.VMEM((rows * (length // LANES), 3 * LANES), BF),
            pltpu.VMEM((CHUNKS * rows, length // CHUNKS), BF),
            pltpu.VMEM((rows * 2 * TILES, LANES), F32),
            pltpu.SemaphoreType.DMA((2,)),
        ],
        compiler_params=pltpu.CompilerParams(vmem_limit_bytes=52 * 2**20),
        cost_estimate=pl.CostEstimate(
            flops=2 * rows * length * 2 * NBIN, bytes_accessed=3 * 2**20, transcendentals=0
        ),
        name="prep",
    )(
        pltpu.with_memory_space_constraint(records, pltpu.HBM),
        pltpu.with_memory_space_constraint(table, pltpu.HBM),
    )


def ring_place(block, count):
    half = block >> 1
    return jnp.where((block & 1) == 0, half, count - 1 - half)


def partner_steps(plan, count):
    me = lax.axis_index("sta")
    mine = ring_place(me, count)
    steps, keys = [], []
    for number in range(ROUNDS):
        step = ring_place(plan[number, me], count) - mine
        step = jnp.where(step < 0, step + count, step)
        steps.append(step)
        keys.append(jnp.minimum(step, count - step) * ROUNDS + number)
    ranks = []
    for number in range(ROUNDS):
        rank = jnp.int32(0)
        for other in range(ROUNDS):
            if other != number:
                rank = rank + jnp.where(keys[other] < keys[number], 1, 0)
        ranks.append(rank)
    return steps, ranks


def expected(microseconds):
    return pl.CostEstimate(
        flops=int(microseconds * 1.15e9), bytes_accessed=1024, transcendentals=0
    )


def widen_kernel(*refs):
    blocks, own = refs[:-1], refs[-1]
    windows = blocks[0].shape[0]
    for j, block in enumerate(blocks):

        def widen(w, carry, j=j, block=block):
            raw = block[w].astype(F32)
            real, imag = raw[:, :TILES], raw[:, TILES:]
            own[0, j * windows + w] = real + imag
            own[1, j * windows + w] = real
            own[2, j * windows + w] = imag
            return carry

        lax.fori_loop(0, windows, widen, 0)


def widen_own(blocks):
    windows, stations = blocks[0].shape[:2]
    vmem = pl.BlockSpec(memory_space=pltpu.VMEM)
    return pl.pallas_call(
        widen_kernel,
        out_shape=jax.ShapeDtypeStruct((3, len(blocks) * windows, stations, TILES, LANES), F32),
        in_specs=[vmem] * len(blocks),
        out_specs=vmem,
        compiler_params=pltpu.CompilerParams(vmem_limit_bytes=16 * 2**20),
        cost_estimate=expected(0.05),
        name="widen",
    )(*blocks)


def widen_others(first_slot, slots, count, offsets, plan, candidates, first, other):
    steps, ranks = partner_steps(plan, count)
    windows = candidates[0].shape[0]
    for slot in range(slots):
        step = jnp.int32(0)
        for number in range(ROUNDS):
            step = jnp.where(ranks[number] == first_slot + slot, steps[number], step)
        for offset, candidate in zip(offsets, candidates):

            @pl.when(step == offset)
            def _(candidate=candidate, slot=slot):
                def widen_other(w, carry):
                    raw = candidate[w].astype(F32)
                    real, imag = raw[:, :TILES], raw[:, TILES:]
                    other[0, slot, first + w] = real
                    other[1, slot, first + w] = real + imag
                    other[2, slot, first + w] = imag - real
                    return carry

                lax.fori_loop(0, windows, widen_other, 0)


def sum_windows(owns, other, before, crossed):
    windows, stations = owns[0].shape[1:3]
    slots, _, quarter = other.shape[1:4]
    width = stations * quarter
    group = 4
    groups = stations // group

    def one_group(slot, index):
        first = index * group

        def sums(kind):
            totals = [None] * (group * quarter)
            for part, own in enumerate(owns):
                for w in range(windows):
                    left = [own[kind, w, first + s] for s in range(group)]
                    right = [other[kind, slot, part * windows + w, t] for t in range(quarter)]
                    for s in range(group):
                        for t in range(quarter):
                            term = left[s] * right[t]
                            place = s * quarter + t
                            old = totals[place]
                            totals[place] = term if old is None else old + term
            return totals

        def store(place, part, value):
            at = pl.multiple_of((base + place) * 2 * TILES + part * TILES, TILES)
            if before is not None:
                value = value + before[pl.ds(at, TILES), :]
            crossed[pl.ds(at, TILES), :] = value

        base = slot * width + first * quarter
        shared = sums(0)
        third = sums(2)
        for place in range(group * quarter):
            store(place, 0, shared[place] + third[place])
        second = sums(1)
        for place in range(group * quarter):
            store(place, 1, shared[place] - second[place])

    for slot in range(slots):

        def body(index, carry, slot=slot):
            one_group(slot, index)
            return carry

        lax.fori_loop(0, groups, body, 0)


def near_kernel(first_slot, slots, count, offsets, plan, own, *rest):
    candidates = rest[: len(offsets)]
    crossed, other = rest[len(offsets) :]
    widen_others(first_slot, slots, count, offsets, plan, candidates, 0, other)
    sum_windows([own], other, None, crossed)


def near_sums(plan, own, offsets, candidates, first_slot, slots, count):
    windows, stations = own.shape[1:3]
    quarter = candidates[0].shape[1]
    columns = slots * stations * quarter
    vmem = pl.BlockSpec(memory_space=pltpu.VMEM)
    return pl.pallas_call(
        functools.partial(near_kernel, first_slot, slots, count, tuple(offsets)),
        out_shape=jax.ShapeDtypeStruct((columns * 2 * TILES, LANES), F32),
        in_specs=[pl.BlockSpec(memory_space=pltpu.SMEM)] + [vmem] * (1 + len(candidates)),
        out_specs=vmem,
        scratch_shapes=[pltpu.VMEM((3, slots, windows, quarter, TILES, LANES), F32)],
        compiler_params=pltpu.CompilerParams(vmem_limit_bytes=16 * 2**20),
        cost_estimate=expected(0.05),
        name="near",
    )(plan, own, *candidates)


def cross_kernel(first_slot, slots, count, scaling, offsets, parts, joint, plan, table, *rest):
    size = len(offsets)
    owns, rest = rest[: 1 + joint], rest[1 + joint :]
    before = None
    if not joint:
        before, rest = rest[0], rest[1:]
    others, rest = rest[: size * (1 + joint)], rest[size * (1 + joint) :]
    outs = rest[:parts]
    other, crossed, operand, result = rest[parts:]
    windows, stations = owns[0].shape[1:3]
    for part in range(1 + joint):
        widen_others(
            first_slot, slots, count, offsets, plan, others[part * size : (part + 1) * size],
            part * windows, other,
        )
    sum_windows(owns, other, before, crossed)
    width = stations * other.shape[3]
    columns = slots * width
    even = even_lanes((columns, LANES))
    sign_real = lane_cycle([1.0, -1.0, -1.0, 1.0])
    sign_imag = lane_cycle([1.0, 1.0, -1.0, -1.0])
    cosine, sine = eighth_turn()
    lane = lax.broadcasted_iota(jnp.int32, (1, LANES), 1)
    first_weight = jnp.where(lane == 0, 1.0, 2.0).astype(F32)
    for j in range(TILES):
        at = slice(j * LANES, (j + 1) * LANES)
        at_imag = slice(NBIN + j * LANES, NBIN + (j + 1) * LANES)
        weight = first_weight if j == 0 else 2.0
        real = crossed[pl.ds(j, columns, stride=2 * TILES), :] * weight
        imag = crossed[pl.ds(TILES + j, columns, stride=2 * TILES), :] * weight
        turned = [(real, imag), (real * cosine - imag * sine, imag * cosine + real * sine)]
        turned += [quarter_turns(r, i, even, sign_real, sign_imag) for r, i in turned]
        for q in range(CHUNKS):
            rows = slice(q * columns, (q + 1) * columns)
            operand[rows, at] = turned[q][0].astype(BF)
            operand[rows, at_imag] = turned[q][1].astype(BF)
    block = lax.dot_general(
        table[...], operand[...], (((1,), (1,)), ((), ())), preferred_element_type=F32
    )
    block = block * scaling
    if slots == 1:
        half = table.shape[0] // 2
        low_lanes = lax.broadcasted_iota(jnp.int32, (half, LANES), 1) < width
        for p in range(CHUNKS // 2):
            at = slice(p * LANES, (p + 1) * LANES)
            low, high = block[:half, at], block[half:, at]
            pair = (
                jnp.where(low_lanes, low, pltpu.roll(high, width, 1)),
                jnp.where(low_lanes, pltpu.roll(low, width, 1), high),
            )
            for second in range(2):
                result[2 * p + second] = pair[second].astype(BF)
    else:
        for q in range(CHUNKS):
            result[q] = block[:, q * columns : (q + 1) * columns].astype(BF)
    me = lax.axis_index("seg")
    for j in range(parts):
        outs[j][...] = result[me ^ j]


def cross_lags(
    plan, table, owns, before, offsets, candidates, first_slot, slots, count, parts, scaling
):
    joint = len(owns) - 1
    windows, stations = owns[0].shape[1:3]
    quarter = candidates[0].shape[1]
    columns = slots * stations * quarter
    share = LAGS // parts
    out = (share, columns) if slots > 1 else (share // 2, 2 * columns)
    smem = pl.BlockSpec(memory_space=pltpu.SMEM)
    vmem = pl.BlockSpec(memory_space=pltpu.VMEM)
    operands = [table, *owns] + ([] if joint else [before]) + list(candidates)
    return pl.pallas_call(
        functools.partial(
            cross_kernel, first_slot, slots, count, scaling, tuple(offsets), parts, joint
        ),
        out_shape=[jax.ShapeDtypeStruct(out, BF)] * parts,
        in_specs=[smem] + [vmem] * len(operands),
        out_specs=[vmem] * parts,
        scratch_shapes=[
            pltpu.VMEM((3, slots, (1 + joint) * windows, quarter, TILES, LANES), F32),
            pltpu.VMEM((columns * 2 * TILES, LANES), F32),
            pltpu.VMEM((CHUNKS * columns, 2 * NBIN), BF),
            pltpu.VMEM((parts,) + out, BF),
        ],
        compiler_params=pltpu.CompilerParams(vmem_limit_bytes=24 * 2**20),
        cost_estimate=expected(1 * (0.6 + 2.0 * slots) if joint else 1.7),
        name="cross",
    )(plan, *operands)


def slot_rounds(plan, count):
    _, ranks = partner_steps(plan, count)
    rounds = []
    for slot in range(ROUNDS):
        number = jnp.int32(0)
        for other in range(1, ROUNDS):
            number = jnp.where(ranks[other] == slot, other, number)
        rounds.append(number)
    return rounds


def placed_block(pieces, matrix, at, half):
    joined = jnp.concatenate([piece[at, :] for piece in pieces], axis=1)
    if pieces[0].shape[0] > half:
        later = slice(half + at.start, half + at.stop)
        high = jnp.concatenate([piece[later, :] for piece in pieces], axis=1)
        joined = jnp.concatenate([joined, high], axis=0)
    return jnp.dot(joined, matrix, preferred_element_type=F32)


def joined_matrix(place, parts):
    me = lax.axis_index("seg")
    return jnp.concatenate([place[me ^ j] for j in range(parts)], axis=0)


def early_kernel(parts, groups, place, *rest):
    pieces, out = rest[:-1], rest[-1]
    half, pairs = out.shape[2:]
    matrix = joined_matrix(place, parts)
    at = slice(0, half)
    for index, (first_slot, slots) in enumerate(groups):
        block = placed_block(pieces[index * parts : (index + 1) * parts], matrix, at, half)
        if slots == 1:
            out[first_slot, 0] = block[:, :pairs]
            out[first_slot, 1] = block[:, pairs:]
        else:
            for slot in range(2):
                columns = slice(slot * pairs, (slot + 1) * pairs)
                out[first_slot + slot, 0] = block[:half, columns]
                out[first_slot + slot, 1] = block[half:, columns]


def late_kernel(count, parts, steps, plan, place, early, *rest):
    pieces = rest[:parts]
    out_hbm, out, sems = rest[parts:]
    half, _, pairs = out.shape[1:]
    rows = half // steps
    rounds = slot_rounds(plan, count)
    matrix = joined_matrix(place, parts)
    block = placed_block(pieces, matrix, slice(0, half), half)
    copies = []
    for step in range(steps):
        at = slice(step * rows, (step + 1) * rows)
        for h in range(2):
            for slot in range(ROUNDS - 1):
                out[h, at, rounds[slot], :] = early[slot, h, at, :]
            out[h, at, rounds[ROUNDS - 1], :] = block[at, h * pairs : (h + 1) * pairs]
            copy = pltpu.make_async_copy(
                out.at[h, at], out_hbm.at[h, at], sems.at[2 * step + h]
            )
            copy.start()
            copies.append(copy)
    for copy in copies:
        copy.wait()


def place_lags(plan, groups, pieces, count, stations, parts):
    pairs = stations * stations
    share = LAGS // parts
    half = share // 2
    steps = 4
    place = jnp.asarray(make_placing(stations, stations // parts, parts))
    vmem = pl.BlockSpec(memory_space=pltpu.VMEM)
    early = pl.pallas_call(
        functools.partial(early_kernel, parts, tuple(groups[:-1])),
        out_shape=jax.ShapeDtypeStruct((ROUNDS - 1, 2, half, pairs), F32),
        in_specs=[vmem] * (1 + len(pieces) - parts),
        out_specs=vmem,
        compiler_params=pltpu.CompilerParams(vmem_limit_bytes=16 * 2**20),
        cost_estimate=expected(0.05),
        name="early",
    )(place, *pieces[:-parts])
    shape = (2, half, ROUNDS, pairs)
    out = pl.pallas_call(
        functools.partial(late_kernel, count, parts, steps),
        out_shape=jax.ShapeDtypeStruct(shape, F32),
        in_specs=[pl.BlockSpec(memory_space=pltpu.SMEM)] + [vmem] * (2 + parts),
        out_specs=pl.BlockSpec(memory_space=pl.ANY),
        scratch_shapes=[pltpu.VMEM(shape, F32), pltpu.SemaphoreType.DMA((2 * steps,))],
        compiler_params=pltpu.CompilerParams(vmem_limit_bytes=24 * 2**20),
        cost_estimate=expected(0.05),
        name="late",
    )(plan, place, early, *pieces[-parts:])
    return out.reshape(share, ROUNDS, pairs)


def swap(value, j):
    parts = lax.axis_size("seg")
    return lax.ppermute(value, "seg", [(i, i ^ j) for i in range(parts)])


def exchange(pieces):
    return [pieces[0]] + [swap(pieces[j], j) for j in range(1, len(pieces))]


def after(value, others):
    return lax.optimization_barrier((value, others))[0]


def per_device(records, plan):
    stations, windows, length = records.shape
    count = lax.axis_size("sta")
    parts = lax.axis_size("seg")
    quarter = stations // parts
    table = jnp.asarray(make_table(length // CHUNKS, 2 * length))
    scaling = 1.0 / math.sqrt(4.0 * NBIN * windows * parts)

    white, mine, *far = prepare(records, table, parts)
    sibling = swap(white, 1)
    first = lax.axis_index("seg") * quarter
    near = jnp.concatenate([mine, lax.dynamic_slice_in_dim(sibling, first, quarter, 1)])
    far = jnp.concatenate([swap(piece, 2 + j) for j, piece in enumerate(far)])

    ring = sorted(range(count), key=lambda b: b // 2 if b % 2 == 0 else count - 1 - b // 2)
    upward = [(ring[i], ring[(i + 1) % count]) for i in range(count)]
    downward = [(ring[i], ring[i - 1]) for i in range(count)]

    def up(value):
        return lax.ppermute(value, "sta", upward)

    def down(value):
        return lax.ppermute(value, "sta", downward)

    far, white_far = lax.optimization_barrier((far, white))
    across = swap(white_far, 2)
    near_up = near_down = near
    far_up = far_down = far
    near_own = widen_own([white, sibling])
    steps = (count - 1) // 2
    groups = [(0, 1), (1, 2), (3, 1)]
    arrived = []
    spots, near_blocks, far_blocks = [], [], []
    lags, pieces = [], []

    def group_lags(index, near_own, far_own):
        first_slot, slots = groups[index]
        at, nears, fars = arrived[index - len(groups)]
        return cross_lags(
            plan, table, [near_own, far_own], None, at, nears + fars, first_slot, slots, count,
            parts, scaling,
        )

    for step in range(1, steps + 1):
        if step == 2:
            near_up, near_down = lax.optimization_barrier((near_up, near_down))
        elif step > 2:
            near_up, near_down, last_up, last_down = lax.optimization_barrier(
                (near_up, near_down, last_up, last_down)
            )
        last_up, last_down = far_up, far_down
        next_near = up(near_up), down(near_down)
        if step == 2:
            far_up, far_down, near_up, near_down, near_own = lax.optimization_barrier(
                (far_up, far_down, near_up, near_down, near_own)
            )
        elif step == 3:
            far_up, far_down, near_up, near_down, across = lax.optimization_barrier(
                (far_up, far_down, near_up, near_down, across)
            )
        elif step > 3:
            far_up, far_down, near_up, near_down = lax.optimization_barrier(
                (far_up, far_down, near_up, near_down)
            )
        if step == steps and step > 1:
            at, nears, _ = arrived[-1]
            first_sums = near_sums(plan, near_own, at, nears, 0, 1, count)
        far_up, far_down = up(far_up), down(far_down)
        near_up, near_down = next_near
        spots += [count - step, step]
        near_blocks += [near_up, near_down]
        far_blocks += [far_up, far_down]
        arrived.append((list(spots), list(near_blocks), list(far_blocks)))
    far_own = widen_own([across, swap(across, 1)])
    arrived.append(arrived[-1])
    at, _, fars = arrived[-3]
    lags = cross_lags(
        plan, table, [far_own], first_sums, at, fars, 0, 1, count, parts, scaling
    )
    pieces = exchange(lags)
    if count % 2 == 0:
        near_up = after(near_up, lags)
        middle_up = up(near_up)
        far_down = after(far_down, (near_up, near_down))
        arrived[-1] = (
            spots + [count // 2], near_blocks + [middle_up], far_blocks + [down(far_down)]
        )
    for index in range(1, len(groups)):
        if index == 2:
            near_own = after(near_own, pieces[:parts])
        near_own = after(near_own, lags)
        lags = group_lags(index, near_own, far_own)
        pieces = pieces + exchange(lags)
    return place_lags(plan, groups, pieces, count, stations, parts)


def solution(mesh):
    in_specs = (P("sta", "seg", None), P())
    out_specs = P("seg", None, "sta")
    return jax.shard_map(
        per_device, mesh=mesh, in_specs=in_specs, out_specs=out_specs, check_vma=False
    )
```

```python
import functools
import math

import jax
import jax.numpy as jnp
import ml_dtypes
import numpy as np
from jax import lax
from jax.experimental import pallas as pl
from jax.experimental.pallas import tpu as pltpu
from jax.sharding import PartitionSpec as P

NBIN = 1024
HALF = 64
ROUNDS = 4
LAGS = 2048
LANES = 128
TILES = NBIN // LANES
CHUNKS = 4
BF = jnp.bfloat16
F32 = jnp.float32


def make_table(rows, transform):
    phase = (np.arange(rows)[:, None] * np.arange(NBIN)[None, :]) % transform
    angle = phase * (2.0 * math.pi / transform)
    return np.concatenate([np.cos(angle), -np.sin(angle)], axis=1).astype(ml_dtypes.bfloat16)


def band_matrix():
    source = lax.broadcasted_iota(jnp.int32, (3 * LANES, LANES), 0) - LANES
    target = lax.broadcasted_iota(jnp.int32, (3 * LANES, LANES), 1)
    return jnp.where(jnp.abs(source - target) <= HALF, 1.0, 0.0).astype(BF)


def inverse_count(block, length):
    position = lax.broadcasted_iota(jnp.int32, (1, LANES), 1) + block * LANES
    counted = jnp.minimum(position, HALF) + jnp.minimum(length - 1 - position, HALF) + 1
    return 1.0 / counted.astype(F32)


def make_placing(stations, quarter, parts):
    width = stations * quarter
    place = np.zeros((parts, 2 * width, 2 * stations * stations), np.float32)
    for part in range(parts):
        for second in range(2):
            for s in range(stations):
                for t in range(quarter):
                    row = second * width + s * quarter + t
                    column = (second * stations + s) * stations + part * quarter + t
                    place[part, row, column] = 1.0
    return place.astype(ml_dtypes.bfloat16)


def lane_cycle(values):
    period = len(values)
    phase = lax.broadcasted_iota(jnp.int32, (1, LANES), 1) % period
    out = jnp.full((1, LANES), values[-1], F32)
    for index in range(period - 1):
        out = jnp.where(phase == index, values[index], out)
    return out


def even_lanes(shape):
    return lax.broadcasted_iota(jnp.int32, shape, 1) % 2 == 0


def eighth_turn():
    turns = [math.pi * k / 4.0 for k in range(8)]
    return lane_cycle([math.cos(t) for t in turns]), lane_cycle([math.sin(t) for t in turns])


def quarter_turns(real, imag, even, sign_real, sign_imag):
    return sign_real * jnp.where(even, real, imag), sign_imag * jnp.where(even, imag, real)


def banded_sum(stack, values, band):
    rows, length = values.shape
    blocks = length // LANES
    zero = jnp.zeros((rows, LANES), BF)
    for j in range(blocks):
        at = pl.ds(j * rows, rows)
        for k in range(3):
            b = j + k - 1
            block = values[:, b * LANES : (b + 1) * LANES] if 0 <= b < blocks else zero
            stack[at, k * LANES : (k + 1) * LANES] = block
    total = jnp.dot(stack[: blocks * rows, :], band, preferred_element_type=F32)
    return [total[j * rows : (j + 1) * rows, :] for j in range(blocks)]


def prep_kernel(parts, records_hbm, table_hbm, white, mine, *rest):
    others = rest[: parts - 1]
    records, table, stack, flat, spread, sems = rest[parts - 1 :]
    records_copy = pltpu.make_async_copy(records_hbm, records, sems.at[0])
    records_copy.start()
    copy = pltpu.make_async_copy(table_hbm, table, sems.at[1])
    copy.start()
    band_values = band_matrix()
    records_copy.wait()
    stations, windows, length = records.shape
    rows = stations * windows
    chunk = length // CHUNKS
    signal = jnp.concatenate([records[:, w, :] for w in range(windows)], axis=0)
    sums = banded_sum(stack, jnp.abs(signal).astype(BF), band_values)
    for j, total in enumerate(sums):
        at = slice(j * LANES, (j + 1) * LANES)
        level = total * inverse_count(j, length)
        value = (signal[:, at] / (level + 1e-05)).astype(BF)
        q, inside = divmod(j * LANES, chunk)
        flat[q * rows : (q + 1) * rows, inside : inside + LANES] = value
    copy.wait()
    product = jnp.dot(flat[...], table[...], preferred_element_type=F32)
    even = even_lanes((rows, LANES))
    sign_real = lane_cycle([1.0, 1.0, -1.0, -1.0])
    sign_imag = lane_cycle([1.0, -1.0, -1.0, 1.0])
    cosine, sine = eighth_turn()
    reals, imags, mags = [], [], []
    for j in range(TILES):
        at = slice(j * LANES, (j + 1) * LANES)
        at_imag = slice(NBIN + j * LANES, NBIN + (j + 1) * LANES)
        pr = [product[q * rows : (q + 1) * rows, at] for q in range(CHUNKS)]
        pi = [product[q * rows : (q + 1) * rows, at_imag] for q in range(CHUNKS)]
        turned = [
            quarter_turns(pr[q], pi[q], even, sign_real, sign_imag) for q in range(2, CHUNKS)
        ]
        first_real, first_imag = pr[0] + turned[0][0], pi[0] + turned[0][1]
        odd_real, odd_imag = pr[1] + turned[1][0], pi[1] + turned[1][1]
        real = first_real + (odd_real * cosine + odd_imag * sine)
        imag = first_imag + (odd_imag * cosine - odd_real * sine)
        reals.append(real)
        imags.append(imag)
        mags.append(jnp.sqrt(real * real + imag * imag).astype(BF))
    sums = banded_sum(stack, jnp.concatenate(mags, axis=1), band_values)
    for j, total in enumerate(sums):
        at = slice(j * LANES, (j + 1) * LANES)
        smooth = total * inverse_count(j, NBIN) + 1e-06
        spread[pl.ds(j, rows, stride=2 * TILES), :] = reals[j] / smooth
        spread[pl.ds(TILES + j, rows, stride=2 * TILES), :] = imags[j] / smooth
    me = lax.axis_index("seg")
    quarter = stations // parts
    white[...] = spread[...].reshape(windows, stations, 2 * TILES, LANES).astype(BF)
    for j, out in enumerate((mine, *others)):
        for w in range(windows):
            out[w] = white[w, pl.ds((me ^ j) * quarter, quarter)]


def prepare(records, table, parts):
    stations, windows, length = records.shape
    rows = stations * windows
    quarter = stations // parts
    small = jax.ShapeDtypeStruct((windows, quarter, 2 * TILES, LANES), BF)
    vmem = pl.BlockSpec(memory_space=pltpu.VMEM)
    return pl.pallas_call(
        functools.partial(prep_kernel, parts),
        out_shape=[jax.ShapeDtypeStruct((windows, stations, 2 * TILES, LANES), BF)]
        + [small] * parts,
        in_specs=[pl.BlockSpec(memory_space=pltpu.HBM)] * 2,
        out_specs=[vmem] * (1 + parts),
        scratch_shapes=[
            pltpu.VMEM(records.shape, F32),
            pltpu.VMEM(table.shape, BF),
            pltpu.VMEM((rows * (length // LANES), 3 * LANES), BF),
            pltpu.VMEM((CHUNKS * rows, length // CHUNKS), BF),
            pltpu.VMEM((rows * 2 * TILES, LANES), F32),
            pltpu.SemaphoreType.DMA((2,)),
        ],
        compiler_params=pltpu.CompilerParams(vmem_limit_bytes=52 * 2**20),
        cost_estimate=pl.CostEstimate(
            flops=2 * rows * length * 2 * NBIN, bytes_accessed=3 * 2**20, transcendentals=0
        ),
        name="prep",
    )(
        pltpu.with_memory_space_constraint(records, pltpu.HBM),
        pltpu.with_memory_space_constraint(table, pltpu.HBM),
    )


def ring_place(block, count):
    half = block >> 1
    return jnp.where((block & 1) == 0, half, count - 1 - half)


def partner_steps(plan, count):
    me = lax.axis_index("sta")
    mine = ring_place(me, count)
    steps, keys = [], []
    for number in range(ROUNDS):
        step = ring_place(plan[number, me], count) - mine
        step = jnp.where(step < 0, step + count, step)
        steps.append(step)
        keys.append(jnp.minimum(step, count - step) * ROUNDS + number)
    ranks = []
    for number in range(ROUNDS):
        rank = jnp.int32(0)
        for other in range(ROUNDS):
            if other != number:
                rank = rank + jnp.where(keys[other] < keys[number], 1, 0)
        ranks.append(rank)
    return steps, ranks


def expected(microseconds):
    return pl.CostEstimate(
        flops=int(microseconds * 1.15e9), bytes_accessed=1024, transcendentals=0
    )


def widen_kernel(*refs):
    blocks, own = refs[:-1], refs[-1]
    windows = blocks[0].shape[0]
    for j, block in enumerate(blocks):

        def widen(w, carry, j=j, block=block):
            raw = block[w].astype(F32)
            real, imag = raw[:, :TILES], raw[:, TILES:]
            own[0, j * windows + w] = real + imag
            own[1, j * windows + w] = real
            own[2, j * windows + w] = imag
            return carry

        lax.fori_loop(0, windows, widen, 0)


def widen_own(blocks):
    windows, stations = blocks[0].shape[:2]
    vmem = pl.BlockSpec(memory_space=pltpu.VMEM)
    return pl.pallas_call(
        widen_kernel,
        out_shape=jax.ShapeDtypeStruct((3, len(blocks) * windows, stations, TILES, LANES), F32),
        in_specs=[vmem] * len(blocks),
        out_specs=vmem,
        compiler_params=pltpu.CompilerParams(vmem_limit_bytes=16 * 2**20),
        cost_estimate=expected(0.05),
        name="widen",
    )(*blocks)


def widen_others(first_slot, slots, count, places, plan, candidates, other):
    steps, ranks = partner_steps(plan, count)
    for slot in range(slots):
        step = jnp.int32(0)
        for number in range(ROUNDS):
            step = jnp.where(ranks[number] == first_slot + slot, steps[number], step)
        for (offset, first), candidate in zip(places, candidates):

            @pl.when(step == offset)
            def _(candidate=candidate, slot=slot, first=first):
                def widen_other(w, carry):
                    raw = candidate[w].astype(F32)
                    real, imag = raw[:, :TILES], raw[:, TILES:]
                    other[0, slot, first + w] = real
                    other[1, slot, first + w] = real + imag
                    other[2, slot, first + w] = imag - real
                    return carry

                lax.fori_loop(0, candidate.shape[0], widen_other, 0)


def sum_windows(owns, other, crossed):
    windows, stations = owns[0].shape[1:3]
    slots, _, quarter = other.shape[1:4]
    width = stations * quarter
    group = 4
    groups = stations // group

    def one_group(slot, index):
        first = index * group

        def sums(kind):
            totals = [None] * (group * quarter)
            for part, own in enumerate(owns):
                for w in range(windows):
                    left = [own[kind, w, first + s] for s in range(group)]
                    right = [other[kind, slot, part * windows + w, t] for t in range(quarter)]
                    for s in range(group):
                        for t in range(quarter):
                            term = left[s] * right[t]
                            place = s * quarter + t
                            old = totals[place]
                            totals[place] = term if old is None else old + term
            return totals

        def store(place, part, value):
            at = pl.multiple_of((base + place) * 2 * TILES + part * TILES, TILES)
            crossed[pl.ds(at, TILES), :] = value

        base = slot * width + first * quarter
        shared = sums(0)
        third = sums(2)
        for place in range(group * quarter):
            store(place, 0, shared[place] + third[place])
        second = sums(1)
        for place in range(group * quarter):
            store(place, 1, shared[place] - second[place])

    for slot in range(slots):

        def body(index, carry, slot=slot):
            one_group(slot, index)
            return carry

        lax.fori_loop(0, groups, body, 0)


def cross_kernel(first_slot, slots, count, scaling, places, parts, plan, table, *rest):
    owns, rest = rest[:2], rest[2:]
    others, rest = rest[: len(places)], rest[len(places) :]
    outs = rest[:parts]
    other, crossed, operand, result = rest[parts:]
    stations = owns[0].shape[2]
    widen_others(first_slot, slots, count, places, plan, others, other)
    sum_windows(owns, other, crossed)
    width = stations * other.shape[3]
    columns = slots * width
    even = even_lanes((columns, LANES))
    sign_real = lane_cycle([1.0, -1.0, -1.0, 1.0])
    sign_imag = lane_cycle([1.0, 1.0, -1.0, -1.0])
    cosine, sine = eighth_turn()
    lane = lax.broadcasted_iota(jnp.int32, (1, LANES), 1)
    first_weight = jnp.where(lane == 0, 1.0, 2.0).astype(F32)
    for j in range(TILES):
        at = slice(j * LANES, (j + 1) * LANES)
        at_imag = slice(NBIN + j * LANES, NBIN + (j + 1) * LANES)
        weight = first_weight if j == 0 else 2.0
        real = crossed[pl.ds(j, columns, stride=2 * TILES), :] * weight
        imag = crossed[pl.ds(TILES + j, columns, stride=2 * TILES), :] * weight
        turned = [(real, imag), (real * cosine - imag * sine, imag * cosine + real * sine)]
        turned += [quarter_turns(r, i, even, sign_real, sign_imag) for r, i in turned]
        for q in range(CHUNKS):
            rows = slice(q * columns, (q + 1) * columns)
            operand[rows, at] = turned[q][0].astype(BF)
            operand[rows, at_imag] = turned[q][1].astype(BF)
    block = lax.dot_general(
        table[...], operand[...], (((1,), (1,)), ((), ())), preferred_element_type=F32
    )
    block = block * scaling
    if slots == 1:
        half = table.shape[0] // 2
        low_lanes = lax.broadcasted_iota(jnp.int32, (half, LANES), 1) < width
        for p in range(CHUNKS // 2):
            at = slice(p * LANES, (p + 1) * LANES)
            low, high = block[:half, at], block[half:, at]
            pair = (
                jnp.where(low_lanes, low, pltpu.roll(high, width, 1)),
                jnp.where(low_lanes, pltpu.roll(low, width, 1), high),
            )
            for second in range(2):
                result[2 * p + second] = pair[second].astype(BF)
    else:
        for q in range(CHUNKS):
            result[q] = block[:, q * columns : (q + 1) * columns].astype(BF)
    me = lax.axis_index("seg")
    for j in range(parts):
        outs[j][...] = result[me ^ j]


def cross_lags(plan, table, owns, places, candidates, first_slot, slots, count, parts, scaling):
    windows, stations = owns[0].shape[1:3]
    quarter = candidates[0].shape[1]
    columns = slots * stations * quarter
    share = LAGS // parts
    out = (share, columns) if slots > 1 else (share // 2, 2 * columns)
    smem = pl.BlockSpec(memory_space=pltpu.SMEM)
    vmem = pl.BlockSpec(memory_space=pltpu.VMEM)
    operands = [table, *owns, *candidates]
    return pl.pallas_call(
        functools.partial(
            cross_kernel, first_slot, slots, count, scaling, tuple(places), parts
        ),
        out_shape=[jax.ShapeDtypeStruct(out, BF)] * parts,
        in_specs=[smem] + [vmem] * len(operands),
        out_specs=[vmem] * parts,
        scratch_shapes=[
            pltpu.VMEM((3, slots, 2 * windows, quarter, TILES, LANES), F32),
            pltpu.VMEM((columns * 2 * TILES, LANES), F32),
            pltpu.VMEM((CHUNKS * columns, 2 * NBIN), BF),
            pltpu.VMEM((parts,) + out, BF),
        ],
        compiler_params=pltpu.CompilerParams(vmem_limit_bytes=24 * 2**20),
        cost_estimate=expected(0.6 + 2.0 * slots),
        name="cross",
    )(plan, *operands)


def slot_rounds(plan, count):
    _, ranks = partner_steps(plan, count)
    rounds = []
    for slot in range(ROUNDS):
        number = jnp.int32(0)
        for other in range(1, ROUNDS):
            number = jnp.where(ranks[other] == slot, other, number)
        rounds.append(number)
    return rounds


def placed_block(pieces, matrix, at, half):
    joined = jnp.concatenate([piece[at, :] for piece in pieces], axis=1)
    if pieces[0].shape[0] > half:
        later = slice(half + at.start, half + at.stop)
        high = jnp.concatenate([piece[later, :] for piece in pieces], axis=1)
        joined = jnp.concatenate([joined, high], axis=0)
    return jnp.dot(joined, matrix, preferred_element_type=F32)


def joined_matrix(place, parts):
    me = lax.axis_index("seg")
    return jnp.concatenate([place[me ^ j] for j in range(parts)], axis=0)


def early_kernel(parts, groups, place, *rest):
    pieces, out = rest[:-1], rest[-1]
    half, pairs = out.shape[2:]
    matrix = joined_matrix(place, parts)
    at = slice(0, half)
    for index, (first_slot, slots) in enumerate(groups):
        block = placed_block(pieces[index * parts : (index + 1) * parts], matrix, at, half)
        if slots == 1:
            out[first_slot, 0] = block[:, :pairs]
            out[first_slot, 1] = block[:, pairs:]
        else:
            for slot in range(2):
                columns = slice(slot * pairs, (slot + 1) * pairs)
                out[first_slot + slot, 0] = block[:half, columns]
                out[first_slot + slot, 1] = block[half:, columns]


def late_kernel(count, parts, steps, plan, place, early, *rest):
    pieces = rest[:parts]
    out_hbm, out, sems = rest[parts:]
    half, _, pairs = out.shape[1:]
    rows = half // steps
    rounds = slot_rounds(plan, count)
    matrix = joined_matrix(place, parts)
    block = placed_block(pieces, matrix, slice(0, half), half)
    copies = []
    for step in range(steps):
        at = slice(step * rows, (step + 1) * rows)
        for h in range(2):
            for slot in range(ROUNDS - 1):
                out[h, at, rounds[slot], :] = early[slot, h, at, :]
            out[h, at, rounds[ROUNDS - 1], :] = block[at, h * pairs : (h + 1) * pairs]
            copy = pltpu.make_async_copy(
                out.at[h, at], out_hbm.at[h, at], sems.at[2 * step + h]
            )
            copy.start()
            copies.append(copy)
    for copy in copies:
        copy.wait()


def place_lags(plan, groups, pieces, count, stations, parts):
    pairs = stations * stations
    share = LAGS // parts
    half = share // 2
    steps = 4
    place = jnp.asarray(make_placing(stations, stations // parts, parts))
    vmem = pl.BlockSpec(memory_space=pltpu.VMEM)
    early = pl.pallas_call(
        functools.partial(early_kernel, parts, tuple(groups[:-1])),
        out_shape=jax.ShapeDtypeStruct((ROUNDS - 1, 2, half, pairs), F32),
        in_specs=[vmem] * (1 + len(pieces) - parts),
        out_specs=vmem,
        compiler_params=pltpu.CompilerParams(vmem_limit_bytes=16 * 2**20),
        cost_estimate=expected(0.05),
        name="early",
    )(place, *pieces[:-parts])
    shape = (2, half, ROUNDS, pairs)
    out = pl.pallas_call(
        functools.partial(late_kernel, count, parts, steps),
        out_shape=jax.ShapeDtypeStruct(shape, F32),
        in_specs=[pl.BlockSpec(memory_space=pltpu.SMEM)] + [vmem] * (2 + parts),
        out_specs=pl.BlockSpec(memory_space=pl.ANY),
        scratch_shapes=[pltpu.VMEM(shape, F32), pltpu.SemaphoreType.DMA((2 * steps,))],
        compiler_params=pltpu.CompilerParams(vmem_limit_bytes=24 * 2**20),
        cost_estimate=expected(0.05),
        name="late",
    )(plan, place, early, *pieces[-parts:])
    return out.reshape(share, ROUNDS, pairs)


def join_kernel(order, *refs):
    parts, (out_up, out_down) = refs[:4], refs[4:]
    near_up, near_down, far_up, far_down = [parts[order.index(k)] for k in range(4)]
    half = near_up.shape[0]
    for out, first, second in ((out_up, near_up, far_up), (out_down, near_down, far_down)):
        out[:half] = first[...]
        out[half:] = second[...]


def join(near_up, near_down, far_up, far_down, order=(0, 1, 2, 3)):
    values = [near_up, near_down, far_up, far_down]
    vmem = pl.BlockSpec(memory_space=pltpu.VMEM)
    shape = (2 * near_up.shape[0],) + near_up.shape[1:]
    return pl.pallas_call(
        functools.partial(join_kernel, tuple(order)),
        out_shape=[jax.ShapeDtypeStruct(shape, BF)] * 2,
        in_specs=[vmem] * 4,
        out_specs=[vmem] * 2,
        compiler_params=pltpu.CompilerParams(vmem_limit_bytes=16 * 2**20),
        cost_estimate=expected(0.05),
        name="join",
    )(*[values[k] for k in order])


def swap(value, j):
    parts = lax.axis_size("seg")
    return lax.ppermute(value, "seg", [(i, i ^ j) for i in range(parts)])


def exchange(pieces):
    return [pieces[0]] + [swap(pieces[j], j) for j in range(1, len(pieces))]


def after(value, others):
    return lax.optimization_barrier((value, others))[0]


def per_device(records, plan):
    stations, windows, length = records.shape
    count = lax.axis_size("sta")
    parts = lax.axis_size("seg")
    quarter = stations // parts
    table = jnp.asarray(make_table(length // CHUNKS, 2 * length))
    scaling = 1.0 / math.sqrt(4.0 * NBIN * windows * parts)

    white, *quarters = prepare(records, table, parts)
    near = jnp.concatenate([quarters[0], swap(quarters[1], 1)])
    sibling = swap(white, 1)
    far = jnp.concatenate([swap(quarters[j], j) for j in range(2, parts)])
    far = after(far, sibling)
    far, white_far = lax.optimization_barrier((far, white))
    across = swap(white_far, 2)

    ring = sorted(range(count), key=lambda b: b // 2 if b % 2 == 0 else count - 1 - b // 2)
    upward = [(ring[i], ring[(i + 1) % count]) for i in range(count)]
    downward = [(ring[i], ring[i - 1]) for i in range(count)]

    def up(value):
        return lax.ppermute(value, "sta", upward)

    def down(value):
        return lax.ppermute(value, "sta", downward)

    far, white_far = lax.optimization_barrier((far, white))
    across = swap(white_far, 2)
    near_own = widen_own([white, sibling])
    half = near.shape[0]
    places, blocks, arrived = [], [], []

    def arrive(step, first, from_left, from_right):
        places.extend([(count - step, first), (step, first)])
        blocks.extend([from_left, from_right])

    near_up, near_down = up(near), down(near)
    far_up, far_down = up(far), down(far)
    arrive(1, 0, near_up, near_down)
    arrive(1, half, far_up, far_down)
    near_up, near_down, near_own = lax.optimization_barrier((near_up, near_down, near_own))
    near_up, near_down = up(near_up), down(near_down)
    far_up, far_down = lax.optimization_barrier((far_up, far_down))
    far_up, far_down = up(far_up), down(far_down)
    arrive(2, 0, near_up, near_down)
    arrive(2, half, far_up, far_down)
    all_up, all_down = join(near_up, near_down, far_up, far_down)
    for step in range(3, (count - 1) // 2 + 1):
        arrived.append((list(places), list(blocks)))
        all_up, all_down, across = lax.optimization_barrier((all_up, all_down, across))
        all_up, all_down = up(all_up), down(all_down)
        arrive(step, 0, all_up, all_down)
    arrived.append((list(places), list(blocks)))
    far_own = widen_own([across, swap(across, 1)])
    groups = [(0, 1), (1, 2), (3, 1)]
    if count % 2 == 0:
        places.append((count // 2, 0))
        blocks.append(up(all_up))
    arrived.append((places, blocks))
    pieces = []
    for index, (first_slot, slots) in enumerate(groups):
        if index == 2:
            near_own = after(near_own, pieces[:parts])
        if index > 0:
            near_own = after(near_own, lags)
        at, values = arrived[index - len(groups)]
        lags = cross_lags(
            plan, table, [near_own, far_own], at, values, first_slot, slots, count, parts, scaling
        )
        pieces = pieces + exchange(lags)
    return place_lags(plan, groups, pieces, count, stations, parts)


def solution(mesh):
    in_specs = (P("sta", "seg", None), P())
    out_specs = P("seg", None, "sta")
    return jax.shard_map(
        per_device, mesh=mesh, in_specs=in_specs, out_specs=out_specs, check_vma=False
    )
```

```python
import functools
import math

import jax
import jax.numpy as jnp
import ml_dtypes
import numpy as np
from jax import lax
from jax.experimental import pallas as pl
from jax.experimental.pallas import tpu as pltpu
from jax.sharding import PartitionSpec as P

NBIN = 1024
HALF = 64
ROUNDS = 4
LAGS = 2048
LANES = 128
TILES = NBIN // LANES
CHUNKS = 4
BF = jnp.bfloat16
F32 = jnp.float32


def make_table(rows, transform):
    phase = (np.arange(rows)[:, None] * np.arange(NBIN)[None, :]) % transform
    angle = phase * (2.0 * math.pi / transform)
    return np.concatenate([np.cos(angle), -np.sin(angle)], axis=1).astype(ml_dtypes.bfloat16)


def band_matrix():
    source = lax.broadcasted_iota(jnp.int32, (3 * LANES, LANES), 0) - LANES
    target = lax.broadcasted_iota(jnp.int32, (3 * LANES, LANES), 1)
    return jnp.where(jnp.abs(source - target) <= HALF, 1.0, 0.0).astype(BF)


def inverse_count(block, length):
    position = lax.broadcasted_iota(jnp.int32, (1, LANES), 1) + block * LANES
    counted = jnp.minimum(position, HALF) + jnp.minimum(length - 1 - position, HALF) + 1
    return 1.0 / counted.astype(F32)


def make_placing(stations, quarter, parts):
    width = stations * quarter
    place = np.zeros((parts, 2 * width, 2 * stations * stations), np.float32)
    for part in range(parts):
        for second in range(2):
            for s in range(stations):
                for t in range(quarter):
                    row = second * width + s * quarter + t
                    column = (second * stations + s) * stations + part * quarter + t
                    place[part, row, column] = 1.0
    return place.astype(ml_dtypes.bfloat16)


def lane_cycle(values):
    period = len(values)
    phase = lax.broadcasted_iota(jnp.int32, (1, LANES), 1) % period
    out = jnp.full((1, LANES), values[-1], F32)
    for index in range(period - 1):
        out = jnp.where(phase == index, values[index], out)
    return out


def even_lanes(shape):
    return lax.broadcasted_iota(jnp.int32, shape, 1) % 2 == 0


def eighth_turn():
    turns = [math.pi * k / 4.0 for k in range(8)]
    return lane_cycle([math.cos(t) for t in turns]), lane_cycle([math.sin(t) for t in turns])


def quarter_turns(real, imag, even, sign_real, sign_imag):
    return sign_real * jnp.where(even, real, imag), sign_imag * jnp.where(even, imag, real)


def banded_sum(stack, values, band):
    rows, length = values.shape
    blocks = length // LANES
    zero = jnp.zeros((rows, LANES), BF)
    for j in range(blocks):
        at = pl.ds(j * rows, rows)
        for k in range(3):
            b = j + k - 1
            block = values[:, b * LANES : (b + 1) * LANES] if 0 <= b < blocks else zero
            stack[at, k * LANES : (k + 1) * LANES] = block
    total = jnp.dot(stack[: blocks * rows, :], band, preferred_element_type=F32)
    return [total[j * rows : (j + 1) * rows, :] for j in range(blocks)]


def prep_kernel(parts, records_hbm, table_hbm, white, mine, *rest):
    others = rest[: parts - 1]
    records, table, stack, flat, spread, sems = rest[parts - 1 :]
    records_copy = pltpu.make_async_copy(records_hbm, records, sems.at[0])
    records_copy.start()
    copy = pltpu.make_async_copy(table_hbm, table, sems.at[1])
    copy.start()
    band_values = band_matrix()
    records_copy.wait()
    stations, windows, length = records.shape
    rows = stations * windows
    chunk = length // CHUNKS
    signal = jnp.concatenate([records[:, w, :] for w in range(windows)], axis=0)
    sums = banded_sum(stack, jnp.abs(signal).astype(BF), band_values)
    for j, total in enumerate(sums):
        at = slice(j * LANES, (j + 1) * LANES)
        level = total * inverse_count(j, length)
        value = (signal[:, at] / (level + 1e-05)).astype(BF)
        q, inside = divmod(j * LANES, chunk)
        flat[q * rows : (q + 1) * rows, inside : inside + LANES] = value
    copy.wait()
    product = jnp.dot(flat[...], table[...], preferred_element_type=F32)
    even = even_lanes((rows, LANES))
    sign_real = lane_cycle([1.0, 1.0, -1.0, -1.0])
    sign_imag = lane_cycle([1.0, -1.0, -1.0, 1.0])
    cosine, sine = eighth_turn()
    reals, imags, mags = [], [], []
    for j in range(TILES):
        at = slice(j * LANES, (j + 1) * LANES)
        at_imag = slice(NBIN + j * LANES, NBIN + (j + 1) * LANES)
        pr = [product[q * rows : (q + 1) * rows, at] for q in range(CHUNKS)]
        pi = [product[q * rows : (q + 1) * rows, at_imag] for q in range(CHUNKS)]
        turned = [
            quarter_turns(pr[q], pi[q], even, sign_real, sign_imag) for q in range(2, CHUNKS)
        ]
        first_real, first_imag = pr[0] + turned[0][0], pi[0] + turned[0][1]
        odd_real, odd_imag = pr[1] + turned[1][0], pi[1] + turned[1][1]
        real = first_real + (odd_real * cosine + odd_imag * sine)
        imag = first_imag + (odd_imag * cosine - odd_real * sine)
        reals.append(real)
        imags.append(imag)
        mags.append(jnp.sqrt(real * real + imag * imag).astype(BF))
    sums = banded_sum(stack, jnp.concatenate(mags, axis=1), band_values)
    for j, total in enumerate(sums):
        at = slice(j * LANES, (j + 1) * LANES)
        smooth = total * inverse_count(j, NBIN) + 1e-06
        spread[pl.ds(j, rows, stride=2 * TILES), :] = reals[j] / smooth
        spread[pl.ds(TILES + j, rows, stride=2 * TILES), :] = imags[j] / smooth
    me = lax.axis_index("seg")
    quarter = stations // parts
    white[...] = spread[...].reshape(windows, stations, 2 * TILES, LANES).astype(BF)
    for j, out in enumerate((mine, *others)):
        for w in range(windows):
            out[w] = white[w, pl.ds((me ^ j) * quarter, quarter)]


def prepare(records, table, parts):
    stations, windows, length = records.shape
    rows = stations * windows
    quarter = stations // parts
    small = jax.ShapeDtypeStruct((windows, quarter, 2 * TILES, LANES), BF)
    vmem = pl.BlockSpec(memory_space=pltpu.VMEM)
    return pl.pallas_call(
        functools.partial(prep_kernel, parts),
        out_shape=[jax.ShapeDtypeStruct((windows, stations, 2 * TILES, LANES), BF)]
        + [small] * parts,
        in_specs=[pl.BlockSpec(memory_space=pltpu.HBM)] * 2,
        out_specs=[vmem] * (1 + parts),
        scratch_shapes=[
            pltpu.VMEM(records.shape, F32),
            pltpu.VMEM(table.shape, BF),
            pltpu.VMEM((rows * (length // LANES), 3 * LANES), BF),
            pltpu.VMEM((CHUNKS * rows, length // CHUNKS), BF),
            pltpu.VMEM((rows * 2 * TILES, LANES), F32),
            pltpu.SemaphoreType.DMA((2,)),
        ],
        compiler_params=pltpu.CompilerParams(vmem_limit_bytes=52 * 2**20),
        cost_estimate=pl.CostEstimate(
            flops=2 * rows * length * 2 * NBIN, bytes_accessed=3 * 2**20, transcendentals=0
        ),
        name="prep",
    )(
        pltpu.with_memory_space_constraint(records, pltpu.HBM),
        pltpu.with_memory_space_constraint(table, pltpu.HBM),
    )


def ring_place(block, count):
    half = block >> 1
    return jnp.where((block & 1) == 0, half, count - 1 - half)


def partner_steps(plan, count):
    me = lax.axis_index("sta")
    mine = ring_place(me, count)
    steps, keys = [], []
    for number in range(ROUNDS):
        step = ring_place(plan[number, me], count) - mine
        step = jnp.where(step < 0, step + count, step)
        steps.append(step)
        keys.append(jnp.minimum(step, count - step) * ROUNDS + number)
    ranks = []
    for number in range(ROUNDS):
        rank = jnp.int32(0)
        for other in range(ROUNDS):
            if other != number:
                rank = rank + jnp.where(keys[other] < keys[number], 1, 0)
        ranks.append(rank)
    return steps, ranks


def expected(microseconds):
    return pl.CostEstimate(
        flops=int(microseconds * 1.15e9), bytes_accessed=1024, transcendentals=0
    )


def widen_kernel(*refs):
    blocks, own = refs[:-1], refs[-1]
    windows = blocks[0].shape[0]
    for j, block in enumerate(blocks):

        def widen(w, carry, j=j, block=block):
            raw = block[w].astype(F32)
            real, imag = raw[:, :TILES], raw[:, TILES:]
            own[0, j * windows + w] = real + imag
            own[1, j * windows + w] = real
            own[2, j * windows + w] = imag
            return carry

        lax.fori_loop(0, windows, widen, 0)


def widen_own(blocks):
    windows, stations = blocks[0].shape[:2]
    vmem = pl.BlockSpec(memory_space=pltpu.VMEM)
    return pl.pallas_call(
        widen_kernel,
        out_shape=jax.ShapeDtypeStruct((3, len(blocks) * windows, stations, TILES, LANES), F32),
        in_specs=[vmem] * len(blocks),
        out_specs=vmem,
        compiler_params=pltpu.CompilerParams(vmem_limit_bytes=16 * 2**20),
        cost_estimate=expected(0.05),
        name="widen",
    )(*blocks)


def widen_others(first_slot, slots, count, places, plan, candidates, other):
    steps, ranks = partner_steps(plan, count)
    for slot in range(slots):
        step = jnp.int32(0)
        for number in range(ROUNDS):
            step = jnp.where(ranks[number] == first_slot + slot, steps[number], step)
        for (offset, first), candidate in zip(places, candidates):

            @pl.when(step == offset)
            def _(candidate=candidate, slot=slot, first=first):
                def widen_other(w, carry):
                    raw = candidate[w].astype(F32)
                    real, imag = raw[:, :TILES], raw[:, TILES:]
                    other[0, slot, first + w] = real
                    other[1, slot, first + w] = real + imag
                    other[2, slot, first + w] = imag - real
                    return carry

                lax.fori_loop(0, candidate.shape[0], widen_other, 0)


def sum_windows(owns, other, crossed):
    windows, stations = owns[0].shape[1:3]
    slots, _, quarter = other.shape[1:4]
    width = stations * quarter
    group = 4
    groups = stations // group
    shift = groups.bit_length() - 1

    def one_group(slot, index):
        first = index * group

        def sums(kind):
            totals = [None] * (group * quarter)
            for part, own in enumerate(owns):
                for w in range(windows):
                    left = [own[kind, w, first + s] for s in range(group)]
                    right = [other[kind, slot, part * windows + w, t] for t in range(quarter)]
                    for s in range(group):
                        for t in range(quarter):
                            term = left[s] * right[t]
                            place = s * quarter + t
                            old = totals[place]
                            totals[place] = term if old is None else old + term
            return totals

        def store(place, part, value):
            at = pl.multiple_of((base + place) * 2 * TILES + part * TILES, TILES)
            crossed[pl.ds(at, TILES), :] = value

        base = slot * width + first * quarter
        shared = sums(0)
        third = sums(2)
        for place in range(group * quarter):
            store(place, 0, shared[place] + third[place])
        second = sums(1)
        for place in range(group * quarter):
            store(place, 1, shared[place] - second[place])

    def body(index, carry):
        one_group(index >> shift, index & (groups - 1))
        return carry

    lax.fori_loop(0, slots * groups, body, 0)


def cross_kernel(first_slot, slots, count, scaling, places, parts, plan, table, *rest):
    owns, rest = rest[:2], rest[2:]
    others, rest = rest[: len(places)], rest[len(places) :]
    outs = rest[:parts]
    other, crossed, operand = rest[parts:]
    stations = owns[0].shape[2]
    widen_others(first_slot, slots, count, places, plan, others, other)
    sum_windows(owns, other, crossed)
    width = stations * other.shape[3]
    columns = slots * width
    even = even_lanes((columns, LANES))
    sign_real = lane_cycle([1.0, -1.0, -1.0, 1.0])
    sign_imag = lane_cycle([1.0, 1.0, -1.0, -1.0])
    cosine, sine = eighth_turn()
    lane = lax.broadcasted_iota(jnp.int32, (1, LANES), 1)
    first_weight = jnp.where(lane == 0, 1.0, 2.0).astype(F32)
    me = lax.axis_index("seg")
    rows = [pl.ds(pl.multiple_of((me ^ q) * columns, columns), columns) for q in range(CHUNKS)]
    for j in range(TILES):
        at = slice(j * LANES, (j + 1) * LANES)
        at_imag = slice(NBIN + j * LANES, NBIN + (j + 1) * LANES)
        weight = first_weight if j == 0 else 2.0
        real = crossed[pl.ds(j, columns, stride=2 * TILES), :] * weight
        imag = crossed[pl.ds(TILES + j, columns, stride=2 * TILES), :] * weight
        turned = [(real, imag), (real * cosine - imag * sine, imag * cosine + real * sine)]
        turned += [quarter_turns(r, i, even, sign_real, sign_imag) for r, i in turned]
        for q in range(CHUNKS):
            operand[rows[q], at] = turned[q][0].astype(BF)
            operand[rows[q], at_imag] = turned[q][1].astype(BF)
    block = lax.dot_general(
        table[...], operand[...], (((1,), (1,)), ((), ())), preferred_element_type=F32
    )
    block = block * scaling
    if slots == 1:
        half = table.shape[0] // 2
        low_lanes = lax.broadcasted_iota(jnp.int32, (half, LANES), 1) < width
        for p in range(CHUNKS // 2):
            at = slice(p * LANES, (p + 1) * LANES)
            low, high = block[:half, at], block[half:, at]
            pair = (
                jnp.where(low_lanes, low, pltpu.roll(high, width, 1)),
                jnp.where(low_lanes, pltpu.roll(low, width, 1), high),
            )
            for second in range(2):
                outs[2 * p + second][...] = pair[second].astype(BF)
    else:
        for j in range(parts):
            outs[j][...] = block[:, j * columns : (j + 1) * columns].astype(BF)


def cross_lags(plan, table, owns, places, candidates, first_slot, slots, count, parts, scaling):
    windows, stations = owns[0].shape[1:3]
    quarter = candidates[0].shape[1]
    columns = slots * stations * quarter
    share = LAGS // parts
    out = (share, columns) if slots > 1 else (share // 2, 2 * columns)
    smem = pl.BlockSpec(memory_space=pltpu.SMEM)
    vmem = pl.BlockSpec(memory_space=pltpu.VMEM)
    operands = [table, *owns, *candidates]
    return pl.pallas_call(
        functools.partial(
            cross_kernel, first_slot, slots, count, scaling, tuple(places), parts
        ),
        out_shape=[jax.ShapeDtypeStruct(out, BF)] * parts,
        in_specs=[smem] + [vmem] * len(operands),
        out_specs=[vmem] * parts,
        scratch_shapes=[
            pltpu.VMEM((3, slots, 2 * windows, quarter, TILES, LANES), F32),
            pltpu.VMEM((columns * 2 * TILES, LANES), F32),
            pltpu.VMEM((CHUNKS * columns, 2 * NBIN), BF),
        ],
        compiler_params=pltpu.CompilerParams(vmem_limit_bytes=24 * 2**20),
        cost_estimate=expected(0.6 + 2.0 * slots),
        name="cross",
    )(plan, *operands)


def slot_rounds(plan, count):
    _, ranks = partner_steps(plan, count)
    rounds = []
    for slot in range(ROUNDS):
        number = jnp.int32(0)
        for other in range(1, ROUNDS):
            number = jnp.where(ranks[other] == slot, other, number)
        rounds.append(number)
    return rounds


def placed_block(pieces, matrix, at, half):
    joined = jnp.concatenate([piece[at, :] for piece in pieces], axis=1)
    if pieces[0].shape[0] > half:
        later = slice(half + at.start, half + at.stop)
        high = jnp.concatenate([piece[later, :] for piece in pieces], axis=1)
        joined = jnp.concatenate([joined, high], axis=0)
    return jnp.dot(joined, matrix, preferred_element_type=F32)


def joined_matrix(place, parts):
    me = lax.axis_index("seg")
    return jnp.concatenate([place[me ^ j] for j in range(parts)], axis=0)


def early_kernel(parts, groups, place, *rest):
    pieces, out = rest[:-1], rest[-1]
    half, pairs = out.shape[2:]
    matrix = joined_matrix(place, parts)
    at = slice(0, half)
    for index, (first_slot, slots) in enumerate(groups):
        block = placed_block(pieces[index * parts : (index + 1) * parts], matrix, at, half)
        if slots == 1:
            out[first_slot, 0] = block[:, :pairs]
            out[first_slot, 1] = block[:, pairs:]
        else:
            for slot in range(2):
                columns = slice(slot * pairs, (slot + 1) * pairs)
                out[first_slot + slot, 0] = block[:half, columns]
                out[first_slot + slot, 1] = block[half:, columns]


def late_kernel(count, parts, steps, plan, place, early, *rest):
    pieces = rest[:parts]
    out_hbm, out, sems = rest[parts:]
    half, pairs = early.shape[2:]
    tiles = pairs // LANES
    lag_rows = tiles * ROUNDS
    rows = half // steps
    rounds = slot_rounds(plan, count)
    matrix = joined_matrix(place, parts)
    block = placed_block(pieces, matrix, slice(0, half), half)
    copies = []
    for step in range(steps):
        at = slice(step * rows, (step + 1) * rows)
        for h in range(2):
            first = (h * half + step * rows) * lag_rows
            for slot in range(ROUNDS):
                for tile in range(tiles):
                    lanes = slice(tile * LANES, (tile + 1) * LANES)
                    if slot < ROUNDS - 1:
                        value = early[slot, h, at, lanes]
                    else:
                        value = block[at, h * pairs + lanes.start : h * pairs + lanes.stop]
                    start = first + tile * ROUNDS + rounds[slot]
                    out[pl.ds(start, rows, stride=lag_rows), :] = value
            chunk = pl.ds(first, rows * lag_rows)
            copy = pltpu.make_async_copy(
                out.at[chunk], out_hbm.at[chunk], sems.at[2 * step + h]
            )
            copy.start()
            copies.append(copy)
    for copy in copies:
        copy.wait()


def place_lags(plan, groups, pieces, count, stations, parts):
    pairs = stations * stations
    share = LAGS // parts
    half = share // 2
    steps = 4
    place = jnp.asarray(make_placing(stations, stations // parts, parts))
    vmem = pl.BlockSpec(memory_space=pltpu.VMEM)
    early = pl.pallas_call(
        functools.partial(early_kernel, parts, tuple(groups[:-1])),
        out_shape=jax.ShapeDtypeStruct((ROUNDS - 1, 2, half, pairs), F32),
        in_specs=[vmem] * (1 + len(pieces) - parts),
        out_specs=vmem,
        compiler_params=pltpu.CompilerParams(vmem_limit_bytes=16 * 2**20),
        cost_estimate=expected(0.05),
        name="early",
    )(place, *pieces[:-parts])
    shape = (share * ROUNDS * pairs // LANES, LANES)
    out = pl.pallas_call(
        functools.partial(late_kernel, count, parts, steps),
        out_shape=jax.ShapeDtypeStruct(shape, F32),
        in_specs=[pl.BlockSpec(memory_space=pltpu.SMEM)] + [vmem] * (2 + parts),
        out_specs=pl.BlockSpec(memory_space=pl.ANY),
        scratch_shapes=[pltpu.VMEM(shape, F32), pltpu.SemaphoreType.DMA((2 * steps,))],
        compiler_params=pltpu.CompilerParams(vmem_limit_bytes=24 * 2**20),
        cost_estimate=expected(0.05),
        name="late",
    )(plan, place, early, *pieces[-parts:])
    out = out.reshape(share, pairs // LANES, ROUNDS, LANES)
    return out.transpose(0, 2, 1, 3).reshape(share, ROUNDS, pairs)


def join_kernel(order, *refs):
    parts, (out_up, out_down) = refs[:4], refs[4:]
    near_up, near_down, far_up, far_down = [parts[order.index(k)] for k in range(4)]
    half = near_up.shape[0]
    for out, first, second in ((out_up, near_up, far_up), (out_down, near_down, far_down)):
        out[:half] = first[...]
        out[half:] = second[...]


def join(near_up, near_down, far_up, far_down, order=(0, 1, 2, 3)):
    values = [near_up, near_down, far_up, far_down]
    vmem = pl.BlockSpec(memory_space=pltpu.VMEM)
    shape = (2 * near_up.shape[0],) + near_up.shape[1:]
    return pl.pallas_call(
        functools.partial(join_kernel, tuple(order)),
        out_shape=[jax.ShapeDtypeStruct(shape, BF)] * 2,
        in_specs=[vmem] * 4,
        out_specs=[vmem] * 2,
        compiler_params=pltpu.CompilerParams(vmem_limit_bytes=16 * 2**20),
        cost_estimate=expected(0.05),
        name="join",
    )(*[values[k] for k in order])


def swap(value, j):
    parts = lax.axis_size("seg")
    return lax.ppermute(value, "seg", [(i, i ^ j) for i in range(parts)])


def exchange(pieces):
    return [pieces[0]] + [swap(pieces[j], j) for j in range(1, len(pieces))]


def after(value, others):
    return lax.optimization_barrier((value, others))[0]


def per_device(records, plan):
    stations, windows, length = records.shape
    count = lax.axis_size("sta")
    parts = lax.axis_size("seg")
    quarter = stations // parts
    table = jnp.asarray(make_table(length // CHUNKS, 2 * length))
    scaling = 1.0 / math.sqrt(4.0 * NBIN * windows * parts)

    white, *quarters = prepare(records, table, parts)
    near = jnp.concatenate([quarters[0], swap(quarters[1], 1)])
    sibling = swap(white, 1)
    far = jnp.concatenate([swap(quarters[j], j) for j in range(2, parts)])
    far = after(far, sibling)
    far, white_far = lax.optimization_barrier((far, white))
    across = swap(white_far, 2)

    ring = sorted(range(count), key=lambda b: b // 2 if b % 2 == 0 else count - 1 - b // 2)
    upward = [(ring[i], ring[(i + 1) % count]) for i in range(count)]
    downward = [(ring[i], ring[i - 1]) for i in range(count)]

    def up(value):
        return lax.ppermute(value, "sta", upward)

    def down(value):
        return lax.ppermute(value, "sta", downward)

    far, white_far = lax.optimization_barrier((far, white))
    across = swap(white_far, 2)
    near_own = widen_own([white, sibling])
    half = near.shape[0]
    places, blocks, arrived = [], [], []

    def arrive(step, first, from_left, from_right):
        places.extend([(count - step, first), (step, first)])
        blocks.extend([from_left, from_right])

    near_up, near_down = up(near), down(near)
    far_up, far_down = up(far), down(far)
    arrive(1, 0, near_up, near_down)
    arrive(1, half, far_up, far_down)
    near_up, near_down, near_own = lax.optimization_barrier((near_up, near_down, near_own))
    near_up, near_down = up(near_up), down(near_down)
    far_up, far_down = lax.optimization_barrier((far_up, far_down))
    far_up, far_down = up(far_up), down(far_down)
    arrive(2, 0, near_up, near_down)
    arrive(2, half, far_up, far_down)
    all_up, all_down = join(near_up, near_down, far_up, far_down)
    for step in range(3, (count - 1) // 2 + 1):
        arrived.append((list(places), list(blocks)))
        all_up, all_down, across = lax.optimization_barrier((all_up, all_down, across))
        all_up, all_down = up(all_up), down(all_down)
        arrive(step, 0, all_up, all_down)
    arrived.append((list(places), list(blocks)))
    far_own = widen_own([across, swap(across, 1)])
    groups = [(0, 1), (1, 2), (3, 1)]
    if count % 2 == 0:
        places.append((count // 2, 0))
        blocks.append(up(all_up))
    arrived.append((places, blocks))
    pieces = []
    for index, (first_slot, slots) in enumerate(groups):
        if index == 2:
            near_own = after(near_own, pieces[:parts])
        if index > 0:
            near_own = after(near_own, lags)
        at, values = arrived[index - len(groups)]
        lags = cross_lags(
            plan, table, [near_own, far_own], at, values, first_slot, slots, count, parts, scaling
        )
        pieces = pieces + exchange(lags)
    return place_lags(plan, groups, pieces, count, stations, parts)


def solution(mesh):
    in_specs = (P("sta", "seg", None), P())
    out_specs = P("seg", None, "sta")
    return jax.shard_map(
        per_device, mesh=mesh, in_specs=in_specs, out_specs=out_specs, check_vma=False
    )
```

```python
import functools
import math

import jax
import jax.numpy as jnp
import ml_dtypes
import numpy as np
from jax import lax
from jax.experimental import pallas as pl
from jax.experimental.pallas import tpu as pltpu
from jax.sharding import PartitionSpec as P

NBIN = 1024
HALF = 64
ROUNDS = 4
LAGS = 2048
LANES = 128
TILES = NBIN // LANES
CHUNKS = 4
GROUP = 4
BF = jnp.bfloat16
F32 = jnp.float32


def make_table(rows, transform):
    phase = (np.arange(rows)[:, None] * np.arange(NBIN)[None, :]) % transform
    angle = phase * (2.0 * math.pi / transform)
    return np.concatenate([np.cos(angle), -np.sin(angle)], axis=1).astype(ml_dtypes.bfloat16)


def band_matrix():
    source = lax.broadcasted_iota(jnp.int32, (3 * LANES, LANES), 0) - LANES
    target = lax.broadcasted_iota(jnp.int32, (3 * LANES, LANES), 1)
    return jnp.where(jnp.abs(source - target) <= HALF, 1.0, 0.0).astype(BF)


def inverse_count(block, length):
    position = lax.broadcasted_iota(jnp.int32, (1, LANES), 1) + block * LANES
    counted = jnp.minimum(position, HALF) + jnp.minimum(length - 1 - position, HALF) + 1
    return 1.0 / counted.astype(F32)


def make_placing(stations, quarter, parts):
    width = stations * quarter
    place = np.zeros((parts, 2 * width, 2 * stations * stations), np.float32)
    for part in range(parts):
        for second in range(2):
            for s in range(stations):
                for t in range(quarter):
                    row = second * width + s * quarter + t
                    column = (second * stations + s) * stations + part * quarter + t
                    place[part, row, column] = 1.0
    return place.astype(ml_dtypes.bfloat16)


def lane_cycle(values):
    period = len(values)
    phase = lax.broadcasted_iota(jnp.int32, (1, LANES), 1) % period
    out = jnp.full((1, LANES), values[-1], F32)
    for index in range(period - 1):
        out = jnp.where(phase == index, values[index], out)
    return out


def even_lanes(shape):
    return lax.broadcasted_iota(jnp.int32, shape, 1) % 2 == 0


def eighth_turn():
    turns = [math.pi * k / 4.0 for k in range(8)]
    return lane_cycle([math.cos(t) for t in turns]), lane_cycle([math.sin(t) for t in turns])


def quarter_turns(real, imag, even, sign_real, sign_imag):
    return sign_real * jnp.where(even, real, imag), sign_imag * jnp.where(even, imag, real)


def banded_sum(stack, values, band):
    rows, length = values.shape
    blocks = length // LANES
    zero = jnp.zeros((rows, LANES), BF)
    for j in range(blocks):
        at = pl.ds(j * rows, rows)
        for k in range(3):
            b = j + k - 1
            block = values[:, b * LANES : (b + 1) * LANES] if 0 <= b < blocks else zero
            stack[at, k * LANES : (k + 1) * LANES] = block
    total = jnp.dot(stack[: blocks * rows, :], band, preferred_element_type=F32)
    return [total[j * rows : (j + 1) * rows, :] for j in range(blocks)]


def prep_kernel(parts, records_hbm, table_hbm, white, mine, *rest):
    others = rest[: parts - 1]
    records, table, stack, flat, spread, sems = rest[parts - 1 :]
    records_copy = pltpu.make_async_copy(records_hbm, records, sems.at[0])
    records_copy.start()
    copy = pltpu.make_async_copy(table_hbm, table, sems.at[1])
    copy.start()
    band_values = band_matrix()
    records_copy.wait()
    stations, windows, length = records.shape
    rows = stations * windows
    chunk = length // CHUNKS
    signal = jnp.concatenate([records[:, w, :] for w in range(windows)], axis=0)
    sums = banded_sum(stack, jnp.abs(signal).astype(BF), band_values)
    for j, total in enumerate(sums):
        at = slice(j * LANES, (j + 1) * LANES)
        level = total * inverse_count(j, length)
        value = (signal[:, at] / (level + 1e-05)).astype(BF)
        q, inside = divmod(j * LANES, chunk)
        flat[q * rows : (q + 1) * rows, inside : inside + LANES] = value
    copy.wait()
    product = jnp.dot(flat[...], table[...], preferred_element_type=F32)
    even = even_lanes((rows, LANES))
    sign_real = lane_cycle([1.0, 1.0, -1.0, -1.0])
    sign_imag = lane_cycle([1.0, -1.0, -1.0, 1.0])
    cosine, sine = eighth_turn()
    reals, imags, mags = [], [], []
    for j in range(TILES):
        at = slice(j * LANES, (j + 1) * LANES)
        at_imag = slice(NBIN + j * LANES, NBIN + (j + 1) * LANES)
        pr = [product[q * rows : (q + 1) * rows, at] for q in range(CHUNKS)]
        pi = [product[q * rows : (q + 1) * rows, at_imag] for q in range(CHUNKS)]
        turned = [
            quarter_turns(pr[q], pi[q], even, sign_real, sign_imag) for q in range(2, CHUNKS)
        ]
        first_real, first_imag = pr[0] + turned[0][0], pi[0] + turned[0][1]
        odd_real, odd_imag = pr[1] + turned[1][0], pi[1] + turned[1][1]
        real = first_real + (odd_real * cosine + odd_imag * sine)
        imag = first_imag + (odd_imag * cosine - odd_real * sine)
        reals.append(real)
        imags.append(imag)
        mags.append(jnp.sqrt(real * real + imag * imag).astype(BF))
    sums = banded_sum(stack, jnp.concatenate(mags, axis=1), band_values)
    for j, total in enumerate(sums):
        at = slice(j * LANES, (j + 1) * LANES)
        smooth = total * inverse_count(j, NBIN) + 1e-06
        spread[pl.ds(j, rows, stride=2 * TILES), :] = reals[j] / smooth
        spread[pl.ds(TILES + j, rows, stride=2 * TILES), :] = imags[j] / smooth
    me = lax.axis_index("seg")
    quarter = stations // parts
    white[...] = spread[...].reshape(windows, stations, 2 * TILES, LANES).astype(BF)
    for j, out in enumerate((mine, *others)):
        for w in range(windows):
            out[w] = white[w, pl.ds((me ^ j) * quarter, quarter)]


def prepare(records, table, parts):
    stations, windows, length = records.shape
    rows = stations * windows
    quarter = stations // parts
    small = jax.ShapeDtypeStruct((windows, quarter, 2 * TILES, LANES), BF)
    vmem = pl.BlockSpec(memory_space=pltpu.VMEM)
    return pl.pallas_call(
        functools.partial(prep_kernel, parts),
        out_shape=[jax.ShapeDtypeStruct((windows, stations, 2 * TILES, LANES), BF)]
        + [small] * parts,
        in_specs=[pl.BlockSpec(memory_space=pltpu.HBM)] * 2,
        out_specs=[vmem] * (1 + parts),
        scratch_shapes=[
            pltpu.VMEM(records.shape, F32),
            pltpu.VMEM(table.shape, BF),
            pltpu.VMEM((rows * (length // LANES), 3 * LANES), BF),
            pltpu.VMEM((CHUNKS * rows, length // CHUNKS), BF),
            pltpu.VMEM((rows * 2 * TILES, LANES), F32),
            pltpu.SemaphoreType.DMA((2,)),
        ],
        compiler_params=pltpu.CompilerParams(vmem_limit_bytes=52 * 2**20),
        cost_estimate=pl.CostEstimate(
            flops=2 * rows * length * 2 * NBIN, bytes_accessed=3 * 2**20, transcendentals=0
        ),
        name="prep",
    )(
        pltpu.with_memory_space_constraint(records, pltpu.HBM),
        pltpu.with_memory_space_constraint(table, pltpu.HBM),
    )


def ring_place(block, count):
    half = block >> 1
    return jnp.where((block & 1) == 0, half, count - 1 - half)


def partner_steps(plan, count):
    me = lax.axis_index("sta")
    mine = ring_place(me, count)
    steps, keys = [], []
    for number in range(ROUNDS):
        step = ring_place(plan[number, me], count) - mine
        step = jnp.where(step < 0, step + count, step)
        steps.append(step)
        keys.append(jnp.minimum(step, count - step) * ROUNDS + number)
    ranks = []
    for number in range(ROUNDS):
        rank = jnp.int32(0)
        for other in range(ROUNDS):
            if other != number:
                rank = rank + jnp.where(keys[other] < keys[number], 1, 0)
        ranks.append(rank)
    return steps, ranks


def expected(microseconds):
    return pl.CostEstimate(
        flops=int(microseconds * 1.15e9), bytes_accessed=1024, transcendentals=0
    )


def widen_kernel(*refs):
    blocks, own = refs[:-1], refs[-1]
    windows = blocks[0].shape[0]
    for j, block in enumerate(blocks):

        def widen(w, carry, j=j, block=block):
            raw = block[w].astype(F32)
            real, imag = raw[:, :TILES], raw[:, TILES:]
            both = real + imag
            for group in range(own.shape[0]):
                at = slice(group * GROUP, (group + 1) * GROUP)
                own[group, 0, j * windows + w] = both[at]
                own[group, 1, j * windows + w] = real[at]
                own[group, 2, j * windows + w] = imag[at]
            return carry

        lax.fori_loop(0, windows, widen, 0)


def widen_own(blocks):
    windows, stations = blocks[0].shape[:2]
    vmem = pl.BlockSpec(memory_space=pltpu.VMEM)
    return pl.pallas_call(
        widen_kernel,
        out_shape=jax.ShapeDtypeStruct(
            (stations // GROUP, 3, len(blocks) * windows, GROUP, TILES, LANES), F32
        ),
        in_specs=[vmem] * len(blocks),
        out_specs=vmem,
        compiler_params=pltpu.CompilerParams(vmem_limit_bytes=16 * 2**20),
        cost_estimate=expected(0.05),
        name="widen",
    )(*blocks)


def widen_others(first_slot, slots, count, places, plan, candidates, other):
    steps, ranks = partner_steps(plan, count)
    for slot in range(slots):
        step = jnp.int32(0)
        for number in range(ROUNDS):
            step = jnp.where(ranks[number] == first_slot + slot, steps[number], step)
        for (offset, first), candidate in zip(places, candidates):

            @pl.when(step == offset)
            def _(candidate=candidate, slot=slot, first=first):
                def widen_other(w, carry):
                    raw = candidate[w].astype(F32)
                    real, imag = raw[:, :TILES], raw[:, TILES:]
                    other[0, slot, first + w] = real
                    other[1, slot, first + w] = real + imag
                    other[2, slot, first + w] = imag - real
                    return carry

                lax.fori_loop(0, candidate.shape[0], widen_other, 0)


def sum_windows(owns, other, crossed):
    groups, _, windows, group = owns[0].shape[:4]
    slots, _, quarter = other.shape[1:4]
    width = groups * group * quarter

    def one_group(slot, index):
        first = index * group
        mine = [own.at[index] for own in owns]

        def sums(kind):
            totals = [None] * (group * quarter)
            for part, own in enumerate(mine):
                for w in range(windows):
                    left = [own[kind, w, s] for s in range(group)]
                    right = [other[kind, slot, part * windows + w, t] for t in range(quarter)]
                    for s in range(group):
                        for t in range(quarter):
                            term = left[s] * right[t]
                            place = s * quarter + t
                            old = totals[place]
                            totals[place] = term if old is None else old + term
            return totals

        def store(place, part, value):
            at = pl.multiple_of((base + place) * 2 * TILES + part * TILES, TILES)
            crossed[pl.ds(at, TILES), :] = value

        base = slot * width + first * quarter
        shared = sums(0)
        third = sums(2)
        for place in range(group * quarter):
            store(place, 0, shared[place] + third[place])
        second = sums(1)
        for place in range(group * quarter):
            store(place, 1, shared[place] - second[place])

    for slot in range(slots):

        def body(index, carry, slot=slot):
            one_group(slot, index)
            return carry

        lax.fori_loop(0, groups, body, 0)


def cross_kernel(first_slot, slots, count, scaling, places, parts, plan, table, *rest):
    owns, rest = rest[:2], rest[2:]
    others, rest = rest[: len(places)], rest[len(places) :]
    outs = rest[:parts]
    other, crossed, operand, result = rest[parts:]
    stations = owns[0].shape[0] * owns[0].shape[3]
    widen_others(first_slot, slots, count, places, plan, others, other)
    sum_windows(owns, other, crossed)
    width = stations * other.shape[3]
    columns = slots * width
    even = even_lanes((columns, LANES))
    sign_real = lane_cycle([1.0, -1.0, -1.0, 1.0])
    sign_imag = lane_cycle([1.0, 1.0, -1.0, -1.0])
    cosine, sine = eighth_turn()
    lane = lax.broadcasted_iota(jnp.int32, (1, LANES), 1)
    first_weight = jnp.where(lane == 0, 1.0, 2.0).astype(F32)
    for j in range(TILES):
        at = slice(j * LANES, (j + 1) * LANES)
        at_imag = slice(NBIN + j * LANES, NBIN + (j + 1) * LANES)
        weight = first_weight if j == 0 else 2.0
        real = crossed[pl.ds(j, columns, stride=2 * TILES), :] * weight
        imag = crossed[pl.ds(TILES + j, columns, stride=2 * TILES), :] * weight
        turned = [(real, imag), (real * cosine - imag * sine, imag * cosine + real * sine)]
        turned += [quarter_turns(r, i, even, sign_real, sign_imag) for r, i in turned]
        for q in range(CHUNKS):
            rows = slice(q * columns, (q + 1) * columns)
            operand[rows, at] = turned[q][0].astype(BF)
            operand[rows, at_imag] = turned[q][1].astype(BF)
    block = lax.dot_general(
        table[...], operand[...], (((1,), (1,)), ((), ())), preferred_element_type=F32
    )
    block = block * scaling
    if slots == 1:
        half = table.shape[0] // 2
        low_lanes = lax.broadcasted_iota(jnp.int32, (half, LANES), 1) < width
        for p in range(CHUNKS // 2):
            at = slice(p * LANES, (p + 1) * LANES)
            low, high = block[:half, at], block[half:, at]
            pair = (
                jnp.where(low_lanes, low, pltpu.roll(high, width, 1)),
                jnp.where(low_lanes, pltpu.roll(low, width, 1), high),
            )
            for second in range(2):
                result[2 * p + second] = pair[second].astype(BF)
    else:
        for q in range(CHUNKS):
            result[q] = block[:, q * columns : (q + 1) * columns].astype(BF)
    me = lax.axis_index("seg")
    for j in range(parts):
        outs[j][...] = result[me ^ j]


def cross_lags(plan, table, owns, places, candidates, first_slot, slots, count, parts, scaling):
    windows, stations = owns[0].shape[2], owns[0].shape[0] * owns[0].shape[3]
    quarter = candidates[0].shape[1]
    columns = slots * stations * quarter
    share = LAGS // parts
    out = (share, columns) if slots > 1 else (share // 2, 2 * columns)
    smem = pl.BlockSpec(memory_space=pltpu.SMEM)
    vmem = pl.BlockSpec(memory_space=pltpu.VMEM)
    operands = [table, *owns, *candidates]
    return pl.pallas_call(
        functools.partial(
            cross_kernel, first_slot, slots, count, scaling, tuple(places), parts
        ),
        out_shape=[jax.ShapeDtypeStruct(out, BF)] * parts,
        in_specs=[smem] + [vmem] * len(operands),
        out_specs=[vmem] * parts,
        scratch_shapes=[
            pltpu.VMEM((3, slots, 2 * windows, quarter, TILES, LANES), F32),
            pltpu.VMEM((columns * 2 * TILES, LANES), F32),
            pltpu.VMEM((CHUNKS * columns, 2 * NBIN), BF),
            pltpu.VMEM((parts,) + out, BF),
        ],
        compiler_params=pltpu.CompilerParams(vmem_limit_bytes=24 * 2**20),
        cost_estimate=expected(0.6 + 2.0 * slots),
        name="cross",
    )(plan, *operands)


def slot_rounds(plan, count):
    _, ranks = partner_steps(plan, count)
    rounds = []
    for slot in range(ROUNDS):
        number = jnp.int32(0)
        for other in range(1, ROUNDS):
            number = jnp.where(ranks[other] == slot, other, number)
        rounds.append(number)
    return rounds


def placed_block(pieces, matrix, at, half):
    joined = jnp.concatenate([piece[at, :] for piece in pieces], axis=1)
    if pieces[0].shape[0] > half:
        later = slice(half + at.start, half + at.stop)
        high = jnp.concatenate([piece[later, :] for piece in pieces], axis=1)
        joined = jnp.concatenate([joined, high], axis=0)
    return jnp.dot(joined, matrix, preferred_element_type=F32)


def joined_matrix(place, parts):
    me = lax.axis_index("seg")
    return jnp.concatenate([place[me ^ j] for j in range(parts)], axis=0)


def store_rows(rows, block, first):
    tiles = block.shape[1] // LANES
    for tile in range(tiles):
        at = pl.ds(first * tiles + tile, block.shape[0], stride=tiles)
        rows[at, :] = block[:, tile * LANES : (tile + 1) * LANES]


def early_kernel(count, parts, groups, half, plan, place, *rest):
    pieces = rest[:-3]
    out_hbm, rows, sems = rest[-3:]
    pairs = place.shape[2] // 2
    rounds = slot_rounds(plan, count)
    matrix = joined_matrix(place, parts)
    at = slice(0, half)
    copies = []
    for index, (first_slot, slots) in enumerate(groups):
        block = placed_block(pieces[index * parts : (index + 1) * parts], matrix, at, half)
        for slot in range(slots):
            if slots == 1:
                low, high = block[:, :pairs], block[:, pairs:]
            else:
                columns = slice(slot * pairs, (slot + 1) * pairs)
                low, high = block[:half, columns], block[half:, columns]
            number = first_slot + slot
            store_rows(rows.at[number], low, 0)
            store_rows(rows.at[number], high, half)
            copy = pltpu.make_async_copy(
                rows.at[number], out_hbm.at[:, rounds[number], 0], sems.at[number]
            )
            copy.start()
            copies.append(copy)
    for copy in copies:
        copy.wait()


def late_kernel(count, parts, half, plan, place, early, *rest):
    pieces = rest[:parts]
    out_hbm, rows, sem = rest[parts:]
    pairs = place.shape[2] // 2
    number = slot_rounds(plan, count)[ROUNDS - 1]
    block = placed_block(pieces, joined_matrix(place, parts), slice(0, half), half)
    store_rows(rows, block[:, :pairs], 0)
    store_rows(rows, block[:, pairs:], half)
    copy = pltpu.make_async_copy(rows, out_hbm.at[:, number, 0], sem)
    copy.start()
    copy.wait()


def place_lags(plan, groups, pieces, count, stations, parts):
    pairs = stations * stations
    share = LAGS // parts
    half = share // 2
    tiles = pairs // LANES
    place = jnp.asarray(make_placing(stations, stations // parts, parts))
    smem = pl.BlockSpec(memory_space=pltpu.SMEM)
    vmem = pl.BlockSpec(memory_space=pltpu.VMEM)
    anywhere = pl.BlockSpec(memory_space=pl.ANY)
    shape = jax.ShapeDtypeStruct((share * tiles, ROUNDS, 1, LANES), F32)
    early = pl.pallas_call(
        functools.partial(early_kernel, count, parts, tuple(groups[:-1]), half),
        out_shape=shape,
        in_specs=[smem] + [vmem] * (1 + len(pieces) - parts),
        out_specs=anywhere,
        scratch_shapes=[
            pltpu.VMEM((ROUNDS - 1, share * tiles, LANES), F32),
            pltpu.SemaphoreType.DMA((ROUNDS - 1,)),
        ],
        compiler_params=pltpu.CompilerParams(vmem_limit_bytes=16 * 2**20),
        cost_estimate=expected(0.05),
        name="early",
    )(plan, place, *pieces[:-parts])
    out = pl.pallas_call(
        functools.partial(late_kernel, count, parts, half),
        out_shape=shape,
        in_specs=[smem, vmem, anywhere] + [vmem] * parts,
        out_specs=anywhere,
        scratch_shapes=[pltpu.VMEM((share * tiles, LANES), F32), pltpu.SemaphoreType.DMA],
        input_output_aliases={2: 0},
        compiler_params=pltpu.CompilerParams(vmem_limit_bytes=16 * 2**20),
        cost_estimate=expected(0.05),
        name="late",
    )(plan, place, early, *pieces[-parts:])
    out = out.reshape(share, tiles, ROUNDS, LANES)
    return out.transpose(0, 2, 1, 3).reshape(share, ROUNDS, pairs)


def join_kernel(order, *refs):
    parts, (out_up, out_down) = refs[:4], refs[4:]
    near_up, near_down, far_up, far_down = [parts[order.index(k)] for k in range(4)]
    half = near_up.shape[0]
    for out, first, second in ((out_up, near_up, far_up), (out_down, near_down, far_down)):
        out[:half] = first[...]
        out[half:] = second[...]


def join(near_up, near_down, far_up, far_down, order=(0, 1, 2, 3)):
    values = [near_up, near_down, far_up, far_down]
    vmem = pl.BlockSpec(memory_space=pltpu.VMEM)
    shape = (2 * near_up.shape[0],) + near_up.shape[1:]
    return pl.pallas_call(
        functools.partial(join_kernel, tuple(order)),
        out_shape=[jax.ShapeDtypeStruct(shape, BF)] * 2,
        in_specs=[vmem] * 4,
        out_specs=[vmem] * 2,
        compiler_params=pltpu.CompilerParams(vmem_limit_bytes=16 * 2**20),
        cost_estimate=expected(0.05),
        name="join",
    )(*[values[k] for k in order])


def swap(value, j):
    parts = lax.axis_size("seg")
    return lax.ppermute(value, "seg", [(i, i ^ j) for i in range(parts)])


def exchange(pieces):
    return [pieces[0]] + [swap(pieces[j], j) for j in range(1, len(pieces))]


def after(value, others):
    return lax.optimization_barrier((value, others))[0]


def per_device(records, plan):
    stations, windows, length = records.shape
    count = lax.axis_size("sta")
    parts = lax.axis_size("seg")
    quarter = stations // parts
    table = jnp.asarray(make_table(length // CHUNKS, 2 * length))
    scaling = 1.0 / math.sqrt(4.0 * NBIN * windows * parts)

    white, *quarters = prepare(records, table, parts)
    near = jnp.concatenate([quarters[0], swap(quarters[1], 1)])
    sibling = swap(white, 1)
    far = jnp.concatenate([swap(quarters[j], j) for j in range(2, parts)])
    far = after(far, sibling)
    far, white_far = lax.optimization_barrier((far, white))
    across = swap(white_far, 2)

    ring = sorted(range(count), key=lambda b: b // 2 if b % 2 == 0 else count - 1 - b // 2)
    upward = [(ring[i], ring[(i + 1) % count]) for i in range(count)]
    downward = [(ring[i], ring[i - 1]) for i in range(count)]

    def up(value):
        return lax.ppermute(value, "sta", upward)

    def down(value):
        return lax.ppermute(value, "sta", downward)

    far, white_far = lax.optimization_barrier((far, white))
    across = swap(white_far, 2)
    near_own = widen_own([white, sibling])
    half = near.shape[0]
    places, blocks, arrived = [], [], []

    def arrive(step, first, from_left, from_right):
        places.extend([(count - step, first), (step, first)])
        blocks.extend([from_left, from_right])

    near_up, near_down = up(near), down(near)
    far_up, far_down = up(far), down(far)
    arrive(1, 0, near_up, near_down)
    arrive(1, half, far_up, far_down)
    near_up, near_down, near_own = lax.optimization_barrier((near_up, near_down, near_own))
    near_up, near_down = up(near_up), down(near_down)
    far_up, far_down = lax.optimization_barrier((far_up, far_down))
    far_up, far_down = up(far_up), down(far_down)
    arrive(2, 0, near_up, near_down)
    arrive(2, half, far_up, far_down)
    all_up, all_down = join(near_up, near_down, far_up, far_down)
    for step in range(3, (count - 1) // 2 + 1):
        arrived.append((list(places), list(blocks)))
        all_up, all_down, across = lax.optimization_barrier((all_up, all_down, across))
        all_up, all_down = up(all_up), down(all_down)
        arrive(step, 0, all_up, all_down)
    arrived.append((list(places), list(blocks)))
    far_own = widen_own([across, swap(across, 1)])
    groups = [(0, 1), (1, 2), (3, 1)]
    if count % 2 == 0:
        places.append((count // 2, 0))
        blocks.append(up(all_up))
    arrived.append((places, blocks))
    pieces = []
    for index, (first_slot, slots) in enumerate(groups):
        if index == 2:
            near_own = after(near_own, pieces[:parts])
        if index > 0:
            near_own = after(near_own, lags)
        at, values = arrived[index - len(groups)]
        lags = cross_lags(
            plan, table, [near_own, far_own], at, values, first_slot, slots, count, parts, scaling
        )
        pieces = pieces + exchange(lags)
    return place_lags(plan, groups, pieces, count, stations, parts)


def solution(mesh):
    in_specs = (P("sta", "seg", None), P())
    out_specs = P("seg", None, "sta")
    return jax.shard_map(
        per_device, mesh=mesh, in_specs=in_specs, out_specs=out_specs, check_vma=False
    )
```

```python
import functools
import math

import jax
import jax.numpy as jnp
import ml_dtypes
import numpy as np
from jax import lax
from jax.experimental import pallas as pl
from jax.experimental.pallas import tpu as pltpu
from jax.sharding import PartitionSpec as P

NBIN = 1024
HALF = 64
ROUNDS = 4
LAGS = 2048
LANES = 128
TILES = NBIN // LANES
CHUNKS = 4
GROUP = 4
BF = jnp.bfloat16
F32 = jnp.float32


def make_table(rows, transform):
    phase = (np.arange(rows)[:, None] * np.arange(NBIN)[None, :]) % transform
    angle = phase * (2.0 * math.pi / transform)
    return np.concatenate([np.cos(angle), -np.sin(angle)], axis=1).astype(ml_dtypes.bfloat16)


def band_matrix():
    source = lax.broadcasted_iota(jnp.int32, (3 * LANES, LANES), 0) - LANES
    target = lax.broadcasted_iota(jnp.int32, (3 * LANES, LANES), 1)
    return jnp.where(jnp.abs(source - target) <= HALF, 1.0, 0.0).astype(BF)


def inverse_count(block, length):
    position = lax.broadcasted_iota(jnp.int32, (1, LANES), 1) + block * LANES
    counted = jnp.minimum(position, HALF) + jnp.minimum(length - 1 - position, HALF) + 1
    return 1.0 / counted.astype(F32)


def make_placing(stations, quarter, parts):
    width = stations * quarter
    place = np.zeros((parts, 2 * width, 2 * stations * stations), np.float32)
    for part in range(parts):
        for second in range(2):
            for s in range(stations):
                for t in range(quarter):
                    row = second * width + s * quarter + t
                    column = (second * stations + s) * stations + part * quarter + t
                    place[part, row, column] = 1.0
    return place.astype(ml_dtypes.bfloat16)


def lane_cycle(values):
    period = len(values)
    phase = lax.broadcasted_iota(jnp.int32, (1, LANES), 1) % period
    out = jnp.full((1, LANES), values[-1], F32)
    for index in range(period - 1):
        out = jnp.where(phase == index, values[index], out)
    return out


def even_lanes(shape):
    return lax.broadcasted_iota(jnp.int32, shape, 1) % 2 == 0


def eighth_turn():
    turns = [math.pi * k / 4.0 for k in range(8)]
    return lane_cycle([math.cos(t) for t in turns]), lane_cycle([math.sin(t) for t in turns])


def quarter_turns(real, imag, even, sign_real, sign_imag):
    return sign_real * jnp.where(even, real, imag), sign_imag * jnp.where(even, imag, real)


def banded_sum(stack, values, band):
    rows, length = values.shape
    blocks = length // LANES
    zero = jnp.zeros((rows, LANES), BF)
    for j in range(blocks):
        at = pl.ds(j * rows, rows)
        for k in range(3):
            b = j + k - 1
            block = values[:, b * LANES : (b + 1) * LANES] if 0 <= b < blocks else zero
            stack[at, k * LANES : (k + 1) * LANES] = block
    total = jnp.dot(stack[: blocks * rows, :], band, preferred_element_type=F32)
    return [total[j * rows : (j + 1) * rows, :] for j in range(blocks)]


def prep_kernel(parts, records_hbm, table_hbm, white, mine, *rest):
    others = rest[: parts - 1]
    records, table, stack, flat, spread, sems = rest[parts - 1 :]
    records_copy = pltpu.make_async_copy(records_hbm, records, sems.at[0])
    records_copy.start()
    copy = pltpu.make_async_copy(table_hbm, table, sems.at[1])
    copy.start()
    band_values = band_matrix()
    records_copy.wait()
    stations, windows, length = records.shape
    rows = stations * windows
    chunk = length // CHUNKS
    signal = jnp.concatenate([records[:, w, :] for w in range(windows)], axis=0)
    sums = banded_sum(stack, jnp.abs(signal).astype(BF), band_values)
    for j, total in enumerate(sums):
        at = slice(j * LANES, (j + 1) * LANES)
        level = total * inverse_count(j, length)
        value = (signal[:, at] / (level + 1e-05)).astype(BF)
        q, inside = divmod(j * LANES, chunk)
        flat[q * rows : (q + 1) * rows, inside : inside + LANES] = value
    copy.wait()
    product = jnp.dot(flat[...], table[...], preferred_element_type=F32)
    even = even_lanes((rows, LANES))
    sign_real = lane_cycle([1.0, 1.0, -1.0, -1.0])
    sign_imag = lane_cycle([1.0, -1.0, -1.0, 1.0])
    cosine, sine = eighth_turn()
    reals, imags, mags = [], [], []
    for j in range(TILES):
        at = slice(j * LANES, (j + 1) * LANES)
        at_imag = slice(NBIN + j * LANES, NBIN + (j + 1) * LANES)
        pr = [product[q * rows : (q + 1) * rows, at] for q in range(CHUNKS)]
        pi = [product[q * rows : (q + 1) * rows, at_imag] for q in range(CHUNKS)]
        turned = [
            quarter_turns(pr[q], pi[q], even, sign_real, sign_imag) for q in range(2, CHUNKS)
        ]
        first_real, first_imag = pr[0] + turned[0][0], pi[0] + turned[0][1]
        odd_real, odd_imag = pr[1] + turned[1][0], pi[1] + turned[1][1]
        real = first_real + (odd_real * cosine + odd_imag * sine)
        imag = first_imag + (odd_imag * cosine - odd_real * sine)
        reals.append(real)
        imags.append(imag)
        mags.append(jnp.sqrt(real * real + imag * imag).astype(BF))
    sums = banded_sum(stack, jnp.concatenate(mags, axis=1), band_values)
    for j, total in enumerate(sums):
        at = slice(j * LANES, (j + 1) * LANES)
        smooth = total * inverse_count(j, NBIN) + 1e-06
        spread[pl.ds(j, rows, stride=2 * TILES), :] = reals[j] / smooth
        spread[pl.ds(TILES + j, rows, stride=2 * TILES), :] = imags[j] / smooth
    me = lax.axis_index("seg")
    quarter = stations // parts
    white[...] = spread[...].reshape(windows, stations, 2 * TILES, LANES).astype(BF)
    for j, out in enumerate((mine, *others)):
        for w in range(windows):
            out[w] = white[w, pl.ds((me ^ j) * quarter, quarter)]


def prepare(records, table, parts):
    stations, windows, length = records.shape
    rows = stations * windows
    quarter = stations // parts
    small = jax.ShapeDtypeStruct((windows, quarter, 2 * TILES, LANES), BF)
    vmem = pl.BlockSpec(memory_space=pltpu.VMEM)
    return pl.pallas_call(
        functools.partial(prep_kernel, parts),
        out_shape=[jax.ShapeDtypeStruct((windows, stations, 2 * TILES, LANES), BF)]
        + [small] * parts,
        in_specs=[pl.BlockSpec(memory_space=pltpu.HBM)] * 2,
        out_specs=[vmem] * (1 + parts),
        scratch_shapes=[
            pltpu.VMEM(records.shape, F32),
            pltpu.VMEM(table.shape, BF),
            pltpu.VMEM((rows * (length // LANES), 3 * LANES), BF),
            pltpu.VMEM((CHUNKS * rows, length // CHUNKS), BF),
            pltpu.VMEM((rows * 2 * TILES, LANES), F32),
            pltpu.SemaphoreType.DMA((2,)),
        ],
        compiler_params=pltpu.CompilerParams(vmem_limit_bytes=52 * 2**20),
        cost_estimate=pl.CostEstimate(
            flops=2 * rows * length * 2 * NBIN, bytes_accessed=3 * 2**20, transcendentals=0
        ),
        name="prep",
    )(
        pltpu.with_memory_space_constraint(records, pltpu.HBM),
        pltpu.with_memory_space_constraint(table, pltpu.HBM),
    )


def ring_place(block, count):
    half = block >> 1
    return jnp.where((block & 1) == 0, half, count - 1 - half)


def partner_steps(plan, count):
    me = lax.axis_index("sta")
    mine = ring_place(me, count)
    steps, keys = [], []
    for number in range(ROUNDS):
        step = ring_place(plan[number, me], count) - mine
        step = jnp.where(step < 0, step + count, step)
        steps.append(step)
        keys.append(jnp.minimum(step, count - step) * ROUNDS + number)
    ranks = []
    for number in range(ROUNDS):
        rank = jnp.int32(0)
        for other in range(ROUNDS):
            if other != number:
                rank = rank + jnp.where(keys[other] < keys[number], 1, 0)
        ranks.append(rank)
    return steps, ranks


def expected(microseconds):
    return pl.CostEstimate(
        flops=int(microseconds * 1.15e9), bytes_accessed=1024, transcendentals=0
    )


def widen_kernel(*refs):
    blocks, own = refs[:-1], refs[-1]
    windows = blocks[0].shape[0]
    for j, block in enumerate(blocks):

        def widen(w, carry, j=j, block=block):
            raw = block[w].astype(F32)
            real, imag = raw[:, :TILES], raw[:, TILES:]
            both = real + imag
            for group in range(own.shape[0]):
                at = slice(group * GROUP, (group + 1) * GROUP)
                own[group, 0, j * windows + w] = both[at]
                own[group, 1, j * windows + w] = real[at]
                own[group, 2, j * windows + w] = imag[at]
            return carry

        lax.fori_loop(0, windows, widen, 0)


def widen_own(blocks):
    windows, stations = blocks[0].shape[:2]
    vmem = pl.BlockSpec(memory_space=pltpu.VMEM)
    return pl.pallas_call(
        widen_kernel,
        out_shape=jax.ShapeDtypeStruct(
            (stations // GROUP, 3, len(blocks) * windows, GROUP, TILES, LANES), F32
        ),
        in_specs=[vmem] * len(blocks),
        out_specs=vmem,
        compiler_params=pltpu.CompilerParams(vmem_limit_bytes=16 * 2**20),
        cost_estimate=expected(0.05),
        name="widen",
    )(*blocks)


def widen_others(first_slot, slots, count, places, plan, candidates, other):
    steps, ranks = partner_steps(plan, count)
    for slot in range(slots):
        step = jnp.int32(0)
        for number in range(ROUNDS):
            step = jnp.where(ranks[number] == first_slot + slot, steps[number], step)
        for (offset, first), candidate in zip(places, candidates):

            @pl.when(step == offset)
            def _(candidate=candidate, slot=slot, first=first):
                def widen_other(w, carry):
                    raw = candidate[w].astype(F32)
                    real, imag = raw[:, :TILES], raw[:, TILES:]
                    other[0, slot, first + w] = real
                    other[1, slot, first + w] = real + imag
                    other[2, slot, first + w] = imag - real
                    return carry

                lax.fori_loop(0, candidate.shape[0], widen_other, 0)


def sum_windows(owns, other, summed):
    groups, _, windows, group = owns[0].shape[:4]
    slots, _, quarter = other.shape[1:4]
    width = groups * group * quarter
    shift = groups.bit_length() - 1

    for slot in range(slots):

        def body(index, carry, slot=slot):
            kind, part = index >> shift, index & (groups - 1)
            mine = [own.at[part, kind] for own in owns]
            theirs = other.at[kind, slot]
            totals = [None] * (group * quarter)
            for half, own in enumerate(mine):
                for w in range(windows):
                    left = [own[w, s] for s in range(group)]
                    right = [theirs[half * windows + w, t] for t in range(quarter)]
                    for s in range(group):
                        for t in range(quarter):
                            term = left[s] * right[t]
                            old = totals[s * quarter + t]
                            totals[s * quarter + t] = term if old is None else old + term
            rows = summed.at[kind]
            base = (slot * width + part * (group * quarter)) * TILES
            for place in range(group * quarter):
                at = pl.multiple_of(base + place * TILES, TILES)
                rows[pl.ds(at, TILES), :] = totals[place]
            return carry

        lax.fori_loop(0, 3 * groups, body, 0)


def cross_kernel(first_slot, slots, count, scaling, places, parts, plan, table, *rest):
    owns, rest = rest[:2], rest[2:]
    others, rest = rest[: len(places)], rest[len(places) :]
    outs = rest[:parts]
    other, summed, operand, result = rest[parts:]
    stations = owns[0].shape[0] * owns[0].shape[3]
    widen_others(first_slot, slots, count, places, plan, others, other)
    sum_windows(owns, other, summed)
    width = stations * other.shape[3]
    columns = slots * width
    even = even_lanes((columns, LANES))
    sign_real = lane_cycle([1.0, -1.0, -1.0, 1.0])
    sign_imag = lane_cycle([1.0, 1.0, -1.0, -1.0])
    cosine, sine = eighth_turn()
    lane = lax.broadcasted_iota(jnp.int32, (1, LANES), 1)
    first_weight = jnp.where(lane == 0, 0.5, 1.0).astype(F32)
    for j in range(TILES):
        at = slice(j * LANES, (j + 1) * LANES)
        at_imag = slice(NBIN + j * LANES, NBIN + (j + 1) * LANES)
        kinds = [summed[kind, pl.ds(j, columns, stride=TILES), :] for kind in range(3)]
        real, imag = kinds[0] + kinds[2], kinds[0] - kinds[1]
        if j == 0:
            real, imag = real * first_weight, imag * first_weight
        turned = [(real, imag), (real * cosine - imag * sine, imag * cosine + real * sine)]
        turned += [quarter_turns(r, i, even, sign_real, sign_imag) for r, i in turned]
        for q in range(CHUNKS):
            rows = slice(q * columns, (q + 1) * columns)
            operand[rows, at] = turned[q][0].astype(BF)
            operand[rows, at_imag] = turned[q][1].astype(BF)
    block = lax.dot_general(
        table[...], operand[...], (((1,), (1,)), ((), ())), preferred_element_type=F32
    )
    block = block * (2.0 * scaling)
    if slots == 1:
        half = table.shape[0] // 2
        low_lanes = lax.broadcasted_iota(jnp.int32, (half, LANES), 1) < width
        for p in range(CHUNKS // 2):
            at = slice(p * LANES, (p + 1) * LANES)
            low, high = block[:half, at], block[half:, at]
            pair = (
                jnp.where(low_lanes, low, pltpu.roll(high, width, 1)),
                jnp.where(low_lanes, pltpu.roll(low, width, 1), high),
            )
            for second in range(2):
                result[2 * p + second] = pair[second].astype(BF)
    else:
        for q in range(CHUNKS):
            result[q] = block[:, q * columns : (q + 1) * columns].astype(BF)
    me = lax.axis_index("seg")
    for j in range(parts):
        outs[j][...] = result[me ^ j]


def cross_lags(plan, table, owns, places, candidates, first_slot, slots, count, parts, scaling):
    windows, stations = owns[0].shape[2], owns[0].shape[0] * owns[0].shape[3]
    quarter = candidates[0].shape[1]
    columns = slots * stations * quarter
    share = LAGS // parts
    out = (share, columns) if slots > 1 else (share // 2, 2 * columns)
    smem = pl.BlockSpec(memory_space=pltpu.SMEM)
    vmem = pl.BlockSpec(memory_space=pltpu.VMEM)
    operands = [table, *owns, *candidates]
    return pl.pallas_call(
        functools.partial(
            cross_kernel, first_slot, slots, count, scaling, tuple(places), parts
        ),
        out_shape=[jax.ShapeDtypeStruct(out, BF)] * parts,
        in_specs=[smem] + [vmem] * len(operands),
        out_specs=[vmem] * parts,
        scratch_shapes=[
            pltpu.VMEM((3, slots, 2 * windows, quarter, TILES, LANES), F32),
            pltpu.VMEM((3, columns * TILES, LANES), F32),
            pltpu.VMEM((CHUNKS * columns, 2 * NBIN), BF),
            pltpu.VMEM((parts,) + out, BF),
        ],
        compiler_params=pltpu.CompilerParams(vmem_limit_bytes=24 * 2**20),
        cost_estimate=expected(0.6 + 2.0 * slots),
        name="cross",
    )(plan, *operands)


def slot_rounds(plan, count):
    _, ranks = partner_steps(plan, count)
    rounds = []
    for slot in range(ROUNDS):
        number = jnp.int32(0)
        for other in range(1, ROUNDS):
            number = jnp.where(ranks[other] == slot, other, number)
        rounds.append(number)
    return rounds


def placed_block(pieces, matrix, at, half):
    joined = jnp.concatenate([piece[at, :] for piece in pieces], axis=1)
    if pieces[0].shape[0] > half:
        later = slice(half + at.start, half + at.stop)
        high = jnp.concatenate([piece[later, :] for piece in pieces], axis=1)
        joined = jnp.concatenate([joined, high], axis=0)
    return jnp.dot(joined, matrix, preferred_element_type=F32)


def joined_matrix(place, parts):
    me = lax.axis_index("seg")
    return jnp.concatenate([place[me ^ j] for j in range(parts)], axis=0)


def store_rows(rows, block, first):
    tiles = block.shape[1] // LANES
    for tile in range(tiles):
        at = pl.ds(first * tiles + tile, block.shape[0], stride=tiles)
        rows[at, :] = block[:, tile * LANES : (tile + 1) * LANES]


def early_kernel(count, parts, groups, half, plan, place, *rest):
    pieces = rest[:-3]
    out_hbm, rows, sems = rest[-3:]
    pairs = place.shape[2] // 2
    rounds = slot_rounds(plan, count)
    matrix = joined_matrix(place, parts)
    at = slice(0, half)
    copies = []
    for index, (first_slot, slots) in enumerate(groups):
        block = placed_block(pieces[index * parts : (index + 1) * parts], matrix, at, half)
        for slot in range(slots):
            if slots == 1:
                low, high = block[:, :pairs], block[:, pairs:]
            else:
                columns = slice(slot * pairs, (slot + 1) * pairs)
                low, high = block[:half, columns], block[half:, columns]
            number = first_slot + slot
            store_rows(rows.at[number], low, 0)
            store_rows(rows.at[number], high, half)
            copy = pltpu.make_async_copy(
                rows.at[number], out_hbm.at[:, rounds[number], 0], sems.at[number]
            )
            copy.start()
            copies.append(copy)
    for copy in copies:
        copy.wait()


def late_kernel(count, parts, half, plan, place, early, *rest):
    pieces = rest[:parts]
    out_hbm, rows, sems = rest[parts:]
    pairs = place.shape[2] // 2
    number = slot_rounds(plan, count)[ROUNDS - 1]
    matrix = joined_matrix(place, parts)
    copies = []
    for h in range(2):
        block = placed_block(
            pieces, matrix[:, h * pairs : (h + 1) * pairs], slice(0, half), half
        )
        store_rows(rows, block, h * half)
        size = rows.shape[0] // 2
        at = pl.ds(h * size, size)
        copy = pltpu.make_async_copy(rows.at[at], out_hbm.at[at, number, 0], sems.at[h])
        copy.start()
        copies.append(copy)
    for copy in copies:
        copy.wait()


def place_lags(plan, groups, pieces, count, stations, parts):
    pairs = stations * stations
    share = LAGS // parts
    half = share // 2
    tiles = pairs // LANES
    place = jnp.asarray(make_placing(stations, stations // parts, parts))
    smem = pl.BlockSpec(memory_space=pltpu.SMEM)
    vmem = pl.BlockSpec(memory_space=pltpu.VMEM)
    anywhere = pl.BlockSpec(memory_space=pl.ANY)
    shape = jax.ShapeDtypeStruct((share * tiles, ROUNDS, 1, LANES), F32)
    early = pl.pallas_call(
        functools.partial(early_kernel, count, parts, tuple(groups[:-1]), half),
        out_shape=shape,
        in_specs=[smem] + [vmem] * (1 + len(pieces) - parts),
        out_specs=anywhere,
        scratch_shapes=[
            pltpu.VMEM((ROUNDS - 1, share * tiles, LANES), F32),
            pltpu.SemaphoreType.DMA((ROUNDS - 1,)),
        ],
        compiler_params=pltpu.CompilerParams(vmem_limit_bytes=16 * 2**20),
        cost_estimate=expected(0.05),
        name="early",
    )(plan, place, *pieces[:-parts])
    out = pl.pallas_call(
        functools.partial(late_kernel, count, parts, half),
        out_shape=shape,
        in_specs=[smem, vmem, anywhere] + [vmem] * parts,
        out_specs=anywhere,
        scratch_shapes=[pltpu.VMEM((share * tiles, LANES), F32), pltpu.SemaphoreType.DMA((2,))],
        input_output_aliases={2: 0},
        compiler_params=pltpu.CompilerParams(vmem_limit_bytes=16 * 2**20),
        cost_estimate=expected(0.05),
        name="late",
    )(plan, place, early, *pieces[-parts:])
    out = out.reshape(share, tiles, ROUNDS, LANES)
    return out.transpose(0, 2, 1, 3).reshape(share, ROUNDS, pairs)


def join_kernel(order, *refs):
    parts, (out_up, out_down) = refs[:4], refs[4:]
    near_up, near_down, far_up, far_down = [parts[order.index(k)] for k in range(4)]
    half = near_up.shape[0]
    for out, first, second in ((out_up, near_up, far_up), (out_down, near_down, far_down)):
        out[:half] = first[...]
        out[half:] = second[...]


def join(near_up, near_down, far_up, far_down, order=(0, 1, 2, 3)):
    values = [near_up, near_down, far_up, far_down]
    vmem = pl.BlockSpec(memory_space=pltpu.VMEM)
    shape = (2 * near_up.shape[0],) + near_up.shape[1:]
    return pl.pallas_call(
        functools.partial(join_kernel, tuple(order)),
        out_shape=[jax.ShapeDtypeStruct(shape, BF)] * 2,
        in_specs=[vmem] * 4,
        out_specs=[vmem] * 2,
        compiler_params=pltpu.CompilerParams(vmem_limit_bytes=16 * 2**20),
        cost_estimate=expected(0.05),
        name="join",
    )(*[values[k] for k in order])


def swap(value, j):
    parts = lax.axis_size("seg")
    return lax.ppermute(value, "seg", [(i, i ^ j) for i in range(parts)])


def exchange(pieces):
    return [pieces[0]] + [swap(pieces[j], j) for j in range(1, len(pieces))]


def after(value, others):
    return lax.optimization_barrier((value, others))[0]


def per_device(records, plan):
    stations, windows, length = records.shape
    count = lax.axis_size("sta")
    parts = lax.axis_size("seg")
    quarter = stations // parts
    table = jnp.asarray(make_table(length // CHUNKS, 2 * length))
    scaling = 1.0 / math.sqrt(4.0 * NBIN * windows * parts)

    white, *quarters = prepare(records, table, parts)
    near = jnp.concatenate([quarters[0], swap(quarters[1], 1)])
    sibling = swap(white, 1)
    far = jnp.concatenate([swap(quarters[j], j) for j in range(2, parts)])
    far = after(far, sibling)
    far, white_far = lax.optimization_barrier((far, white))
    across = swap(white_far, 2)

    ring = sorted(range(count), key=lambda b: b // 2 if b % 2 == 0 else count - 1 - b // 2)
    upward = [(ring[i], ring[(i + 1) % count]) for i in range(count)]
    downward = [(ring[i], ring[i - 1]) for i in range(count)]

    def up(value):
        return lax.ppermute(value, "sta", upward)

    def down(value):
        return lax.ppermute(value, "sta", downward)

    far, white_far = lax.optimization_barrier((far, white))
    across = swap(white_far, 2)
    near_own = widen_own([white, sibling])
    half = near.shape[0]
    places, blocks, arrived = [], [], []

    def arrive(step, first, from_left, from_right):
        places.extend([(count - step, first), (step, first)])
        blocks.extend([from_left, from_right])

    near_up, near_down = up(near), down(near)
    far_up, far_down = up(far), down(far)
    arrive(1, 0, near_up, near_down)
    arrive(1, half, far_up, far_down)
    near_up, near_down, near_own = lax.optimization_barrier((near_up, near_down, near_own))
    near_up, near_down = up(near_up), down(near_down)
    far_up, far_down = lax.optimization_barrier((far_up, far_down))
    far_up, far_down = up(far_up), down(far_down)
    arrive(2, 0, near_up, near_down)
    arrive(2, half, far_up, far_down)
    all_up, all_down = join(near_up, near_down, far_up, far_down)
    for step in range(3, (count - 1) // 2 + 1):
        arrived.append((list(places), list(blocks)))
        all_up, all_down, across = lax.optimization_barrier((all_up, all_down, across))
        all_up, all_down = up(all_up), down(all_down)
        arrive(step, 0, all_up, all_down)
    arrived.append((list(places), list(blocks)))
    far_own = widen_own([across, swap(across, 1)])
    groups = [(0, 1), (1, 2), (3, 1)]
    if count % 2 == 0:
        places.append((count // 2, 0))
        blocks.append(up(all_up))
    arrived.append((places, blocks))
    pieces = []
    for index, (first_slot, slots) in enumerate(groups):
        if index == 2:
            near_own = after(near_own, pieces[:parts])
        if index > 0:
            near_own = after(near_own, lags)
        at, values = arrived[index - len(groups)]
        lags = cross_lags(
            plan, table, [near_own, far_own], at, values, first_slot, slots, count, parts, scaling
        )
        pieces = pieces + exchange(lags)
    return place_lags(plan, groups, pieces, count, stations, parts)


def solution(mesh):
    in_specs = (P("sta", "seg", None), P())
    out_specs = P("seg", None, "sta")
    return jax.shard_map(
        per_device, mesh=mesh, in_specs=in_specs, out_specs=out_specs, check_vma=False
    )
```

```python
import functools
import math

import jax
import jax.numpy as jnp
import ml_dtypes
import numpy as np
from jax import lax
from jax.experimental import pallas as pl
from jax.experimental.pallas import tpu as pltpu
from jax.sharding import PartitionSpec as P

NBIN = 1024
HALF = 64
ROUNDS = 4
LAGS = 2048
LANES = 128
TILES = NBIN // LANES
CHUNKS = 4
GROUP = 4
BF = jnp.bfloat16
F32 = jnp.float32


def make_table(rows, transform):
    phase = (np.arange(rows)[:, None] * np.arange(NBIN)[None, :]) % transform
    angle = phase * (2.0 * math.pi / transform)
    return np.concatenate([np.cos(angle), -np.sin(angle)], axis=1).astype(ml_dtypes.bfloat16)


def band_matrix():
    source = lax.broadcasted_iota(jnp.int32, (3 * LANES, LANES), 0) - LANES
    target = lax.broadcasted_iota(jnp.int32, (3 * LANES, LANES), 1)
    return jnp.where(jnp.abs(source - target) <= HALF, 1.0, 0.0).astype(BF)


def inverse_count(block, length):
    if 0 < block < length // LANES - 1:
        return 1.0 / (2 * HALF + 1)
    position = lax.broadcasted_iota(jnp.int32, (1, LANES), 1) + block * LANES
    counted = jnp.minimum(position, HALF) + jnp.minimum(length - 1 - position, HALF) + 1
    return 1.0 / counted.astype(F32)


def make_placing(stations, quarter, parts):
    width = stations * quarter
    place = np.zeros((parts, 2 * width, 2 * stations * stations), np.float32)
    for part in range(parts):
        for second in range(2):
            for s in range(stations):
                for t in range(quarter):
                    row = second * width + s * quarter + t
                    column = (second * stations + s) * stations + part * quarter + t
                    place[part, row, column] = 1.0
    return place.astype(ml_dtypes.bfloat16)


def lane_cycle(values):
    period = len(values)
    phase = lax.broadcasted_iota(jnp.int32, (1, LANES), 1) % period
    out = jnp.full((1, LANES), values[-1], F32)
    for index in range(period - 1):
        out = jnp.where(phase == index, values[index], out)
    return out


def even_lanes(shape):
    return lax.broadcasted_iota(jnp.int32, shape, 1) % 2 == 0


def eighth_turn():
    turns = [math.pi * k / 4.0 for k in range(8)]
    return lane_cycle([math.cos(t) for t in turns]), lane_cycle([math.sin(t) for t in turns])


def quarter_turns(real, imag, even, sign_real, sign_imag):
    return sign_real * jnp.where(even, real, imag), sign_imag * jnp.where(even, imag, real)


def banded_sum(stack, values, band):
    blocks, rows = len(values), values[0].shape[0]
    zero = jnp.zeros((rows, LANES), BF)
    for j in range(blocks):
        at = pl.ds(j * rows, rows)
        for k in range(3):
            b = j + k - 1
            block = values[b] if 0 <= b < blocks else zero
            stack[at, k * LANES : (k + 1) * LANES] = block
    total = jnp.dot(stack[: blocks * rows, :], band, preferred_element_type=F32)
    return [total[j * rows : (j + 1) * rows, :] for j in range(blocks)]


def prep_kernel(parts, windows, records_hbm, table_hbm, white, mine, *rest):
    others = rest[: parts - 1]
    records, table, stack, flat, spread, sems = rest[parts - 1 :]
    records_copy = pltpu.make_async_copy(records_hbm, records, sems.at[0])
    records_copy.start()
    copy = pltpu.make_async_copy(table_hbm, table, sems.at[1])
    copy.start()
    band_values = band_matrix()
    records_copy.wait()
    stations = white.shape[1]
    rows = stations * windows
    blocks = records.shape[0] // rows
    length = blocks * LANES
    chunk = length // CHUNKS
    signal = [
        jnp.concatenate(
            [
                records[pl.ds(j * windows + w, stations, stride=blocks * windows), :]
                for w in range(windows)
            ],
            axis=0,
        )
        for j in range(blocks)
    ]
    sums = banded_sum(stack, [jnp.abs(block).astype(BF) for block in signal], band_values)
    for j, total in enumerate(sums):
        at = slice(j * LANES, (j + 1) * LANES)
        level = total * inverse_count(j, length)
        value = (signal[j] / (level + 1e-05)).astype(BF)
        q, inside = divmod(j * LANES, chunk)
        flat[q * rows : (q + 1) * rows, inside : inside + LANES] = value
    copy.wait()
    product = jnp.dot(flat[...], table[...], preferred_element_type=F32)
    even = even_lanes((rows, LANES))
    sign_real = lane_cycle([1.0, 1.0, -1.0, -1.0])
    sign_imag = lane_cycle([1.0, -1.0, -1.0, 1.0])
    cosine, sine = eighth_turn()
    reals, imags, mags = [], [], []
    for j in range(TILES):
        at = slice(j * LANES, (j + 1) * LANES)
        at_imag = slice(NBIN + j * LANES, NBIN + (j + 1) * LANES)
        pr = [product[q * rows : (q + 1) * rows, at] for q in range(CHUNKS)]
        pi = [product[q * rows : (q + 1) * rows, at_imag] for q in range(CHUNKS)]
        turned = [
            quarter_turns(pr[q], pi[q], even, sign_real, sign_imag) for q in range(2, CHUNKS)
        ]
        first_real, first_imag = pr[0] + turned[0][0], pi[0] + turned[0][1]
        odd_real, odd_imag = pr[1] + turned[1][0], pi[1] + turned[1][1]
        real = first_real + (odd_real * cosine + odd_imag * sine)
        imag = first_imag + (odd_imag * cosine - odd_real * sine)
        reals.append(real)
        imags.append(imag)
        mags.append(jnp.sqrt(real * real + imag * imag).astype(BF))
    sums = banded_sum(stack, mags, band_values)
    for j, total in enumerate(sums):
        at = slice(j * LANES, (j + 1) * LANES)
        inverse = 1.0 / (total * inverse_count(j, NBIN) + 1e-06)
        spread[pl.ds(j, rows, stride=2 * TILES), :] = reals[j] * inverse
        spread[pl.ds(TILES + j, rows, stride=2 * TILES), :] = imags[j] * inverse
    me = lax.axis_index("seg")
    quarter = stations // parts
    white[...] = spread[...].reshape(windows, stations, 2 * TILES, LANES).astype(BF)
    for j, out in enumerate((mine, *others)):
        for w in range(windows):
            out[w] = white[w, pl.ds((me ^ j) * quarter, quarter)]


def prepare(records, table, parts):
    stations, windows, length = records.shape
    rows = stations * windows
    quarter = stations // parts
    blocks = length // LANES
    flat_records = records.reshape(stations, windows, blocks, LANES).transpose(0, 2, 1, 3)
    flat_records = flat_records.reshape(rows * blocks, LANES)
    small = jax.ShapeDtypeStruct((windows, quarter, 2 * TILES, LANES), BF)
    vmem = pl.BlockSpec(memory_space=pltpu.VMEM)
    return pl.pallas_call(
        functools.partial(prep_kernel, parts, windows),
        out_shape=[jax.ShapeDtypeStruct((windows, stations, 2 * TILES, LANES), BF)]
        + [small] * parts,
        in_specs=[pl.BlockSpec(memory_space=pltpu.HBM)] * 2,
        out_specs=[vmem] * (1 + parts),
        scratch_shapes=[
            pltpu.VMEM(flat_records.shape, F32),
            pltpu.VMEM(table.shape, BF),
            pltpu.VMEM((rows * (length // LANES), 3 * LANES), BF),
            pltpu.VMEM((CHUNKS * rows, length // CHUNKS), BF),
            pltpu.VMEM((rows * 2 * TILES, LANES), F32),
            pltpu.SemaphoreType.DMA((2,)),
        ],
        compiler_params=pltpu.CompilerParams(vmem_limit_bytes=52 * 2**20),
        cost_estimate=pl.CostEstimate(
            flops=2 * rows * length * 2 * NBIN, bytes_accessed=3 * 2**20, transcendentals=0
        ),
        name="prep",
    )(
        pltpu.with_memory_space_constraint(flat_records, pltpu.HBM),
        pltpu.with_memory_space_constraint(table, pltpu.HBM),
    )


def ring_place(block, count):
    half = block >> 1
    return jnp.where((block & 1) == 0, half, count - 1 - half)


def partner_steps(plan, count):
    me = lax.axis_index("sta")
    mine = ring_place(me, count)
    steps, keys = [], []
    for number in range(ROUNDS):
        step = ring_place(plan[number, me], count) - mine
        step = jnp.where(step < 0, step + count, step)
        steps.append(step)
        keys.append(jnp.minimum(step, count - step) * ROUNDS + number)
    ranks = []
    for number in range(ROUNDS):
        rank = jnp.int32(0)
        for other in range(ROUNDS):
            if other != number:
                rank = rank + jnp.where(keys[other] < keys[number], 1, 0)
        ranks.append(rank)
    return steps, ranks


def expected(microseconds):
    return pl.CostEstimate(
        flops=int(microseconds * 1.15e9), bytes_accessed=1024, transcendentals=0
    )


def widen_kernel(*refs):
    blocks, own = refs[:-1], refs[-1]
    windows = blocks[0].shape[0]
    for j, block in enumerate(blocks):

        def widen(w, carry, j=j, block=block):
            raw = block[w].astype(F32)
            real, imag = raw[:, :TILES], raw[:, TILES:]
            both = real + imag
            for group in range(own.shape[0]):
                at = slice(group * GROUP, (group + 1) * GROUP)
                own[group, 0, j * windows + w] = both[at]
                own[group, 1, j * windows + w] = real[at]
                own[group, 2, j * windows + w] = imag[at]
            return carry

        lax.fori_loop(0, windows, widen, 0)


def widen_own(blocks):
    windows, stations = blocks[0].shape[:2]
    vmem = pl.BlockSpec(memory_space=pltpu.VMEM)
    return pl.pallas_call(
        widen_kernel,
        out_shape=jax.ShapeDtypeStruct(
            (stations // GROUP, 3, len(blocks) * windows, GROUP, TILES, LANES), F32
        ),
        in_specs=[vmem] * len(blocks),
        out_specs=vmem,
        compiler_params=pltpu.CompilerParams(vmem_limit_bytes=16 * 2**20),
        cost_estimate=expected(0.05),
        name="widen",
    )(*blocks)


def widen_others(first_slot, slots, count, places, plan, candidates, other):
    steps, ranks = partner_steps(plan, count)
    for slot in range(slots):
        step = jnp.int32(0)
        for number in range(ROUNDS):
            step = jnp.where(ranks[number] == first_slot + slot, steps[number], step)
        for (offset, first), candidate in zip(places, candidates):

            @pl.when(step == offset)
            def _(candidate=candidate, slot=slot, first=first):
                def widen_other(w, carry):
                    raw = candidate[w].astype(F32)
                    real, imag = raw[:, :TILES], raw[:, TILES:]
                    other[0, slot, first + w] = real
                    other[1, slot, first + w] = real + imag
                    other[2, slot, first + w] = imag - real
                    return carry

                lax.fori_loop(0, candidate.shape[0], widen_other, 0)


def sum_windows(owns, other, summed):
    groups, _, windows, group = owns[0].shape[:4]
    slots, _, quarter = other.shape[1:4]
    width = groups * group * quarter
    shift = groups.bit_length() - 1

    for slot in range(slots):

        def body(index, carry, slot=slot):
            kind, part = index >> shift, index & (groups - 1)
            mine = [own.at[part, kind] for own in owns]
            theirs = other.at[kind, slot]
            totals = [None] * (group * quarter)
            for half, own in enumerate(mine):
                for w in range(windows):
                    left = [own[w, s] for s in range(group)]
                    right = [theirs[half * windows + w, t] for t in range(quarter)]
                    for s in range(group):
                        for t in range(quarter):
                            term = left[s] * right[t]
                            old = totals[s * quarter + t]
                            totals[s * quarter + t] = term if old is None else old + term
            rows = summed.at[kind]
            base = (slot * width + part * (group * quarter)) * TILES
            for place in range(group * quarter):
                at = pl.multiple_of(base + place * TILES, TILES)
                rows[pl.ds(at, TILES), :] = totals[place]
            return carry

        lax.fori_loop(0, 3 * groups, body, 0)


def cross_kernel(first_slot, slots, count, scaling, places, parts, plan, table, *rest):
    owns, rest = rest[:2], rest[2:]
    others, rest = rest[: len(places)], rest[len(places) :]
    outs = rest[:parts]
    other, summed, operand, result = rest[parts:]
    stations = owns[0].shape[0] * owns[0].shape[3]
    widen_others(first_slot, slots, count, places, plan, others, other)
    sum_windows(owns, other, summed)
    width = stations * other.shape[3]
    columns = slots * width
    even = even_lanes((columns, LANES))
    sign_real = lane_cycle([1.0, -1.0, -1.0, 1.0])
    sign_imag = lane_cycle([1.0, 1.0, -1.0, -1.0])
    cosine, sine = eighth_turn()
    lane = lax.broadcasted_iota(jnp.int32, (1, LANES), 1)
    first_weight = jnp.where(lane == 0, 0.5, 1.0).astype(F32)
    for j in range(TILES):
        at = slice(j * LANES, (j + 1) * LANES)
        at_imag = slice(NBIN + j * LANES, NBIN + (j + 1) * LANES)
        kinds = [summed[kind, pl.ds(j, columns, stride=TILES), :] for kind in range(3)]
        real, imag = kinds[0] + kinds[2], kinds[0] - kinds[1]
        if j == 0:
            real, imag = real * first_weight, imag * first_weight
        turned = [(real, imag), (real * cosine - imag * sine, imag * cosine + real * sine)]
        turned += [quarter_turns(r, i, even, sign_real, sign_imag) for r, i in turned]
        for q in range(CHUNKS):
            rows = slice(q * columns, (q + 1) * columns)
            operand[rows, at] = turned[q][0].astype(BF)
            operand[rows, at_imag] = turned[q][1].astype(BF)
    block = lax.dot_general(
        table[...], operand[...], (((1,), (1,)), ((), ())), preferred_element_type=F32
    )
    block = block * (2.0 * scaling)
    if slots == 1:
        half = table.shape[0] // 2
        low_lanes = lax.broadcasted_iota(jnp.int32, (half, LANES), 1) < width
        for p in range(CHUNKS // 2):
            at = slice(p * LANES, (p + 1) * LANES)
            low, high = block[:half, at], block[half:, at]
            pair = (
                jnp.where(low_lanes, low, pltpu.roll(high, width, 1)),
                jnp.where(low_lanes, pltpu.roll(low, width, 1), high),
            )
            for second in range(2):
                result[2 * p + second] = pair[second].astype(BF)
    else:
        for q in range(CHUNKS):
            result[q] = block[:, q * columns : (q + 1) * columns].astype(BF)
    me = lax.axis_index("seg")
    for j in range(parts):
        outs[j][...] = result[me ^ j]


def cross_lags(plan, table, owns, places, candidates, first_slot, slots, count, parts, scaling):
    windows, stations = owns[0].shape[2], owns[0].shape[0] * owns[0].shape[3]
    quarter = candidates[0].shape[1]
    columns = slots * stations * quarter
    share = LAGS // parts
    out = (share, columns) if slots > 1 else (share // 2, 2 * columns)
    smem = pl.BlockSpec(memory_space=pltpu.SMEM)
    vmem = pl.BlockSpec(memory_space=pltpu.VMEM)
    operands = [table, *owns, *candidates]
    return pl.pallas_call(
        functools.partial(
            cross_kernel, first_slot, slots, count, scaling, tuple(places), parts
        ),
        out_shape=[jax.ShapeDtypeStruct(out, BF)] * parts,
        in_specs=[smem] + [vmem] * len(operands),
        out_specs=[vmem] * parts,
        scratch_shapes=[
            pltpu.VMEM((3, slots, 2 * windows, quarter, TILES, LANES), F32),
            pltpu.VMEM((3, columns * TILES, LANES), F32),
            pltpu.VMEM((CHUNKS * columns, 2 * NBIN), BF),
            pltpu.VMEM((parts,) + out, BF),
        ],
        compiler_params=pltpu.CompilerParams(vmem_limit_bytes=24 * 2**20),
        cost_estimate=expected(0.6 + 2.0 * slots),
        name="cross",
    )(plan, *operands)


def slot_rounds(plan, count):
    _, ranks = partner_steps(plan, count)
    rounds = []
    for slot in range(ROUNDS):
        number = jnp.int32(0)
        for other in range(1, ROUNDS):
            number = jnp.where(ranks[other] == slot, other, number)
        rounds.append(number)
    return rounds


def placed_block(pieces, matrix, at, half):
    joined = jnp.concatenate([piece[at, :] for piece in pieces], axis=1)
    if pieces[0].shape[0] > half:
        later = slice(half + at.start, half + at.stop)
        high = jnp.concatenate([piece[later, :] for piece in pieces], axis=1)
        joined = jnp.concatenate([joined, high], axis=0)
    return jnp.dot(joined, matrix, preferred_element_type=F32)


def joined_matrix(place, parts):
    me = lax.axis_index("seg")
    return jnp.concatenate([place[me ^ j] for j in range(parts)], axis=0)


def store_rows(rows, block, first):
    tiles = block.shape[1] // LANES
    for tile in range(tiles):
        at = pl.ds(first * tiles + tile, block.shape[0], stride=tiles)
        rows[at, :] = block[:, tile * LANES : (tile + 1) * LANES]


def early_kernel(count, parts, groups, half, plan, place, *rest):
    pieces = rest[:-3]
    out_hbm, rows, sems = rest[-3:]
    pairs = place.shape[2] // 2
    rounds = slot_rounds(plan, count)
    matrix = joined_matrix(place, parts)
    at = slice(0, half)
    copies = []
    for index, (first_slot, slots) in enumerate(groups):
        block = placed_block(pieces[index * parts : (index + 1) * parts], matrix, at, half)
        for slot in range(slots):
            if slots == 1:
                low, high = block[:, :pairs], block[:, pairs:]
            else:
                columns = slice(slot * pairs, (slot + 1) * pairs)
                low, high = block[:half, columns], block[half:, columns]
            number = first_slot + slot
            store_rows(rows.at[number], low, 0)
            store_rows(rows.at[number], high, half)
            copy = pltpu.make_async_copy(
                rows.at[number], out_hbm.at[:, rounds[number], 0], sems.at[number]
            )
            copy.start()
            copies.append(copy)
    for copy in copies:
        copy.wait()


def late_kernel(count, parts, half, plan, place, early, *rest):
    pieces = rest[:parts]
    out_hbm, rows, sems = rest[parts:]
    pairs = place.shape[2] // 2
    number = slot_rounds(plan, count)[ROUNDS - 1]
    matrix = joined_matrix(place, parts)
    copies = []
    for h in range(2):
        block = placed_block(
            pieces, matrix[:, h * pairs : (h + 1) * pairs], slice(0, half), half
        )
        store_rows(rows, block, h * half)
        size = rows.shape[0] // 2
        at = pl.ds(h * size, size)
        copy = pltpu.make_async_copy(rows.at[at], out_hbm.at[at, number, 0], sems.at[h])
        copy.start()
        copies.append(copy)
    for copy in copies:
        copy.wait()


def place_lags(plan, groups, pieces, count, stations, parts):
    pairs = stations * stations
    share = LAGS // parts
    half = share // 2
    tiles = pairs // LANES
    place = jnp.asarray(make_placing(stations, stations // parts, parts))
    smem = pl.BlockSpec(memory_space=pltpu.SMEM)
    vmem = pl.BlockSpec(memory_space=pltpu.VMEM)
    anywhere = pl.BlockSpec(memory_space=pl.ANY)
    shape = jax.ShapeDtypeStruct((share * tiles, ROUNDS, 1, LANES), F32)
    early = pl.pallas_call(
        functools.partial(early_kernel, count, parts, tuple(groups[:-1]), half),
        out_shape=shape,
        in_specs=[smem] + [vmem] * (1 + len(pieces) - parts),
        out_specs=anywhere,
        scratch_shapes=[
            pltpu.VMEM((ROUNDS - 1, share * tiles, LANES), F32),
            pltpu.SemaphoreType.DMA((ROUNDS - 1,)),
        ],
        compiler_params=pltpu.CompilerParams(vmem_limit_bytes=16 * 2**20),
        cost_estimate=expected(0.05),
        name="early",
    )(plan, place, *pieces[:-parts])
    out = pl.pallas_call(
        functools.partial(late_kernel, count, parts, half),
        out_shape=shape,
        in_specs=[smem, vmem, anywhere] + [vmem] * parts,
        out_specs=anywhere,
        scratch_shapes=[pltpu.VMEM((share * tiles, LANES), F32), pltpu.SemaphoreType.DMA((2,))],
        input_output_aliases={2: 0},
        compiler_params=pltpu.CompilerParams(vmem_limit_bytes=16 * 2**20),
        cost_estimate=expected(0.05),
        name="late",
    )(plan, place, early, *pieces[-parts:])
    out = out.reshape(share, tiles, ROUNDS, LANES)
    return out.transpose(0, 2, 1, 3).reshape(share, ROUNDS, pairs)


def join_kernel(order, *refs):
    parts, (out_up, out_down) = refs[:4], refs[4:]
    near_up, near_down, far_up, far_down = [parts[order.index(k)] for k in range(4)]
    half = near_up.shape[0]
    for out, first, second in ((out_up, near_up, far_up), (out_down, near_down, far_down)):
        out[:half] = first[...]
        out[half:] = second[...]


def join(near_up, near_down, far_up, far_down, order=(0, 1, 2, 3)):
    values = [near_up, near_down, far_up, far_down]
    vmem = pl.BlockSpec(memory_space=pltpu.VMEM)
    shape = (2 * near_up.shape[0],) + near_up.shape[1:]
    return pl.pallas_call(
        functools.partial(join_kernel, tuple(order)),
        out_shape=[jax.ShapeDtypeStruct(shape, BF)] * 2,
        in_specs=[vmem] * 4,
        out_specs=[vmem] * 2,
        compiler_params=pltpu.CompilerParams(vmem_limit_bytes=16 * 2**20),
        cost_estimate=expected(0.05),
        name="join",
    )(*[values[k] for k in order])


def swap(value, j):
    parts = lax.axis_size("seg")
    return lax.ppermute(value, "seg", [(i, i ^ j) for i in range(parts)])


def exchange(pieces):
    return [pieces[0]] + [swap(pieces[j], j) for j in range(1, len(pieces))]


def after(value, others):
    return lax.optimization_barrier((value, others))[0]


def per_device(records, plan):
    stations, windows, length = records.shape
    count = lax.axis_size("sta")
    parts = lax.axis_size("seg")
    quarter = stations // parts
    table = jnp.asarray(make_table(length // CHUNKS, 2 * length))
    scaling = 1.0 / math.sqrt(4.0 * NBIN * windows * parts)

    white, *quarters = prepare(records, table, parts)
    near = jnp.concatenate([quarters[0], swap(quarters[1], 1)])
    sibling = swap(white, 1)
    far = jnp.concatenate([swap(quarters[j], j) for j in range(2, parts)])
    far = after(far, sibling)
    far, white_far = lax.optimization_barrier((far, white))
    across = swap(white_far, 2)

    ring = sorted(range(count), key=lambda b: b // 2 if b % 2 == 0 else count - 1 - b // 2)
    upward = [(ring[i], ring[(i + 1) % count]) for i in range(count)]
    downward = [(ring[i], ring[i - 1]) for i in range(count)]

    def up(value):
        return lax.ppermute(value, "sta", upward)

    def down(value):
        return lax.ppermute(value, "sta", downward)

    far, white_far = lax.optimization_barrier((far, white))
    across = swap(white_far, 2)
    near_own = widen_own([white, sibling])
    half = near.shape[0]
    places, blocks, arrived = [], [], []

    def arrive(step, first, from_left, from_right):
        places.extend([(count - step, first), (step, first)])
        blocks.extend([from_left, from_right])

    near_up, near_down = up(near), down(near)
    far_up, far_down = up(far), down(far)
    arrive(1, 0, near_up, near_down)
    arrive(1, half, far_up, far_down)
    near_up, near_down, near_own = lax.optimization_barrier((near_up, near_down, near_own))
    near_up, near_down = up(near_up), down(near_down)
    far_up, far_down = lax.optimization_barrier((far_up, far_down))
    far_up, far_down = up(far_up), down(far_down)
    arrive(2, 0, near_up, near_down)
    arrive(2, half, far_up, far_down)
    all_up, all_down = join(near_up, near_down, far_up, far_down)
    for step in range(3, (count - 1) // 2 + 1):
        arrived.append((list(places), list(blocks)))
        all_up, all_down, across = lax.optimization_barrier((all_up, all_down, across))
        all_up, all_down = up(all_up), down(all_down)
        arrive(step, 0, all_up, all_down)
    arrived.append((list(places), list(blocks)))
    far_own = widen_own([across, swap(across, 1)])
    groups = [(0, 1), (1, 2), (3, 1)]
    if count % 2 == 0:
        places.append((count // 2, 0))
        blocks.append(up(all_up))
    arrived.append((places, blocks))
    pieces = []
    for index, (first_slot, slots) in enumerate(groups):
        if index == 2:
            near_own = after(near_own, pieces[:parts])
        if index > 0:
            near_own = after(near_own, lags)
        at, values = arrived[index - len(groups)]
        lags = cross_lags(
            plan, table, [near_own, far_own], at, values, first_slot, slots, count, parts, scaling
        )
        pieces = pieces + exchange(lags)
    return place_lags(plan, groups, pieces, count, stations, parts)


def solution(mesh):
    in_specs = (P("sta", "seg", None), P())
    out_specs = P("seg", None, "sta")
    return jax.shard_map(
        per_device, mesh=mesh, in_specs=in_specs, out_specs=out_specs, check_vma=False
    )
```

```python
import functools
import math

import jax
import jax.numpy as jnp
import ml_dtypes
import numpy as np
from jax import lax
from jax.experimental import pallas as pl
from jax.experimental.pallas import tpu as pltpu
from jax.sharding import PartitionSpec as P

NBIN = 1024
HALF = 64
ROUNDS = 4
LAGS = 2048
LANES = 128
TILES = NBIN // LANES
CHUNKS = 4
GROUP = 4
BF = jnp.bfloat16
F32 = jnp.float32


def make_table(rows, transform):
    phase = (np.arange(rows)[:, None] * np.arange(NBIN)[None, :]) % transform
    angle = phase * (2.0 * math.pi / transform)
    return np.concatenate([np.cos(angle), -np.sin(angle)], axis=1).astype(ml_dtypes.bfloat16)


def band_matrix():
    source = lax.broadcasted_iota(jnp.int32, (3 * LANES, LANES), 0) - LANES
    target = lax.broadcasted_iota(jnp.int32, (3 * LANES, LANES), 1)
    return jnp.where(jnp.abs(source - target) <= HALF, 1.0, 0.0).astype(BF)


def inverse_count(block, length):
    if 0 < block < length // LANES - 1:
        return 1.0 / (2 * HALF + 1)
    position = lax.broadcasted_iota(jnp.int32, (1, LANES), 1) + block * LANES
    counted = jnp.minimum(position, HALF) + jnp.minimum(length - 1 - position, HALF) + 1
    return 1.0 / counted.astype(F32)


def make_placing(stations, quarter, parts):
    width = stations * quarter
    place = np.zeros((parts, 2 * width, 2 * stations * stations), np.float32)
    for part in range(parts):
        for second in range(2):
            for s in range(stations):
                for t in range(quarter):
                    row = second * width + s * quarter + t
                    column = (second * stations + s) * stations + part * quarter + t
                    place[part, row, column] = 1.0
    return place.astype(ml_dtypes.bfloat16)


def lane_cycle(values):
    period = len(values)
    phase = lax.broadcasted_iota(jnp.int32, (1, LANES), 1) % period
    out = jnp.full((1, LANES), values[-1], F32)
    for index in range(period - 1):
        out = jnp.where(phase == index, values[index], out)
    return out


def even_lanes(shape):
    return lax.broadcasted_iota(jnp.int32, shape, 1) % 2 == 0


def eighth_turn():
    turns = [math.pi * k / 4.0 for k in range(8)]
    return lane_cycle([math.cos(t) for t in turns]), lane_cycle([math.sin(t) for t in turns])


def quarter_turns(real, imag, even, sign_real, sign_imag):
    return sign_real * jnp.where(even, real, imag), sign_imag * jnp.where(even, imag, real)


def banded_sum(stack, values, band):
    blocks, rows = len(values), values[0].shape[0]
    zero = jnp.zeros((rows, LANES), BF)
    for j in range(blocks):
        at = pl.ds(j * rows, rows)
        for k in range(3):
            b = j + k - 1
            block = values[b] if 0 <= b < blocks else zero
            stack[at, k * LANES : (k + 1) * LANES] = block
    total = jnp.dot(stack[: blocks * rows, :], band, preferred_element_type=F32)
    return [total[j * rows : (j + 1) * rows, :] for j in range(blocks)]


def prep_kernel(parts, windows, records_hbm, table_hbm, white, mine, *rest):
    others = rest[: parts - 1]
    records, table, stack, flat, product, spread, sems = rest[parts - 1 :]
    records_copy = pltpu.make_async_copy(records_hbm, records, sems.at[0])
    records_copy.start()
    width = table.shape[1] // CHUNKS
    copies = []
    for q in range(CHUNKS):
        at = pl.ds(q * width, width)
        copy = pltpu.make_async_copy(table_hbm.at[:, at], table.at[:, at], sems.at[1 + q])
        copy.start()
        copies.append(copy)
    band_values = band_matrix()
    records_copy.wait()
    stations = white.shape[1]
    rows = stations * windows
    blocks = records.shape[0] // rows
    length = blocks * LANES
    chunk = length // CHUNKS
    signal = [
        jnp.concatenate(
            [
                records[pl.ds(j * windows + w, stations, stride=blocks * windows), :]
                for w in range(windows)
            ],
            axis=0,
        )
        for j in range(blocks)
    ]
    sums = banded_sum(stack, [jnp.abs(block).astype(BF) for block in signal], band_values)
    for j, total in enumerate(sums):
        at = slice(j * LANES, (j + 1) * LANES)
        level = total * inverse_count(j, length)
        value = (signal[j] / (level + 1e-05)).astype(BF)
        q, inside = divmod(j * LANES, chunk)
        flat[q * rows : (q + 1) * rows, inside : inside + LANES] = value
    for q in range(CHUNKS):
        at = slice(q * width, (q + 1) * width)
        copies[q].wait()
        product[:, at] = jnp.dot(flat[...], table[:, at], preferred_element_type=F32)
    even = even_lanes((rows, LANES))
    sign_real = lane_cycle([1.0, 1.0, -1.0, -1.0])
    sign_imag = lane_cycle([1.0, -1.0, -1.0, 1.0])
    cosine, sine = eighth_turn()
    reals, imags, mags = [], [], []
    for j in range(TILES):
        at = slice(j * LANES, (j + 1) * LANES)
        at_imag = slice(NBIN + j * LANES, NBIN + (j + 1) * LANES)
        pr = [product[q * rows : (q + 1) * rows, at] for q in range(CHUNKS)]
        pi = [product[q * rows : (q + 1) * rows, at_imag] for q in range(CHUNKS)]
        turned = [
            quarter_turns(pr[q], pi[q], even, sign_real, sign_imag) for q in range(2, CHUNKS)
        ]
        first_real, first_imag = pr[0] + turned[0][0], pi[0] + turned[0][1]
        odd_real, odd_imag = pr[1] + turned[1][0], pi[1] + turned[1][1]
        real = first_real + (odd_real * cosine + odd_imag * sine)
        imag = first_imag + (odd_imag * cosine - odd_real * sine)
        reals.append(real)
        imags.append(imag)
        mags.append(jnp.sqrt(real * real + imag * imag).astype(BF))
    sums = banded_sum(stack, mags, band_values)
    for j, total in enumerate(sums):
        at = slice(j * LANES, (j + 1) * LANES)
        inverse = 1.0 / (total * inverse_count(j, NBIN) + 1e-06)
        spread[pl.ds(j, rows, stride=2 * TILES), :] = reals[j] * inverse
        spread[pl.ds(TILES + j, rows, stride=2 * TILES), :] = imags[j] * inverse
    me = lax.axis_index("seg")
    quarter = stations // parts
    white[...] = spread[...].reshape(windows, stations, 2 * TILES, LANES).astype(BF)
    for j, out in enumerate((mine, *others)):
        for w in range(windows):
            out[w] = white[w, pl.ds((me ^ j) * quarter, quarter)]


def prepare(records, table, parts):
    stations, windows, length = records.shape
    rows = stations * windows
    quarter = stations // parts
    blocks = length // LANES
    flat_records = records.reshape(stations, windows, blocks, LANES).transpose(0, 2, 1, 3)
    flat_records = flat_records.reshape(rows * blocks, LANES)
    small = jax.ShapeDtypeStruct((windows, quarter, 2 * TILES, LANES), BF)
    vmem = pl.BlockSpec(memory_space=pltpu.VMEM)
    return pl.pallas_call(
        functools.partial(prep_kernel, parts, windows),
        out_shape=[jax.ShapeDtypeStruct((windows, stations, 2 * TILES, LANES), BF)]
        + [small] * parts,
        in_specs=[pl.BlockSpec(memory_space=pltpu.HBM)] * 2,
        out_specs=[vmem] * (1 + parts),
        scratch_shapes=[
            pltpu.VMEM(flat_records.shape, F32),
            pltpu.VMEM(table.shape, BF),
            pltpu.VMEM((rows * (length // LANES), 3 * LANES), BF),
            pltpu.VMEM((CHUNKS * rows, length // CHUNKS), BF),
            pltpu.VMEM((CHUNKS * rows, 2 * NBIN), F32),
            pltpu.VMEM((rows * 2 * TILES, LANES), F32),
            pltpu.SemaphoreType.DMA((1 + CHUNKS,)),
        ],
        compiler_params=pltpu.CompilerParams(vmem_limit_bytes=52 * 2**20),
        cost_estimate=pl.CostEstimate(
            flops=2 * rows * length * 2 * NBIN, bytes_accessed=3 * 2**20, transcendentals=0
        ),
        name="prep",
    )(
        pltpu.with_memory_space_constraint(flat_records, pltpu.HBM),
        pltpu.with_memory_space_constraint(table, pltpu.HBM),
    )


def ring_place(block, count):
    half = block >> 1
    return jnp.where((block & 1) == 0, half, count - 1 - half)


def partner_steps(plan, count):
    me = lax.axis_index("sta")
    mine = ring_place(me, count)
    steps, keys = [], []
    for number in range(ROUNDS):
        step = ring_place(plan[number, me], count) - mine
        step = jnp.where(step < 0, step + count, step)
        steps.append(step)
        keys.append(jnp.minimum(step, count - step) * ROUNDS + number)
    ranks = []
    for number in range(ROUNDS):
        rank = jnp.int32(0)
        for other in range(ROUNDS):
            if other != number:
                rank = rank + jnp.where(keys[other] < keys[number], 1, 0)
        ranks.append(rank)
    return steps, ranks


def expected(microseconds):
    return pl.CostEstimate(
        flops=int(microseconds * 1.15e9), bytes_accessed=1024, transcendentals=0
    )


def turn_kernel(*refs):
    blocks, own = refs[:-1], refs[-1]
    windows = blocks[0].shape[0]
    for j, block in enumerate(blocks):

        def turn(w, carry, j=j, block=block):
            plain = block[w]
            raw = plain.astype(F32)
            turned = jnp.concatenate([raw[:, TILES:], -raw[:, :TILES]], axis=1).astype(BF)
            for group in range(own.shape[0]):
                at = slice(group * GROUP, (group + 1) * GROUP)
                own[group, 0, j * windows + w] = plain[at]
                own[group, 1, j * windows + w] = turned[at]
            return carry

        lax.fori_loop(0, windows, turn, 0)


def turn_own(blocks):
    windows, stations = blocks[0].shape[:2]
    vmem = pl.BlockSpec(memory_space=pltpu.VMEM)
    return pl.pallas_call(
        turn_kernel,
        out_shape=jax.ShapeDtypeStruct(
            (stations // GROUP, 2, len(blocks) * windows, GROUP, 2 * TILES, LANES), BF
        ),
        in_specs=[vmem] * len(blocks),
        out_specs=vmem,
        compiler_params=pltpu.CompilerParams(vmem_limit_bytes=16 * 2**20),
        cost_estimate=expected(0.05),
        name="turn",
    )(*blocks)


def pick_others(first_slot, slots, count, places, plan, candidates, other):
    steps, ranks = partner_steps(plan, count)
    for slot in range(slots):
        step = jnp.int32(0)
        for number in range(ROUNDS):
            step = jnp.where(ranks[number] == first_slot + slot, steps[number], step)
        for (offset, first), candidate in zip(places, candidates):

            @pl.when(step == offset)
            def _(candidate=candidate, slot=slot, first=first):
                def pick(w, carry):
                    other[slot, first + w] = candidate[w]
                    return carry

                lax.fori_loop(0, candidate.shape[0], pick, 0)


def sum_windows(owns, other, crossed):
    groups, _, windows, group = owns[0].shape[:4]
    slots, _, quarter = other.shape[:3]
    width = groups * group * quarter
    size = 2 * TILES

    for slot in range(slots):

        def body(index, carry, slot=slot):
            base = (slot * width + index * (group * quarter)) * size
            for half, own in enumerate(owns):
                mine = own.at[index]
                totals = [None] * (2 * group * quarter)
                for w in range(windows):
                    left = [[mine[kind, w, s] for s in range(group)] for kind in range(2)]
                    right = [other[slot, half * windows + w, t] for t in range(quarter)]
                    for kind in range(2):
                        for s in range(group):
                            for t in range(quarter):
                                term = left[kind][s] * right[t]
                                place = (s * quarter + t) * 2 + kind
                                old = totals[place]
                                totals[place] = term if old is None else old + term
                for place in range(group * quarter):
                    sums = []
                    for kind in range(2):
                        wide = totals[2 * place + kind].astype(F32)
                        sums.append(wide[:TILES] + wide[TILES:])
                    at = pl.ds(pl.multiple_of(base + place * size, size), size)
                    value = jnp.concatenate(sums, axis=0)
                    crossed[at, :] = value if half == 0 else crossed[at, :] + value
            return carry

        lax.fori_loop(0, groups, body, 0)


def cross_kernel(first_slot, slots, count, scaling, places, parts, plan, table, *rest):
    owns, rest = rest[:2], rest[2:]
    others, rest = rest[: len(places)], rest[len(places) :]
    outs = rest[:parts]
    other, crossed, operand, result = rest[parts:]
    stations = owns[0].shape[0] * owns[0].shape[3]
    pick_others(first_slot, slots, count, places, plan, others, other)
    sum_windows(owns, other, crossed)
    width = stations * other.shape[2]
    columns = slots * width
    even = even_lanes((columns, LANES))
    sign_real = lane_cycle([1.0, -1.0, -1.0, 1.0])
    sign_imag = lane_cycle([1.0, 1.0, -1.0, -1.0])
    cosine, sine = eighth_turn()
    lane = lax.broadcasted_iota(jnp.int32, (1, LANES), 1)
    first_weight = jnp.where(lane == 0, 0.5, 1.0).astype(F32)
    for j in range(TILES):
        at = slice(j * LANES, (j + 1) * LANES)
        at_imag = slice(NBIN + j * LANES, NBIN + (j + 1) * LANES)
        real = crossed[pl.ds(j, columns, stride=2 * TILES), :]
        imag = crossed[pl.ds(TILES + j, columns, stride=2 * TILES), :]
        if j == 0:
            real, imag = real * first_weight, imag * first_weight
        turned = [(real, imag), (real * cosine - imag * sine, imag * cosine + real * sine)]
        turned += [quarter_turns(r, i, even, sign_real, sign_imag) for r, i in turned]
        for q in range(CHUNKS):
            rows = slice(q * columns, (q + 1) * columns)
            operand[rows, at] = turned[q][0].astype(BF)
            operand[rows, at_imag] = turned[q][1].astype(BF)
    block = lax.dot_general(
        table[...], operand[...], (((1,), (1,)), ((), ())), preferred_element_type=F32
    )
    block = block * (2.0 * scaling)
    if slots == 1:
        half = table.shape[0] // 2
        low_lanes = lax.broadcasted_iota(jnp.int32, (half, LANES), 1) < width
        for p in range(CHUNKS // 2):
            at = slice(p * LANES, (p + 1) * LANES)
            low, high = block[:half, at], block[half:, at]
            pair = (
                jnp.where(low_lanes, low, pltpu.roll(high, width, 1)),
                jnp.where(low_lanes, pltpu.roll(low, width, 1), high),
            )
            for second in range(2):
                result[2 * p + second] = pair[second].astype(BF)
    else:
        for q in range(CHUNKS):
            result[q] = block[:, q * columns : (q + 1) * columns].astype(BF)
    me = lax.axis_index("seg")
    for j in range(parts):
        outs[j][...] = result[me ^ j]


def cross_lags(plan, table, owns, places, candidates, first_slot, slots, count, parts, scaling):
    windows, stations = owns[0].shape[2], owns[0].shape[0] * owns[0].shape[3]
    quarter = candidates[0].shape[1]
    columns = slots * stations * quarter
    share = LAGS // parts
    out = (share, columns) if slots > 1 else (share // 2, 2 * columns)
    smem = pl.BlockSpec(memory_space=pltpu.SMEM)
    vmem = pl.BlockSpec(memory_space=pltpu.VMEM)
    operands = [table, *owns, *candidates]
    return pl.pallas_call(
        functools.partial(
            cross_kernel, first_slot, slots, count, scaling, tuple(places), parts
        ),
        out_shape=[jax.ShapeDtypeStruct(out, BF)] * parts,
        in_specs=[smem] + [vmem] * len(operands),
        out_specs=[vmem] * parts,
        scratch_shapes=[
            pltpu.VMEM((slots, 2 * windows, quarter, 2 * TILES, LANES), BF),
            pltpu.VMEM((columns * 2 * TILES, LANES), F32),
            pltpu.VMEM((CHUNKS * columns, 2 * NBIN), BF),
            pltpu.VMEM((parts,) + out, BF),
        ],
        compiler_params=pltpu.CompilerParams(vmem_limit_bytes=24 * 2**20),
        cost_estimate=expected(0.6 + 2.0 * slots),
        name="cross",
    )(plan, *operands)


def slot_rounds(plan, count):
    _, ranks = partner_steps(plan, count)
    rounds = []
    for slot in range(ROUNDS):
        number = jnp.int32(0)
        for other in range(1, ROUNDS):
            number = jnp.where(ranks[other] == slot, other, number)
        rounds.append(number)
    return rounds


def placed_block(pieces, matrix, at, half):
    joined = jnp.concatenate([piece[at, :] for piece in pieces], axis=1)
    if pieces[0].shape[0] > half:
        later = slice(half + at.start, half + at.stop)
        high = jnp.concatenate([piece[later, :] for piece in pieces], axis=1)
        joined = jnp.concatenate([joined, high], axis=0)
    return jnp.dot(joined, matrix, preferred_element_type=F32)


def joined_matrix(place, parts):
    me = lax.axis_index("seg")
    return jnp.concatenate([place[me ^ j] for j in range(parts)], axis=0)


def store_rows(rows, block, first):
    tiles = block.shape[1] // LANES
    for tile in range(tiles):
        at = pl.ds(first * tiles + tile, block.shape[0], stride=tiles)
        rows[at, :] = block[:, tile * LANES : (tile + 1) * LANES]


def early_kernel(count, parts, groups, half, plan, place, *rest):
    pieces = rest[:-3]
    out_hbm, rows, sems = rest[-3:]
    pairs = place.shape[2] // 2
    rounds = slot_rounds(plan, count)
    matrix = joined_matrix(place, parts)
    at = slice(0, half)
    copies = []
    for index, (first_slot, slots) in enumerate(groups):
        block = placed_block(pieces[index * parts : (index + 1) * parts], matrix, at, half)
        for slot in range(slots):
            if slots == 1:
                low, high = block[:, :pairs], block[:, pairs:]
            else:
                columns = slice(slot * pairs, (slot + 1) * pairs)
                low, high = block[:half, columns], block[half:, columns]
            number = first_slot + slot
            store_rows(rows.at[number], low, 0)
            store_rows(rows.at[number], high, half)
            copy = pltpu.make_async_copy(
                rows.at[number], out_hbm.at[:, rounds[number], 0], sems.at[number]
            )
            copy.start()
            copies.append(copy)
    for copy in copies:
        copy.wait()


def late_kernel(count, parts, half, plan, place, early, *rest):
    pieces = rest[:parts]
    out_hbm, rows, sems = rest[parts:]
    pairs = place.shape[2] // 2
    number = slot_rounds(plan, count)[ROUNDS - 1]
    matrix = joined_matrix(place, parts)
    copies = []
    for h in range(2):
        block = placed_block(
            pieces, matrix[:, h * pairs : (h + 1) * pairs], slice(0, half), half
        )
        store_rows(rows, block, h * half)
        size = rows.shape[0] // 2
        at = pl.ds(h * size, size)
        copy = pltpu.make_async_copy(rows.at[at], out_hbm.at[at, number, 0], sems.at[h])
        copy.start()
        copies.append(copy)
    for copy in copies:
        copy.wait()


def place_lags(plan, groups, pieces, count, stations, parts):
    pairs = stations * stations
    share = LAGS // parts
    half = share // 2
    tiles = pairs // LANES
    place = jnp.asarray(make_placing(stations, stations // parts, parts))
    smem = pl.BlockSpec(memory_space=pltpu.SMEM)
    vmem = pl.BlockSpec(memory_space=pltpu.VMEM)
    anywhere = pl.BlockSpec(memory_space=pl.ANY)
    shape = jax.ShapeDtypeStruct((share * tiles, ROUNDS, 1, LANES), F32)
    early = pl.pallas_call(
        functools.partial(early_kernel, count, parts, tuple(groups[:-1]), half),
        out_shape=shape,
        in_specs=[smem] + [vmem] * (1 + len(pieces) - parts),
        out_specs=anywhere,
        scratch_shapes=[
            pltpu.VMEM((ROUNDS - 1, share * tiles, LANES), F32),
            pltpu.SemaphoreType.DMA((ROUNDS - 1,)),
        ],
        compiler_params=pltpu.CompilerParams(vmem_limit_bytes=16 * 2**20),
        cost_estimate=expected(0.05),
        name="early",
    )(plan, place, *pieces[:-parts])
    out = pl.pallas_call(
        functools.partial(late_kernel, count, parts, half),
        out_shape=shape,
        in_specs=[smem, vmem, anywhere] + [vmem] * parts,
        out_specs=anywhere,
        scratch_shapes=[pltpu.VMEM((share * tiles, LANES), F32), pltpu.SemaphoreType.DMA((2,))],
        input_output_aliases={2: 0},
        compiler_params=pltpu.CompilerParams(vmem_limit_bytes=16 * 2**20),
        cost_estimate=expected(0.05),
        name="late",
    )(plan, place, early, *pieces[-parts:])
    out = out.reshape(share, tiles, ROUNDS, LANES)
    return out.transpose(0, 2, 1, 3).reshape(share, ROUNDS, pairs)


def join_kernel(order, *refs):
    parts, (out_up, out_down) = refs[:4], refs[4:]
    near_up, near_down, far_up, far_down = [parts[order.index(k)] for k in range(4)]
    half = near_up.shape[0]
    for out, first, second in ((out_up, near_up, far_up), (out_down, near_down, far_down)):
        out[:half] = first[...]
        out[half:] = second[...]


def join(near_up, near_down, far_up, far_down, order=(0, 1, 2, 3)):
    values = [near_up, near_down, far_up, far_down]
    vmem = pl.BlockSpec(memory_space=pltpu.VMEM)
    shape = (2 * near_up.shape[0],) + near_up.shape[1:]
    return pl.pallas_call(
        functools.partial(join_kernel, tuple(order)),
        out_shape=[jax.ShapeDtypeStruct(shape, BF)] * 2,
        in_specs=[vmem] * 4,
        out_specs=[vmem] * 2,
        compiler_params=pltpu.CompilerParams(vmem_limit_bytes=16 * 2**20),
        cost_estimate=expected(0.05),
        name="join",
    )(*[values[k] for k in order])


def swap(value, j):
    parts = lax.axis_size("seg")
    return lax.ppermute(value, "seg", [(i, i ^ j) for i in range(parts)])


def exchange(pieces):
    return [pieces[0]] + [swap(pieces[j], j) for j in range(1, len(pieces))]


def after(value, others):
    return lax.optimization_barrier((value, others))[0]


def per_device(records, plan):
    stations, windows, length = records.shape
    count = lax.axis_size("sta")
    parts = lax.axis_size("seg")
    quarter = stations // parts
    table = jnp.asarray(make_table(length // CHUNKS, 2 * length))
    scaling = 1.0 / math.sqrt(4.0 * NBIN * windows * parts)

    white, *quarters = prepare(records, table, parts)
    near = jnp.concatenate([quarters[0], swap(quarters[1], 1)])
    sibling = swap(white, 1)
    far = jnp.concatenate([swap(quarters[j], j) for j in range(2, parts)])
    far = after(far, sibling)
    far, white_far = lax.optimization_barrier((far, white))
    across = swap(white_far, 2)

    ring = sorted(range(count), key=lambda b: b // 2 if b % 2 == 0 else count - 1 - b // 2)
    upward = [(ring[i], ring[(i + 1) % count]) for i in range(count)]
    downward = [(ring[i], ring[i - 1]) for i in range(count)]

    def up(value):
        return lax.ppermute(value, "sta", upward)

    def down(value):
        return lax.ppermute(value, "sta", downward)

    far, white_far = lax.optimization_barrier((far, white))
    across = swap(white_far, 2)
    near_own = turn_own([white, sibling])
    half = near.shape[0]
    places, blocks, arrived = [], [], []

    def arrive(step, first, from_left, from_right):
        places.extend([(count - step, first), (step, first)])
        blocks.extend([from_left, from_right])

    near_up, near_down = up(near), down(near)
    far_up, far_down = up(far), down(far)
    arrive(1, 0, near_up, near_down)
    arrive(1, half, far_up, far_down)
    near_up, near_down, near_own = lax.optimization_barrier((near_up, near_down, near_own))
    near_up, near_down = up(near_up), down(near_down)
    far_up, far_down = lax.optimization_barrier((far_up, far_down))
    far_up, far_down = up(far_up), down(far_down)
    arrive(2, 0, near_up, near_down)
    arrive(2, half, far_up, far_down)
    all_up, all_down = join(near_up, near_down, far_up, far_down)
    for step in range(3, (count - 1) // 2 + 1):
        arrived.append((list(places), list(blocks)))
        all_up, all_down, across = lax.optimization_barrier((all_up, all_down, across))
        all_up, all_down = up(all_up), down(all_down)
        arrive(step, 0, all_up, all_down)
    arrived.append((list(places), list(blocks)))
    far_own = turn_own([across, swap(across, 1)])
    groups = [(0, 1), (1, 2), (3, 1)]
    if count % 2 == 0:
        places.append((count // 2, 0))
        blocks.append(up(all_up))
    arrived.append((places, blocks))
    pieces = []
    for index, (first_slot, slots) in enumerate(groups):
        if index == 2:
            near_own = after(near_own, pieces[:parts])
        if index > 0:
            near_own = after(near_own, lags)
        at, values = arrived[index - len(groups)]
        lags = cross_lags(
            plan, table, [near_own, far_own], at, values, first_slot, slots, count, parts, scaling
        )
        pieces = pieces + exchange(lags)
    return place_lags(plan, groups, pieces, count, stations, parts)


def solution(mesh):
    in_specs = (P("sta", "seg", None), P())
    out_specs = P("seg", None, "sta")
    return jax.shard_map(
        per_device, mesh=mesh, in_specs=in_specs, out_specs=out_specs, check_vma=False
    )
```

```python
import functools
import math

import jax
import jax.numpy as jnp
import ml_dtypes
import numpy as np
from jax import lax
from jax.experimental import pallas as pl
from jax.experimental.pallas import tpu as pltpu
from jax.sharding import PartitionSpec as P

NBIN = 1024
HALF = 64
ROUNDS = 4
LAGS = 2048
LANES = 128
TILES = NBIN // LANES
CHUNKS = 4
GROUP = 4
BF = jnp.bfloat16
F32 = jnp.float32


def make_table(rows, transform):
    phase = (np.arange(rows)[:, None] * np.arange(NBIN)[None, :]) % transform
    angle = phase * (2.0 * math.pi / transform)
    return np.concatenate([np.cos(angle), -np.sin(angle)], axis=1).astype(ml_dtypes.bfloat16)


def band_matrix():
    source = lax.broadcasted_iota(jnp.int32, (3 * LANES, LANES), 0) - LANES
    target = lax.broadcasted_iota(jnp.int32, (3 * LANES, LANES), 1)
    return jnp.where(jnp.abs(source - target) <= HALF, 1.0, 0.0).astype(BF)


def inverse_count(block, length):
    if 0 < block < length // LANES - 1:
        return 1.0 / (2 * HALF + 1)
    position = lax.broadcasted_iota(jnp.int32, (1, LANES), 1) + block * LANES
    counted = jnp.minimum(position, HALF) + jnp.minimum(length - 1 - position, HALF) + 1
    return 1.0 / counted.astype(F32)


def make_placing(stations, quarter, parts):
    width = stations * quarter
    place = np.zeros((parts, 2 * width, 2 * stations * stations), np.float32)
    for part in range(parts):
        for second in range(2):
            for s in range(stations):
                for t in range(quarter):
                    row = second * width + s * quarter + t
                    column = (second * stations + s) * stations + part * quarter + t
                    place[part, row, column] = 1.0
    return place.astype(ml_dtypes.bfloat16)


def lane_cycle(values):
    period = len(values)
    phase = lax.broadcasted_iota(jnp.int32, (1, LANES), 1) % period
    out = jnp.full((1, LANES), values[-1], F32)
    for index in range(period - 1):
        out = jnp.where(phase == index, values[index], out)
    return out


def even_lanes(shape):
    return lax.broadcasted_iota(jnp.int32, shape, 1) % 2 == 0


def eighth_turn():
    turns = [math.pi * k / 4.0 for k in range(8)]
    return lane_cycle([math.cos(t) for t in turns]), lane_cycle([math.sin(t) for t in turns])


def quarter_turns(real, imag, even, sign_real, sign_imag):
    return sign_real * jnp.where(even, real, imag), sign_imag * jnp.where(even, imag, real)


def banded_sum(stack, values, band):
    blocks, rows = len(values), values[0].shape[0]
    zero = jnp.zeros((rows, LANES), BF)
    for j in range(blocks):
        at = pl.ds(j * rows, rows)
        for k in range(3):
            b = j + k - 1
            block = values[b] if 0 <= b < blocks else zero
            stack[at, k * LANES : (k + 1) * LANES] = block
    total = jnp.dot(stack[: blocks * rows, :], band, preferred_element_type=F32)
    return [total[j * rows : (j + 1) * rows, :] for j in range(blocks)]


def prep_kernel(parts, windows, records_hbm, table_hbm, white, mine, *rest):
    others = rest[: parts - 1]
    records, table, stack, flat, spread, sems = rest[parts - 1 :]
    records_copy = pltpu.make_async_copy(records_hbm, records, sems.at[0])
    records_copy.start()
    copy = pltpu.make_async_copy(table_hbm, table, sems.at[1])
    copy.start()
    band_values = band_matrix()
    records_copy.wait()
    stations = white.shape[1]
    rows = stations * windows
    blocks = records.shape[0] // rows
    length = blocks * LANES
    chunk = length // CHUNKS
    signal = [
        jnp.concatenate(
            [
                records[pl.ds(j * windows + w, stations, stride=blocks * windows), :]
                for w in range(windows)
            ],
            axis=0,
        )
        for j in range(blocks)
    ]
    sums = banded_sum(stack, [jnp.abs(block).astype(BF) for block in signal], band_values)
    for j, total in enumerate(sums):
        at = slice(j * LANES, (j + 1) * LANES)
        level = total * inverse_count(j, length)
        value = (signal[j] / (level + 1e-05)).astype(BF)
        q, inside = divmod(j * LANES, chunk)
        flat[q * rows : (q + 1) * rows, inside : inside + LANES] = value
    copy.wait()
    product = jnp.dot(flat[...], table[...], preferred_element_type=F32)
    even = even_lanes((rows, LANES))
    sign_real = lane_cycle([1.0, 1.0, -1.0, -1.0])
    sign_imag = lane_cycle([1.0, -1.0, -1.0, 1.0])
    cosine, sine = eighth_turn()
    reals, imags, mags = [], [], []
    for j in range(TILES):
        at = slice(j * LANES, (j + 1) * LANES)
        at_imag = slice(NBIN + j * LANES, NBIN + (j + 1) * LANES)
        pr = [product[q * rows : (q + 1) * rows, at] for q in range(CHUNKS)]
        pi = [product[q * rows : (q + 1) * rows, at_imag] for q in range(CHUNKS)]
        turned = [
            quarter_turns(pr[q], pi[q], even, sign_real, sign_imag) for q in range(2, CHUNKS)
        ]
        first_real, first_imag = pr[0] + turned[0][0], pi[0] + turned[0][1]
        odd_real, odd_imag = pr[1] + turned[1][0], pi[1] + turned[1][1]
        real = first_real + (odd_real * cosine + odd_imag * sine)
        imag = first_imag + (odd_imag * cosine - odd_real * sine)
        reals.append(real)
        imags.append(imag)
        mags.append(jnp.sqrt(real * real + imag * imag).astype(BF))
    sums = banded_sum(stack, mags, band_values)
    for j, total in enumerate(sums):
        at = slice(j * LANES, (j + 1) * LANES)
        inverse = 1.0 / (total * inverse_count(j, NBIN) + 1e-06)
        spread[pl.ds(j, rows, stride=2 * TILES), :] = reals[j] * inverse
        spread[pl.ds(TILES + j, rows, stride=2 * TILES), :] = imags[j] * inverse
    me = lax.axis_index("seg")
    quarter = stations // parts
    white[...] = spread[...].reshape(windows, stations, 2 * TILES, LANES).astype(BF)
    for j, out in enumerate((mine, *others)):
        for w in range(windows):
            out[w] = white[w, pl.ds((me ^ j) * quarter, quarter)]


def prepare(records, table, parts):
    stations, windows, length = records.shape
    rows = stations * windows
    quarter = stations // parts
    blocks = length // LANES
    flat_records = records.reshape(stations, windows, blocks, LANES).transpose(0, 2, 1, 3)
    flat_records = flat_records.reshape(rows * blocks, LANES)
    small = jax.ShapeDtypeStruct((windows, quarter, 2 * TILES, LANES), BF)
    vmem = pl.BlockSpec(memory_space=pltpu.VMEM)
    return pl.pallas_call(
        functools.partial(prep_kernel, parts, windows),
        out_shape=[jax.ShapeDtypeStruct((windows, stations, 2 * TILES, LANES), BF)]
        + [small] * parts,
        in_specs=[pl.BlockSpec(memory_space=pltpu.HBM)] * 2,
        out_specs=[vmem] * (1 + parts),
        scratch_shapes=[
            pltpu.VMEM(flat_records.shape, F32),
            pltpu.VMEM(table.shape, BF),
            pltpu.VMEM((rows * (length // LANES), 3 * LANES), BF),
            pltpu.VMEM((CHUNKS * rows, length // CHUNKS), BF),
            pltpu.VMEM((rows * 2 * TILES, LANES), F32),
            pltpu.SemaphoreType.DMA((2,)),
        ],
        compiler_params=pltpu.CompilerParams(vmem_limit_bytes=52 * 2**20),
        cost_estimate=pl.CostEstimate(
            flops=2 * rows * length * 2 * NBIN, bytes_accessed=3 * 2**20, transcendentals=0
        ),
        name="prep",
    )(
        pltpu.with_memory_space_constraint(flat_records, pltpu.HBM),
        pltpu.with_memory_space_constraint(table, pltpu.HBM),
    )


def ring_place(block, count):
    half = block >> 1
    return jnp.where((block & 1) == 0, half, count - 1 - half)


def partner_steps(plan, count):
    me = lax.axis_index("sta")
    mine = ring_place(me, count)
    steps, keys = [], []
    for number in range(ROUNDS):
        step = ring_place(plan[number, me], count) - mine
        step = jnp.where(step < 0, step + count, step)
        steps.append(step)
        keys.append(jnp.minimum(step, count - step) * ROUNDS + number)
    ranks = []
    for number in range(ROUNDS):
        rank = jnp.int32(0)
        for other in range(ROUNDS):
            if other != number:
                rank = rank + jnp.where(keys[other] < keys[number], 1, 0)
        ranks.append(rank)
    return steps, ranks


def expected(microseconds):
    return pl.CostEstimate(
        flops=int(microseconds * 1.15e9), bytes_accessed=1024, transcendentals=0
    )


def widen_kernel(*refs):
    blocks, own = refs[:-1], refs[-1]
    windows = blocks[0].shape[0]
    for j, block in enumerate(blocks):

        def widen(w, carry, j=j, block=block):
            raw = block[w].astype(F32)
            real, imag = raw[:, :TILES], raw[:, TILES:]
            both = real + imag
            for group in range(own.shape[0]):
                at = slice(group * GROUP, (group + 1) * GROUP)
                own[group, 0, j * windows + w] = both[at]
                own[group, 1, j * windows + w] = real[at]
                own[group, 2, j * windows + w] = imag[at]
            return carry

        lax.fori_loop(0, windows, widen, 0)


def widen_own(blocks):
    windows, stations = blocks[0].shape[:2]
    vmem = pl.BlockSpec(memory_space=pltpu.VMEM)
    return pl.pallas_call(
        widen_kernel,
        out_shape=jax.ShapeDtypeStruct(
            (stations // GROUP, 3, len(blocks) * windows, GROUP, TILES, LANES), F32
        ),
        in_specs=[vmem] * len(blocks),
        out_specs=vmem,
        compiler_params=pltpu.CompilerParams(vmem_limit_bytes=16 * 2**20),
        cost_estimate=expected(0.05),
        name="widen",
    )(*blocks)


def widen_others(first_slot, slots, count, places, plan, candidates, other):
    steps, ranks = partner_steps(plan, count)
    for slot in range(slots):
        step = jnp.int32(0)
        for number in range(ROUNDS):
            step = jnp.where(ranks[number] == first_slot + slot, steps[number], step)
        for (offset, first), candidate in zip(places, candidates):

            @pl.when(step == offset)
            def _(candidate=candidate, slot=slot, first=first):
                def widen_other(w, carry):
                    raw = candidate[w].astype(F32)
                    real, imag = raw[:, :TILES], raw[:, TILES:]
                    other[0, slot, first + w] = real
                    other[1, slot, first + w] = real + imag
                    other[2, slot, first + w] = imag - real
                    return carry

                lax.fori_loop(0, candidate.shape[0], widen_other, 0)


def sum_windows(owns, other, slot, crossed, beside=None):
    groups, _, windows, group = owns[0].shape[:4]
    quarter = other.shape[3]
    size = 2 * TILES

    def body(index, carry):
        mine = [own.at[index] for own in owns]

        def sums(kind):
            totals = [None] * (group * quarter)
            for half, own in enumerate(mine):
                for w in range(windows):
                    left = [own[kind, w, s] for s in range(group)]
                    right = [other[kind, slot, half * windows + w, t] for t in range(quarter)]
                    for s in range(group):
                        for t in range(quarter):
                            term = left[s] * right[t]
                            old = totals[s * quarter + t]
                            totals[s * quarter + t] = term if old is None else old + term
            return totals

        def store(place, part, value):
            at = pl.multiple_of(base + place * size + part * TILES, TILES)
            crossed[pl.ds(at, TILES), :] = value

        if beside is not None:
            beside(index)
        base = index * (group * quarter * size)
        shared = sums(0)
        third = sums(2)
        for place in range(group * quarter):
            store(place, 0, shared[place] + third[place])
        second = sums(1)
        for place in range(group * quarter):
            store(place, 1, shared[place] - second[place])
        return carry

    lax.fori_loop(0, groups, body, 0)


def fill_operand(crossed, operand):
    columns = operand.shape[0] // CHUNKS
    even = even_lanes((columns, LANES))
    sign_real = lane_cycle([1.0, -1.0, -1.0, 1.0])
    sign_imag = lane_cycle([1.0, 1.0, -1.0, -1.0])
    cosine, sine = eighth_turn()
    lane = lax.broadcasted_iota(jnp.int32, (1, LANES), 1)
    first_weight = jnp.where(lane == 0, 0.5, 1.0).astype(F32)
    for j in range(TILES):
        at = slice(j * LANES, (j + 1) * LANES)
        at_imag = slice(NBIN + j * LANES, NBIN + (j + 1) * LANES)
        real = crossed[pl.ds(j, columns, stride=2 * TILES), :]
        imag = crossed[pl.ds(TILES + j, columns, stride=2 * TILES), :]
        if j == 0:
            real, imag = real * first_weight, imag * first_weight
        turned = [(real, imag), (real * cosine - imag * sine, imag * cosine + real * sine)]
        turned += [quarter_turns(r, i, even, sign_real, sign_imag) for r, i in turned]
        for q in range(CHUNKS):
            rows = slice(q * columns, (q + 1) * columns)
            operand[rows, at] = turned[q][0].astype(BF)
            operand[rows, at_imag] = turned[q][1].astype(BF)


def cross_kernel(first_slot, slots, count, scaling, places, parts, plan, table, *rest):
    owns, rest = rest[:2], rest[2:]
    others, rest = rest[: len(places)], rest[len(places) :]
    outs = rest[:parts]
    other, crossed, operand, result, *stash = rest[parts:]
    groups = owns[0].shape[0]
    widen_others(first_slot, slots, count, places, plan, others, other)
    width = operand.shape[0] // CHUNKS
    share = table.shape[0]

    def lags(first, size):
        block = lax.dot_general(
            table[pl.ds(first, size), :],
            operand[...],
            (((1,), (1,)), ((), ())),
            preferred_element_type=F32,
        )
        return block * (2.0 * scaling)

    sum_windows(owns, other, 0, crossed)
    fill_operand(crossed, operand)
    if slots == 2:
        size = share // groups

        def beside(index):
            first = pl.multiple_of(index * size, size)
            stash[0][pl.ds(first, size), :] = lags(first, size)

        sum_windows(owns, other, 1, crossed, beside)
        fill_operand(crossed, operand)
    block = lags(0, share)
    if slots == 2:
        low_block, high_block = stash[0][...], block
    else:
        low_block, high_block = block[: share // 2], block[share // 2 :]
    low_lanes = lax.broadcasted_iota(jnp.int32, (low_block.shape[0], LANES), 1) < width
    for p in range(CHUNKS // 2):
        at = slice(p * LANES, (p + 1) * LANES)
        low, high = low_block[:, at], high_block[:, at]
        result[2 * p] = jnp.where(low_lanes, low, pltpu.roll(high, width, 1)).astype(BF)
        result[2 * p + 1] = jnp.where(low_lanes, pltpu.roll(low, width, 1), high).astype(BF)
    me = lax.axis_index("seg")
    for j in range(parts):
        outs[j][...] = result[me ^ j]


def cross_lags(plan, table, owns, places, candidates, first_slot, slots, count, parts, scaling):
    windows, stations = owns[0].shape[2], owns[0].shape[0] * owns[0].shape[3]
    quarter = candidates[0].shape[1]
    columns = slots * stations * quarter
    share = LAGS // parts
    out = (share, columns) if slots > 1 else (share // 2, 2 * columns)
    smem = pl.BlockSpec(memory_space=pltpu.SMEM)
    vmem = pl.BlockSpec(memory_space=pltpu.VMEM)
    operands = [table, *owns, *candidates]
    return pl.pallas_call(
        functools.partial(
            cross_kernel, first_slot, slots, count, scaling, tuple(places), parts
        ),
        out_shape=[jax.ShapeDtypeStruct(out, BF)] * parts,
        in_specs=[smem] + [vmem] * len(operands),
        out_specs=[vmem] * parts,
        scratch_shapes=[
            pltpu.VMEM((3, slots, 2 * windows, quarter, TILES, LANES), F32),
            pltpu.VMEM((columns // slots * 2 * TILES, LANES), F32),
            pltpu.VMEM((CHUNKS * columns // slots, 2 * NBIN), BF),
            pltpu.VMEM((parts,) + out, BF),
        ]
        + [pltpu.VMEM((share, CHUNKS * columns // slots), F32)] * (slots - 1),
        compiler_params=pltpu.CompilerParams(vmem_limit_bytes=24 * 2**20),
        cost_estimate=expected(0.6 + 2.0 * slots),
        name="cross",
    )(plan, *operands)


def slot_rounds(plan, count):
    _, ranks = partner_steps(plan, count)
    rounds = []
    for slot in range(ROUNDS):
        number = jnp.int32(0)
        for other in range(1, ROUNDS):
            number = jnp.where(ranks[other] == slot, other, number)
        rounds.append(number)
    return rounds


def placed_block(pieces, matrix, at, half):
    joined = jnp.concatenate([piece[at, :] for piece in pieces], axis=1)
    if pieces[0].shape[0] > half:
        later = slice(half + at.start, half + at.stop)
        high = jnp.concatenate([piece[later, :] for piece in pieces], axis=1)
        joined = jnp.concatenate([joined, high], axis=0)
    return jnp.dot(joined, matrix, preferred_element_type=F32)


def joined_matrix(place, parts):
    me = lax.axis_index("seg")
    return jnp.concatenate([place[me ^ j] for j in range(parts)], axis=0)


def store_rows(rows, block, first):
    tiles = block.shape[1] // LANES
    for tile in range(tiles):
        at = pl.ds(first * tiles + tile, block.shape[0], stride=tiles)
        rows[at, :] = block[:, tile * LANES : (tile + 1) * LANES]


def early_kernel(count, parts, groups, half, plan, place, *rest):
    pieces = rest[:-3]
    out_hbm, rows, sems = rest[-3:]
    pairs = place.shape[2] // 2
    rounds = slot_rounds(plan, count)
    matrix = joined_matrix(place, parts)
    at = slice(0, half)
    copies = []
    for index, (first_slot, slots) in enumerate(groups):
        block = placed_block(pieces[index * parts : (index + 1) * parts], matrix, at, half)
        for slot in range(slots):
            if slots == 1:
                low, high = block[:, :pairs], block[:, pairs:]
            else:
                columns = slice(slot * pairs, (slot + 1) * pairs)
                low, high = block[:half, columns], block[half:, columns]
            number = first_slot + slot
            store_rows(rows.at[number], low, 0)
            store_rows(rows.at[number], high, half)
            copy = pltpu.make_async_copy(
                rows.at[number], out_hbm.at[:, rounds[number], 0], sems.at[number]
            )
            copy.start()
            copies.append(copy)
    for copy in copies:
        copy.wait()


def late_kernel(count, parts, half, plan, place, early, *rest):
    pieces = rest[:parts]
    out_hbm, rows, sems = rest[parts:]
    pairs = place.shape[2] // 2
    number = slot_rounds(plan, count)[ROUNDS - 1]
    matrix = joined_matrix(place, parts)
    copies = []
    for h in range(2):
        block = placed_block(
            pieces, matrix[:, h * pairs : (h + 1) * pairs], slice(0, half), half
        )
        size = rows.shape[0] // 4
        for q in range(2):
            lags = half // 2
            store_rows(rows, block[q * lags : (q + 1) * lags], h * half + q * lags)
            at = pl.ds((2 * h + q) * size, size)
            copy = pltpu.make_async_copy(
                rows.at[at], out_hbm.at[at, number, 0], sems.at[2 * h + q]
            )
            copy.start()
            copies.append(copy)
    for copy in copies:
        copy.wait()


def place_lags(plan, groups, pieces, count, stations, parts):
    pairs = stations * stations
    share = LAGS // parts
    half = share // 2
    tiles = pairs // LANES
    place = jnp.asarray(make_placing(stations, stations // parts, parts))
    smem = pl.BlockSpec(memory_space=pltpu.SMEM)
    vmem = pl.BlockSpec(memory_space=pltpu.VMEM)
    anywhere = pl.BlockSpec(memory_space=pl.ANY)
    shape = jax.ShapeDtypeStruct((share * tiles, ROUNDS, 1, LANES), F32)
    early = pl.pallas_call(
        functools.partial(early_kernel, count, parts, tuple(groups[:-1]), half),
        out_shape=shape,
        in_specs=[smem] + [vmem] * (1 + len(pieces) - parts),
        out_specs=anywhere,
        scratch_shapes=[
            pltpu.VMEM((ROUNDS - 1, share * tiles, LANES), F32),
            pltpu.SemaphoreType.DMA((ROUNDS - 1,)),
        ],
        compiler_params=pltpu.CompilerParams(vmem_limit_bytes=16 * 2**20),
        cost_estimate=expected(0.05),
        name="early",
    )(plan, place, *pieces[:-parts])
    out = pl.pallas_call(
        functools.partial(late_kernel, count, parts, half),
        out_shape=shape,
        in_specs=[smem, vmem, anywhere] + [vmem] * parts,
        out_specs=anywhere,
        scratch_shapes=[pltpu.VMEM((share * tiles, LANES), F32), pltpu.SemaphoreType.DMA((4,))],
        input_output_aliases={2: 0},
        compiler_params=pltpu.CompilerParams(vmem_limit_bytes=16 * 2**20),
        cost_estimate=expected(0.05),
        name="late",
    )(plan, place, early, *pieces[-parts:])
    out = out.reshape(share, tiles, ROUNDS, LANES)
    return out.transpose(0, 2, 1, 3).reshape(share, ROUNDS, pairs)


def join_kernel(order, *refs):
    parts, (out_up, out_down) = refs[:4], refs[4:]
    near_up, near_down, far_up, far_down = [parts[order.index(k)] for k in range(4)]
    half = near_up.shape[0]
    for out, first, second in ((out_up, near_up, far_up), (out_down, near_down, far_down)):
        out[:half] = first[...]
        out[half:] = second[...]


def join(near_up, near_down, far_up, far_down, order=(0, 1, 2, 3)):
    values = [near_up, near_down, far_up, far_down]
    vmem = pl.BlockSpec(memory_space=pltpu.VMEM)
    shape = (2 * near_up.shape[0],) + near_up.shape[1:]
    return pl.pallas_call(
        functools.partial(join_kernel, tuple(order)),
        out_shape=[jax.ShapeDtypeStruct(shape, BF)] * 2,
        in_specs=[vmem] * 4,
        out_specs=[vmem] * 2,
        compiler_params=pltpu.CompilerParams(vmem_limit_bytes=16 * 2**20),
        cost_estimate=expected(0.05),
        name="join",
    )(*[values[k] for k in order])


def swap(value, j):
    parts = lax.axis_size("seg")
    return lax.ppermute(value, "seg", [(i, i ^ j) for i in range(parts)])


def exchange(pieces):
    return [pieces[0]] + [swap(pieces[j], j) for j in range(1, len(pieces))]


def after(value, others):
    return lax.optimization_barrier((value, others))[0]


def per_device(records, plan):
    stations, windows, length = records.shape
    count = lax.axis_size("sta")
    parts = lax.axis_size("seg")
    quarter = stations // parts
    table = jnp.asarray(make_table(length // CHUNKS, 2 * length))
    scaling = 1.0 / math.sqrt(4.0 * NBIN * windows * parts)

    white, *quarters = prepare(records, table, parts)
    near = jnp.concatenate([quarters[0], swap(quarters[1], 1)])
    sibling = swap(white, 1)
    far = jnp.concatenate([swap(quarters[j], j) for j in range(2, parts)])
    far = after(far, sibling)
    far, white_far = lax.optimization_barrier((far, white))
    across = swap(white_far, 2)

    ring = sorted(range(count), key=lambda b: b // 2 if b % 2 == 0 else count - 1 - b // 2)
    upward = [(ring[i], ring[(i + 1) % count]) for i in range(count)]
    downward = [(ring[i], ring[i - 1]) for i in range(count)]

    def up(value):
        return lax.ppermute(value, "sta", upward)

    def down(value):
        return lax.ppermute(value, "sta", downward)

    far, white_far = lax.optimization_barrier((far, white))
    across = swap(white_far, 2)
    near_own = widen_own([white, sibling])
    half = near.shape[0]
    places, blocks, arrived = [], [], []

    def arrive(step, first, from_left, from_right):
        places.extend([(count - step, first), (step, first)])
        blocks.extend([from_left, from_right])

    near_up, near_down = up(near), down(near)
    far_up, far_down = up(far), down(far)
    arrive(1, 0, near_up, near_down)
    arrive(1, half, far_up, far_down)
    near_up, near_down, near_own = lax.optimization_barrier((near_up, near_down, near_own))
    near_up, near_down = up(near_up), down(near_down)
    far_up, far_down = lax.optimization_barrier((far_up, far_down))
    far_up, far_down = up(far_up), down(far_down)
    arrive(2, 0, near_up, near_down)
    arrive(2, half, far_up, far_down)
    all_up, all_down = join(near_up, near_down, far_up, far_down)
    for step in range(3, (count - 1) // 2 + 1):
        arrived.append((list(places), list(blocks)))
        all_up, all_down, across = lax.optimization_barrier((all_up, all_down, across))
        all_up, all_down = up(all_up), down(all_down)
        arrive(step, 0, all_up, all_down)
    arrived.append((list(places), list(blocks)))
    far_own = widen_own([across, swap(across, 1)])
    groups = [(0, 1), (1, 2), (3, 1)]
    if count % 2 == 0:
        places.append((count // 2, 0))
        blocks.append(up(all_up))
    arrived.append((places, blocks))
    pieces = []
    for index, (first_slot, slots) in enumerate(groups):
        if index == 2:
            near_own = after(near_own, pieces[:parts])
        if index > 0:
            near_own = after(near_own, lags)
        at, values = arrived[index - len(groups)]
        lags = cross_lags(
            plan, table, [near_own, far_own], at, values, first_slot, slots, count, parts, scaling
        )
        pieces = pieces + exchange(lags)
    return place_lags(plan, groups, pieces, count, stations, parts)


def solution(mesh):
    in_specs = (P("sta", "seg", None), P())
    out_specs = P("seg", None, "sta")
    return jax.shard_map(
        per_device, mesh=mesh, in_specs=in_specs, out_specs=out_specs, check_vma=False
    )
```

```python
import functools
import math

import jax
import jax.numpy as jnp
import ml_dtypes
import numpy as np
from jax import lax
from jax.experimental import pallas as pl
from jax.experimental.pallas import tpu as pltpu
from jax.sharding import PartitionSpec as P

NBIN = 1024
HALF = 64
ROUNDS = 4
LAGS = 2048
LANES = 128
TILES = NBIN // LANES
CHUNKS = 4
GROUP = 4
BF = jnp.bfloat16
F32 = jnp.float32


def make_table(rows, transform):
    phase = (np.arange(rows)[:, None] * np.arange(NBIN)[None, :]) % transform
    angle = phase * (2.0 * math.pi / transform)
    return np.concatenate([np.cos(angle), -np.sin(angle)], axis=1).astype(ml_dtypes.bfloat16)


def band_matrix():
    source = lax.broadcasted_iota(jnp.int32, (3 * LANES, LANES), 0) - LANES
    target = lax.broadcasted_iota(jnp.int32, (3 * LANES, LANES), 1)
    return jnp.where(jnp.abs(source - target) <= HALF, 1.0, 0.0).astype(BF)


def inverse_count(block, length):
    if 0 < block < length // LANES - 1:
        return 1.0 / (2 * HALF + 1)
    position = lax.broadcasted_iota(jnp.int32, (1, LANES), 1) + block * LANES
    counted = jnp.minimum(position, HALF) + jnp.minimum(length - 1 - position, HALF) + 1
    return 1.0 / counted.astype(F32)


def make_placing(stations, quarter, parts):
    width = stations * quarter
    place = np.zeros((parts, 2 * width, 2 * stations * stations), np.float32)
    for part in range(parts):
        for second in range(2):
            for s in range(stations):
                for t in range(quarter):
                    row = second * width + s * quarter + t
                    column = (second * stations + s) * stations + part * quarter + t
                    place[part, row, column] = 1.0
    return place.astype(ml_dtypes.bfloat16)


def lane_cycle(values):
    period = len(values)
    phase = lax.broadcasted_iota(jnp.int32, (1, LANES), 1) % period
    out = jnp.full((1, LANES), values[-1], F32)
    for index in range(period - 1):
        out = jnp.where(phase == index, values[index], out)
    return out


def even_lanes(shape):
    return lax.broadcasted_iota(jnp.int32, shape, 1) % 2 == 0


def eighth_turn():
    turns = [math.pi * k / 4.0 for k in range(8)]
    return lane_cycle([math.cos(t) for t in turns]), lane_cycle([math.sin(t) for t in turns])


def quarter_turns(real, imag, even, sign_real, sign_imag):
    return sign_real * jnp.where(even, real, imag), sign_imag * jnp.where(even, imag, real)


def banded_sum(stack, values, band):
    blocks, rows = len(values), values[0].shape[0]
    zero = jnp.zeros((rows, LANES), BF)
    for j in range(blocks):
        at = pl.ds(j * rows, rows)
        for k in range(3):
            b = j + k - 1
            block = values[b] if 0 <= b < blocks else zero
            stack[at, k * LANES : (k + 1) * LANES] = block
    total = jnp.dot(stack[: blocks * rows, :], band, preferred_element_type=F32)
    return [total[j * rows : (j + 1) * rows, :] for j in range(blocks)]


def prep_kernel(parts, windows, records_hbm, table_hbm, white, mine, *rest):
    others = rest[: parts - 1]
    records, table, stack, flat, spread, sems = rest[parts - 1 :]
    records_copy = pltpu.make_async_copy(records_hbm, records, sems.at[0])
    records_copy.start()
    copy = pltpu.make_async_copy(table_hbm, table, sems.at[1])
    copy.start()
    band_values = band_matrix()
    records_copy.wait()
    stations = white.shape[1]
    rows = stations * windows
    blocks = records.shape[0] // rows
    length = blocks * LANES
    chunk = length // CHUNKS
    signal = [
        jnp.concatenate(
            [
                records[pl.ds(j * windows + w, stations, stride=blocks * windows), :]
                for w in range(windows)
            ],
            axis=0,
        )
        for j in range(blocks)
    ]
    sums = banded_sum(stack, [jnp.abs(block).astype(BF) for block in signal], band_values)
    for j, total in enumerate(sums):
        at = slice(j * LANES, (j + 1) * LANES)
        level = total * inverse_count(j, length)
        value = (signal[j] / (level + 1e-05)).astype(BF)
        q, inside = divmod(j * LANES, chunk)
        flat[q * rows : (q + 1) * rows, inside : inside + LANES] = value
    copy.wait()
    product = jnp.dot(flat[...], table[...], preferred_element_type=F32)
    even = even_lanes((rows, LANES))
    sign_real = lane_cycle([1.0, 1.0, -1.0, -1.0])
    sign_imag = lane_cycle([1.0, -1.0, -1.0, 1.0])
    cosine, sine = eighth_turn()
    reals, imags, mags = [], [], []
    for j in range(TILES):
        at = slice(j * LANES, (j + 1) * LANES)
        at_imag = slice(NBIN + j * LANES, NBIN + (j + 1) * LANES)
        pr = [product[q * rows : (q + 1) * rows, at] for q in range(CHUNKS)]
        pi = [product[q * rows : (q + 1) * rows, at_imag] for q in range(CHUNKS)]
        turned = [
            quarter_turns(pr[q], pi[q], even, sign_real, sign_imag) for q in range(2, CHUNKS)
        ]
        first_real, first_imag = pr[0] + turned[0][0], pi[0] + turned[0][1]
        odd_real, odd_imag = pr[1] + turned[1][0], pi[1] + turned[1][1]
        real = first_real + (odd_real * cosine + odd_imag * sine)
        imag = first_imag + (odd_imag * cosine - odd_real * sine)
        reals.append(real)
        imags.append(imag)
        mags.append(jnp.sqrt(real * real + imag * imag).astype(BF))
    sums = banded_sum(stack, mags, band_values)
    for j, total in enumerate(sums):
        at = slice(j * LANES, (j + 1) * LANES)
        inverse = 1.0 / (total * inverse_count(j, NBIN) + 1e-06)
        spread[pl.ds(j, rows, stride=2 * TILES), :] = reals[j] * inverse
        spread[pl.ds(TILES + j, rows, stride=2 * TILES), :] = imags[j] * inverse
    me = lax.axis_index("seg")
    quarter = stations // parts
    white[...] = spread[...].reshape(windows, stations, 2 * TILES, LANES).astype(BF)
    for j, out in enumerate((mine, *others)):
        for w in range(windows):
            out[w] = white[w, pl.ds((me ^ j) * quarter, quarter)]


def prepare(records, table, parts):
    stations, windows, length = records.shape
    rows = stations * windows
    quarter = stations // parts
    blocks = length // LANES
    flat_records = records.reshape(stations, windows, blocks, LANES).transpose(0, 2, 1, 3)
    flat_records = flat_records.reshape(rows * blocks, LANES)
    small = jax.ShapeDtypeStruct((windows, quarter, 2 * TILES, LANES), BF)
    vmem = pl.BlockSpec(memory_space=pltpu.VMEM)
    return pl.pallas_call(
        functools.partial(prep_kernel, parts, windows),
        out_shape=[jax.ShapeDtypeStruct((windows, stations, 2 * TILES, LANES), BF)]
        + [small] * parts,
        in_specs=[pl.BlockSpec(memory_space=pltpu.HBM)] * 2,
        out_specs=[vmem] * (1 + parts),
        scratch_shapes=[
            pltpu.VMEM(flat_records.shape, F32),
            pltpu.VMEM(table.shape, BF),
            pltpu.VMEM((rows * (length // LANES), 3 * LANES), BF),
            pltpu.VMEM((CHUNKS * rows, length // CHUNKS), BF),
            pltpu.VMEM((rows * 2 * TILES, LANES), F32),
            pltpu.SemaphoreType.DMA((2,)),
        ],
        compiler_params=pltpu.CompilerParams(vmem_limit_bytes=52 * 2**20),
        cost_estimate=pl.CostEstimate(
            flops=2 * rows * length * 2 * NBIN, bytes_accessed=3 * 2**20, transcendentals=0
        ),
        name="prep",
    )(
        pltpu.with_memory_space_constraint(flat_records, pltpu.HBM),
        pltpu.with_memory_space_constraint(table, pltpu.HBM),
    )


def ring_place(block, count):
    half = block >> 1
    return jnp.where((block & 1) == 0, half, count - 1 - half)


def partner_steps(plan, count):
    me = lax.axis_index("sta")
    mine = ring_place(me, count)
    steps, keys = [], []
    for number in range(ROUNDS):
        step = ring_place(plan[number, me], count) - mine
        step = jnp.where(step < 0, step + count, step)
        steps.append(step)
        keys.append(jnp.minimum(step, count - step) * ROUNDS + number)
    ranks = []
    for number in range(ROUNDS):
        rank = jnp.int32(0)
        for other in range(ROUNDS):
            if other != number:
                rank = rank + jnp.where(keys[other] < keys[number], 1, 0)
        ranks.append(rank)
    return steps, ranks


def expected(microseconds):
    return pl.CostEstimate(
        flops=int(microseconds * 1.15e9), bytes_accessed=1024, transcendentals=0
    )


def widen_kernel(*refs):
    blocks, own = refs[:-1], refs[-1]
    windows = blocks[0].shape[0]
    for j, block in enumerate(blocks):

        def widen(w, carry, j=j, block=block):
            raw = block[w].astype(F32)
            real, imag = raw[:, :TILES], raw[:, TILES:]
            both = real + imag
            for group in range(own.shape[0]):
                at = slice(group * GROUP, (group + 1) * GROUP)
                own[group, 0, j * windows + w] = both[at]
                own[group, 1, j * windows + w] = real[at]
                own[group, 2, j * windows + w] = imag[at]
            return carry

        lax.fori_loop(0, windows, widen, 0)


def widen_own(blocks):
    windows, stations = blocks[0].shape[:2]
    vmem = pl.BlockSpec(memory_space=pltpu.VMEM)
    return pl.pallas_call(
        widen_kernel,
        out_shape=jax.ShapeDtypeStruct(
            (stations // GROUP, 3, len(blocks) * windows, GROUP, TILES, LANES), F32
        ),
        in_specs=[vmem] * len(blocks),
        out_specs=vmem,
        compiler_params=pltpu.CompilerParams(vmem_limit_bytes=16 * 2**20),
        cost_estimate=expected(0.05),
        name="widen",
    )(*blocks)


def widen_others(first_slot, slots, count, places, plan, candidates, other):
    steps, ranks = partner_steps(plan, count)
    for slot in range(slots):
        step = jnp.int32(0)
        for number in range(ROUNDS):
            step = jnp.where(ranks[number] == first_slot + slot, steps[number], step)
        for (offset, first), candidate in zip(places, candidates):

            @pl.when(step == offset)
            def _(candidate=candidate, slot=slot, first=first):
                def widen_other(w, carry):
                    raw = candidate[w].astype(F32)
                    real, imag = raw[:, :TILES], raw[:, TILES:]
                    other[0, slot, first + w] = real
                    other[1, slot, first + w] = real + imag
                    other[2, slot, first + w] = imag - real
                    return carry

                lax.fori_loop(0, candidate.shape[0], widen_other, 0)


def sum_windows(owns, other, summed):
    groups, _, windows, group = owns[0].shape[:4]
    slots, _, quarter = other.shape[1:4]
    width = groups * group * quarter
    shift = groups.bit_length() - 1

    for slot in range(slots):

        def body(index, carry, slot=slot):
            kind, part = index >> shift, index & (groups - 1)
            mine = [own.at[part, kind] for own in owns]
            theirs = other.at[kind, slot]
            totals = [None] * (group * quarter)
            for half, own in enumerate(mine):
                for w in range(windows):
                    left = [own[w, s] for s in range(group)]
                    right = [theirs[half * windows + w, t] for t in range(quarter)]
                    for s in range(group):
                        for t in range(quarter):
                            term = left[s] * right[t]
                            old = totals[s * quarter + t]
                            totals[s * quarter + t] = term if old is None else old + term
            rows = summed.at[kind]
            base = (slot * width + part * (group * quarter)) * TILES
            for place in range(group * quarter):
                at = pl.multiple_of(base + place * TILES, TILES)
                rows[pl.ds(at, TILES), :] = totals[place]
            return carry

        lax.fori_loop(0, 3 * groups, body, 0)


def cross_kernel(first_slot, slots, count, scaling, places, parts, plan, table, *rest):
    owns, rest = rest[:2], rest[2:]
    others, rest = rest[: len(places)], rest[len(places) :]
    outs = rest[:parts]
    other, summed, operand, result = rest[parts:]
    stations = owns[0].shape[0] * owns[0].shape[3]
    widen_others(first_slot, slots, count, places, plan, others, other)
    sum_windows(owns, other, summed)
    width = stations * other.shape[3]
    columns = slots * width
    even = even_lanes((columns, LANES))
    sign_real = lane_cycle([1.0, -1.0, -1.0, 1.0])
    sign_imag = lane_cycle([1.0, 1.0, -1.0, -1.0])
    cosine, sine = eighth_turn()
    lane = lax.broadcasted_iota(jnp.int32, (1, LANES), 1)
    first_weight = jnp.where(lane == 0, 0.5, 1.0).astype(F32)
    for j in range(TILES):
        at = slice(j * LANES, (j + 1) * LANES)
        at_imag = slice(NBIN + j * LANES, NBIN + (j + 1) * LANES)
        kinds = [summed[kind, pl.ds(j, columns, stride=TILES), :] for kind in range(3)]
        real, imag = kinds[0] + kinds[2], kinds[0] - kinds[1]
        if j == 0:
            real, imag = real * first_weight, imag * first_weight
        turned = [(real, imag), (real * cosine - imag * sine, imag * cosine + real * sine)]
        turned += [quarter_turns(r, i, even, sign_real, sign_imag) for r, i in turned]
        for q in range(CHUNKS):
            rows = slice(q * columns, (q + 1) * columns)
            operand[rows, at] = turned[q][0].astype(BF)
            operand[rows, at_imag] = turned[q][1].astype(BF)
    block = jnp.dot(operand[...], table[...], preferred_element_type=F32)
    block = block * (2.0 * scaling)
    for q in range(CHUNKS):
        result[q] = block[q * columns : (q + 1) * columns].astype(BF)
    me = lax.axis_index("seg")
    for j in range(parts):
        outs[j][...] = result[me ^ j]


def cross_lags(plan, table, owns, places, candidates, first_slot, slots, count, parts, scaling):
    windows, stations = owns[0].shape[2], owns[0].shape[0] * owns[0].shape[3]
    quarter = candidates[0].shape[1]
    columns = slots * stations * quarter
    share = LAGS // parts
    out = (columns, share)
    smem = pl.BlockSpec(memory_space=pltpu.SMEM)
    vmem = pl.BlockSpec(memory_space=pltpu.VMEM)
    operands = [table, *owns, *candidates]
    return pl.pallas_call(
        functools.partial(
            cross_kernel, first_slot, slots, count, scaling, tuple(places), parts
        ),
        out_shape=[jax.ShapeDtypeStruct(out, BF)] * parts,
        in_specs=[smem] + [vmem] * len(operands),
        out_specs=[vmem] * parts,
        scratch_shapes=[
            pltpu.VMEM((3, slots, 2 * windows, quarter, TILES, LANES), F32),
            pltpu.VMEM((3, columns * TILES, LANES), F32),
            pltpu.VMEM((CHUNKS * columns, 2 * NBIN), BF),
            pltpu.VMEM((parts,) + out, BF),
        ],
        compiler_params=pltpu.CompilerParams(vmem_limit_bytes=24 * 2**20),
        cost_estimate=expected(0.6 + 2.0 * slots),
        name="cross",
    )(plan, *operands)


def slot_rounds(plan, count):
    _, ranks = partner_steps(plan, count)
    rounds = []
    for slot in range(ROUNDS):
        number = jnp.int32(0)
        for other in range(1, ROUNDS):
            number = jnp.where(ranks[other] == slot, other, number)
        rounds.append(number)
    return rounds


def placed_block(pieces, matrix, at):
    joined = jnp.concatenate([piece[:, at] for piece in pieces], axis=0)
    return lax.dot_general(
        joined, matrix, (((0,), (0,)), ((), ())), preferred_element_type=F32
    )


def joined_matrix(place, parts, slots):
    me = lax.axis_index("seg")
    rows, columns = place.shape[1] * slots // 2, place.shape[2] * slots // 2
    return jnp.concatenate([place[me ^ j, :rows, :columns] for j in range(parts)], axis=0)


def store_rows(rows, block, first):
    tiles = block.shape[1] // LANES
    for tile in range(tiles):
        at = pl.ds(first * tiles + tile, block.shape[0], stride=tiles)
        rows[at, :] = block[:, tile * LANES : (tile + 1) * LANES]


def early_kernel(count, parts, groups, plan, place, *rest):
    pieces = rest[:-3]
    out_hbm, rows, sems = rest[-3:]
    pairs = place.shape[2] // 2
    rounds = slot_rounds(plan, count)
    copies = []
    for index, (first_slot, slots) in enumerate(groups):
        own = pieces[index * parts : (index + 1) * parts]
        block = placed_block(own, joined_matrix(place, parts, slots), slice(None))
        for slot in range(slots):
            number = first_slot + slot
            store_rows(rows.at[number], block[:, slot * pairs : (slot + 1) * pairs], 0)
            copy = pltpu.make_async_copy(
                rows.at[number], out_hbm.at[:, rounds[number], 0], sems.at[number]
            )
            copy.start()
            copies.append(copy)
    for copy in copies:
        copy.wait()


def late_kernel(count, parts, plan, place, early, *rest):
    pieces = rest[:parts]
    out_hbm, rows, sems = rest[parts:]
    number = slot_rounds(plan, count)[ROUNDS - 1]
    matrix = joined_matrix(place, parts, 1)
    half = pieces[0].shape[1] // 2
    size = rows.shape[0] // 2
    copies = []
    for h in range(2):
        block = placed_block(pieces, matrix, slice(h * half, (h + 1) * half))
        store_rows(rows, block, h * half)
        at = pl.ds(h * size, size)
        copy = pltpu.make_async_copy(rows.at[at], out_hbm.at[at, number, 0], sems.at[h])
        copy.start()
        copies.append(copy)
    for copy in copies:
        copy.wait()


def place_lags(plan, groups, pieces, count, stations, parts):
    pairs = stations * stations
    share = LAGS // parts
    tiles = pairs // LANES
    place = jnp.asarray(make_placing(stations, stations // parts, parts))
    smem = pl.BlockSpec(memory_space=pltpu.SMEM)
    vmem = pl.BlockSpec(memory_space=pltpu.VMEM)
    anywhere = pl.BlockSpec(memory_space=pl.ANY)
    shape = jax.ShapeDtypeStruct((share * tiles, ROUNDS, 1, LANES), F32)
    early = pl.pallas_call(
        functools.partial(early_kernel, count, parts, tuple(groups[:-1])),
        out_shape=shape,
        in_specs=[smem] + [vmem] * (1 + len(pieces) - parts),
        out_specs=anywhere,
        scratch_shapes=[
            pltpu.VMEM((ROUNDS - 1, share * tiles, LANES), F32),
            pltpu.SemaphoreType.DMA((ROUNDS - 1,)),
        ],
        compiler_params=pltpu.CompilerParams(vmem_limit_bytes=16 * 2**20),
        cost_estimate=expected(0.05),
        name="early",
    )(plan, place, *pieces[:-parts])
    out = pl.pallas_call(
        functools.partial(late_kernel, count, parts),
        out_shape=shape,
        in_specs=[smem, vmem, anywhere] + [vmem] * parts,
        out_specs=anywhere,
        scratch_shapes=[pltpu.VMEM((share * tiles, LANES), F32), pltpu.SemaphoreType.DMA((2,))],
        input_output_aliases={2: 0},
        compiler_params=pltpu.CompilerParams(vmem_limit_bytes=16 * 2**20),
        cost_estimate=expected(0.05),
        name="late",
    )(plan, place, early, *pieces[-parts:])
    out = out.reshape(share, tiles, ROUNDS, LANES)
    return out.transpose(0, 2, 1, 3).reshape(share, ROUNDS, pairs)


def join_kernel(order, *refs):
    parts, (out_up, out_down) = refs[:4], refs[4:]
    near_up, near_down, far_up, far_down = [parts[order.index(k)] for k in range(4)]
    half = near_up.shape[0]
    for out, first, second in ((out_up, near_up, far_up), (out_down, near_down, far_down)):
        out[:half] = first[...]
        out[half:] = second[...]


def join(near_up, near_down, far_up, far_down, order=(0, 1, 2, 3)):
    values = [near_up, near_down, far_up, far_down]
    vmem = pl.BlockSpec(memory_space=pltpu.VMEM)
    shape = (2 * near_up.shape[0],) + near_up.shape[1:]
    return pl.pallas_call(
        functools.partial(join_kernel, tuple(order)),
        out_shape=[jax.ShapeDtypeStruct(shape, BF)] * 2,
        in_specs=[vmem] * 4,
        out_specs=[vmem] * 2,
        compiler_params=pltpu.CompilerParams(vmem_limit_bytes=16 * 2**20),
        cost_estimate=expected(0.05),
        name="join",
    )(*[values[k] for k in order])


def swap(value, j):
    parts = lax.axis_size("seg")
    return lax.ppermute(value, "seg", [(i, i ^ j) for i in range(parts)])


def exchange(pieces):
    return [pieces[0]] + [swap(pieces[j], j) for j in range(1, len(pieces))]


def after(value, others):
    return lax.optimization_barrier((value, others))[0]


def per_device(records, plan):
    stations, windows, length = records.shape
    count = lax.axis_size("sta")
    parts = lax.axis_size("seg")
    quarter = stations // parts
    constants = make_table(length // CHUNKS, 2 * length)
    table, lag_table = jnp.asarray(constants), jnp.asarray(constants.T.copy())
    scaling = 1.0 / math.sqrt(4.0 * NBIN * windows * parts)

    white, *quarters = prepare(records, table, parts)
    near = jnp.concatenate([quarters[0], swap(quarters[1], 1)])
    sibling = swap(white, 1)
    far = jnp.concatenate([swap(quarters[j], j) for j in range(2, parts)])
    far = after(far, sibling)
    far, white_far = lax.optimization_barrier((far, white))
    across = swap(white_far, 2)

    ring = sorted(range(count), key=lambda b: b // 2 if b % 2 == 0 else count - 1 - b // 2)
    upward = [(ring[i], ring[(i + 1) % count]) for i in range(count)]
    downward = [(ring[i], ring[i - 1]) for i in range(count)]

    def up(value):
        return lax.ppermute(value, "sta", upward)

    def down(value):
        return lax.ppermute(value, "sta", downward)

    far, white_far = lax.optimization_barrier((far, white))
    across = swap(white_far, 2)
    near_own = widen_own([white, sibling])
    half = near.shape[0]
    places, blocks, arrived = [], [], []

    def arrive(step, first, from_left, from_right):
        places.extend([(count - step, first), (step, first)])
        blocks.extend([from_left, from_right])

    near_up, near_down = up(near), down(near)
    far_up, far_down = up(far), down(far)
    arrive(1, 0, near_up, near_down)
    arrive(1, half, far_up, far_down)
    near_up, near_down, near_own = lax.optimization_barrier((near_up, near_down, near_own))
    near_up, near_down = up(near_up), down(near_down)
    far_up, far_down = lax.optimization_barrier((far_up, far_down))
    far_up, far_down = up(far_up), down(far_down)
    arrive(2, 0, near_up, near_down)
    arrive(2, half, far_up, far_down)
    all_up, all_down = join(near_up, near_down, far_up, far_down)
    for step in range(3, (count - 1) // 2 + 1):
        arrived.append((list(places), list(blocks)))
        all_up, all_down, across = lax.optimization_barrier((all_up, all_down, across))
        all_up, all_down = up(all_up), down(all_down)
        arrive(step, 0, all_up, all_down)
    arrived.append((list(places), list(blocks)))
    far_own = widen_own([across, swap(across, 1)])
    groups = [(0, 1), (1, 2), (3, 1)]
    if count % 2 == 0:
        places.append((count // 2, 0))
        blocks.append(up(all_up))
    arrived.append((places, blocks))
    pieces = []
    for index, (first_slot, slots) in enumerate(groups):
        if index == 2:
            near_own = after(near_own, pieces[:parts])
        if index > 0:
            near_own = after(near_own, lags)
        at, values = arrived[index - len(groups)]
        lags = cross_lags(
            plan, lag_table, [near_own, far_own], at, values, first_slot, slots, count, parts, scaling
        )
        pieces = pieces + exchange(lags)
    return place_lags(plan, groups, pieces, count, stations, parts)


def solution(mesh):
    in_specs = (P("sta", "seg", None), P())
    out_specs = P("seg", None, "sta")
    return jax.shard_map(
        per_device, mesh=mesh, in_specs=in_specs, out_specs=out_specs, check_vma=False
    )
```

```python
import functools
import math

import jax
import jax.numpy as jnp
import ml_dtypes
import numpy as np
from jax import lax
from jax.experimental import pallas as pl
from jax.experimental.pallas import tpu as pltpu
from jax.sharding import PartitionSpec as P

NBIN = 1024
HALF = 64
ROUNDS = 4
LAGS = 2048
LANES = 128
TILES = NBIN // LANES
CHUNKS = 4
GROUP = 4
BF = jnp.bfloat16
F32 = jnp.float32


def make_table(rows, transform):
    phase = (np.arange(rows)[:, None] * np.arange(NBIN)[None, :]) % transform
    angle = phase * (2.0 * math.pi / transform)
    return np.concatenate([np.cos(angle), -np.sin(angle)], axis=1).astype(ml_dtypes.bfloat16)


def band_matrix():
    source = lax.broadcasted_iota(jnp.int32, (3 * LANES, LANES), 0) - LANES
    target = lax.broadcasted_iota(jnp.int32, (3 * LANES, LANES), 1)
    return jnp.where(jnp.abs(source - target) <= HALF, 1.0, 0.0).astype(BF)


def inverse_count(block, length):
    if 0 < block < length // LANES - 1:
        return 1.0 / (2 * HALF + 1)
    position = lax.broadcasted_iota(jnp.int32, (1, LANES), 1) + block * LANES
    counted = jnp.minimum(position, HALF) + jnp.minimum(length - 1 - position, HALF) + 1
    return 1.0 / counted.astype(F32)


def make_placing(stations, quarter, parts):
    width = stations * quarter
    place = np.zeros((parts, 2 * width, 2 * stations * stations), np.float32)
    for part in range(parts):
        for second in range(2):
            for s in range(stations):
                for t in range(quarter):
                    row = second * width + s * quarter + t
                    column = (second * stations + s) * stations + part * quarter + t
                    place[part, row, column] = 1.0
    return place.astype(ml_dtypes.bfloat16)


def lane_cycle(values):
    period = len(values)
    phase = lax.broadcasted_iota(jnp.int32, (1, LANES), 1) % period
    out = jnp.full((1, LANES), values[-1], F32)
    for index in range(period - 1):
        out = jnp.where(phase == index, values[index], out)
    return out


def even_lanes(shape):
    return lax.broadcasted_iota(jnp.int32, shape, 1) % 2 == 0


def eighth_turn():
    turns = [math.pi * k / 4.0 for k in range(8)]
    return lane_cycle([math.cos(t) for t in turns]), lane_cycle([math.sin(t) for t in turns])


def quarter_turns(real, imag, even, sign_real, sign_imag):
    return sign_real * jnp.where(even, real, imag), sign_imag * jnp.where(even, imag, real)


def banded_sum(stack, values, band):
    blocks, rows = len(values), values[0].shape[0]
    zero = jnp.zeros((rows, LANES), BF)
    for j in range(blocks):
        at = pl.ds(j * rows, rows)
        for k in range(3):
            b = j + k - 1
            block = values[b] if 0 <= b < blocks else zero
            stack[at, k * LANES : (k + 1) * LANES] = block
    total = jnp.dot(stack[: blocks * rows, :], band, preferred_element_type=F32)
    return [total[j * rows : (j + 1) * rows, :] for j in range(blocks)]


def prep_kernel(parts, windows, records_hbm, table_hbm, white, mine, *rest):
    others = rest[: parts - 1]
    records, table, stack, flat, spread, sems = rest[parts - 1 :]
    records_copy = pltpu.make_async_copy(records_hbm, records, sems.at[0])
    records_copy.start()
    copy = pltpu.make_async_copy(table_hbm, table, sems.at[1])
    copy.start()
    band_values = band_matrix()
    records_copy.wait()
    stations = white.shape[1]
    rows = stations * windows
    blocks = records.shape[0] // rows
    length = blocks * LANES
    chunk = length // CHUNKS
    signal = [
        jnp.concatenate(
            [
                records[pl.ds(j * windows + w, stations, stride=blocks * windows), :]
                for w in range(windows)
            ],
            axis=0,
        )
        for j in range(blocks)
    ]
    sums = banded_sum(stack, [jnp.abs(block).astype(BF) for block in signal], band_values)
    for j, total in enumerate(sums):
        at = slice(j * LANES, (j + 1) * LANES)
        level = total * inverse_count(j, length)
        value = (signal[j] / (level + 1e-05)).astype(BF)
        q, inside = divmod(j * LANES, chunk)
        flat[q * rows : (q + 1) * rows, inside : inside + LANES] = value
    copy.wait()
    product = jnp.dot(flat[...], table[...], preferred_element_type=F32)
    even = even_lanes((rows, LANES))
    sign_real = lane_cycle([1.0, 1.0, -1.0, -1.0])
    sign_imag = lane_cycle([1.0, -1.0, -1.0, 1.0])
    cosine, sine = eighth_turn()
    reals, imags, mags = [], [], []
    for j in range(TILES):
        at = slice(j * LANES, (j + 1) * LANES)
        at_imag = slice(NBIN + j * LANES, NBIN + (j + 1) * LANES)
        pr = [product[q * rows : (q + 1) * rows, at] for q in range(CHUNKS)]
        pi = [product[q * rows : (q + 1) * rows, at_imag] for q in range(CHUNKS)]
        turned = [
            quarter_turns(pr[q], pi[q], even, sign_real, sign_imag) for q in range(2, CHUNKS)
        ]
        first_real, first_imag = pr[0] + turned[0][0], pi[0] + turned[0][1]
        odd_real, odd_imag = pr[1] + turned[1][0], pi[1] + turned[1][1]
        real = first_real + (odd_real * cosine + odd_imag * sine)
        imag = first_imag + (odd_imag * cosine - odd_real * sine)
        reals.append(real)
        imags.append(imag)
        mags.append(jnp.sqrt(real * real + imag * imag).astype(BF))
    sums = banded_sum(stack, mags, band_values)
    for j, total in enumerate(sums):
        at = slice(j * LANES, (j + 1) * LANES)
        inverse = 1.0 / (total * inverse_count(j, NBIN) + 1e-06)
        spread[pl.ds(j, rows, stride=2 * TILES), :] = reals[j] * inverse
        spread[pl.ds(TILES + j, rows, stride=2 * TILES), :] = imags[j] * inverse
    me = lax.axis_index("seg")
    quarter = stations // parts
    white[...] = spread[...].reshape(windows, stations, 2 * TILES, LANES).astype(BF)
    for j, out in enumerate((mine, *others)):
        for w in range(windows):
            out[w] = white[w, pl.ds((me ^ j) * quarter, quarter)]


def prepare(records, table, parts):
    stations, windows, length = records.shape
    rows = stations * windows
    quarter = stations // parts
    blocks = length // LANES
    flat_records = records.reshape(stations, windows, blocks, LANES).transpose(0, 2, 1, 3)
    flat_records = flat_records.reshape(rows * blocks, LANES)
    small = jax.ShapeDtypeStruct((windows, quarter, 2 * TILES, LANES), BF)
    vmem = pl.BlockSpec(memory_space=pltpu.VMEM)
    return pl.pallas_call(
        functools.partial(prep_kernel, parts, windows),
        out_shape=[jax.ShapeDtypeStruct((windows, stations, 2 * TILES, LANES), BF)]
        + [small] * parts,
        in_specs=[pl.BlockSpec(memory_space=pltpu.HBM)] * 2,
        out_specs=[vmem] * (1 + parts),
        scratch_shapes=[
            pltpu.VMEM(flat_records.shape, F32),
            pltpu.VMEM(table.shape, BF),
            pltpu.VMEM((rows * (length // LANES), 3 * LANES), BF),
            pltpu.VMEM((CHUNKS * rows, length // CHUNKS), BF),
            pltpu.VMEM((rows * 2 * TILES, LANES), F32),
            pltpu.SemaphoreType.DMA((2,)),
        ],
        compiler_params=pltpu.CompilerParams(vmem_limit_bytes=52 * 2**20),
        cost_estimate=pl.CostEstimate(
            flops=2 * rows * length * 2 * NBIN, bytes_accessed=3 * 2**20, transcendentals=0
        ),
        name="prep",
    )(
        pltpu.with_memory_space_constraint(flat_records, pltpu.HBM),
        pltpu.with_memory_space_constraint(table, pltpu.HBM),
    )


def ring_place(block, count):
    half = block >> 1
    return jnp.where((block & 1) == 0, half, count - 1 - half)


def partner_steps(plan, count):
    me = lax.axis_index("sta")
    mine = ring_place(me, count)
    steps, keys = [], []
    for number in range(ROUNDS):
        step = ring_place(plan[number, me], count) - mine
        step = jnp.where(step < 0, step + count, step)
        steps.append(step)
        keys.append(jnp.minimum(step, count - step) * ROUNDS + number)
    ranks = []
    for number in range(ROUNDS):
        rank = jnp.int32(0)
        for other in range(ROUNDS):
            if other != number:
                rank = rank + jnp.where(keys[other] < keys[number], 1, 0)
        ranks.append(rank)
    return steps, ranks


def expected(microseconds):
    return pl.CostEstimate(
        flops=int(microseconds * 1.15e9), bytes_accessed=1024, transcendentals=0
    )


def widen_kernel(*refs):
    blocks, own = refs[:-1], refs[-1]
    windows = blocks[0].shape[0]
    for j, block in enumerate(blocks):

        def widen(w, carry, j=j, block=block):
            raw = block[w].astype(F32)
            real, imag = raw[:, :TILES], raw[:, TILES:]
            both = real + imag
            for group in range(own.shape[0]):
                at = slice(group * GROUP, (group + 1) * GROUP)
                own[group, 0, j * windows + w] = both[at]
                own[group, 1, j * windows + w] = real[at]
                own[group, 2, j * windows + w] = imag[at]
            return carry

        lax.fori_loop(0, windows, widen, 0)


def widen_own(blocks):
    windows, stations = blocks[0].shape[:2]
    vmem = pl.BlockSpec(memory_space=pltpu.VMEM)
    return pl.pallas_call(
        widen_kernel,
        out_shape=jax.ShapeDtypeStruct(
            (stations // GROUP, 3, len(blocks) * windows, GROUP, TILES, LANES), F32
        ),
        in_specs=[vmem] * len(blocks),
        out_specs=vmem,
        compiler_params=pltpu.CompilerParams(vmem_limit_bytes=16 * 2**20),
        cost_estimate=expected(0.05),
        name="widen",
    )(*blocks)


def widen_others(first_slot, slots, count, places, plan, candidates, other):
    steps, ranks = partner_steps(plan, count)
    for slot in range(slots):
        step = jnp.int32(0)
        for number in range(ROUNDS):
            step = jnp.where(ranks[number] == first_slot + slot, steps[number], step)
        for (offset, first), candidate in zip(places, candidates):

            @pl.when(step == offset)
            def _(candidate=candidate, slot=slot, first=first):
                def widen_other(turn, carry):
                    raw = candidate[pl.ds(turn * GROUP, GROUP)].astype(F32)
                    real, imag = raw[:, :, :TILES], raw[:, :, TILES:]
                    at = pl.ds(first + turn * GROUP, GROUP)
                    other[0, slot, at] = real
                    other[1, slot, at] = real + imag
                    other[2, slot, at] = imag - real
                    return carry

                lax.fori_loop(0, candidate.shape[0] // GROUP, widen_other, 0)


def sum_windows(owns, other, slot, crossed, turns, beside=None):
    groups, _, windows, group = owns[0].shape[:4]
    quarter = other.shape[3]
    size = 2 * TILES

    def one_group(index):
        mine = [own.at[index] for own in owns]

        def sums(kind):
            totals = [None] * (group * quarter)
            for half, own in enumerate(mine):
                for w in range(windows):
                    left = [own[kind, w, s] for s in range(group)]
                    right = [other[kind, slot, half * windows + w, t] for t in range(quarter)]
                    for s in range(group):
                        for t in range(quarter):
                            term = left[s] * right[t]
                            old = totals[s * quarter + t]
                            totals[s * quarter + t] = term if old is None else old + term
            return totals

        def store(place, part, value):
            at = pl.multiple_of(base + place * size + part * TILES, TILES)
            crossed[pl.ds(at, TILES), :] = value

        base = index * (group * quarter * size)
        shared = sums(0)
        third = sums(2)
        for place in range(group * quarter):
            store(place, 0, shared[place] + third[place])
        second = sums(1)
        for place in range(group * quarter):
            store(place, 1, shared[place] - second[place])

    def body(turn, carry):
        if beside is not None:
            beside(turn)
        for index in range(groups // turns):
            one_group(turn * (groups // turns) + index)
        return carry

    lax.fori_loop(0, turns, body, 0)


def fill_operand(crossed, operand):
    columns = operand.shape[0] // CHUNKS
    even = even_lanes((columns, LANES))
    sign_real = lane_cycle([1.0, -1.0, -1.0, 1.0])
    sign_imag = lane_cycle([1.0, 1.0, -1.0, -1.0])
    cosine, sine = eighth_turn()
    lane = lax.broadcasted_iota(jnp.int32, (1, LANES), 1)
    first_weight = jnp.where(lane == 0, 0.5, 1.0).astype(F32)
    for j in range(TILES):
        at = slice(j * LANES, (j + 1) * LANES)
        at_imag = slice(NBIN + j * LANES, NBIN + (j + 1) * LANES)
        real = crossed[pl.ds(j, columns, stride=2 * TILES), :]
        imag = crossed[pl.ds(TILES + j, columns, stride=2 * TILES), :]
        if j == 0:
            real, imag = real * first_weight, imag * first_weight
        turned = [(real, imag), (real * cosine - imag * sine, imag * cosine + real * sine)]
        turned += [quarter_turns(r, i, even, sign_real, sign_imag) for r, i in turned]
        for q in range(CHUNKS):
            rows = slice(q * columns, (q + 1) * columns)
            operand[rows, at] = turned[q][0].astype(BF)
            operand[rows, at_imag] = turned[q][1].astype(BF)


def cross_kernel(first_slot, slots, count, scaling, places, parts, plan, table, *rest):
    owns, rest = rest[:2], rest[2:]
    others, rest = rest[: len(places)], rest[len(places) :]
    outs = rest[:parts]
    other, crossed, operand, result = rest[parts:]
    groups = owns[0].shape[0]
    widen_others(first_slot, slots, count, places, plan, others, other)
    width = operand.shape[0] // CHUNKS
    share = table.shape[1]

    def lags(slot, at):
        block = jnp.dot(operand[...], table[:, at], preferred_element_type=F32)
        block = (block * (2.0 * scaling)).astype(BF)
        for q in range(CHUNKS):
            result[q, slot * width : (slot + 1) * width, at] = block[q * width : (q + 1) * width]

    sum_windows(owns, other, 0, crossed, groups)
    fill_operand(crossed, operand)
    for slot in range(1, slots):
        turns = 2
        size = share // turns

        def beside(turn, slot=slot, size=size):
            lags(slot - 1, pl.ds(pl.multiple_of(turn * size, size), size))

        sum_windows(owns, other, slot, crossed, turns, beside)
        fill_operand(crossed, operand)
    lags(slots - 1, slice(None))
    me = lax.axis_index("seg")
    for j in range(parts):
        outs[j][...] = result[me ^ j]


def cross_lags(plan, table, owns, places, candidates, first_slot, slots, count, parts, scaling):
    windows, stations = owns[0].shape[2], owns[0].shape[0] * owns[0].shape[3]
    quarter = candidates[0].shape[1]
    columns = slots * stations * quarter
    share = LAGS // parts
    out = (columns, share)
    smem = pl.BlockSpec(memory_space=pltpu.SMEM)
    vmem = pl.BlockSpec(memory_space=pltpu.VMEM)
    operands = [table, *owns, *candidates]
    return pl.pallas_call(
        functools.partial(
            cross_kernel, first_slot, slots, count, scaling, tuple(places), parts
        ),
        out_shape=[jax.ShapeDtypeStruct(out, BF)] * parts,
        in_specs=[smem] + [vmem] * len(operands),
        out_specs=[vmem] * parts,
        scratch_shapes=[
            pltpu.VMEM((3, slots, 2 * windows, quarter, TILES, LANES), F32),
            pltpu.VMEM((columns // slots * 2 * TILES, LANES), F32),
            pltpu.VMEM((CHUNKS * columns // slots, 2 * NBIN), BF),
            pltpu.VMEM((parts,) + out, BF),
        ],
        compiler_params=pltpu.CompilerParams(vmem_limit_bytes=24 * 2**20),
        cost_estimate=expected(0.6 + 2.0 * slots),
        name="cross",
    )(plan, *operands)


def slot_rounds(plan, count):
    _, ranks = partner_steps(plan, count)
    rounds = []
    for slot in range(ROUNDS):
        number = jnp.int32(0)
        for other in range(1, ROUNDS):
            number = jnp.where(ranks[other] == slot, other, number)
        rounds.append(number)
    return rounds


def placed_block(pieces, matrix, at):
    joined = jnp.concatenate([piece[:, at] for piece in pieces], axis=0)
    return lax.dot_general(
        joined, matrix, (((0,), (0,)), ((), ())), preferred_element_type=F32
    )


def joined_matrix(place, parts, slots):
    me = lax.axis_index("seg")
    rows, columns = place.shape[1] * slots // 2, place.shape[2] * slots // 2
    return jnp.concatenate([place[me ^ j, :rows, :columns] for j in range(parts)], axis=0)


def store_rows(rows, block, first):
    tiles = block.shape[1] // LANES
    for tile in range(tiles):
        at = pl.ds(first * tiles + tile, block.shape[0], stride=tiles)
        rows[at, :] = block[:, tile * LANES : (tile + 1) * LANES]


def early_kernel(count, parts, groups, plan, place, *rest):
    pieces = rest[:-3]
    out_hbm, rows, sems = rest[-3:]
    pairs = place.shape[2] // 2
    rounds = slot_rounds(plan, count)
    copies = []
    for index, (first_slot, slots) in enumerate(groups):
        own = pieces[index * parts : (index + 1) * parts]
        block = placed_block(own, joined_matrix(place, parts, slots), slice(None))
        for slot in range(slots):
            number = first_slot + slot
            store_rows(rows.at[number], block[:, slot * pairs : (slot + 1) * pairs], 0)
            copy = pltpu.make_async_copy(
                rows.at[number], out_hbm.at[:, rounds[number], 0], sems.at[number]
            )
            copy.start()
            copies.append(copy)
    for copy in copies:
        copy.wait()


def late_kernel(count, parts, plan, place, early, *rest):
    pieces = rest[:parts]
    out_hbm, rows, sems = rest[parts:]
    number = slot_rounds(plan, count)[ROUNDS - 1]
    matrix = joined_matrix(place, parts, 1)
    half = pieces[0].shape[1] // 2
    size = rows.shape[0] // 2
    copies = []
    for h in range(2):
        block = placed_block(pieces, matrix, slice(h * half, (h + 1) * half))
        store_rows(rows, block, h * half)
        at = pl.ds(h * size, size)
        copy = pltpu.make_async_copy(rows.at[at], out_hbm.at[at, number, 0], sems.at[h])
        copy.start()
        copies.append(copy)
    for copy in copies:
        copy.wait()


def place_lags(plan, groups, pieces, count, stations, parts):
    pairs = stations * stations
    share = LAGS // parts
    tiles = pairs // LANES
    place = jnp.asarray(make_placing(stations, stations // parts, parts))
    smem = pl.BlockSpec(memory_space=pltpu.SMEM)
    vmem = pl.BlockSpec(memory_space=pltpu.VMEM)
    anywhere = pl.BlockSpec(memory_space=pl.ANY)
    shape = jax.ShapeDtypeStruct((share * tiles, ROUNDS, 1, LANES), F32)
    early = pl.pallas_call(
        functools.partial(early_kernel, count, parts, tuple(groups[:-1])),
        out_shape=shape,
        in_specs=[smem] + [vmem] * (1 + len(pieces) - parts),
        out_specs=anywhere,
        scratch_shapes=[
            pltpu.VMEM((ROUNDS - 1, share * tiles, LANES), F32),
            pltpu.SemaphoreType.DMA((ROUNDS - 1,)),
        ],
        compiler_params=pltpu.CompilerParams(vmem_limit_bytes=16 * 2**20),
        cost_estimate=expected(0.05),
        name="early",
    )(plan, place, *pieces[:-parts])
    out = pl.pallas_call(
        functools.partial(late_kernel, count, parts),
        out_shape=shape,
        in_specs=[smem, vmem, anywhere] + [vmem] * parts,
        out_specs=anywhere,
        scratch_shapes=[pltpu.VMEM((share * tiles, LANES), F32), pltpu.SemaphoreType.DMA((2,))],
        input_output_aliases={2: 0},
        compiler_params=pltpu.CompilerParams(vmem_limit_bytes=16 * 2**20),
        cost_estimate=expected(0.05),
        name="late",
    )(plan, place, early, *pieces[-parts:])
    out = out.reshape(share, tiles, ROUNDS, LANES)
    return out.transpose(0, 2, 1, 3).reshape(share, ROUNDS, pairs)


def join_kernel(order, *refs):
    parts, (out_up, out_down) = refs[:4], refs[4:]
    near_up, near_down, far_up, far_down = [parts[order.index(k)] for k in range(4)]
    half = near_up.shape[0]
    for out, first, second in ((out_up, near_up, far_up), (out_down, near_down, far_down)):
        out[:half] = first[...]
        out[half:] = second[...]


def join(near_up, near_down, far_up, far_down, order=(0, 1, 2, 3)):
    values = [near_up, near_down, far_up, far_down]
    vmem = pl.BlockSpec(memory_space=pltpu.VMEM)
    shape = (2 * near_up.shape[0],) + near_up.shape[1:]
    return pl.pallas_call(
        functools.partial(join_kernel, tuple(order)),
        out_shape=[jax.ShapeDtypeStruct(shape, BF)] * 2,
        in_specs=[vmem] * 4,
        out_specs=[vmem] * 2,
        compiler_params=pltpu.CompilerParams(vmem_limit_bytes=16 * 2**20),
        cost_estimate=expected(0.05),
        name="join",
    )(*[values[k] for k in order])


def swap(value, j):
    parts = lax.axis_size("seg")
    return lax.ppermute(value, "seg", [(i, i ^ j) for i in range(parts)])


def exchange(pieces):
    return [pieces[0]] + [swap(pieces[j], j) for j in range(1, len(pieces))]


def after(value, others):
    return lax.optimization_barrier((value, others))[0]


def per_device(records, plan):
    stations, windows, length = records.shape
    count = lax.axis_size("sta")
    parts = lax.axis_size("seg")
    quarter = stations // parts
    constants = make_table(length // CHUNKS, 2 * length)
    table, lag_table = jnp.asarray(constants), jnp.asarray(constants.T.copy())
    scaling = 1.0 / math.sqrt(4.0 * NBIN * windows * parts)

    white, *quarters = prepare(records, table, parts)
    near = jnp.concatenate([quarters[0], swap(quarters[1], 1)])
    sibling = swap(white, 1)
    far = jnp.concatenate([swap(quarters[j], j) for j in range(2, parts)])
    far = after(far, sibling)
    far, white_far = lax.optimization_barrier((far, white))
    across = swap(white_far, 2)

    ring = sorted(range(count), key=lambda b: b // 2 if b % 2 == 0 else count - 1 - b // 2)
    upward = [(ring[i], ring[(i + 1) % count]) for i in range(count)]
    downward = [(ring[i], ring[i - 1]) for i in range(count)]

    def up(value):
        return lax.ppermute(value, "sta", upward)

    def down(value):
        return lax.ppermute(value, "sta", downward)

    far, white_far = lax.optimization_barrier((far, white))
    across = swap(white_far, 2)
    near_own = widen_own([white, sibling])
    half = near.shape[0]
    places, blocks, arrived = [], [], []

    def arrive(step, first, from_left, from_right):
        places.extend([(count - step, first), (step, first)])
        blocks.extend([from_left, from_right])

    near_up, near_down = up(near), down(near)
    far_up, far_down = up(far), down(far)
    arrive(1, 0, near_up, near_down)
    arrive(1, half, far_up, far_down)
    near_up, near_down, near_own = lax.optimization_barrier((near_up, near_down, near_own))
    near_up, near_down = up(near_up), down(near_down)
    far_up, far_down = lax.optimization_barrier((far_up, far_down))
    far_up, far_down = up(far_up), down(far_down)
    arrive(2, 0, near_up, near_down)
    arrive(2, half, far_up, far_down)
    all_up, all_down = join(near_up, near_down, far_up, far_down)
    for step in range(3, (count - 1) // 2 + 1):
        arrived.append((list(places), list(blocks)))
        all_up, all_down, across = lax.optimization_barrier((all_up, all_down, across))
        all_up, all_down = up(all_up), down(all_down)
        arrive(step, 0, all_up, all_down)
    arrived.append((list(places), list(blocks)))
    far_own = widen_own([across, swap(across, 1)])
    groups = [(0, 1), (1, 2), (3, 1)]
    if count % 2 == 0:
        places.append((count // 2, 0))
        blocks.append(up(all_up))
    arrived.append((places, blocks))
    pieces = []
    for index, (first_slot, slots) in enumerate(groups):
        if index == 2:
            near_own = after(near_own, pieces[:parts])
        if index > 0:
            near_own = after(near_own, lags)
        at, values = arrived[index - len(groups)]
        lags = cross_lags(
            plan, lag_table, [near_own, far_own], at, values, first_slot, slots, count, parts, scaling
        )
        pieces = pieces + exchange(lags)
    return place_lags(plan, groups, pieces, count, stations, parts)


def solution(mesh):
    in_specs = (P("sta", "seg", None), P())
    out_specs = P("seg", None, "sta")
    return jax.shard_map(
        per_device, mesh=mesh, in_specs=in_specs, out_specs=out_specs, check_vma=False
    )
```

```python
import functools
import math

import jax
import jax.numpy as jnp
import ml_dtypes
import numpy as np
from jax import lax
from jax.experimental import pallas as pl
from jax.experimental.pallas import tpu as pltpu
from jax.sharding import PartitionSpec as P

NBIN = 1024
HALF = 64
ROUNDS = 4
LAGS = 2048
LANES = 128
TILES = NBIN // LANES
CHUNKS = 4
GROUP = 8
BF = jnp.bfloat16
F32 = jnp.float32


def make_table(rows, transform):
    phase = (np.arange(rows)[:, None] * np.arange(NBIN)[None, :]) % transform
    angle = phase * (2.0 * math.pi / transform)
    return np.concatenate([np.cos(angle), -np.sin(angle)], axis=1).astype(ml_dtypes.bfloat16)


def band_matrix():
    source = lax.broadcasted_iota(jnp.int32, (3 * LANES, LANES), 0) - LANES
    target = lax.broadcasted_iota(jnp.int32, (3 * LANES, LANES), 1)
    return jnp.where(jnp.abs(source - target) <= HALF, 1.0, 0.0).astype(BF)


def inverse_count(block, length):
    if 0 < block < length // LANES - 1:
        return 1.0 / (2 * HALF + 1)
    position = lax.broadcasted_iota(jnp.int32, (1, LANES), 1) + block * LANES
    counted = jnp.minimum(position, HALF) + jnp.minimum(length - 1 - position, HALF) + 1
    return 1.0 / counted.astype(F32)


def make_placing(stations, quarter, parts):
    width = stations * quarter
    place = np.zeros((parts, 2 * width, 2 * stations * stations), np.float32)
    for part in range(parts):
        for second in range(2):
            for s in range(stations):
                for t in range(quarter):
                    row = second * width + s * quarter + t
                    column = (second * stations + s) * stations + part * quarter + t
                    place[part, row, column] = 1.0
    return place.astype(ml_dtypes.bfloat16)


def lane_cycle(values):
    period = len(values)
    phase = lax.broadcasted_iota(jnp.int32, (1, LANES), 1) % period
    out = jnp.full((1, LANES), values[-1], F32)
    for index in range(period - 1):
        out = jnp.where(phase == index, values[index], out)
    return out


def even_lanes(shape):
    return lax.broadcasted_iota(jnp.int32, shape, 1) % 2 == 0


def eighth_turn():
    turns = [math.pi * k / 4.0 for k in range(8)]
    return lane_cycle([math.cos(t) for t in turns]), lane_cycle([math.sin(t) for t in turns])


def quarter_turns(real, imag, even, sign_real, sign_imag):
    return sign_real * jnp.where(even, real, imag), sign_imag * jnp.where(even, imag, real)


def banded_sum(stack, values, band):
    blocks, rows = len(values), values[0].shape[0]
    zero = jnp.zeros((rows, LANES), BF)
    for j in range(blocks):
        at = pl.ds(j * rows, rows)
        for k in range(3):
            b = j + k - 1
            block = values[b] if 0 <= b < blocks else zero
            stack[at, k * LANES : (k + 1) * LANES] = block
    total = jnp.dot(stack[: blocks * rows, :], band, preferred_element_type=F32)
    return [total[j * rows : (j + 1) * rows, :] for j in range(blocks)]


def prep_kernel(parts, windows, records_hbm, table_hbm, white, mine, *rest):
    others = rest[: parts - 1]
    records, table, stack, flat, spread, sems = rest[parts - 1 :]
    records_copy = pltpu.make_async_copy(records_hbm, records, sems.at[0])
    records_copy.start()
    copy = pltpu.make_async_copy(table_hbm, table, sems.at[1])
    copy.start()
    band_values = band_matrix()
    records_copy.wait()
    stations = white.shape[1]
    rows = stations * windows
    blocks = records.shape[0] // rows
    length = blocks * LANES
    chunk = length // CHUNKS
    signal = [
        jnp.concatenate(
            [
                records[pl.ds(j * windows + w, stations, stride=blocks * windows), :]
                for w in range(windows)
            ],
            axis=0,
        )
        for j in range(blocks)
    ]
    sums = banded_sum(stack, [jnp.abs(block).astype(BF) for block in signal], band_values)
    for j, total in enumerate(sums):
        at = slice(j * LANES, (j + 1) * LANES)
        level = total * inverse_count(j, length)
        value = (signal[j] / (level + 1e-05)).astype(BF)
        q, inside = divmod(j * LANES, chunk)
        flat[q * rows : (q + 1) * rows, inside : inside + LANES] = value
    copy.wait()
    product = jnp.dot(flat[...], table[...], preferred_element_type=F32)
    even = even_lanes((rows, LANES))
    sign_real = lane_cycle([1.0, 1.0, -1.0, -1.0])
    sign_imag = lane_cycle([1.0, -1.0, -1.0, 1.0])
    cosine, sine = eighth_turn()
    reals, imags, mags = [], [], []
    for j in range(TILES):
        at = slice(j * LANES, (j + 1) * LANES)
        at_imag = slice(NBIN + j * LANES, NBIN + (j + 1) * LANES)
        pr = [product[q * rows : (q + 1) * rows, at] for q in range(CHUNKS)]
        pi = [product[q * rows : (q + 1) * rows, at_imag] for q in range(CHUNKS)]
        turned = [
            quarter_turns(pr[q], pi[q], even, sign_real, sign_imag) for q in range(2, CHUNKS)
        ]
        first_real, first_imag = pr[0] + turned[0][0], pi[0] + turned[0][1]
        odd_real, odd_imag = pr[1] + turned[1][0], pi[1] + turned[1][1]
        real = first_real + (odd_real * cosine + odd_imag * sine)
        imag = first_imag + (odd_imag * cosine - odd_real * sine)
        reals.append(real)
        imags.append(imag)
        mags.append(jnp.sqrt(real * real + imag * imag).astype(BF))
    sums = banded_sum(stack, mags, band_values)
    for j, total in enumerate(sums):
        at = slice(j * LANES, (j + 1) * LANES)
        inverse = 1.0 / (total * inverse_count(j, NBIN) + 1e-06)
        spread[pl.ds(j, rows, stride=2 * TILES), :] = reals[j] * inverse
        spread[pl.ds(TILES + j, rows, stride=2 * TILES), :] = imags[j] * inverse
    me = lax.axis_index("seg")
    quarter = stations // parts
    white[...] = spread[...].reshape(windows, stations, 2 * TILES, LANES).astype(BF)
    for j, out in enumerate((mine, *others)):
        for w in range(windows):
            out[w] = white[w, pl.ds((me ^ j) * quarter, quarter)]


def prepare(records, table, parts):
    stations, windows, length = records.shape
    rows = stations * windows
    quarter = stations // parts
    blocks = length // LANES
    flat_records = records.reshape(stations, windows, blocks, LANES).transpose(0, 2, 1, 3)
    flat_records = flat_records.reshape(rows * blocks, LANES)
    small = jax.ShapeDtypeStruct((windows, quarter, 2 * TILES, LANES), BF)
    vmem = pl.BlockSpec(memory_space=pltpu.VMEM)
    return pl.pallas_call(
        functools.partial(prep_kernel, parts, windows),
        out_shape=[jax.ShapeDtypeStruct((windows, stations, 2 * TILES, LANES), BF)]
        + [small] * parts,
        in_specs=[pl.BlockSpec(memory_space=pltpu.HBM)] * 2,
        out_specs=[vmem] * (1 + parts),
        scratch_shapes=[
            pltpu.VMEM(flat_records.shape, F32),
            pltpu.VMEM(table.shape, BF),
            pltpu.VMEM((rows * (length // LANES), 3 * LANES), BF),
            pltpu.VMEM((CHUNKS * rows, length // CHUNKS), BF),
            pltpu.VMEM((rows * 2 * TILES, LANES), F32),
            pltpu.SemaphoreType.DMA((2,)),
        ],
        compiler_params=pltpu.CompilerParams(vmem_limit_bytes=52 * 2**20),
        cost_estimate=pl.CostEstimate(
            flops=2 * rows * length * 2 * NBIN, bytes_accessed=3 * 2**20, transcendentals=0
        ),
        name="prep",
    )(
        pltpu.with_memory_space_constraint(flat_records, pltpu.HBM),
        pltpu.with_memory_space_constraint(table, pltpu.HBM),
    )


def ring_place(block, count):
    half = block >> 1
    return jnp.where((block & 1) == 0, half, count - 1 - half)


def partner_steps(plan, count):
    me = lax.axis_index("sta")
    mine = ring_place(me, count)
    steps, keys = [], []
    for number in range(ROUNDS):
        step = ring_place(plan[number, me], count) - mine
        step = jnp.where(step < 0, step + count, step)
        steps.append(step)
        keys.append(jnp.minimum(step, count - step) * ROUNDS + number)
    ranks = []
    for number in range(ROUNDS):
        rank = jnp.int32(0)
        for other in range(ROUNDS):
            if other != number:
                rank = rank + jnp.where(keys[other] < keys[number], 1, 0)
        ranks.append(rank)
    return steps, ranks


def expected(microseconds):
    return pl.CostEstimate(
        flops=int(microseconds * 1.15e9), bytes_accessed=1024, transcendentals=0
    )


def widen_kernel(*refs):
    blocks, own = refs[:-1], refs[-1]
    windows = blocks[0].shape[0]
    for j, block in enumerate(blocks):

        def widen(w, carry, j=j, block=block):
            raw = block[w].astype(F32)
            real, imag = raw[:, :TILES], raw[:, TILES:]
            both = real + imag
            for group in range(own.shape[0]):
                at = slice(group * GROUP, (group + 1) * GROUP)
                own[group, 0, j * windows + w] = both[at]
                own[group, 1, j * windows + w] = real[at]
                own[group, 2, j * windows + w] = imag[at]
            return carry

        lax.fori_loop(0, windows, widen, 0)


def widen_own(blocks):
    windows, stations = blocks[0].shape[:2]
    vmem = pl.BlockSpec(memory_space=pltpu.VMEM)
    return pl.pallas_call(
        widen_kernel,
        out_shape=jax.ShapeDtypeStruct(
            (stations // GROUP, 3, len(blocks) * windows, GROUP, TILES, LANES), F32
        ),
        in_specs=[vmem] * len(blocks),
        out_specs=vmem,
        compiler_params=pltpu.CompilerParams(vmem_limit_bytes=16 * 2**20),
        cost_estimate=expected(0.05),
        name="widen",
    )(*blocks)


def widen_others(first_slot, slots, count, places, plan, candidates, other):
    steps, ranks = partner_steps(plan, count)
    for slot in range(slots):
        step = jnp.int32(0)
        for number in range(ROUNDS):
            step = jnp.where(ranks[number] == first_slot + slot, steps[number], step)
        for (offset, first), candidate in zip(places, candidates):

            @pl.when(step == offset)
            def _(candidate=candidate, slot=slot, first=first):
                def widen_other(w, carry):
                    raw = candidate[w].astype(F32)
                    real, imag = raw[:, :TILES], raw[:, TILES:]
                    other[0, slot, first + w] = real
                    other[1, slot, first + w] = real + imag
                    other[2, slot, first + w] = imag - real
                    return carry

                lax.fori_loop(0, candidate.shape[0], widen_other, 0)


def sum_windows(owns, other, summed):
    groups, _, windows, group = owns[0].shape[:4]
    slots, _, quarter = other.shape[1:4]
    width = groups * group * quarter
    shift = groups.bit_length() - 1

    for slot in range(slots):

        def body(index, carry, slot=slot):
            kind, part = index >> shift, index & (groups - 1)
            mine = [own.at[part, kind] for own in owns]
            theirs = other.at[kind, slot]
            totals = [None] * (group * quarter)
            for half, own in enumerate(mine):
                for w in range(windows):
                    left = [own[w, s] for s in range(group)]
                    right = [theirs[half * windows + w, t] for t in range(quarter)]
                    for s in range(group):
                        for t in range(quarter):
                            term = left[s] * right[t]
                            old = totals[s * quarter + t]
                            totals[s * quarter + t] = term if old is None else old + term
            rows = summed.at[kind]
            base = (slot * width + part * (group * quarter)) * TILES
            for place in range(group * quarter):
                at = pl.multiple_of(base + place * TILES, TILES)
                rows[pl.ds(at, TILES), :] = totals[place]
            return carry

        lax.fori_loop(0, 3 * groups, body, 0)


def cross_kernel(first_slot, slots, count, scaling, places, parts, plan, table, *rest):
    owns, rest = rest[:2], rest[2:]
    others, rest = rest[: len(places)], rest[len(places) :]
    outs = rest[:parts]
    other, summed, operand, result = rest[parts:]
    stations = owns[0].shape[0] * owns[0].shape[3]
    widen_others(first_slot, slots, count, places, plan, others, other)
    sum_windows(owns, other, summed)
    width = stations * other.shape[3]
    columns = slots * width
    even = even_lanes((columns, LANES))
    sign_real = lane_cycle([1.0, -1.0, -1.0, 1.0])
    sign_imag = lane_cycle([1.0, 1.0, -1.0, -1.0])
    cosine, sine = eighth_turn()
    lane = lax.broadcasted_iota(jnp.int32, (1, LANES), 1)
    first_weight = jnp.where(lane == 0, 0.5, 1.0).astype(F32)
    for j in range(TILES):
        at = slice(j * LANES, (j + 1) * LANES)
        at_imag = slice(NBIN + j * LANES, NBIN + (j + 1) * LANES)
        kinds = [summed[kind, pl.ds(j, columns, stride=TILES), :] for kind in range(3)]
        real, imag = kinds[0] + kinds[2], kinds[0] - kinds[1]
        if j == 0:
            real, imag = real * first_weight, imag * first_weight
        turned = [(real, imag), (real * cosine - imag * sine, imag * cosine + real * sine)]
        turned += [quarter_turns(r, i, even, sign_real, sign_imag) for r, i in turned]
        for q in range(CHUNKS):
            rows = slice(q * columns, (q + 1) * columns)
            operand[rows, at] = turned[q][0].astype(BF)
            operand[rows, at_imag] = turned[q][1].astype(BF)
    block = jnp.dot(operand[...], table[...], preferred_element_type=F32)
    block = block * (2.0 * scaling)
    for q in range(CHUNKS):
        result[q] = block[q * columns : (q + 1) * columns].astype(BF)
    me = lax.axis_index("seg")
    for j in range(parts):
        outs[j][...] = result[me ^ j]


def cross_lags(plan, table, owns, places, candidates, first_slot, slots, count, parts, scaling):
    windows, stations = owns[0].shape[2], owns[0].shape[0] * owns[0].shape[3]
    quarter = candidates[0].shape[1]
    columns = slots * stations * quarter
    share = LAGS // parts
    out = (columns, share)
    smem = pl.BlockSpec(memory_space=pltpu.SMEM)
    vmem = pl.BlockSpec(memory_space=pltpu.VMEM)
    operands = [table, *owns, *candidates]
    return pl.pallas_call(
        functools.partial(
            cross_kernel, first_slot, slots, count, scaling, tuple(places), parts
        ),
        out_shape=[jax.ShapeDtypeStruct(out, BF)] * parts,
        in_specs=[smem] + [vmem] * len(operands),
        out_specs=[vmem] * parts,
        scratch_shapes=[
            pltpu.VMEM((3, slots, 2 * windows, quarter, TILES, LANES), F32),
            pltpu.VMEM((3, columns * TILES, LANES), F32),
            pltpu.VMEM((CHUNKS * columns, 2 * NBIN), BF),
            pltpu.VMEM((parts,) + out, BF),
        ],
        compiler_params=pltpu.CompilerParams(vmem_limit_bytes=24 * 2**20),
        cost_estimate=expected(0.6 + 2.0 * slots),
        name="cross",
    )(plan, *operands)


def slot_rounds(plan, count):
    _, ranks = partner_steps(plan, count)
    rounds = []
    for slot in range(ROUNDS):
        number = jnp.int32(0)
        for other in range(1, ROUNDS):
            number = jnp.where(ranks[other] == slot, other, number)
        rounds.append(number)
    return rounds


def placed_block(pieces, matrix, at):
    joined = jnp.concatenate([piece[:, at] for piece in pieces], axis=0)
    return lax.dot_general(
        joined, matrix, (((0,), (0,)), ((), ())), preferred_element_type=F32
    )


def joined_matrix(place, parts, slots):
    me = lax.axis_index("seg")
    rows, columns = place.shape[1] * slots // 2, place.shape[2] * slots // 2
    return jnp.concatenate([place[me ^ j, :rows, :columns] for j in range(parts)], axis=0)


def store_rows(rows, block, first):
    tiles = block.shape[1] // LANES
    for tile in range(tiles):
        at = pl.ds(first * tiles + tile, block.shape[0], stride=tiles)
        rows[at, :] = block[:, tile * LANES : (tile + 1) * LANES]


def early_kernel(count, parts, groups, plan, place, *rest):
    pieces = rest[:-3]
    out_hbm, rows, sems = rest[-3:]
    pairs = place.shape[2] // 2
    rounds = slot_rounds(plan, count)
    copies = []
    for index, (first_slot, slots) in enumerate(groups):
        own = pieces[index * parts : (index + 1) * parts]
        block = placed_block(own, joined_matrix(place, parts, slots), slice(None))
        for slot in range(slots):
            number = first_slot + slot
            store_rows(rows.at[number], block[:, slot * pairs : (slot + 1) * pairs], 0)
            copy = pltpu.make_async_copy(
                rows.at[number], out_hbm.at[:, rounds[number], 0], sems.at[number]
            )
            copy.start()
            copies.append(copy)
    for copy in copies:
        copy.wait()


def late_kernel(count, parts, plan, place, early, *rest):
    pieces = rest[:parts]
    out_hbm, rows, sems = rest[parts:]
    number = slot_rounds(plan, count)[ROUNDS - 1]
    matrix = joined_matrix(place, parts, 1)
    half = pieces[0].shape[1] // 2
    size = rows.shape[0] // 2
    copies = []
    for h in range(2):
        block = placed_block(pieces, matrix, slice(h * half, (h + 1) * half))
        store_rows(rows, block, h * half)
        at = pl.ds(h * size, size)
        copy = pltpu.make_async_copy(rows.at[at], out_hbm.at[at, number, 0], sems.at[h])
        copy.start()
        copies.append(copy)
    for copy in copies:
        copy.wait()


def place_lags(plan, groups, pieces, count, stations, parts):
    pairs = stations * stations
    share = LAGS // parts
    tiles = pairs // LANES
    place = jnp.asarray(make_placing(stations, stations // parts, parts))
    smem = pl.BlockSpec(memory_space=pltpu.SMEM)
    vmem = pl.BlockSpec(memory_space=pltpu.VMEM)
    anywhere = pl.BlockSpec(memory_space=pl.ANY)
    shape = jax.ShapeDtypeStruct((share * tiles, ROUNDS, 1, LANES), F32)
    early = pl.pallas_call(
        functools.partial(early_kernel, count, parts, tuple(groups[:-1])),
        out_shape=shape,
        in_specs=[smem] + [vmem] * (1 + len(pieces) - parts),
        out_specs=anywhere,
        scratch_shapes=[
            pltpu.VMEM((ROUNDS - 1, share * tiles, LANES), F32),
            pltpu.SemaphoreType.DMA((ROUNDS - 1,)),
        ],
        compiler_params=pltpu.CompilerParams(vmem_limit_bytes=16 * 2**20),
        cost_estimate=expected(0.05),
        name="early",
    )(plan, place, *pieces[:-parts])
    out = pl.pallas_call(
        functools.partial(late_kernel, count, parts),
        out_shape=shape,
        in_specs=[smem, vmem, anywhere] + [vmem] * parts,
        out_specs=anywhere,
        scratch_shapes=[pltpu.VMEM((share * tiles, LANES), F32), pltpu.SemaphoreType.DMA((2,))],
        input_output_aliases={2: 0},
        compiler_params=pltpu.CompilerParams(vmem_limit_bytes=16 * 2**20),
        cost_estimate=expected(0.05),
        name="late",
    )(plan, place, early, *pieces[-parts:])
    out = out.reshape(share, tiles, ROUNDS, LANES)
    return out.transpose(0, 2, 1, 3).reshape(share, ROUNDS, pairs)


def join_kernel(order, *refs):
    parts, (out_up, out_down) = refs[:4], refs[4:]
    near_up, near_down, far_up, far_down = [parts[order.index(k)] for k in range(4)]
    half = near_up.shape[0]
    for out, first, second in ((out_up, near_up, far_up), (out_down, near_down, far_down)):
        out[:half] = first[...]
        out[half:] = second[...]


def join(near_up, near_down, far_up, far_down, order=(0, 1, 2, 3)):
    values = [near_up, near_down, far_up, far_down]
    vmem = pl.BlockSpec(memory_space=pltpu.VMEM)
    shape = (2 * near_up.shape[0],) + near_up.shape[1:]
    return pl.pallas_call(
        functools.partial(join_kernel, tuple(order)),
        out_shape=[jax.ShapeDtypeStruct(shape, BF)] * 2,
        in_specs=[vmem] * 4,
        out_specs=[vmem] * 2,
        compiler_params=pltpu.CompilerParams(vmem_limit_bytes=16 * 2**20),
        cost_estimate=expected(0.05),
        name="join",
    )(*[values[k] for k in order])


def swap(value, j):
    parts = lax.axis_size("seg")
    return lax.ppermute(value, "seg", [(i, i ^ j) for i in range(parts)])


def exchange(pieces):
    return [pieces[0]] + [swap(pieces[j], j) for j in range(1, len(pieces))]


def after(value, others):
    return lax.optimization_barrier((value, others))[0]


def per_device(records, plan):
    stations, windows, length = records.shape
    count = lax.axis_size("sta")
    parts = lax.axis_size("seg")
    quarter = stations // parts
    constants = make_table(length // CHUNKS, 2 * length)
    table, lag_table = jnp.asarray(constants), jnp.asarray(constants.T.copy())
    scaling = 1.0 / math.sqrt(4.0 * NBIN * windows * parts)

    white, *quarters = prepare(records, table, parts)
    near = jnp.concatenate([quarters[0], swap(quarters[1], 1)])
    sibling = swap(white, 1)
    far = jnp.concatenate([swap(quarters[j], j) for j in range(2, parts)])
    far = after(far, sibling)
    far, white_far = lax.optimization_barrier((far, white))
    across = swap(white_far, 2)

    ring = sorted(range(count), key=lambda b: b // 2 if b % 2 == 0 else count - 1 - b // 2)
    upward = [(ring[i], ring[(i + 1) % count]) for i in range(count)]
    downward = [(ring[i], ring[i - 1]) for i in range(count)]

    def up(value):
        return lax.ppermute(value, "sta", upward)

    def down(value):
        return lax.ppermute(value, "sta", downward)

    far, white_far = lax.optimization_barrier((far, white))
    across = swap(white_far, 2)
    near_own = widen_own([white, sibling])
    half = near.shape[0]
    places, blocks, arrived = [], [], []

    def arrive(step, first, from_left, from_right):
        places.extend([(count - step, first), (step, first)])
        blocks.extend([from_left, from_right])

    near_up, near_down = up(near), down(near)
    far_up, far_down = up(far), down(far)
    arrive(1, 0, near_up, near_down)
    arrive(1, half, far_up, far_down)
    near_up, near_down, near_own = lax.optimization_barrier((near_up, near_down, near_own))
    near_up, near_down = up(near_up), down(near_down)
    far_up, far_down = lax.optimization_barrier((far_up, far_down))
    far_up, far_down = up(far_up), down(far_down)
    arrive(2, 0, near_up, near_down)
    arrive(2, half, far_up, far_down)
    all_up, all_down = join(near_up, near_down, far_up, far_down)
    for step in range(3, (count - 1) // 2 + 1):
        arrived.append((list(places), list(blocks)))
        all_up, all_down, across = lax.optimization_barrier((all_up, all_down, across))
        all_up, all_down = up(all_up), down(all_down)
        arrive(step, 0, all_up, all_down)
    arrived.append((list(places), list(blocks)))
    far_own = widen_own([across, swap(across, 1)])
    groups = [(0, 1), (1, 2), (3, 1)]
    if count % 2 == 0:
        places.append((count // 2, 0))
        blocks.append(up(all_up))
    arrived.append((places, blocks))
    pieces = []
    for index, (first_slot, slots) in enumerate(groups):
        if index == 2:
            near_own = after(near_own, pieces[:parts])
        if index > 0:
            near_own = after(near_own, lags)
        at, values = arrived[index - len(groups)]
        lags = cross_lags(
            plan, lag_table, [near_own, far_own], at, values, first_slot, slots, count, parts, scaling
        )
        pieces = pieces + exchange(lags)
    return place_lags(plan, groups, pieces, count, stations, parts)


def solution(mesh):
    in_specs = (P("sta", "seg", None), P())
    out_specs = P("seg", None, "sta")
    return jax.shard_map(
        per_device, mesh=mesh, in_specs=in_specs, out_specs=out_specs, check_vma=False
    )
```

```python
import functools
import math

import jax
import jax.numpy as jnp
import ml_dtypes
import numpy as np
from jax import lax
from jax.experimental import pallas as pl
from jax.experimental.pallas import tpu as pltpu
from jax.sharding import PartitionSpec as P

NBIN = 1024
HALF = 64
ROUNDS = 4
LAGS = 2048
LANES = 128
TILES = NBIN // LANES
CHUNKS = 4
GROUP = 8
BF = jnp.bfloat16
F32 = jnp.float32


def make_table(rows, transform):
    phase = (np.arange(rows)[:, None] * np.arange(NBIN)[None, :]) % transform
    angle = phase * (2.0 * math.pi / transform)
    return np.concatenate([np.cos(angle), -np.sin(angle)], axis=1).astype(ml_dtypes.bfloat16)


def band_matrix():
    source = lax.broadcasted_iota(jnp.int32, (3 * LANES, LANES), 0) - LANES
    target = lax.broadcasted_iota(jnp.int32, (3 * LANES, LANES), 1)
    return jnp.where(jnp.abs(source - target) <= HALF, 1.0, 0.0).astype(BF)


def inverse_count(block, length):
    if 0 < block < length // LANES - 1:
        return 1.0 / (2 * HALF + 1)
    position = lax.broadcasted_iota(jnp.int32, (1, LANES), 1) + block * LANES
    counted = jnp.minimum(position, HALF) + jnp.minimum(length - 1 - position, HALF) + 1
    return 1.0 / counted.astype(F32)


def make_placing(stations, quarter, parts):
    width = stations * quarter
    place = np.zeros((parts, 2 * width, 2 * stations * stations), np.float32)
    for part in range(parts):
        for second in range(2):
            for s in range(stations):
                for t in range(quarter):
                    row = second * width + s * quarter + t
                    column = (second * stations + s) * stations + part * quarter + t
                    place[part, row, column] = 1.0
    return place.astype(ml_dtypes.bfloat16)


def lane_cycle(values):
    period = len(values)
    phase = lax.broadcasted_iota(jnp.int32, (1, LANES), 1) % period
    out = jnp.full((1, LANES), values[-1], F32)
    for index in range(period - 1):
        out = jnp.where(phase == index, values[index], out)
    return out


def even_lanes(shape):
    return lax.broadcasted_iota(jnp.int32, shape, 1) % 2 == 0


def eighth_turn():
    turns = [math.pi * k / 4.0 for k in range(8)]
    return lane_cycle([math.cos(t) for t in turns]), lane_cycle([math.sin(t) for t in turns])


def quarter_turns(real, imag, even, sign_real, sign_imag):
    return sign_real * jnp.where(even, real, imag), sign_imag * jnp.where(even, imag, real)


def banded_sum(stack, values, band):
    blocks, rows = len(values), values[0].shape[0]
    zero = jnp.zeros((rows, LANES), BF)
    for j in range(blocks):
        at = pl.ds(j * rows, rows)
        for k in range(3):
            b = j + k - 1
            block = values[b] if 0 <= b < blocks else zero
            stack[at, k * LANES : (k + 1) * LANES] = block
    total = jnp.dot(stack[: blocks * rows, :], band, preferred_element_type=F32)
    return [total[j * rows : (j + 1) * rows, :] for j in range(blocks)]


def prep_kernel(parts, windows, records_hbm, table_hbm, white, mine, *rest):
    others = rest[: parts - 1]
    records, table, stack, flat, spread, sems = rest[parts - 1 :]
    records_copy = pltpu.make_async_copy(records_hbm, records, sems.at[0])
    records_copy.start()
    copy = pltpu.make_async_copy(table_hbm, table, sems.at[1])
    copy.start()
    band_values = band_matrix()
    records_copy.wait()
    stations = white.shape[1]
    rows = stations * windows
    blocks = records.shape[0] // rows
    length = blocks * LANES
    chunk = length // CHUNKS
    signal = [
        jnp.concatenate(
            [
                records[pl.ds(j * windows + w, stations, stride=blocks * windows), :]
                for w in range(windows)
            ],
            axis=0,
        )
        for j in range(blocks)
    ]
    sums = banded_sum(stack, [jnp.abs(block).astype(BF) for block in signal], band_values)
    for j, total in enumerate(sums):
        at = slice(j * LANES, (j + 1) * LANES)
        level = total * inverse_count(j, length)
        value = (signal[j] / (level + 1e-05)).astype(BF)
        q, inside = divmod(j * LANES, chunk)
        flat[q * rows : (q + 1) * rows, inside : inside + LANES] = value
    copy.wait()
    product = jnp.dot(flat[...], table[...], preferred_element_type=F32)
    even = even_lanes((rows, LANES))
    sign_real = lane_cycle([1.0, 1.0, -1.0, -1.0])
    sign_imag = lane_cycle([1.0, -1.0, -1.0, 1.0])
    cosine, sine = eighth_turn()
    reals, imags, mags = [], [], []
    for j in range(TILES):
        at = slice(j * LANES, (j + 1) * LANES)
        at_imag = slice(NBIN + j * LANES, NBIN + (j + 1) * LANES)
        pr = [product[q * rows : (q + 1) * rows, at] for q in range(CHUNKS)]
        pi = [product[q * rows : (q + 1) * rows, at_imag] for q in range(CHUNKS)]
        turned = [
            quarter_turns(pr[q], pi[q], even, sign_real, sign_imag) for q in range(2, CHUNKS)
        ]
        first_real, first_imag = pr[0] + turned[0][0], pi[0] + turned[0][1]
        odd_real, odd_imag = pr[1] + turned[1][0], pi[1] + turned[1][1]
        real = first_real + (odd_real * cosine + odd_imag * sine)
        imag = first_imag + (odd_imag * cosine - odd_real * sine)
        reals.append(real)
        imags.append(imag)
        mags.append(jnp.sqrt(real * real + imag * imag).astype(BF))
    sums = banded_sum(stack, mags, band_values)
    for j, total in enumerate(sums):
        at = slice(j * LANES, (j + 1) * LANES)
        inverse = 1.0 / (total * inverse_count(j, NBIN) + 1e-06)
        spread[pl.ds(j, rows, stride=2 * TILES), :] = reals[j] * inverse
        spread[pl.ds(TILES + j, rows, stride=2 * TILES), :] = imags[j] * inverse
    me = lax.axis_index("seg")
    quarter = stations // parts
    white[...] = spread[...].reshape(windows, stations, 2 * TILES, LANES).astype(BF)
    for j, out in enumerate((mine, *others)):
        for w in range(windows):
            out[w] = white[w, pl.ds((me ^ j) * quarter, quarter)]


def prepare(records, table, parts):
    stations, windows, length = records.shape
    rows = stations * windows
    quarter = stations // parts
    blocks = length // LANES
    flat_records = records.reshape(stations, windows, blocks, LANES).transpose(0, 2, 1, 3)
    flat_records = flat_records.reshape(rows * blocks, LANES)
    small = jax.ShapeDtypeStruct((windows, quarter, 2 * TILES, LANES), BF)
    vmem = pl.BlockSpec(memory_space=pltpu.VMEM)
    return pl.pallas_call(
        functools.partial(prep_kernel, parts, windows),
        out_shape=[jax.ShapeDtypeStruct((windows, stations, 2 * TILES, LANES), BF)]
        + [small] * parts,
        in_specs=[pl.BlockSpec(memory_space=pltpu.HBM)] * 2,
        out_specs=[vmem] * (1 + parts),
        scratch_shapes=[
            pltpu.VMEM(flat_records.shape, F32),
            pltpu.VMEM(table.shape, BF),
            pltpu.VMEM((rows * (length // LANES), 3 * LANES), BF),
            pltpu.VMEM((CHUNKS * rows, length // CHUNKS), BF),
            pltpu.VMEM((rows * 2 * TILES, LANES), F32),
            pltpu.SemaphoreType.DMA((2,)),
        ],
        compiler_params=pltpu.CompilerParams(vmem_limit_bytes=52 * 2**20),
        cost_estimate=pl.CostEstimate(
            flops=2 * rows * length * 2 * NBIN, bytes_accessed=3 * 2**20, transcendentals=0
        ),
        name="prep",
    )(
        pltpu.with_memory_space_constraint(flat_records, pltpu.HBM),
        pltpu.with_memory_space_constraint(table, pltpu.HBM),
    )


def ring_place(block, count):
    half = block >> 1
    return jnp.where((block & 1) == 0, half, count - 1 - half)


def partner_steps(plan, count):
    me = lax.axis_index("sta")
    mine = ring_place(me, count)
    steps, keys = [], []
    for number in range(ROUNDS):
        step = ring_place(plan[number, me], count) - mine
        step = jnp.where(step < 0, step + count, step)
        steps.append(step)
        keys.append(jnp.minimum(step, count - step) * ROUNDS + number)
    ranks = []
    for number in range(ROUNDS):
        rank = jnp.int32(0)
        for other in range(ROUNDS):
            if other != number:
                rank = rank + jnp.where(keys[other] < keys[number], 1, 0)
        ranks.append(rank)
    return steps, ranks


def expected(microseconds):
    return pl.CostEstimate(
        flops=int(microseconds * 1.15e9), bytes_accessed=1024, transcendentals=0
    )


def widen_kernel(*refs):
    blocks, own = refs[:-1], refs[-1]
    windows = blocks[0].shape[0]
    for j, block in enumerate(blocks):

        def widen(w, carry, j=j, block=block):
            raw = block[w].astype(F32)
            real, imag = raw[:, :TILES], raw[:, TILES:]
            both = real + imag
            for group in range(own.shape[0]):
                at = slice(group * GROUP, (group + 1) * GROUP)
                own[group, 0, j * windows + w] = both[at]
                own[group, 1, j * windows + w] = real[at]
                own[group, 2, j * windows + w] = imag[at]
            return carry

        lax.fori_loop(0, windows, widen, 0)


def widen_own(blocks):
    windows, stations = blocks[0].shape[:2]
    vmem = pl.BlockSpec(memory_space=pltpu.VMEM)
    return pl.pallas_call(
        widen_kernel,
        out_shape=jax.ShapeDtypeStruct(
            (stations // GROUP, 3, len(blocks) * windows, GROUP, TILES, LANES), F32
        ),
        in_specs=[vmem] * len(blocks),
        out_specs=vmem,
        compiler_params=pltpu.CompilerParams(vmem_limit_bytes=16 * 2**20),
        cost_estimate=expected(0.05),
        name="widen",
    )(*blocks)


def widen_others(first_slot, slots, count, places, plan, candidates, other):
    steps, ranks = partner_steps(plan, count)
    for slot in range(slots):
        step = jnp.int32(0)
        for number in range(ROUNDS):
            step = jnp.where(ranks[number] == first_slot + slot, steps[number], step)
        for (offset, first), candidate in zip(places, candidates):

            @pl.when(step == offset)
            def _(candidate=candidate, slot=slot, first=first):
                def widen_other(turn, carry):
                    raw = candidate[pl.ds(turn * 4, 4)].astype(F32)
                    real, imag = raw[:, :, :TILES], raw[:, :, TILES:]
                    at = pl.ds(first + turn * 4, 4)
                    other[0, slot, at] = real
                    other[1, slot, at] = real + imag
                    other[2, slot, at] = imag - real
                    return carry

                lax.fori_loop(0, candidate.shape[0] // 4, widen_other, 0)


def sum_windows(owns, other, summed):
    groups, _, windows, group = owns[0].shape[:4]
    slots, _, quarter = other.shape[1:4]
    width = groups * group * quarter
    shift = groups.bit_length() - 1

    for slot in range(slots):

        def body(index, carry, slot=slot):
            kind, part = index >> shift, index & (groups - 1)
            mine = [own.at[part, kind] for own in owns]
            theirs = other.at[kind, slot]
            totals = [None] * (group * quarter)
            for half, own in enumerate(mine):
                for w in range(windows):
                    left = [own[w, s] for s in range(group)]
                    right = [theirs[half * windows + w, t] for t in range(quarter)]
                    for s in range(group):
                        for t in range(quarter):
                            term = left[s] * right[t]
                            old = totals[s * quarter + t]
                            totals[s * quarter + t] = term if old is None else old + term
            rows = summed.at[kind]
            base = (slot * width + part * (group * quarter)) * TILES
            for place in range(group * quarter):
                at = pl.multiple_of(base + place * TILES, TILES)
                rows[pl.ds(at, TILES), :] = totals[place]
            return carry

        lax.fori_loop(0, 3 * groups, body, 0)


def cross_kernel(first_slot, slots, count, scaling, places, parts, plan, table, *rest):
    owns, rest = rest[:2], rest[2:]
    others, rest = rest[: len(places)], rest[len(places) :]
    outs = rest[:parts]
    other, summed, operand = rest[parts:]
    stations = owns[0].shape[0] * owns[0].shape[3]
    widen_others(first_slot, slots, count, places, plan, others, other)
    sum_windows(owns, other, summed)
    width = stations * other.shape[3]
    columns = slots * width
    even = even_lanes((columns, LANES))
    sign_real = lane_cycle([1.0, -1.0, -1.0, 1.0])
    sign_imag = lane_cycle([1.0, 1.0, -1.0, -1.0])
    cosine, sine = eighth_turn()
    lane = lax.broadcasted_iota(jnp.int32, (1, LANES), 1)
    first_weight = jnp.where(lane == 0, 0.5, 1.0).astype(F32)
    for j in range(TILES):
        at = slice(j * LANES, (j + 1) * LANES)
        at_imag = slice(NBIN + j * LANES, NBIN + (j + 1) * LANES)
        kinds = [summed[kind, pl.ds(j, columns, stride=TILES), :] for kind in range(3)]
        real, imag = kinds[0] + kinds[2], kinds[0] - kinds[1]
        if j == 0:
            real, imag = real * first_weight, imag * first_weight
        turned = [(real, imag), (real * cosine - imag * sine, imag * cosine + real * sine)]
        turned += [quarter_turns(r, i, even, sign_real, sign_imag) for r, i in turned]
        for q in range(CHUNKS):
            rows = slice(q * columns, (q + 1) * columns)
            operand[rows, at] = turned[q][0].astype(BF)
            operand[rows, at_imag] = turned[q][1].astype(BF)
    block = jnp.dot(operand[...], table[...], preferred_element_type=F32)
    block = (block * (2.0 * scaling)).astype(BF)
    me = lax.axis_index("seg")
    for place in range(parts):

        @pl.when(me == place)
        def _(place=place):
            for j in range(parts):
                q = place ^ j
                outs[j][...] = block[q * columns : (q + 1) * columns]


def cross_lags(plan, table, owns, places, candidates, first_slot, slots, count, parts, scaling):
    windows, stations = owns[0].shape[2], owns[0].shape[0] * owns[0].shape[3]
    quarter = candidates[0].shape[1]
    columns = slots * stations * quarter
    share = LAGS // parts
    out = (columns, share)
    smem = pl.BlockSpec(memory_space=pltpu.SMEM)
    vmem = pl.BlockSpec(memory_space=pltpu.VMEM)
    operands = [table, *owns, *candidates]
    return pl.pallas_call(
        functools.partial(
            cross_kernel, first_slot, slots, count, scaling, tuple(places), parts
        ),
        out_shape=[jax.ShapeDtypeStruct(out, BF)] * parts,
        in_specs=[smem] + [vmem] * len(operands),
        out_specs=[vmem] * parts,
        scratch_shapes=[
            pltpu.VMEM((3, slots, 2 * windows, quarter, TILES, LANES), F32),
            pltpu.VMEM((3, columns * TILES, LANES), F32),
            pltpu.VMEM((CHUNKS * columns, 2 * NBIN), BF),
        ],
        compiler_params=pltpu.CompilerParams(vmem_limit_bytes=24 * 2**20),
        cost_estimate=expected(0.6 + 2.0 * slots),
        name="cross",
    )(plan, *operands)


def slot_rounds(plan, count):
    _, ranks = partner_steps(plan, count)
    rounds = []
    for slot in range(ROUNDS):
        number = jnp.int32(0)
        for other in range(1, ROUNDS):
            number = jnp.where(ranks[other] == slot, other, number)
        rounds.append(number)
    return rounds


def placed_block(pieces, matrix, at):
    joined = jnp.concatenate([piece[:, at] for piece in pieces], axis=0)
    return lax.dot_general(
        joined, matrix, (((0,), (0,)), ((), ())), preferred_element_type=F32
    )


def joined_matrix(place, parts, slots):
    me = lax.axis_index("seg")
    rows, columns = place.shape[1] * slots // 2, place.shape[2] * slots // 2
    return jnp.concatenate([place[me ^ j, :rows, :columns] for j in range(parts)], axis=0)


def store_rows(rows, block, first):
    tiles = block.shape[1] // LANES
    for tile in range(tiles):
        at = pl.ds(first * tiles + tile, block.shape[0], stride=tiles)
        rows[at, :] = block[:, tile * LANES : (tile + 1) * LANES]


def early_kernel(count, parts, groups, plan, place, *rest):
    pieces = rest[:-3]
    out_hbm, rows, sems = rest[-3:]
    pairs = place.shape[2] // 2
    rounds = slot_rounds(plan, count)
    copies = []
    for index, (first_slot, slots) in enumerate(groups):
        own = pieces[index * parts : (index + 1) * parts]
        block = placed_block(own, joined_matrix(place, parts, slots), slice(None))
        for slot in range(slots):
            number = first_slot + slot
            store_rows(rows.at[number], block[:, slot * pairs : (slot + 1) * pairs], 0)
            copy = pltpu.make_async_copy(
                rows.at[number], out_hbm.at[:, rounds[number], 0], sems.at[number]
            )
            copy.start()
            copies.append(copy)
    for copy in copies:
        copy.wait()


def late_kernel(count, parts, plan, place, early, *rest):
    pieces = rest[:parts]
    out_hbm, rows, sems = rest[parts:]
    number = slot_rounds(plan, count)[ROUNDS - 1]
    matrix = joined_matrix(place, parts, 1)
    half = pieces[0].shape[1] // 2
    size = rows.shape[0] // 2
    copies = []
    for h in range(2):
        block = placed_block(pieces, matrix, slice(h * half, (h + 1) * half))
        store_rows(rows, block, h * half)
        at = pl.ds(h * size, size)
        copy = pltpu.make_async_copy(rows.at[at], out_hbm.at[at, number, 0], sems.at[h])
        copy.start()
        copies.append(copy)
    for copy in copies:
        copy.wait()


def place_lags(plan, groups, pieces, count, stations, parts):
    pairs = stations * stations
    share = LAGS // parts
    tiles = pairs // LANES
    place = jnp.asarray(make_placing(stations, stations // parts, parts))
    smem = pl.BlockSpec(memory_space=pltpu.SMEM)
    vmem = pl.BlockSpec(memory_space=pltpu.VMEM)
    anywhere = pl.BlockSpec(memory_space=pl.ANY)
    shape = jax.ShapeDtypeStruct((share * tiles, ROUNDS, 1, LANES), F32)
    early = pl.pallas_call(
        functools.partial(early_kernel, count, parts, tuple(groups[:-1])),
        out_shape=shape,
        in_specs=[smem] + [vmem] * (1 + len(pieces) - parts),
        out_specs=anywhere,
        scratch_shapes=[
            pltpu.VMEM((ROUNDS - 1, share * tiles, LANES), F32),
            pltpu.SemaphoreType.DMA((ROUNDS - 1,)),
        ],
        compiler_params=pltpu.CompilerParams(vmem_limit_bytes=16 * 2**20),
        cost_estimate=expected(0.05),
        name="early",
    )(plan, place, *pieces[:-parts])
    out = pl.pallas_call(
        functools.partial(late_kernel, count, parts),
        out_shape=shape,
        in_specs=[smem, vmem, anywhere] + [vmem] * parts,
        out_specs=anywhere,
        scratch_shapes=[pltpu.VMEM((share * tiles, LANES), F32), pltpu.SemaphoreType.DMA((2,))],
        input_output_aliases={2: 0},
        compiler_params=pltpu.CompilerParams(vmem_limit_bytes=16 * 2**20),
        cost_estimate=expected(0.05),
        name="late",
    )(plan, place, early, *pieces[-parts:])
    out = out.reshape(share, tiles, ROUNDS, LANES)
    return out.transpose(0, 2, 1, 3).reshape(share, ROUNDS, pairs)


def join_kernel(order, *refs):
    parts, (out_up, out_down) = refs[:4], refs[4:]
    near_up, near_down, far_up, far_down = [parts[order.index(k)] for k in range(4)]
    half = near_up.shape[0]
    for out, first, second in ((out_up, near_up, far_up), (out_down, near_down, far_down)):
        out[:half] = first[...]
        out[half:] = second[...]


def join(near_up, near_down, far_up, far_down, order=(0, 1, 2, 3)):
    values = [near_up, near_down, far_up, far_down]
    vmem = pl.BlockSpec(memory_space=pltpu.VMEM)
    shape = (2 * near_up.shape[0],) + near_up.shape[1:]
    return pl.pallas_call(
        functools.partial(join_kernel, tuple(order)),
        out_shape=[jax.ShapeDtypeStruct(shape, BF)] * 2,
        in_specs=[vmem] * 4,
        out_specs=[vmem] * 2,
        compiler_params=pltpu.CompilerParams(vmem_limit_bytes=16 * 2**20),
        cost_estimate=expected(0.05),
        name="join",
    )(*[values[k] for k in order])


def swap(value, j):
    parts = lax.axis_size("seg")
    return lax.ppermute(value, "seg", [(i, i ^ j) for i in range(parts)])


def exchange(pieces):
    return [pieces[0]] + [swap(pieces[j], j) for j in range(1, len(pieces))]


def after(value, others):
    return lax.optimization_barrier((value, others))[0]


def per_device(records, plan):
    stations, windows, length = records.shape
    count = lax.axis_size("sta")
    parts = lax.axis_size("seg")
    quarter = stations // parts
    constants = make_table(length // CHUNKS, 2 * length)
    table, lag_table = jnp.asarray(constants), jnp.asarray(constants.T.copy())
    scaling = 1.0 / math.sqrt(4.0 * NBIN * windows * parts)

    white, *quarters = prepare(records, table, parts)
    near = jnp.concatenate([quarters[0], swap(quarters[1], 1)])
    sibling = swap(white, 1)
    far = jnp.concatenate([swap(quarters[j], j) for j in range(2, parts)])
    far = after(far, sibling)
    far, white_far = lax.optimization_barrier((far, white))
    across = swap(white_far, 2)

    ring = sorted(range(count), key=lambda b: b // 2 if b % 2 == 0 else count - 1 - b // 2)
    upward = [(ring[i], ring[(i + 1) % count]) for i in range(count)]
    downward = [(ring[i], ring[i - 1]) for i in range(count)]

    def up(value):
        return lax.ppermute(value, "sta", upward)

    def down(value):
        return lax.ppermute(value, "sta", downward)

    far, white_far = lax.optimization_barrier((far, white))
    across = swap(white_far, 2)
    near_own = widen_own([white, sibling])
    half = near.shape[0]
    places, blocks, arrived = [], [], []

    def arrive(step, first, from_left, from_right):
        places.extend([(count - step, first), (step, first)])
        blocks.extend([from_left, from_right])

    near_up, near_down = up(near), down(near)
    far_up, far_down = up(far), down(far)
    arrive(1, 0, near_up, near_down)
    arrive(1, half, far_up, far_down)
    near_up, near_down, near_own = lax.optimization_barrier((near_up, near_down, near_own))
    near_up, near_down = up(near_up), down(near_down)
    far_up, far_down = lax.optimization_barrier((far_up, far_down))
    far_up, far_down = up(far_up), down(far_down)
    arrive(2, 0, near_up, near_down)
    arrive(2, half, far_up, far_down)
    all_up, all_down = join(near_up, near_down, far_up, far_down)
    for step in range(3, (count - 1) // 2 + 1):
        arrived.append((list(places), list(blocks)))
        all_up, all_down, across = lax.optimization_barrier((all_up, all_down, across))
        all_up, all_down = up(all_up), down(all_down)
        arrive(step, 0, all_up, all_down)
    arrived.append((list(places), list(blocks)))
    far_own = widen_own([across, swap(across, 1)])
    groups = [(0, 1), (1, 2), (3, 1)]
    if count % 2 == 0:
        places.append((count // 2, 0))
        blocks.append(up(all_up))
    arrived.append((places, blocks))
    pieces = []
    for index, (first_slot, slots) in enumerate(groups):
        if index == 2:
            near_own = after(near_own, pieces[:parts])
        if index > 0:
            near_own = after(near_own, lags)
        at, values = arrived[index - len(groups)]
        lags = cross_lags(
            plan, lag_table, [near_own, far_own], at, values, first_slot, slots, count, parts, scaling
        )
        pieces = pieces + exchange(lags)
    return place_lags(plan, groups, pieces, count, stations, parts)


def solution(mesh):
    in_specs = (P("sta", "seg", None), P())
    out_specs = P("seg", None, "sta")
    return jax.shard_map(
        per_device, mesh=mesh, in_specs=in_specs, out_specs=out_specs, check_vma=False
    )
```

```python
import functools
import math

import jax
import jax.numpy as jnp
import ml_dtypes
import numpy as np
from jax import lax
from jax.experimental import pallas as pl
from jax.experimental.pallas import tpu as pltpu
from jax.sharding import PartitionSpec as P

NBIN = 1024
HALF = 64
ROUNDS = 4
LAGS = 2048
LANES = 128
TILES = NBIN // LANES
CHUNKS = 4
GROUP = 8
BF = jnp.bfloat16
F32 = jnp.float32


def make_table(rows, transform):
    phase = (np.arange(rows)[:, None] * np.arange(NBIN)[None, :]) % transform
    angle = phase * (2.0 * math.pi / transform)
    return np.concatenate([np.cos(angle), -np.sin(angle)], axis=1).astype(ml_dtypes.bfloat16)


def band_matrix():
    source = lax.broadcasted_iota(jnp.int32, (3 * LANES, LANES), 0) - LANES
    target = lax.broadcasted_iota(jnp.int32, (3 * LANES, LANES), 1)
    return jnp.where(jnp.abs(source - target) <= HALF, 1.0, 0.0).astype(BF)


def inverse_count(block, length):
    if 0 < block < length // LANES - 1:
        return 1.0 / (2 * HALF + 1)
    position = lax.broadcasted_iota(jnp.int32, (1, LANES), 1) + block * LANES
    counted = jnp.minimum(position, HALF) + jnp.minimum(length - 1 - position, HALF) + 1
    return 1.0 / counted.astype(F32)


def make_placing(stations, quarter, parts):
    width = stations * quarter
    place = np.zeros((parts, 2 * width, 2 * stations * stations), np.float32)
    for part in range(parts):
        for second in range(2):
            for s in range(stations):
                for t in range(quarter):
                    row = second * width + s * quarter + t
                    column = (second * stations + s) * stations + part * quarter + t
                    place[part, row, column] = 1.0
    return place.astype(ml_dtypes.bfloat16)


def lane_cycle(values):
    period = len(values)
    phase = lax.broadcasted_iota(jnp.int32, (1, LANES), 1) % period
    out = jnp.full((1, LANES), values[-1], F32)
    for index in range(period - 1):
        out = jnp.where(phase == index, values[index], out)
    return out


def even_lanes(shape):
    return lax.broadcasted_iota(jnp.int32, shape, 1) % 2 == 0


def eighth_turn():
    turns = [math.pi * k / 4.0 for k in range(8)]
    return lane_cycle([math.cos(t) for t in turns]), lane_cycle([math.sin(t) for t in turns])


def quarter_turns(real, imag, even, sign_real, sign_imag):
    return sign_real * jnp.where(even, real, imag), sign_imag * jnp.where(even, imag, real)


def banded_sum(stack, values, band):
    blocks, rows = len(values), values[0].shape[0]
    zero = jnp.zeros((rows, LANES), BF)
    for j in range(blocks):
        at = pl.ds(j * rows, rows)
        for k in range(3):
            b = j + k - 1
            block = values[b] if 0 <= b < blocks else zero
            stack[at, k * LANES : (k + 1) * LANES] = block
    total = jnp.dot(stack[: blocks * rows, :], band, preferred_element_type=F32)
    return [total[j * rows : (j + 1) * rows, :] for j in range(blocks)]


def prep_kernel(parts, windows, records_hbm, table_hbm, white, mine, *rest):
    others = rest[: parts - 1]
    records, table, stack, flat, spread, sems = rest[parts - 1 :]
    records_copy = pltpu.make_async_copy(records_hbm, records, sems.at[0])
    records_copy.start()
    copy = pltpu.make_async_copy(table_hbm, table, sems.at[1])
    copy.start()
    band_values = band_matrix()
    records_copy.wait()
    stations = white.shape[1]
    rows = stations * windows
    blocks = records.shape[0] // rows
    length = blocks * LANES
    chunk = length // CHUNKS
    signal = [
        jnp.concatenate(
            [
                records[pl.ds(j * windows + w, stations, stride=blocks * windows), :]
                for w in range(windows)
            ],
            axis=0,
        )
        for j in range(blocks)
    ]
    sums = banded_sum(stack, [jnp.abs(block).astype(BF) for block in signal], band_values)
    for j, total in enumerate(sums):
        at = slice(j * LANES, (j + 1) * LANES)
        level = total * inverse_count(j, length)
        value = (signal[j] / (level + 1e-05)).astype(BF)
        q, inside = divmod(j * LANES, chunk)
        flat[q * rows : (q + 1) * rows, inside : inside + LANES] = value
    copy.wait()
    product = jnp.dot(flat[...], table[...], preferred_element_type=F32)
    even = even_lanes((rows, LANES))
    sign_real = lane_cycle([1.0, 1.0, -1.0, -1.0])
    sign_imag = lane_cycle([1.0, -1.0, -1.0, 1.0])
    cosine, sine = eighth_turn()
    reals, imags, mags = [], [], []
    for j in range(TILES):
        at = slice(j * LANES, (j + 1) * LANES)
        at_imag = slice(NBIN + j * LANES, NBIN + (j + 1) * LANES)
        pr = [product[q * rows : (q + 1) * rows, at] for q in range(CHUNKS)]
        pi = [product[q * rows : (q + 1) * rows, at_imag] for q in range(CHUNKS)]
        turned = [
            quarter_turns(pr[q], pi[q], even, sign_real, sign_imag) for q in range(2, CHUNKS)
        ]
        first_real, first_imag = pr[0] + turned[0][0], pi[0] + turned[0][1]
        odd_real, odd_imag = pr[1] + turned[1][0], pi[1] + turned[1][1]
        real = first_real + (odd_real * cosine + odd_imag * sine)
        imag = first_imag + (odd_imag * cosine - odd_real * sine)
        reals.append(real)
        imags.append(imag)
        mags.append(jnp.sqrt(real * real + imag * imag).astype(BF))
    sums = banded_sum(stack, mags, band_values)
    for j, total in enumerate(sums):
        at = slice(j * LANES, (j + 1) * LANES)
        inverse = 1.0 / (total * inverse_count(j, NBIN) + 1e-06)
        spread[pl.ds(j, rows, stride=2 * TILES), :] = reals[j] * inverse
        spread[pl.ds(TILES + j, rows, stride=2 * TILES), :] = imags[j] * inverse
    me = lax.axis_index("seg")
    quarter = stations // parts
    white[...] = spread[...].reshape(windows, stations, 2 * TILES, LANES).astype(BF)
    for j, out in enumerate((mine, *others)):
        for w in range(windows):
            out[w] = white[w, pl.ds((me ^ j) * quarter, quarter)]


def prepare(records, table, parts):
    stations, windows, length = records.shape
    rows = stations * windows
    quarter = stations // parts
    blocks = length // LANES
    flat_records = records.reshape(stations, windows, blocks, LANES).transpose(0, 2, 1, 3)
    flat_records = flat_records.reshape(rows * blocks, LANES)
    small = jax.ShapeDtypeStruct((windows, quarter, 2 * TILES, LANES), BF)
    vmem = pl.BlockSpec(memory_space=pltpu.VMEM)
    return pl.pallas_call(
        functools.partial(prep_kernel, parts, windows),
        out_shape=[jax.ShapeDtypeStruct((windows, stations, 2 * TILES, LANES), BF)]
        + [small] * parts,
        in_specs=[pl.BlockSpec(memory_space=pltpu.HBM)] * 2,
        out_specs=[vmem] * (1 + parts),
        scratch_shapes=[
            pltpu.VMEM(flat_records.shape, F32),
            pltpu.VMEM(table.shape, BF),
            pltpu.VMEM((rows * (length // LANES), 3 * LANES), BF),
            pltpu.VMEM((CHUNKS * rows, length // CHUNKS), BF),
            pltpu.VMEM((rows * 2 * TILES, LANES), F32),
            pltpu.SemaphoreType.DMA((2,)),
        ],
        compiler_params=pltpu.CompilerParams(vmem_limit_bytes=52 * 2**20),
        cost_estimate=pl.CostEstimate(
            flops=2 * rows * length * 2 * NBIN, bytes_accessed=3 * 2**20, transcendentals=0
        ),
        name="prep",
    )(
        pltpu.with_memory_space_constraint(flat_records, pltpu.HBM),
        pltpu.with_memory_space_constraint(table, pltpu.HBM),
    )


def ring_place(block, count):
    half = block >> 1
    return jnp.where((block & 1) == 0, half, count - 1 - half)


def partner_steps(plan, count):
    me = lax.axis_index("sta")
    mine = ring_place(me, count)
    steps, keys = [], []
    for number in range(ROUNDS):
        step = ring_place(plan[number, me], count) - mine
        step = jnp.where(step < 0, step + count, step)
        steps.append(step)
        keys.append(jnp.minimum(step, count - step) * ROUNDS + number)
    ranks = []
    for number in range(ROUNDS):
        rank = jnp.int32(0)
        for other in range(ROUNDS):
            if other != number:
                rank = rank + jnp.where(keys[other] < keys[number], 1, 0)
        ranks.append(rank)
    return steps, ranks


def expected(microseconds):
    return pl.CostEstimate(
        flops=int(microseconds * 1.15e9), bytes_accessed=1024, transcendentals=0
    )


def widen_kernel(scale, *refs):
    blocks, own = refs[:-1], refs[-1]
    windows = blocks[0].shape[0]
    for j, block in enumerate(blocks):

        def widen(w, carry, j=j, block=block):
            raw = block[w].astype(F32) * scale
            real, imag = raw[:, :TILES], raw[:, TILES:]
            both = real + imag
            for group in range(own.shape[0]):
                at = slice(group * GROUP, (group + 1) * GROUP)
                own[group, 0, j * windows + w] = both[at]
                own[group, 1, j * windows + w] = real[at]
                own[group, 2, j * windows + w] = imag[at]
            return carry

        lax.fori_loop(0, windows, widen, 0)


def widen_own(blocks, scale):
    windows, stations = blocks[0].shape[:2]
    vmem = pl.BlockSpec(memory_space=pltpu.VMEM)
    return pl.pallas_call(
        functools.partial(widen_kernel, scale),
        out_shape=jax.ShapeDtypeStruct(
            (stations // GROUP, 3, len(blocks) * windows, GROUP, TILES, LANES), F32
        ),
        in_specs=[vmem] * len(blocks),
        out_specs=vmem,
        compiler_params=pltpu.CompilerParams(vmem_limit_bytes=16 * 2**20),
        cost_estimate=expected(0.05),
        name="widen",
    )(*blocks)


def widen_others(first_slot, slots, count, places, plan, candidates, other):
    steps, ranks = partner_steps(plan, count)
    for slot in range(slots):
        step = jnp.int32(0)
        for number in range(ROUNDS):
            step = jnp.where(ranks[number] == first_slot + slot, steps[number], step)
        for (offset, first), candidate in zip(places, candidates):

            @pl.when(step == offset)
            def _(candidate=candidate, slot=slot, first=first):
                def widen_other(turn, carry):
                    raw = candidate[pl.ds(turn * 4, 4)].astype(F32)
                    real, imag = raw[:, :, :TILES], raw[:, :, TILES:]
                    at = pl.ds(first + turn * 4, 4)
                    other[0, slot, at] = real
                    other[1, slot, at] = real + imag
                    other[2, slot, at] = imag - real
                    return carry

                lax.fori_loop(0, candidate.shape[0] // 4, widen_other, 0)


def sum_windows(owns, other, summed):
    groups, _, windows, group = owns[0].shape[:4]
    slots, _, quarter = other.shape[1:4]
    width = groups * group * quarter
    shift = groups.bit_length() - 1

    for slot in range(slots):

        def body(index, carry, slot=slot):
            kind, part = index >> shift, index & (groups - 1)
            mine = [own.at[part, kind] for own in owns]
            theirs = other.at[kind, slot]
            totals = [None] * (group * quarter)
            for half, own in enumerate(mine):
                for w in range(windows):
                    left = [own[w, s] for s in range(group)]
                    right = [theirs[half * windows + w, t] for t in range(quarter)]
                    for s in range(group):
                        for t in range(quarter):
                            term = left[s] * right[t]
                            old = totals[s * quarter + t]
                            totals[s * quarter + t] = term if old is None else old + term
            rows = summed.at[kind]
            base = (slot * width + part * (group * quarter)) * TILES
            for place in range(group * quarter):
                at = pl.multiple_of(base + place * TILES, TILES)
                rows[pl.ds(at, TILES), :] = totals[place]
            return carry

        lax.fori_loop(0, 3 * groups, body, 0)


def cross_kernel(first_slot, slots, count, places, parts, plan, table, *rest):
    owns, rest = rest[:2], rest[2:]
    others, rest = rest[: len(places)], rest[len(places) :]
    outs = rest[:parts]
    other, summed, operand = rest[parts:]
    stations = owns[0].shape[0] * owns[0].shape[3]
    widen_others(first_slot, slots, count, places, plan, others, other)
    sum_windows(owns, other, summed)
    width = stations * other.shape[3]
    columns = slots * width
    even = even_lanes((columns, LANES))
    sign_real = lane_cycle([1.0, -1.0, -1.0, 1.0])
    sign_imag = lane_cycle([1.0, 1.0, -1.0, -1.0])
    cosine, sine = eighth_turn()
    lane = lax.broadcasted_iota(jnp.int32, (1, LANES), 1)
    first_weight = jnp.where(lane == 0, 0.5, 1.0).astype(F32)
    for j in range(TILES):
        at = slice(j * LANES, (j + 1) * LANES)
        at_imag = slice(NBIN + j * LANES, NBIN + (j + 1) * LANES)
        kinds = [summed[kind, pl.ds(j, columns, stride=TILES), :] for kind in range(3)]
        real, imag = kinds[0] + kinds[2], kinds[0] - kinds[1]
        if j == 0:
            real, imag = real * first_weight, imag * first_weight
        turned = [(real, imag), (real * cosine - imag * sine, imag * cosine + real * sine)]
        turned += [quarter_turns(r, i, even, sign_real, sign_imag) for r, i in turned]
        for q in range(CHUNKS):
            rows = slice(q * columns, (q + 1) * columns)
            operand[rows, at] = turned[q][0].astype(BF)
            operand[rows, at_imag] = turned[q][1].astype(BF)
    block = jnp.dot(operand[...], table[...], preferred_element_type=F32)
    block = block.astype(BF)
    me = lax.axis_index("seg")
    for place in range(parts):

        @pl.when(me == place)
        def _(place=place):
            for j in range(parts):
                q = place ^ j
                outs[j][...] = block[q * columns : (q + 1) * columns]


def cross_lags(plan, table, owns, places, candidates, first_slot, slots, count, parts):
    windows, stations = owns[0].shape[2], owns[0].shape[0] * owns[0].shape[3]
    quarter = candidates[0].shape[1]
    columns = slots * stations * quarter
    share = LAGS // parts
    out = (columns, share)
    smem = pl.BlockSpec(memory_space=pltpu.SMEM)
    vmem = pl.BlockSpec(memory_space=pltpu.VMEM)
    operands = [table, *owns, *candidates]
    return pl.pallas_call(
        functools.partial(
            cross_kernel, first_slot, slots, count, tuple(places), parts
        ),
        out_shape=[jax.ShapeDtypeStruct(out, BF)] * parts,
        in_specs=[smem] + [vmem] * len(operands),
        out_specs=[vmem] * parts,
        scratch_shapes=[
            pltpu.VMEM((3, slots, 2 * windows, quarter, TILES, LANES), F32),
            pltpu.VMEM((3, columns * TILES, LANES), F32),
            pltpu.VMEM((CHUNKS * columns, 2 * NBIN), BF),
        ],
        compiler_params=pltpu.CompilerParams(vmem_limit_bytes=24 * 2**20),
        cost_estimate=expected(0.6 + 2.0 * slots),
        name="cross",
    )(plan, *operands)


def slot_rounds(plan, count):
    _, ranks = partner_steps(plan, count)
    rounds = []
    for slot in range(ROUNDS):
        number = jnp.int32(0)
        for other in range(1, ROUNDS):
            number = jnp.where(ranks[other] == slot, other, number)
        rounds.append(number)
    return rounds


def placed_block(pieces, matrix, at):
    joined = jnp.concatenate([piece[:, at] for piece in pieces], axis=0)
    return lax.dot_general(
        joined, matrix, (((0,), (0,)), ((), ())), preferred_element_type=F32
    )


def joined_matrix(place, parts, slots):
    me = lax.axis_index("seg")
    rows, columns = place.shape[1] * slots // 2, place.shape[2] * slots // 2
    return jnp.concatenate([place[me ^ j, :rows, :columns] for j in range(parts)], axis=0)


def store_rows(rows, block, first):
    tiles = block.shape[1] // LANES
    for tile in range(tiles):
        at = pl.ds(first * tiles + tile, block.shape[0], stride=tiles)
        rows[at, :] = block[:, tile * LANES : (tile + 1) * LANES]


def early_kernel(count, parts, groups, plan, place, *rest):
    pieces = rest[:-3]
    out_hbm, rows, sems = rest[-3:]
    pairs = place.shape[2] // 2
    rounds = slot_rounds(plan, count)
    copies = []
    for index, (first_slot, slots) in enumerate(groups):
        own = pieces[index * parts : (index + 1) * parts]
        block = placed_block(own, joined_matrix(place, parts, slots), slice(None))
        for slot in range(slots):
            number = first_slot + slot
            store_rows(rows.at[number], block[:, slot * pairs : (slot + 1) * pairs], 0)
            copy = pltpu.make_async_copy(
                rows.at[number], out_hbm.at[:, rounds[number], 0], sems.at[number]
            )
            copy.start()
            copies.append(copy)
    for copy in copies:
        copy.wait()


def late_kernel(count, parts, plan, place, early, *rest):
    pieces = rest[:parts]
    out_hbm, rows, sems = rest[parts:]
    number = slot_rounds(plan, count)[ROUNDS - 1]
    matrix = joined_matrix(place, parts, 1)
    half = pieces[0].shape[1] // 2
    size = rows.shape[0] // 2
    copies = []
    for h in range(2):
        block = placed_block(pieces, matrix, slice(h * half, (h + 1) * half))
        store_rows(rows, block, h * half)
        at = pl.ds(h * size, size)
        copy = pltpu.make_async_copy(rows.at[at], out_hbm.at[at, number, 0], sems.at[h])
        copy.start()
        copies.append(copy)
    for copy in copies:
        copy.wait()


def place_lags(plan, groups, pieces, count, stations, parts):
    pairs = stations * stations
    share = LAGS // parts
    tiles = pairs // LANES
    place = jnp.asarray(make_placing(stations, stations // parts, parts))
    smem = pl.BlockSpec(memory_space=pltpu.SMEM)
    vmem = pl.BlockSpec(memory_space=pltpu.VMEM)
    anywhere = pl.BlockSpec(memory_space=pl.ANY)
    shape = jax.ShapeDtypeStruct((share * tiles, ROUNDS, 1, LANES), F32)
    early = pl.pallas_call(
        functools.partial(early_kernel, count, parts, tuple(groups[:-1])),
        out_shape=shape,
        in_specs=[smem] + [vmem] * (1 + len(pieces) - parts),
        out_specs=anywhere,
        scratch_shapes=[
            pltpu.VMEM((ROUNDS - 1, share * tiles, LANES), F32),
            pltpu.SemaphoreType.DMA((ROUNDS - 1,)),
        ],
        compiler_params=pltpu.CompilerParams(vmem_limit_bytes=16 * 2**20),
        cost_estimate=expected(0.05),
        name="early",
    )(plan, place, *pieces[:-parts])
    out = pl.pallas_call(
        functools.partial(late_kernel, count, parts),
        out_shape=shape,
        in_specs=[smem, vmem, anywhere] + [vmem] * parts,
        out_specs=anywhere,
        scratch_shapes=[pltpu.VMEM((share * tiles, LANES), F32), pltpu.SemaphoreType.DMA((2,))],
        input_output_aliases={2: 0},
        compiler_params=pltpu.CompilerParams(vmem_limit_bytes=16 * 2**20),
        cost_estimate=expected(0.05),
        name="late",
    )(plan, place, early, *pieces[-parts:])
    out = out.reshape(share, tiles, ROUNDS, LANES)
    return out.transpose(0, 2, 1, 3).reshape(share, ROUNDS, pairs)


def join_kernel(order, *refs):
    parts, (out_up, out_down) = refs[:4], refs[4:]
    near_up, near_down, far_up, far_down = [parts[order.index(k)] for k in range(4)]
    half = near_up.shape[0]
    for out, first, second in ((out_up, near_up, far_up), (out_down, near_down, far_down)):
        out[:half] = first[...]
        out[half:] = second[...]


def join(near_up, near_down, far_up, far_down, order=(0, 1, 2, 3)):
    values = [near_up, near_down, far_up, far_down]
    vmem = pl.BlockSpec(memory_space=pltpu.VMEM)
    shape = (2 * near_up.shape[0],) + near_up.shape[1:]
    return pl.pallas_call(
        functools.partial(join_kernel, tuple(order)),
        out_shape=[jax.ShapeDtypeStruct(shape, BF)] * 2,
        in_specs=[vmem] * 4,
        out_specs=[vmem] * 2,
        compiler_params=pltpu.CompilerParams(vmem_limit_bytes=16 * 2**20),
        cost_estimate=expected(0.05),
        name="join",
    )(*[values[k] for k in order])


def swap(value, j):
    parts = lax.axis_size("seg")
    return lax.ppermute(value, "seg", [(i, i ^ j) for i in range(parts)])


def exchange(pieces):
    return [pieces[0]] + [swap(pieces[j], j) for j in range(1, len(pieces))]


def after(value, others):
    return lax.optimization_barrier((value, others))[0]


def per_device(records, plan):
    stations, windows, length = records.shape
    count = lax.axis_size("sta")
    parts = lax.axis_size("seg")
    quarter = stations // parts
    constants = make_table(length // CHUNKS, 2 * length)
    table, lag_table = jnp.asarray(constants), jnp.asarray(constants.T.copy())
    scaling = 1.0 / math.sqrt(4.0 * NBIN * windows * parts)

    white, *quarters = prepare(records, table, parts)
    near = jnp.concatenate([quarters[0], swap(quarters[1], 1)])
    sibling = swap(white, 1)
    far = jnp.concatenate([swap(quarters[j], j) for j in range(2, parts)])
    far = after(far, sibling)
    far, white_far = lax.optimization_barrier((far, white))
    across = swap(white_far, 2)

    ring = sorted(range(count), key=lambda b: b // 2 if b % 2 == 0 else count - 1 - b // 2)
    upward = [(ring[i], ring[(i + 1) % count]) for i in range(count)]
    downward = [(ring[i], ring[i - 1]) for i in range(count)]

    def up(value):
        return lax.ppermute(value, "sta", upward)

    def down(value):
        return lax.ppermute(value, "sta", downward)

    far, white_far = lax.optimization_barrier((far, white))
    across = swap(white_far, 2)
    near_own = widen_own([white, sibling], 2.0 * scaling)
    half = near.shape[0]
    places, blocks, arrived = [], [], []

    def arrive(step, first, from_left, from_right):
        places.extend([(count - step, first), (step, first)])
        blocks.extend([from_left, from_right])

    near_up, near_down = up(near), down(near)
    far_up, far_down = up(far), down(far)
    arrive(1, 0, near_up, near_down)
    arrive(1, half, far_up, far_down)
    near_up, near_down, near_own = lax.optimization_barrier((near_up, near_down, near_own))
    near_up, near_down = up(near_up), down(near_down)
    far_up, far_down = lax.optimization_barrier((far_up, far_down))
    far_up, far_down = up(far_up), down(far_down)
    arrive(2, 0, near_up, near_down)
    arrive(2, half, far_up, far_down)
    all_up, all_down = join(near_up, near_down, far_up, far_down)
    for step in range(3, (count - 1) // 2 + 1):
        arrived.append((list(places), list(blocks)))
        all_up, all_down, across = lax.optimization_barrier((all_up, all_down, across))
        all_up, all_down = up(all_up), down(all_down)
        arrive(step, 0, all_up, all_down)
    arrived.append((list(places), list(blocks)))
    far_own = widen_own([across, swap(across, 1)], 2.0 * scaling)
    groups = [(0, 1), (1, 2), (3, 1)]
    if count % 2 == 0:
        places.append((count // 2, 0))
        blocks.append(up(all_up))
    arrived.append((places, blocks))
    pieces = []
    for index, (first_slot, slots) in enumerate(groups):
        if index == 2:
            near_own = after(near_own, pieces[:parts])
        if index > 0:
            near_own = after(near_own, lags)
        at, values = arrived[index - len(groups)]
        lags = cross_lags(
            plan, lag_table, [near_own, far_own], at, values, first_slot, slots, count, parts
        )
        pieces = pieces + exchange(lags)
    return place_lags(plan, groups, pieces, count, stations, parts)


def solution(mesh):
    in_specs = (P("sta", "seg", None), P())
    out_specs = P("seg", None, "sta")
    return jax.shard_map(
        per_device, mesh=mesh, in_specs=in_specs, out_specs=out_specs, check_vma=False
    )
```
